32 devices in a mesh: batch: 16 (over z, y, core), rows: 2 (over x).
Axes of the slice: x: 2, y: 2, z: 4, core: 2. Of those that a mesh axis runs over, the one named last changes fastest.
Arguments:
- images: bfloat16 [16, 4, 80, 2048], P('batch', 'rows'), may hold values from -6 to 6
- crop_height: int32 [16], replicated, may hold values from 3 to 4, as said below
- crop_width: int32 [16], replicated, may hold values from 21 to 80, as said below
- w_first: bfloat16 [2048, 512], P('batch'), may hold values from -0.125 to 0.125
- gain_first: bfloat16 [512], P('batch'), may hold values from 0.5 to 1.5
- shift_first: bfloat16 [512], P('batch'), may hold values from -3 to 3
- w_middle: bfloat16 [9, 512, 512], P(None, 'batch'), may hold values from -0.09375 to 0.09375
- gain_middle: bfloat16 [512], P('batch'), may hold values from 0.5 to 1.5
- shift_middle: bfloat16 [512], P('batch'), may hold values from -3 to 3
- w_last: bfloat16 [512, 2048], P('batch'), may hold values from -0.25 to 0.25
- gain_last: bfloat16 [2048], P('batch'), may hold values from 0.5 to 1.5
- shift_last: bfloat16 [2048], P('batch'), may hold values from -3 to 3
- w_reduce: bfloat16 [2048, 512], P('batch'), may hold values from -0.125 to 0.125
- w_heads: bfloat16 [4, 9, 512, 512], P('rows', None, 'batch'), may hold values from -0.09375 to 0.09375
- w_message: bfloat16 [4, 9, 512, 512], P('rows', None, 'batch'), may hold values from -0.09375 to 0.09375
- w_gates: bfloat16 [2, 512, 512], P(None, 'batch'), may hold values from -0.25 to 0.25
- w_classes: bfloat16 [512, 40], P('batch'), may hold values from -0.25 to 0.25
- depth_cot: bfloat16 [16, 4, 80, 512], P('batch', 'rows'), may hold values from -6 to 6
- class_cot: bfloat16 [16, 4, 80, 40], P('batch', 'rows'), may hold values from -6 to 6
Outputs:
- depth_stream: bfloat16 [16, 4, 80, 512], P('batch', 'rows')
- class_logits: bfloat16 [16, 4, 80, 40], P('batch', 'rows')
- image_grad: float32 [16, 4, 80, 2048], P('batch', 'rows')
- grad_first: float32 [2048, 512], P('batch')
- grad_gain_first: float32 [512], P('batch')
- grad_shift_first: float32 [512], P('batch')
- grad_middle: float32 [9, 512, 512], P(None, 'batch')
- grad_gain_middle: float32 [512], P('batch')
- grad_shift_middle: float32 [512], P('batch')
- grad_last: float32 [512, 2048], P('batch')
- grad_gain_last: float32 [2048], P('batch')
- grad_shift_last: float32 [2048], P('batch')
- grad_reduce: float32 [2048, 512], P('batch')
- grad_heads: float32 [4, 9, 512, 512], P('rows', None, 'batch')
- grad_message: float32 [4, 9, 512, 512], P('rows', None, 'batch')
- grad_gates: float32 [2, 512, 512], P(None, 'batch')
- grad_classes: float32 [512, 40], P('batch')
The draws below stay inside these ranges and needn't reach their ends.
Inputs may be any that keep to these rules, and one draw needn't show every extreme that they name: `crop_height`: every image's crop reaches into the last row block: crop heights exceed 4 - 2; some image has the full height. `crop_width`: crops of the coarse maps use at most half of the columns; some image has the full width.
All inputs are finite; a program needn't handle non-finite values.
Results may differ from the reference program's by a relative error of at most 0.02.
Values may be sent and summed in bfloat16 or wider, within the bound.
A program may use at most 384 MiB of HBM per device.

```python
import jax
import jax.numpy as jnp
from jax import lax

CB = 2048
C = 512
NCLS = 40
TASKS = 4
W = 80
ROW_DEV = 2
IMAGES = 16
HEIGHT = 4


def crop_pair(key):
    keys = jax.random.split(key, 5)
    positions = jnp.arange(IMAGES, dtype=jnp.int32)
    chosen = jax.random.randint(keys[0], (), 0, IMAGES)
    heights = jax.random.randint(keys[1], (IMAGES,), HEIGHT - ROW_DEV + 1, HEIGHT + 1)
    heights = jnp.where(positions == chosen, HEIGHT, heights)
    coarse = jax.random.randint(keys[2], (IMAGES,), 0, 2)
    wide_cols = jax.random.randint(keys[3], (IMAGES,), W // 2 + 1, W + 1)
    narrow_cols = jax.random.randint(keys[4], (IMAGES,), W // 4 + 1, W // 2 + 1)
    widths = jnp.where(coarse == 1, narrow_cols, wide_cols)
    widths = jnp.where(positions == chosen, W, widths)
    return (heights.astype(jnp.int32), widths.astype(jnp.int32))


def draw_crop_height(key, part):
    return crop_pair(key)[0]


def draw_crop_width(key, part):
    return crop_pair(key)[1]


def shard_levels(key, extent, cuts, low, high):
    level, own = 1.0, jax.random.fold_in(key, 6)
    for axis_at, blocks in cuts:
        steps = jnp.exp(jax.random.uniform(jax.random.fold_in(own, axis_at), (blocks,), jnp.float32, low / len(cuts), high / len(cuts)))
        level = level * jnp.repeat(steps, extent[axis_at] // blocks).reshape([-1 if axis == axis_at else 1 for axis in range(len(extent))])
    return level


def normal_values(key, shape, width, bound, cuts=(), kind=jnp.bfloat16):
    loudness = shard_levels(key, shape, cuts, -0.22, 0.18) if cuts else 1.0
    array = jax.random.normal(key, shape, jnp.float32) * width * loudness
    return jnp.minimum(jnp.maximum(array, -bound), bound).astype(kind)


def setup_inputs(seed: int = 0) -> dict:
    key_of = jax.random.split(jax.random.key(seed), 20)
    return {
        "images": normal_values(key_of[0], (IMAGES, HEIGHT, W, CB), 1.0, 6.0, ((0, 16), (1, 2))),
        "crop_height": draw_crop_height(jax.random.fold_in(key_of[19], 71), 0),
        "crop_width": draw_crop_width(jax.random.fold_in(key_of[19], 71), 0),
        "w_first": normal_values(key_of[3], (CB, C), CB ** -0.5, 0.125, ((0, 16),)),
        "gain_first": jnp.clip(0.5 + 1.0 * jax.random.uniform(key_of[4], (C,), jnp.float32) ** shard_levels(key_of[4], (C,), ((0, 16),), -0.2, 0.2), 0.5, 1.5).astype(jnp.bfloat16),
        "shift_first": normal_values(key_of[5], (C,), 0.5, 3.0, ((0, 16),)),
        "w_middle": normal_values(key_of[6], (9, C, C), (9 * C) ** -0.5, 0.09375, ((1, 16),)),
        "gain_middle": jnp.clip(0.5 + 1.0 * jax.random.uniform(key_of[7], (C,), jnp.float32) ** shard_levels(key_of[7], (C,), ((0, 16),), -0.2, 0.2), 0.5, 1.5).astype(jnp.bfloat16),
        "shift_middle": normal_values(key_of[8], (C,), 0.5, 3.0, ((0, 16),)),
        "w_last": normal_values(key_of[9], (C, CB), C ** -0.5, 0.25, ((0, 16),)),
        "gain_last": jnp.clip(0.5 + 1.0 * jax.random.uniform(key_of[10], (CB,), jnp.float32) ** shard_levels(key_of[10], (CB,), ((0, 16),), -0.2, 0.2), 0.5, 1.5).astype(jnp.bfloat16),
        "shift_last": normal_values(key_of[11], (CB,), 0.5, 3.0, ((0, 16),)),
        "w_reduce": normal_values(key_of[12], (CB, C), CB ** -0.5, 0.125, ((0, 16),)),
        "w_heads": normal_values(key_of[13], (TASKS, 9, C, C), (9 * C) ** -0.5, 0.09375, ((0, 2), (2, 16))),
        "w_message": normal_values(key_of[14], (TASKS, 9, C, C), (9 * C) ** -0.5, 0.09375, ((0, 2), (2, 16))),
        "w_gates": normal_values(key_of[15], (2, C, C), C ** -0.5, 0.25, ((1, 16),)),
        "w_classes": normal_values(key_of[16], (C, NCLS), C ** -0.5, 0.25, ((0, 16),)),
        "depth_cot": normal_values(key_of[17], (IMAGES, HEIGHT, W, C), 1.0, 6.0, ((0, 16), (1, 2))),
        "class_cot": normal_values(key_of[18], (IMAGES, HEIGHT, W, NCLS), 1.0, 6.0, ((0, 16), (1, 2))),
    }


EPS = 1e-05

@jax.custom_vjp
def low(v):
    return lax.optimization_barrier(v.astype(jnp.bfloat16)).astype(jnp.float32)

@jax.custom_vjp
def low_back(v):
    return v

def low_keep(v):
    return (low(v), None)

def low_pass(kept, grad):
    return (grad,)

def back_keep(v):
    return (v, None)

def back_low(kept, grad):
    return (low(grad),)
low.defvjp(low_keep, low_pass)
low_back.defvjp(back_keep, back_low)

def gelu_tanh(values):
    return jax.nn.gelu(values, approximate=True)

def project(values, weight):
    return jnp.einsum('nhwj,jk->nhwk', values, weight, precision=lax.Precision.HIGHEST)

def conv_same(values, kernel):
    shaped = kernel.reshape(3, 3, kernel.shape[1], kernel.shape[2])
    return lax.conv_general_dilated(values, shaped, (1, 1), 'SAME', dimension_numbers=('NHWC', 'HWIO', 'NHWC'), precision=lax.Precision.HIGHEST)

def batch_norm(pre_act, gain_vec, shift_vec, pixel_mask, valid_count):
    mean_vec = lax.optimization_barrier(jnp.sum(pre_act * pixel_mask, axis=(0, 1, 2))) / valid_count
    variance = lax.optimization_barrier(jnp.sum(pre_act * pre_act * pixel_mask, axis=(0, 1, 2))) / valid_count - mean_vec * mean_vec
    return (pre_act - mean_vec) * lax.rsqrt(variance + EPS) * gain_vec + shift_vec

def crop_mask(crop_height, crop_width):
    row_ids = jnp.arange(HEIGHT, dtype=jnp.int32)
    col_ids = jnp.arange(W, dtype=jnp.int32)
    inside = (row_ids[None, :, None] < crop_height[:, None, None]) & (col_ids[None, None, :] < crop_width[:, None, None])
    return inside.astype(jnp.float32)[..., None]

def forward(images, w_first, gain_first, shift_first, w_middle, gain_middle, shift_middle, w_last, gain_last, shift_last, w_reduce, w_heads, w_message, w_gates, w_classes, pixel_mask, valid_count):
    masked_in = images * pixel_mask
    pre_first = low_back(project(low(masked_in), w_first))
    act_first = low(gelu_tanh(batch_norm(pre_first, gain_first, shift_first, pixel_mask, valid_count)) * pixel_mask)
    pre_middle = low_back(conv_same(act_first, w_middle))
    act_middle = low(gelu_tanh(batch_norm(pre_middle, gain_middle, shift_middle, pixel_mask, valid_count)) * pixel_mask)
    pre_last = low_back(project(act_middle, w_last))
    block_out = low(gelu_tanh(batch_norm(pre_last, gain_last, shift_last, pixel_mask, valid_count) + masked_in) * pixel_mask)
    reduced = low(low_back(project(block_out, w_reduce)))
    features = []
    messages = []
    for task in range(TASKS):
        feature = low(gelu_tanh(low_back(conv_same(reduced, w_heads[task]))) * pixel_mask)
        features.append(feature)
        messages.append(low(low_back(conv_same(feature, w_message[task]))))
    gate_depth = jax.nn.sigmoid(low_back(project(features[0], w_gates[0])))
    gate_class = jax.nn.sigmoid(low_back(project(features[3], w_gates[1])))
    depth_stream = (features[0] + gate_depth * (messages[1] + messages[2] + messages[3])) * pixel_mask
    merged = low(features[3] + gate_class * (messages[0] + messages[1] + messages[2]))
    class_logits = project(merged, w_classes) * pixel_mask
    return (depth_stream, class_logits)

def reference(images, crop_height, crop_width, w_first, gain_first, shift_first, w_middle, gain_middle, shift_middle, w_last, gain_last, shift_last, w_reduce, w_heads, w_message, w_gates, w_classes, depth_cot, class_cot):
    pixel_mask = crop_mask(crop_height, crop_width)
    valid_count = jnp.sum(crop_height * crop_width).astype(jnp.float32)

    def run(images_f, first_f, gfirst_f, sfirst_f, middle_f, gmiddle_f, smiddle_f, last_f, glast_f, slast_f, reduce_f, heads_f, message_f, gates_f, classes_f):
        return forward(images_f, first_f, gfirst_f, sfirst_f, middle_f, gmiddle_f, smiddle_f, last_f, glast_f, slast_f, reduce_f, heads_f, message_f, gates_f, classes_f, pixel_mask, valid_count)
    inputs = [member.astype(jnp.float32) for member in (images, w_first, gain_first, shift_first, w_middle, gain_middle, shift_middle, w_last, gain_last, shift_last, w_reduce, w_heads, w_message, w_gates, w_classes)]
    outputs, pull = jax.vjp(run, *inputs)
    grads = pull((depth_cot.astype(jnp.float32), class_cot.astype(jnp.float32)))
    return (outputs[0].astype(jnp.bfloat16), outputs[1].astype(jnp.bfloat16), grads[0], grads[1], grads[2], grads[3], grads[4], grads[5], grads[6], grads[7], grads[8], grads[9], grads[10], grads[11], grads[12], grads[13], grads[14])
```

```python
import functools
from types import SimpleNamespace

import numpy as np
import jax
import jax.numpy as jnp
from jax import lax
from jax.sharding import PartitionSpec as P
from jax.experimental import pallas as pl
from jax.experimental.pallas import tpu as pltpu

EPS = 1e-05
MESH = pl.DeviceIdType.MESH
F32 = jnp.float32
BF16 = jnp.bfloat16
ROOT = 0.7978845608028654
CUBE = 0.044715
SEMS = 320


def dot(left, right):
    return jnp.dot(left, right, preferred_element_type=F32)


def dot_last(left, right):
    return lax.dot_general(left, right, (((1,), (1,)), ((), ())), preferred_element_type=F32)


def dot_first(left, right):
    return lax.dot_general(left, right, (((0,), (0,)), ((), ())), preferred_element_type=F32)


def gelu_of(v):
    return 0.5 * v * (1.0 + jnp.tanh(ROOT * (v + CUBE * v * v * v)))


def slope_of(v):
    t = jnp.tanh(ROOT * (v + CUBE * v * v * v))
    return 0.5 * (1.0 + t) + 0.5 * v * (1.0 - t * t) * (ROOT * (1.0 + 3.0 * CUBE * v * v))


def rows_loop(total, chunk, step):
    def body(index, carry):
        step(pl.multiple_of(index * chunk, chunk))
        return carry

    lax.fori_loop(0, total // chunk, body, 0)


class Copy:
    def __init__(self, remote, links, index, like):
        self.remote, self.links, self.index, self.like = remote, links, index, like

    def wait_recv(self):
        if self.like is None:
            self.remote.wait_recv()
        else:
            ref = self.like(1)
            pltpu.make_async_copy(ref, ref, self.links.recv.at[self.index]).wait()

    def wait_send(self):
        if self.like is None:
            self.remote.wait_send()
        else:
            ref = self.like(0)
            pltpu.make_async_copy(ref, ref, self.links.send.at[self.index]).wait()


class Links:
    def __init__(self, send, recv, local):
        self.send, self.recv, self.local = send, recv, local
        self.used, self.local_used = 0, 0
        self.open = []

    def push(self, src, dst, device, when=None, like=None):
        i = self.used
        self.used += 1
        send, recv = self.send.at[i], self.recv.at[i]
        remote = pltpu.make_async_remote_copy(
            src_ref=src, dst_ref=dst, send_sem=send, recv_sem=recv, device_id=device, device_id_type=MESH
        )
        if when is None:
            remote.start()
        else:
            pl.when(when)(remote.start)
        cp = Copy(remote, self, i, like)
        self.open.append((cp, when))
        return cp

    def near(self, src, dst):
        i = self.local_used
        self.local_used += 1
        cp = pltpu.make_async_copy(src, dst, self.local.at[i])
        cp.start()
        return cp

    def drain(self, scoped=False):
        kept = []
        for cp, when in self.open:
            if scoped and cp.like is not None:
                kept.append((cp, when))
            elif when is None:
                cp.wait_send()
            else:
                pl.when(when)(cp.wait_send)
        self.open = kept


def wait(copies, when=None):
    def run():
        for cp in copies:
            cp.wait_recv()

    if when is None:
        run()
    else:
        pl.when(when)(run)


def lanes(mask, width):
    return jnp.concatenate([mask] * (width // 128), axis=1) if width > 128 else mask


def padded_2(cells, sides, width):
    for axis, dim in sides:
        count = lax.axis_size(axis)
        ends = count - 1
        head = lax.slice_in_dim(cells, 0, width, axis=dim)
        tail = lax.slice_in_dim(cells, cells.shape[dim] - width, cells.shape[dim], axis=dim)
        cells = jnp.concatenate(
            [
                lax.ppermute(tail, axis, [(i, (i + 1) % count) for i in range(ends)]),
                cells,
                lax.ppermute(head, axis, [((i + 1) % count, i) for i in range(ends)]),
            ],
            axis=dim,
        )
    return cells


def gelu_tanh(values):
    return jax.nn.gelu(values, approximate=True)


def gelu_slope(values, upstream):
    return jax.vjp(gelu_tanh, values)[1](upstream)[0]


def project(values, weight):
    return jnp.einsum("nrcj,jk->nrck", values, weight, preferred_element_type=jnp.float32)


def project_back(upstream, weight):
    return jnp.einsum("nrck,jk->nrcj", upstream, weight, preferred_element_type=jnp.float32)


def outer_sum(values, upstream):
    return jnp.einsum("nrcj,nrck->jk", values, upstream, preferred_element_type=jnp.float32)


def widen(padded):
    return jnp.pad(padded, ((0, 0), (0, 0), (1, 1), (0, 0)))


def halo_value(values):
    return padded_2(values, (("rows", 1),), 1)


def halo_grad(values):
    return padded_2(values, (("rows", 1),), 1)


def conv_apply(padded, kernel):
    row_count = padded.shape[1] - 2
    col_count = padded.shape[2]
    widened = widen(padded)
    running = jnp.zeros((padded.shape[0], row_count, col_count, kernel.shape[2]), jnp.float32)
    for tap_index in range(9):
        shift_down = tap_index // 3
        shift_right = tap_index % 3
        running = running + project(
            widened[
                :, shift_down : shift_down + row_count, shift_right : shift_right + col_count, :
            ],
            kernel[tap_index],
        )
    return running


def conv_kernel_grad(padded, upstream):
    row_count = upstream.shape[1]
    col_count = upstream.shape[2]
    widened = widen(padded)
    return jnp.stack(
        [
            outer_sum(
                widened[
                    :,
                    tap_index // 3 : tap_index // 3 + row_count,
                    tap_index % 3 : tap_index % 3 + col_count,
                    :,
                ],
                upstream,
            )
            for tap_index in range(9)
        ]
    )


def conv_input_grad(padded_grad, kernel):
    row_count = padded_grad.shape[1] - 2
    col_count = padded_grad.shape[2]
    widened = widen(padded_grad)
    running = jnp.zeros((padded_grad.shape[0], row_count, col_count, kernel.shape[1]), jnp.float32)
    for tap_index in range(9):
        shift_down = tap_index // 3
        shift_right = tap_index % 3
        running = running + project_back(
            widened[
                :,
                2 - shift_down : 2 - shift_down + row_count,
                2 - shift_right : 2 - shift_right + col_count,
                :,
            ],
            kernel[tap_index],
        )
    return running


def crop_mask(height, width, first_row, row_count, col_count):
    row_ids = first_row + jnp.arange(row_count, dtype=jnp.int32)
    col_ids = jnp.arange(col_count, dtype=jnp.int32)
    inside = (row_ids[None, :, None] < height[:, None, None]) & (
        col_ids[None, None, :] < width[:, None, None]
    )
    return inside.astype(jnp.float32)[..., None]


def norm_forward(pre_act, pixel_mask, gain_vec, shift_vec, valid_count):
    sums = jnp.sum(pre_act * pixel_mask, axis=(0, 1, 2))
    squares = jnp.sum(pre_act * pre_act * pixel_mask, axis=(0, 1, 2))
    sums, squares = lax.psum((sums, squares), ("batch", "rows"))
    mean_vec = sums / valid_count
    inv_std = lax.rsqrt(squares / valid_count - mean_vec * mean_vec + EPS)
    normal = (pre_act - mean_vec) * inv_std
    return (normal, inv_std, normal * gain_vec + shift_vec)


def norm_backward(upstream, normal, inv_std, gain_vec, pixel_mask, valid_count):
    shift_part = jnp.sum(upstream, axis=(0, 1, 2))
    gain_part = jnp.sum(upstream * normal, axis=(0, 1, 2))
    shift_part, gain_part = lax.psum((shift_part, gain_part), ("batch", "rows"))
    d_pre = (
        pixel_mask
        * gain_vec
        * inv_std
        * (upstream - shift_part / valid_count - normal * gain_part / valid_count)
    )
    return (d_pre, gain_part, shift_part)


def task_forward(padded_in, heads, messages, pixel_mask, pad_rows):
    pre_list = []
    feat_list = []
    padded_feats = []
    message_list = []
    for task in range(heads.shape[0]):
        pre_act = conv_apply(padded_in, heads[task])
        feature = (gelu_tanh(pre_act) * pixel_mask).astype(jnp.bfloat16)
        padded_feat = pad_rows(feature)
        pre_list.append(pre_act)
        feat_list.append(feature)
        padded_feats.append(padded_feat)
        message_list.append(conv_apply(padded_feat, messages[task]).astype(jnp.bfloat16))
    return (pre_list, feat_list, padded_feats, message_list)


def task_backward(
    padded_in,
    heads,
    messages,
    pixel_mask,
    pre_list,
    padded_feats,
    feat_grads,
    message_grads,
    pad_grad,
):
    input_grad = jnp.zeros(
        padded_in.shape[:1] + (padded_in.shape[1] - 2,) + padded_in.shape[2:], jnp.float32
    )
    head_grads = []
    kernel_grads = []
    for task in range(heads.shape[0]):
        low_message = message_grads[task].astype(jnp.bfloat16)
        kernel_grads.append(conv_kernel_grad(padded_feats[task], low_message))
        feat_grad = feat_grads[task] + conv_input_grad(pad_grad(low_message), messages[task])
        low_pre = gelu_slope(pre_list[task], feat_grad * pixel_mask).astype(jnp.bfloat16)
        head_grads.append(conv_kernel_grad(padded_in, low_pre))
        input_grad = input_grad + conv_input_grad(pad_grad(low_pre), heads[task])
    return (input_grad, jnp.stack(head_grads), jnp.stack(kernel_grads))


def streams_forward(features, messages, gates_all, classes_all, pixel_mask):
    gate_depth = jax.nn.sigmoid(project(features[0], gates_all[0]))
    gate_class = jax.nn.sigmoid(project(features[3], gates_all[1]))
    depth_sum = (
        messages[1].astype(jnp.float32)
        + messages[2].astype(jnp.float32)
        + messages[3].astype(jnp.float32)
    )
    class_sum = (
        messages[0].astype(jnp.float32)
        + messages[1].astype(jnp.float32)
        + messages[2].astype(jnp.float32)
    )
    depth_stream = (features[0].astype(jnp.float32) + gate_depth * depth_sum) * pixel_mask
    merged = (features[3].astype(jnp.float32) + gate_class * class_sum).astype(jnp.bfloat16)
    class_logits = project(merged, classes_all) * pixel_mask
    return (depth_stream, class_logits, merged, gate_depth, gate_class, depth_sum, class_sum)


def streams_backward(
    features,
    merged,
    gate_depth,
    gate_class,
    depth_sum,
    class_sum,
    depth_cot,
    class_cot,
    gates_all,
    classes_all,
    pixel_mask,
):
    depth_grad = depth_cot.astype(jnp.float32) * pixel_mask
    logit_grad = (class_cot.astype(jnp.float32) * pixel_mask).astype(jnp.bfloat16)
    grad_classes = outer_sum(merged, logit_grad)
    merged_grad = project_back(logit_grad, classes_all)
    gate_depth_grad = (depth_grad * depth_sum * gate_depth * (1.0 - gate_depth)).astype(
        jnp.bfloat16
    )
    gate_class_grad = (merged_grad * class_sum * gate_class * (1.0 - gate_class)).astype(
        jnp.bfloat16
    )
    grad_gates = jnp.stack(
        [outer_sum(features[0], gate_depth_grad), outer_sum(features[3], gate_class_grad)]
    )
    depth_feat = depth_grad + project_back(gate_depth_grad, gates_all[0])
    class_feat = merged_grad + project_back(gate_class_grad, gates_all[1])
    depth_message = depth_grad * gate_depth
    class_message = merged_grad * gate_class
    nothing = jnp.zeros_like(depth_grad)
    feat_grads = [depth_feat, nothing, nothing, class_feat]
    message_grads = [
        class_message,
        depth_message + class_message,
        depth_message + class_message,
        depth_message,
    ]
    return (feat_grads, message_grads, grad_gates, grad_classes)


def shards(
    images,
    crop_height,
    crop_width,
    w_first,
    gain_first,
    shift_first,
    w_middle,
    gain_middle,
    shift_middle,
    w_last,
    gain_last,
    shift_last,
    w_reduce,
    w_heads,
    w_message,
    w_gates,
    w_classes,
    depth_cot,
    class_cot,
):
    image_index = lax.axis_index("batch")
    batch_count = lax.axis_size("batch")
    row_count = images.shape[1]
    col_count = images.shape[2]
    height = lax.dynamic_slice_in_dim(crop_height, image_index, 1, 0)
    width = lax.dynamic_slice_in_dim(crop_width, image_index, 1, 0)
    pixel_mask = crop_mask(height, width, lax.axis_index("rows") * row_count, row_count, col_count)
    valid_count = jnp.sum(crop_height * crop_width).astype(jnp.float32)
    gathered = (
        lax.all_gather(w_first, "batch", axis=0, tiled=True),
        lax.all_gather(w_middle, "batch", axis=1, tiled=True),
        lax.all_gather(w_last, "batch", axis=0, tiled=True),
        lax.all_gather(w_reduce, "batch", axis=0, tiled=True),
        lax.all_gather(w_gates, "batch", axis=1, tiled=True),
        lax.all_gather(w_classes, "batch", axis=0, tiled=True),
        lax.all_gather(gain_first, "batch", axis=0, tiled=True),
        lax.all_gather(shift_first, "batch", axis=0, tiled=True),
        lax.all_gather(gain_middle, "batch", axis=0, tiled=True),
        lax.all_gather(shift_middle, "batch", axis=0, tiled=True),
        lax.all_gather(gain_last, "batch", axis=0, tiled=True),
        lax.all_gather(shift_last, "batch", axis=0, tiled=True),
        lax.all_gather(w_heads, "batch", axis=2, tiled=True),
        lax.all_gather(w_message, "batch", axis=2, tiled=True),
    )
    first_all = gathered[0]
    middle_all = gathered[1]
    last_all = gathered[2]
    reduce_all = gathered[3]
    gates_all = gathered[4]
    classes_all = gathered[5]
    gain_one = gathered[6].astype(jnp.float32)
    shift_one = gathered[7].astype(jnp.float32)
    gain_two = gathered[8].astype(jnp.float32)
    shift_two = gathered[9].astype(jnp.float32)
    gain_three = gathered[10].astype(jnp.float32)
    shift_three = gathered[11].astype(jnp.float32)
    heads_own = gathered[12]
    message_own = gathered[13]
    masked_in = images.astype(jnp.float32) * pixel_mask
    low_in = masked_in.astype(jnp.bfloat16)
    pre_first = project(low_in, first_all)
    normal_first, std_first, out_first = norm_forward(
        pre_first, pixel_mask, gain_one, shift_one, valid_count
    )
    act_first = (gelu_tanh(out_first) * pixel_mask).astype(jnp.bfloat16)
    padded_first = halo_value(act_first)
    pre_middle = conv_apply(padded_first, middle_all)
    normal_middle, std_middle, out_middle = norm_forward(
        pre_middle, pixel_mask, gain_two, shift_two, valid_count
    )
    act_middle = (gelu_tanh(out_middle) * pixel_mask).astype(jnp.bfloat16)
    pre_last = project(act_middle, last_all)
    normal_last, std_last, out_last = norm_forward(
        pre_last, pixel_mask, gain_three, shift_three, valid_count
    )
    summed = out_last + masked_in
    block_out = (gelu_tanh(summed) * pixel_mask).astype(jnp.bfloat16)
    low_reduced = project(block_out, reduce_all).astype(jnp.bfloat16)
    heads_all, message_all = (
        lax.all_gather(heads_own, "rows", axis=0, tiled=True),
        lax.all_gather(message_own, "rows", axis=0, tiled=True),
    )
    padded_in = halo_value(low_reduced)
    pre_list, feat_list, padded_feats, message_list = task_forward(
        padded_in, heads_all, message_all, pixel_mask, halo_value
    )
    depth_stream, class_logits, merged, gate_depth, gate_class, depth_sum, class_sum = (
        streams_forward(feat_list, message_list, gates_all, classes_all, pixel_mask)
    )
    feat_grads, message_grads, grad_gates, grad_classes = streams_backward(
        feat_list,
        merged,
        gate_depth,
        gate_class,
        depth_sum,
        class_sum,
        depth_cot,
        class_cot,
        gates_all,
        classes_all,
        pixel_mask,
    )
    reduced_grad, grad_heads, grad_message = task_backward(
        padded_in,
        heads_all,
        message_all,
        pixel_mask,
        pre_list,
        padded_feats,
        feat_grads,
        message_grads,
        halo_grad,
    )
    low_reduced_grad = reduced_grad.astype(jnp.bfloat16)
    grad_reduce = outer_sum(block_out, low_reduced_grad)
    block_grad = project_back(low_reduced_grad, reduce_all)
    sum_grad = gelu_slope(summed, block_grad * pixel_mask)
    d_last, gain_grad_three, shift_grad_three = norm_backward(
        sum_grad, normal_last, std_last, gain_three, pixel_mask, valid_count
    )
    low_last = d_last.astype(jnp.bfloat16)
    grad_last = outer_sum(act_middle, low_last)
    middle_grad = project_back(low_last, last_all)
    d_middle, gain_grad_two, shift_grad_two = norm_backward(
        gelu_slope(out_middle, middle_grad * pixel_mask),
        normal_middle,
        std_middle,
        gain_two,
        pixel_mask,
        valid_count,
    )
    low_middle = d_middle.astype(jnp.bfloat16)
    grad_middle = conv_kernel_grad(padded_first, low_middle)
    first_grad = conv_input_grad(halo_grad(low_middle), middle_all)
    d_first, gain_grad_one, shift_grad_one = norm_backward(
        gelu_slope(out_first, first_grad * pixel_mask),
        normal_first,
        std_first,
        gain_one,
        pixel_mask,
        valid_count,
    )
    low_first = d_first.astype(jnp.bfloat16)
    grad_first = outer_sum(low_in, low_first)
    image_grad = (project_back(low_first, first_all) + sum_grad) * pixel_mask
    summed_grads = (
        lax.psum_scatter(grad_first, "batch", scatter_dimension=0, tiled=True),
        lax.psum_scatter(grad_middle, "batch", scatter_dimension=1, tiled=True),
        lax.psum_scatter(grad_last, "batch", scatter_dimension=0, tiled=True),
        lax.psum_scatter(grad_reduce, "batch", scatter_dimension=0, tiled=True),
        lax.psum_scatter(grad_gates, "batch", scatter_dimension=1, tiled=True),
        lax.psum_scatter(grad_classes, "batch", scatter_dimension=0, tiled=True),
        lax.psum_scatter(grad_heads, "batch", scatter_dimension=2, tiled=True),
        lax.psum_scatter(grad_message, "batch", scatter_dimension=2, tiled=True),
    )
    shared = (
        lax.psum(summed_grads[0].astype(jnp.bfloat16), "rows").astype(jnp.float32),
        lax.psum(summed_grads[1].astype(jnp.bfloat16), "rows").astype(jnp.float32),
        lax.psum(summed_grads[2].astype(jnp.bfloat16), "rows").astype(jnp.float32),
        lax.psum(summed_grads[3].astype(jnp.bfloat16), "rows").astype(jnp.float32),
        lax.psum(summed_grads[4].astype(jnp.bfloat16), "rows").astype(jnp.float32),
        lax.psum(summed_grads[5].astype(jnp.bfloat16), "rows").astype(jnp.float32),
    )
    heads_out, message_out = (
        lax.psum_scatter(
            summed_grads[6].astype(jnp.bfloat16), "rows", scatter_dimension=0, tiled=True
        ).astype(jnp.float32),
        lax.psum_scatter(
            summed_grads[7].astype(jnp.bfloat16), "rows", scatter_dimension=0, tiled=True
        ).astype(jnp.float32),
    )

    def own_share(member):
        share = member.shape[0] // batch_count
        return lax.dynamic_slice_in_dim(member, image_index * share, share, 0)

    return (
        depth_stream.astype(jnp.bfloat16),
        class_logits.astype(jnp.bfloat16),
        image_grad,
        shared[0],
        own_share(gain_grad_one),
        own_share(shift_grad_one),
        shared[1],
        own_share(gain_grad_two),
        own_share(shift_grad_two),
        shared[2],
        own_share(gain_grad_three),
        own_share(shift_grad_three),
        shared[3],
        heads_out,
        message_out,
        shared[4],
        shared[5],
    )


SHAPES = dict(
    wf=((4, 2, 2, 128, 256), BF16),
    wm=((9, 4, 2, 2, 32, 256), BF16),
    wl=((4, 2, 2, 32, 1024), BF16),
    wr=((2, 2, 2, 128, 512), BF16),
    wc=((16, 32, 128), BF16),
    wh=((9, 4, 2, 2, 32, 256), BF16),
    wq=((9, 4, 2, 2, 32, 256), BF16),
    wg=((4, 2, 2, 32, 256), BF16),
    xall=((320, 2048), BF16),
    maskp=((1280, 128), F32),
    pre1=((320, 256), F32),
    pre2=((320, 256), F32),
    pre3=((320, 1024), F32),
    bnp1=((8, 256), F32),
    bnp2=((8, 256), F32),
    bnp3=((8, 1024), F32),
    a1=((320, 512), BF16),
    a2=((320, 512), BF16),
    a3=((480, 1536), BF16),
    blk=((320, 1024), BF16),
    rps=((160, 512), BF16),
    rpr=((160, 512), BF16),
    rbuf=((1280, 512), BF16),
    fown=((1280, 256), BF16),
    ffull=((1280, 512), BF16),
    msgb=((1280, 256), BF16),
    gateb=((1280, 256), BF16),
    frecv=((2, 160, 512), BF16),
    grecv=((2, 160, 512), BF16),
    mrecv=((4, 160, 512), BF16),
    dcotv=((160, 512), BF16),
    ccotv=((160, 128), BF16),
    ods=((160, 512), BF16),
    olg=((160, 128), BF16),
    mrg=((160, 512), BF16),
    dm=((4, 160, 512), BF16),
    ex=((2, 2, 160, 512), BF16),
    dmg=((1280, 256), BF16),
    exg=((2, 1280, 256), BF16),
    gm=((9, 4, 2, 2, 32, 256), BF16),
    gh=((9, 4, 2, 2, 32, 256), BF16),
    gg=((4, 2, 2, 32, 256), BF16),
    rg=((3, 2, 2, 32, 256), BF16),
    pg=((2, 2, 32, 256), BF16),
    zst=((3, 3, 2, 2, 32, 256), BF16),
    psm=((9, 2, 2, 32, 256), BF16),
    psh=((9, 2, 2, 32, 256), BF16),
    gcls=((16, 32, 128), BF16),
    rcls=((15, 32, 128), BF16),
    clss=((32, 128), F32),
    clsr=((32, 128), F32),
    clso=((32, 128), F32),
    dfs=((1280, 256), BF16),
    dfr=((1280, 256), BF16),
    drs=((640, 512), BF16),
    drr=((640, 512), BF16),
    drq=((640, 512), BF16),
    dro=((3, 160, 512), BF16),
    dred=((320, 512), BF16),
    dsr=((160, 1024), BF16),
    par2=((320, 256), BF16),
    par1=((320, 256), BF16),
    dp1r=((160, 256), BF16),
    rcr=((2, 2, 128, 512), BF16),
    rcl=((4, 2, 32, 1024), BF16),
    rcm=((9, 4, 2, 32, 256), BF16),
    rcf=((4, 2, 128, 256), BF16),
    ryr=((2, 128, 512), BF16),
    ryl=((4, 32, 1024), BF16),
    rym=((9, 4, 32, 256), BF16),
    ryf=((4, 128, 256), BF16),
    rzr=((3, 128, 512), BF16),
    rzl=((3, 32, 1024), BF16),
    rzm=((3, 9, 32, 256), BF16),
    rzf=((3, 128, 256), BF16),
    fnr=((128, 512), BF16),
    fnl=((32, 1024), BF16),
    fnm=((9, 32, 256), BF16),
    fnf=((128, 256), BF16),
)
for _i, _w in enumerate((256, 256, 512, 512, 256, 256)):
    SHAPES["am%d" % _i] = ((8, _w), F32)
    SHAPES["as%d" % _i] = ((8, _w), F32)
    SHAPES["at%d" % _i] = ((8, _w), F32)
    SHAPES["ar%d" % _i] = ((3, 8, _w), F32)
    SHAPES["az%d" % _i] = ((3, 8, _w), F32)

INS = (
    "crop_h", "crop_w", "images", "first", "middle", "last", "reduce", "gates",
    "classes", "heads", "messages", "st1", "st2", "st3", "dcot", "ccot",
)
OUTS = dict(
    o_depth=((160, 512), BF16),
    o_logits=((160, 128), BF16),
    o_img=((160, 2048), BF16),
    o_first=((128, 512), BF16),
    o_gs1=((2, 8, 256), F32),
    o_mid=((9, 32, 512), BF16),
    o_gs2=((2, 8, 256), F32),
    o_last=((32, 2048), BF16),
    o_gs3=((2, 8, 512), F32),
    o_red=((128, 512), BF16),
    o_heads=((2, 9, 32, 512), BF16),
    o_mess=((2, 9, 32, 512), BF16),
    o_gates=((2, 32, 512), BF16),
    o_cls=((32, 128), F32),
    rm=((3, 9, 2, 2, 32, 256), BF16),
    rh=((3, 9, 2, 2, 32, 256), BF16),
    wfo=((4, 2, 2, 128, 256), BF16),
)


def shift_columns(v):
    rows, width = v.shape
    col = lax.broadcasted_iota(jnp.int32, (rows, width), 0)
    left = jnp.where(col == 0, 0.0, pltpu.roll(v, 1, 0))
    right = jnp.where(col == rows - 1, 0.0, pltpu.roll(v, rows - 1, 0))
    return left, right


def spread(src, dst, n_img, width):
    zero = jnp.zeros((80, 3 * width), BF16)
    for pad in range(n_img + 1):
        dst[pl.ds(pad * 400, 80), :] = zero

    def body(i, carry):
        v = src[pl.ds(pl.multiple_of(i * 80, 16), 80), :]
        left, right = shift_columns(v.astype(F32))
        row = pl.multiple_of((i + lax.div(i, np.int32(4)) + 1) * 80, 16)
        dst[pl.ds(row, 80), 0:width] = left.astype(BF16)
        dst[pl.ds(row, 80), width : 2 * width] = v
        dst[pl.ds(row, 80), 2 * width : 3 * width] = right.astype(BF16)
        return carry

    lax.fori_loop(0, 4 * n_img, body, 0)


def conv_rows(a3, w, img):
    acc = None
    for a in range(3):
        base = pl.multiple_of((5 * img + a) * 80, 16)
        part = dot(a3[pl.ds(base, 320), :], w[3 * a : 3 * a + 3].reshape(1536, 256))
        acc = part if acc is None else acc + part
    return acc


def conv_back(d3, w, img):
    acc = None
    for a in range(3):
        for q in range(3):
            base = pl.multiple_of((5 * img + a) * 80, 16)
            tap = 3 * (2 - a) + (2 - q)
            part = dot_last(d3[pl.ds(base, 320), 256 * q : 256 * q + 256], w[tap].reshape(512, 256))
            acc = part if acc is None else acc + part
    return acc


def conv_weight(a3, d3, out, n_img):
    depth = (5 * n_img - 1) * 80

    def body(tap, carry):
        a = lax.div(tap, np.int32(3))
        q = tap - 3 * a
        left = a3[pl.ds(pl.multiple_of(a * 80, 16), depth), pl.ds(pl.multiple_of(q * 512, 128), 512)]
        out[tap] = dot_first(left, d3[pl.ds(80, depth), 256:512]).astype(BF16).reshape(out.shape[1:])
        return carry

    lax.fori_loop(0, 9, body, 0)


def body(names, *refs):
    s = SimpleNamespace(**dict(zip(names, refs)))
    b, r = lax.axis_index("batch"), lax.axis_index("rows")
    z = lax.div(b, np.int32(4))
    y = lax.rem(lax.div(b, np.int32(2)), np.int32(2))
    c = lax.rem(b, np.int32(2))
    ln = Links(s.send_sems, s.recv_sems, s.near_sems)
    half, fhalf = 256 * r, 256 * c

    def dev(zz, yy, cc, rr):
        return (4 * zz + 2 * yy + cc, rr)

    def zk(k):
        return lax.rem(z + k, np.int32(4))

    core, ypeer, xpeer = dev(z, y, 1 - c, r), dev(z, 1 - y, c, r), dev(z, y, c, 1 - r)
    special = r == y
    task = 2 * r + y
    img = 2 * y + c
    own_px = pl.multiple_of(320 * img + 160 * r, 16)
    my_rows = pl.multiple_of(160 * r, 16)
    other_rows = pl.multiple_of(160 * (1 - r), 16)
    half = pl.multiple_of(half, 128)
    ohalf = pl.multiple_of(256 * (1 - r), 128)
    fhalf = pl.multiple_of(fhalf, 128)
    offsets = [(dr, dy, dc) for dr in range(2) for dy in range(2) for dc in range(2) if dr + dy + dc]

    def peer(dr, dy, dc):
        rr = 1 - r if dr else r
        yy = 1 - y if dy else y
        cc = 1 - c if dc else c
        return rr, yy, cc

    def px_of(rr, yy, cc):
        return pl.multiple_of(320 * (2 * yy + cc) + 160 * rr, 16)

    near0 = [
        ln.near(s.images, s.xall.at[pl.ds(my_rows, 160)]),
        ln.near(s.first.at[:, pl.ds(half, 256)], s.wf.at[z, y, c]),
        ln.near(s.middle.at[:, :, pl.ds(half, 256)], s.wm.at[:, z, y, c]),
        ln.near(s.last.at[:, pl.ds(pl.multiple_of(1024 * r, 128), 1024)], s.wl.at[z, y, c]),
        ln.near(s.classes, s.wc.at[b]),
        ln.near(s.dcot, s.dcotv),
        ln.near(s.ccot, s.ccotv),
        ln.near(s.heads.at[y, :, :, pl.ds(fhalf, 256)], s.wh.at[:, z, y, c]),
        ln.near(s.messages.at[y, :, :, pl.ds(fhalf, 256)], s.wq.at[:, z, y, c]),
        ln.near(s.gates.at[r, :, pl.ds(fhalf, 256)], s.wg.at[z, y, c]),
    ]
    owner = lax.div(z, np.int32(2)) == r
    zl = lax.rem(z, np.int32(2))
    red_local = pltpu.make_async_copy(s.reduce, s.wr.at[zl, y, c], s.near_sems.at[SEMS - 1])
    pl.when(owner)(red_local.start)

    wf_z = [ln.push(s.first.at[:, pl.ds(half, 256)], s.wf.at[z, y, c], dev(zk(k), y, c, r)) for k in (1, 2, 3)]
    img_x = ln.push(s.images, s.xall.at[pl.ds(my_rows, 160)], xpeer)
    wm_z = [ln.push(s.middle.at[:, :, pl.ds(half, 256)], s.wm.at[:, z, y, c], dev(zk(k), y, c, r)) for k in (1, 2, 3)]

    for i in range(4):
        high, wide = s.crop_h[4 * z + i], s.crop_w[4 * z + i]
        for row in range(4):
            col = lax.broadcasted_iota(jnp.int32, (80, 128), 0)
            inside = (col < wide) & (row < high)
            s.maskp[pl.ds(320 * i + 80 * row, 80), :] = jnp.where(inside, 1.0, 0.0)
    total = s.crop_h[0] * s.crop_w[0]
    for i in range(1, 16):
        total = total + s.crop_h[i] * s.crop_w[i]
    count = total.astype(F32)
    mine = pl.multiple_of(320 * img, 16)

    def mask_at(base, rows, width):
        return lanes(s.maskp[pl.ds(mine + base, rows), :], width)

    for cp in near0:
        cp.wait()
    pl.when(owner)(red_local.wait)
    wait(wf_z)
    wf_y = ln.push(s.wf.at[:, y, c], s.wf.at[:, y, c], ypeer)
    wf_c0 = ln.push(s.wf.at[:, y, c], s.wf.at[:, y, c], core)
    lastl = pl.ds(pl.multiple_of(1024 * r, 128), 1024)
    wl_z = [ln.push(s.last.at[:, lastl], s.wl.at[z, y, c], dev(zk(k), y, c, r)) for k in (1, 2, 3)]
    wr_z = [ln.push(s.reduce, s.wr.at[zl, y, c], dev(zk(k), y, c, r), owner) for k in (1, 2, 3)]
    wait([wf_y])
    wf_c1 = ln.push(s.wf.at[:, 1 - y, c], s.wf.at[:, 1 - y, c], core)
    wait([img_x])

    def mask_x(base):
        s.xall[pl.ds(base, 80), :] = (s.xall[pl.ds(base, 80), :].astype(F32) * mask_at(base, 80, 2048)).astype(BF16)

    rows_loop(320, 80, mask_x)
    wait(wm_z)
    wm_y = ln.push(s.wm.at[:, :, y, c], s.wm.at[:, :, y, c], ypeer)
    wm_c0 = ln.push(s.wm.at[:, :, y, c], s.wm.at[:, :, y, c], core)
    wait([wf_c0, wf_c1])

    def task_push(src, dst):
        out = {}
        for k in range(4):
            for j in range(2):
                for i in range(2):
                    if k + j + i == 0:
                        continue
                    yy = 1 - y if j else y
                    cc = 1 - c if i else c
                    out[k, j, i] = ln.push(
                        src.at[yy, :, :, pl.ds(pl.multiple_of(256 * cc, 128), 256)],
                        dst.at[:, z, y, c],
                        dev(zk(k) if k else z, yy, cc, r),
                        mid_or_end(k),
                    )
        return out

    ends = (z == 0) | (z == 3)

    def mid_or_end(k):
        return ends if k == 2 else None

    def task_relay(got, dst):
        wait([got[k, j, i] for k in (0, 1, 3) for j in range(2) for i in range(2) if k + j + i])
        inner = jnp.logical_not(ends)
        wait([got[2, j, i] for j in range(2) for i in range(2)], inner)
        source = 3 - z
        target = jnp.where(z == 1, 0, 3)
        hand = ln.push(dst.at[:, source], dst.at[:, source], dev(target, y, c, r), inner)
        return hand

    def reduce_all(n, out):
        m, sm, t, ar, az = (getattr(s, p + str(n)) for p in ("am", "as", "at", "ar", "az"))
        one = []
        for i in (1, 2, 3):
            yy = 1 - y if i & 2 else y
            cc = 1 - c if i & 1 else c
            one.append(ln.push(m, ar.at[i - 1], dev(z, yy, cc, r)))
        wait(one)
        sm[...] = (m[...] + ar[0]) + (ar[1] + ar[2])
        two = [ln.push(sm, az.at[k - 1], dev(zk(k), y, c, r)) for k in (1, 2, 3)]
        wait(two)
        t[...] = (sm[...] + az[0]) + (az[1] + az[2])
        return t[...]

    def stats_of(pre, width, msg):
        m = lanes(s.maskp[pl.ds(mine, 320), :], width)
        v = pre * m
        sums = jnp.sum(v, axis=0, keepdims=True)
        squares = jnp.sum(v * pre, axis=0, keepdims=True)
        return sums, squares

    def norm_terms(n, bnp, width):
        t = reduce_all(n, None)
        if width == 256:
            rows = [t[i : i + 1] for i in range(4)]
        else:
            rows = [jnp.concatenate([t[2 * i : 2 * i + 1], t[2 * i + 1 : 2 * i + 2]], axis=1) for i in range(4)]
        mean = rows[0] / count
        inv = lax.rsqrt(rows[1] / count - mean * mean + EPS)
        bnp[0:1], bnp[1:2], bnp[2:3], bnp[3:4] = mean, inv, rows[2], rows[3]

    def put_stats(n, first, second, width, template):
        m = getattr(s, "am%d" % n)
        if template is None:
            m[...] = jnp.zeros(m.shape, F32)
        else:
            m[...] = template[...]
        if width == 256:
            m[0:1], m[1:2] = first, second
        else:
            m[0:1], m[1:2] = first[:, :512], first[:, 512:]
            m[2:3], m[3:4] = second[:, :512], second[:, 512:]

    pre = dot(s.xall[...], s.wf[...].reshape(2048, 256))
    s.pre1[...] = pre
    first_sum, first_sq = stats_of(pre, 256, None)
    put_stats(0, first_sum, first_sq, 256, s.st1)
    wait([wm_y])
    wm_c1 = ln.push(s.wm.at[:, :, 1 - y, c], s.wm.at[:, :, 1 - y, c], core)
    norm_terms(0, s.bnp1, 256)
    heads_got = task_push(s.heads, s.wh)

    def act_from(prebuf, bnp, dst):
        def step(base):
            x = (prebuf[pl.ds(base, 80), :] - bnp[0:1]) * bnp[1:2] * bnp[2:3] + bnp[3:4]
            dst[pl.ds(base, 80), pl.ds(half, 256)] = (gelu_of(x) * mask_at(base, 80, 256)).astype(BF16)

        rows_loop(320, 80, step)

    act_from(s.pre1, s.bnp1, s.a1)
    a1_x = ln.push(s.a1.at[:, pl.ds(half, 256)], s.a1.at[:, pl.ds(half, 256)], xpeer)
    wait(wl_z)
    wl_y = ln.push(s.wl.at[:, y, c], s.wl.at[:, y, c], ypeer)
    wl_c0 = ln.push(s.wl.at[:, y, c], s.wl.at[:, y, c], core)
    wait([wm_c0, wm_c1])
    wait([a1_x])
    spread(s.a1, s.a3, 1, 512)
    pre = conv_rows(s.a3, s.wm, 0)
    s.pre2[...] = pre
    first_sum, first_sq = stats_of(pre, 256, None)
    put_stats(1, first_sum, first_sq, 256, s.st2)
    norm_terms(1, s.bnp2, 256)
    act_from(s.pre2, s.bnp2, s.a2)
    a2_x = ln.push(s.a2.at[:, pl.ds(half, 256)], s.a2.at[:, pl.ds(half, 256)], xpeer)
    wait([wr_z[0]], lax.div(zk(3), np.int32(2)) == r)
    wait([wr_z[1]], lax.div(zk(2), np.int32(2)) == r)
    wait([wr_z[2]], lax.div(zk(1), np.int32(2)) == r)
    wr_y = ln.push(s.wr.at[:, y, c], s.wr.at[:, y, c], ypeer)
    wr_c0 = ln.push(s.wr.at[:, y, c], s.wr.at[:, y, c], core)
    wait([wl_y])
    wl_c1 = ln.push(s.wl.at[:, 1 - y, c], s.wl.at[:, 1 - y, c], core)
    wait([wl_c0, wl_c1, a2_x])
    pre = dot(s.a2[...], s.wl[...].reshape(512, 1024))
    s.pre3[...] = pre
    first_sum, first_sq = stats_of(pre, 1024, None)
    put_stats(2, first_sum, first_sq, 1024, s.st3)
    norm_terms(2, s.bnp3, 1024)
    mess_got = task_push(s.messages, s.wq)
    gate_got = {}
    cls_got = {}
    for k in range(4):
        for j in range(2):
            for i in range(2):
                if k + j + i == 0:
                    continue
                yy = 1 - y if j else y
                cc = 1 - c if i else c
                to = dev(zk(k) if k else z, yy, cc, r)
                gate_got[k, j, i] = ln.push(
                    s.gates.at[r, :, pl.ds(pl.multiple_of(256 * cc, 128), 256)], s.wg.at[z, y, c], to, yy == r
                )
                cls_got[k, j, i] = ln.push(s.classes, s.wc.at[b], to)
    xhalf = pl.ds(pl.multiple_of(1024 * r, 128), 1024)

    def summed_at(base, rows):
        x = (s.pre3[pl.ds(base, rows), :] - s.bnp3[0:1]) * s.bnp3[1:2]
        return x, x * s.bnp3[2:3] + s.bnp3[3:4] + s.xall[pl.ds(base, rows), xhalf].astype(F32)

    def block_step(base):
        _, v = summed_at(base, 32)
        s.blk[pl.ds(base, 32), :] = (gelu_of(v) * mask_at(base, 32, 1024)).astype(BF16)

    rows_loop(320, 32, block_step)
    wait([wr_y])
    wr_c1 = ln.push(s.wr.at[:, 1 - y, c], s.wr.at[:, 1 - y, c], core)
    wait([wr_c0, wr_c1])
    wred = s.wr[...].reshape(1024, 512)
    s.rps[...] = dot(s.blk[pl.ds(other_rows, 160), :], wred).astype(BF16)
    red_x = ln.push(s.rps, s.rpr, xpeer)
    part = dot(s.blk[pl.ds(my_rows, 160), :], wred)
    wait([red_x])
    s.rbuf[pl.ds(own_px, 160), :] = (part + s.rpr[...].astype(F32)).astype(BF16)

    def block_of(rr, yy, cc, lo=0, n=160):
        return s.rbuf.at[pl.ds(pl.multiple_of(px_of(rr, yy, cc) + lo, 16), n)]

    own = block_of(r, y, c)
    g_x = ln.push(own, own, xpeer)
    g_y = ln.push(own, own, ypeer)
    g_c = ln.push(own, own, core)
    wait([g_x])
    bx = block_of(1 - r, y, c, 0, 80)
    g_xy = ln.push(bx, bx, ypeer)
    wait([g_y])
    by = block_of(r, 1 - y, c, 80, 80)
    g_yx = ln.push(by, by, xpeer)
    bx = block_of(1 - r, y, c)
    g_c1 = ln.push(bx, bx, core)
    by = block_of(r, 1 - y, c)
    g_c2 = ln.push(by, by, core)
    wait([g_xy, g_yx])
    bd = block_of(1 - r, 1 - y, c)
    g_c3 = ln.push(bd, bd, core)
    heads_hand = task_relay(heads_got, s.wh)
    wait([heads_hand], ends)
    wait([g_c, g_c1, g_c2, g_c3])

    def tasks(r3, f3, d3, preh, dfull):
        spread(s.rbuf, r3, 4, 512)

        def head_step(i, carry):
            v = conv_rows(r3, s.wh, i)
            px = pl.multiple_of(i * 320, 16)
            preh[pl.ds(px, 320), :] = v
            return carry

        lax.fori_loop(0, 4, head_step, 0)

        def feat_step(base):
            m = lanes(s.maskp[pl.ds(base, 80), :], 256)
            s.fown[pl.ds(base, 80), :] = (gelu_of(preh[pl.ds(base, 80), :]) * m).astype(BF16)

        rows_loop(1280, 80, feat_step)
        f_c = ln.push(s.fown, s.ffull.at[:, pl.ds(fhalf, 256)], core)
        f_n = ln.near(s.fown, s.ffull.at[:, pl.ds(fhalf, 256)])

        def to_owners(src, dst_of, when):
            got = {}
            for o in offsets:
                rr, yy, cc = peer(*o)
                got[o] = ln.push(
                    src.at[pl.ds(px_of(rr, yy, cc), 160)], dst_of().at[:, pl.ds(fhalf, 256)], dev(z, yy, cc, rr), when
                )
            return got

        f_own = to_owners(s.fown, lambda: s.frecv.at[r], special)

        def keep(dst, src):
            def run():
                dst[:, pl.ds(fhalf, 256)] = src[pl.ds(own_px, 160), :]

            return run

        pl.when(special)(keep(s.frecv.at[r], s.fown))
        f_n.wait()
        wait([f_c])

        def gate_ready():
            for key, cp in gate_got.items():
                cp.wait_recv()

        pl.when(special)(gate_ready)

        @pl.when(special)
        def _():
            def gate_step(base):
                v = dot(s.ffull[pl.ds(base, 320), :], s.wg[...].reshape(512, 256))
                s.gateb[pl.ds(base, 320), :] = (1.0 / (1.0 + jnp.exp(-v))).astype(BF16)

            rows_loop(1280, 320, gate_step)

        g_own = to_owners(s.gateb, lambda: s.grecv.at[r], special)
        pl.when(special)(keep(s.grecv.at[r], s.gateb))
        spread(s.ffull, f3, 4, 512)
        mess_hand = task_relay(mess_got, s.wq)
        wait([mess_hand], ends)

        def mess_step(i, carry):
            px = pl.multiple_of(i * 320, 16)
            s.msgb[pl.ds(px, 320), :] = conv_rows(f3, s.wq, i).astype(BF16)
            return carry

        lax.fori_loop(0, 4, mess_step, 0)
        m_own = to_owners(s.msgb, lambda: s.mrecv.at[task], None)
        keep(s.mrecv.at[task], s.msgb)()

        for key, cp in cls_got.items():
            cp.wait_recv()
        for o in offsets:
            wait([f_own[o], g_own[o]], (r != y) if (o[0] + o[1]) % 2 else special)
            wait([m_own[o]])

        def stream_step(base):
            rows = pl.ds(base, 32)
            m = lanes(s.maskp[pl.ds(own_px + base, 32), :], 512)
            m0, m1, m2, m3 = (s.mrecv[t, rows, :].astype(F32) for t in range(4))
            mid = m1 + m2
            sd, sc = mid + m3, m0 + mid
            gd, gc = s.grecv[0, rows, :].astype(F32), s.grecv[1, rows, :].astype(F32)
            s.ods[rows, :] = ((s.frecv[0, rows, :].astype(F32) + gd * sd) * m).astype(BF16)
            merged = (s.frecv[1, rows, :].astype(F32) + gc * sc).astype(BF16)
            s.mrg[rows, :] = merged
            m1l = m[:, :128]
            wcls = s.wc[...].reshape(512, 128)
            s.olg[rows, :] = (dot(merged, wcls) * m1l).astype(BF16)
            dj = (s.ccotv[rows, :].astype(F32) * m1l).astype(BF16)
            s.ccotv[rows, :] = dj
            dd = s.dcotv[rows, :].astype(F32) * m
            dmer = dot_last(dj, wcls)
            s.ex[0, 0, rows, :] = dd.astype(BF16)
            s.ex[1, 0, rows, :] = dmer.astype(BF16)
            s.ex[0, 1, rows, :] = (dd * sd * gd * (1.0 - gd)).astype(BF16)
            s.ex[1, 1, rows, :] = (dmer * sc * gc * (1.0 - gc)).astype(BF16)
            down, up = dd * gd, dmer * gc
            both = (down + up).astype(BF16)
            s.dm[0, rows, :] = up.astype(BF16)
            s.dm[1, rows, :] = both
            s.dm[2, rows, :] = both
            s.dm[3, rows, :] = down.astype(BF16)

        rows_loop(160, 32, stream_step)
        d_got = {}
        e_got = {}
        for o in offsets:
            rr, yy, cc = peer(*o)
            tt = 2 * rr + yy
            ll = pl.ds(pl.multiple_of(256 * cc, 128), 256)
            d_got[o] = ln.push(s.dm.at[tt, :, ll], s.dmg.at[pl.ds(own_px, 160)], dev(z, yy, cc, rr))
        for o in offsets:
            rr, yy, cc = peer(*o)
            ll = pl.ds(pl.multiple_of(256 * cc, 128), 256)
            e_got[o] = ln.push(s.ex.at[rr, :, :, ll], s.exg.at[:, pl.ds(own_px, 160)], dev(z, yy, cc, rr), rr == yy)
        s.dmg[pl.ds(own_px, 160), :] = s.dm[task, :, pl.ds(fhalf, 256)]

        @pl.when(special)
        def _():
            for e in range(2):
                s.exg[e, pl.ds(own_px, 160), :] = s.ex[r, e, :, pl.ds(fhalf, 256)]

        @pl.when(jnp.logical_not(special))
        def _():
            s.exg[...] = jnp.zeros(s.exg.shape, BF16)

        out_near = [ln.near(s.ods, s.o_depth), ln.near(s.olg, s.o_logits)]
        s.gcls[...] = dot_first(s.mrg[...], s.ccotv[...]).astype(BF16).reshape(16, 32, 128)
        cg = []
        for k in range(4):
            for j in range(2):
                for i in range(2):
                    if k + j + i == 0:
                        continue
                    yy = 1 - y if j else y
                    cc = 1 - c if i else c
                    zz = zk(k) if k else z
                    like = lambda side, n=len(cg): s.rcls.at[n] if side else s.gcls.at[0]
                    cg.append(ln.push(s.gcls.at[4 * zz + 2 * yy + cc], s.rcls.at[len(cg)], dev(zz, yy, cc, r), None, like))
        wait([d_got[o] for o in offsets])
        spread(s.dmg, d3, 4, 256)
        conv_weight(f3, d3, s.gm, 4)
        gm_z = [ln.push(s.gm.at[:, zk(k)], s.rm.at[k - 1], dev(zk(k), y, c, r), None, lambda side, k=k: s.rm.at[k - 1] if side else s.gm.at[:, 0]) for k in (1, 2, 3)]
        wait([e_got[o] for o in offsets], special)

        def back_step(i, carry):
            px = pl.multiple_of(i * 320, 16)
            dfull[pl.ds(px, 320), :] = conv_back(d3, s.wq, i)
            return carry

        lax.fori_loop(0, 4, back_step, 0)

        @pl.when(special)
        def _():
            def gate_back(base):
                rows = pl.ds(base, 320)
                dfull[rows, :] = dfull[rows, :] + dot_last(s.exg[1, rows, :], s.wg[...].reshape(512, 256))

            rows_loop(1280, 320, gate_back)

        chalf = pl.ds(pl.multiple_of(256 * (1 - c), 128), 256)

        def give(base):
            rows = pl.ds(base, 80)
            s.dfs[rows, :] = dfull[rows, chalf].astype(BF16)

        rows_loop(1280, 80, give)
        df_c = ln.push(s.dfs, s.dfr, core)

        @pl.when(special)
        def _():
            s.gg[...] = dot_first(s.ffull[...], s.exg[1]).astype(BF16).reshape(s.gg.shape)

        gg_z = [ln.push(s.gg.at[zk(k)], s.rg.at[k - 1], dev(zk(k), y, c, r), special, lambda side, k=k: s.rg.at[k - 1] if side else s.gg.at[0]) for k in (1, 2, 3)]
        wait([df_c])

        def dhead_step(base):
            rows = pl.ds(base, 80)
            m = lanes(s.maskp[rows, :], 256)
            d = dfull[rows, pl.ds(fhalf, 256)] + s.dfr[rows, :].astype(F32) + s.exg[0, rows, :].astype(F32)
            s.dfs2[rows, :] = (slope_of(preh[rows, :]) * d * m).astype(BF16)

        rows_loop(1280, 80, dhead_step)
        spread(s.dfs2, d3, 4, 256)

        def back_step2(i, carry):
            px = pl.multiple_of(i * 320, 16)
            dfull[pl.ds(px, 320), :] = conv_back(d3, s.wh, i)
            return carry

        lax.fori_loop(0, 4, back_step2, 0)
        for yy in range(2):
            src = pl.multiple_of(320 * (2 * yy) + 320 * (1 - c), 16)
            s.drs[pl.ds(320 * yy, 320), :] = dfull[pl.ds(src, 320), :].astype(BF16)
        dr_c = ln.push(s.drs, s.drr, core)
        conv_weight(r3, d3, s.gh, 4)
        gh_z = [ln.push(s.gh.at[:, zk(k)], s.rh.at[k - 1], dev(zk(k), y, c, r), None, lambda side, k=k: s.rh.at[k - 1] if side else s.gh.at[:, 0]) for k in (1, 2, 3)]
        wait([dr_c])
        for yy in range(2):
            src = pl.multiple_of(320 * (2 * yy) + 320 * c, 16)
            rows = pl.ds(320 * yy, 320)
            s.drq[rows, :] = (dfull[pl.ds(src, 320), :] + s.drr[rows, :].astype(F32)).astype(BF16)
        ro = []
        for dr, dy in ((1, 0), (0, 1), (1, 1)):
            rr, yy, _ = peer(dr, dy, 0)
            src = s.drq.at[pl.ds(pl.multiple_of(320 * yy + 160 * rr, 16), 160)]
            ro.append(ln.push(src, s.dro.at[len(ro)], dev(z, yy, c, rr)))
        wait(ro)
        keep_rows = pl.ds(pl.multiple_of(320 * y + 160 * r, 16), 160)
        total_red = s.drq[keep_rows, :].astype(F32)
        for i in range(3):
            total_red = total_red + s.dro[i].astype(F32)
        s.dred[pl.ds(my_rows, 160), :] = total_red.astype(BF16)
        for cp in out_near:
            cp.wait()
        ln.drain(scoped=True)
        return cg, gm_z, gg_z, gh_z

    state = {}

    def scope_tasks(*scr):
        state["t"] = tasks(*scr)

    pl.run_scoped(
        scope_tasks,
        pltpu.VMEM((1680, 1536), BF16),
        pltpu.VMEM((1680, 1536), BF16),
        pltpu.VMEM((1680, 768), BF16),
        pltpu.VMEM((1280, 256), F32),
        pltpu.VMEM((1280, 512), F32),
    )
    cg, gm_z, gg_z, gh_z = state["t"]

    dr_x = ln.push(s.dred.at[pl.ds(my_rows, 160)], s.dred.at[pl.ds(my_rows, 160)], xpeer)
    wfo_x = ln.push(s.wf, s.wfo, xpeer)

    def block_back(*late):
        for name, ref in zip(LATE, late):
            setattr(s, name, ref)
        gr, gl, gq, gf = s.gr, s.gl, s.gq, s.gf

        def to_core(g, rc, lead):
            at = g.at[:, :, :, 1 - c] if lead else g.at[:, :, 1 - c]
            return ln.push(at, rc, core)

        def add_core(g, rc, lead):
            if lead:
                for t in range(9):
                    rc[t] = (rc[t].astype(F32) + g[t, :, :, c].astype(F32)).astype(BF16)
            else:
                for t in range(rc.shape[0]):
                    rc[t] = (rc[t].astype(F32) + g[t, :, c].astype(F32)).astype(BF16)

        def to_y(rc, ry, lead):
            return ln.push(rc.at[:, :, 1 - y] if lead else rc.at[:, 1 - y], ry, ypeer)

        def add_y(rc, ry, lead):
            for t in range(ry.shape[0]):
                mine_y = rc[t, :, y] if lead else rc[t, y]
                ry[t] = (ry[t].astype(F32) + mine_y.astype(F32)).astype(BF16)

        def to_z(ry, rz, lead):
            return [
                ln.push(ry.at[:, zk(k)] if lead else ry.at[zk(k)], rz.at[k - 1], dev(zk(k), y, c, r)) for k in (1, 2, 3)
            ]

        def add_z(ry, rz, fin, lead):
            mine_z = (ry[:, z] if lead else ry[z]).astype(F32)
            fin[...] = ((mine_z + rz[0].astype(F32)) + (rz[1].astype(F32) + rz[2].astype(F32))).astype(BF16)

        wait([dr_x])

        def d3_step(i, carry):
            su, sux = carry
            rows = pl.ds(pl.multiple_of(i * 32, 16), 32)
            x, v = summed_at(i * 32, 32)
            u = slope_of(v) * s.u3[rows, :] * mask_at(i * 32, 32, 1024)
            s.u3[rows, :] = u
            s.dsum[rows, :] = u.astype(BF16)
            return su + jnp.sum(u, axis=0, keepdims=True), sux + jnp.sum(u * x, axis=0, keepdims=True)

        s.u3[...] = dot_last(s.dred[...], s.wr[...].reshape(1024, 512))
        nil = jnp.zeros((1, 1024), F32)
        su, sux = lax.fori_loop(0, 10, d3_step, (nil, nil))
        put_stats(3, su, sux, 1024, None)
        ds_x = ln.push(s.dsum.at[pl.ds(other_rows, 160)], s.dsr, xpeer)
        gr[...] = dot_first(s.blk[...], s.dred[...]).astype(BF16).reshape(gr.shape)
        gr_c = to_core(gr, s.rcr, False)
        t = reduce_all(3, None)
        gs3 = ln.push(s.at3, s.o_gs3.at[r], xpeer)
        gs3n = ln.near(s.at3, s.o_gs3.at[r])
        mu = jnp.concatenate([t[0:1], t[1:2]], axis=1) / count
        mux = jnp.concatenate([t[2:3], t[3:4]], axis=1) / count

        def dp3_step(base):
            rows = pl.ds(base, 32)
            x = (s.pre3[rows, :] - s.bnp3[0:1]) * s.bnp3[1:2]
            d = mask_at(base, 32, 1024) * (s.bnp3[2:3] * s.bnp3[1:2]) * (s.u3[rows, :] - mu - x * mux)
            s.dp3[rows, :] = d.astype(BF16)

        rows_loop(320, 32, dp3_step)

        def partial_out(pas, value_of):
            pas[...] = value_of(ohalf).astype(BF16)

        wlast = s.wl
        s.u3[:, 0:512] = dot_last(s.dp3[...], wlast[...].reshape(512, 1024))
        s.pas2[...] = s.u3[:, pl.ds(ohalf, 256)].astype(BF16)
        pa2 = ln.push(s.pas2, s.par2, xpeer)
        gl[...] = dot_first(s.a2[...], s.dp3[...]).astype(BF16).reshape(gl.shape)
        gl_c = to_core(gl, s.rcl, False)
        wait([gr_c])
        add_core(gr, s.rcr, False)
        gr_y = to_y(s.rcr, s.ryr, False)
        wait([pa2])

        def norm_back(n, par, prebuf, bnp, dst, out_gs):
            def u_step(i, carry):
                su_, sux_ = carry
                base = pl.multiple_of(i * 80, 16)
                rows = pl.ds(base, 80)
                x = (prebuf[rows, :] - bnp[0:1]) * bnp[1:2]
                v = x * bnp[2:3] + bnp[3:4]
                d = s.u3[rows, pl.ds(half, 256)] + par[rows, :].astype(F32)
                u = slope_of(v) * d * mask_at(base, 80, 256)
                s.u3[rows, 512:768] = u
                return su_ + jnp.sum(u, axis=0, keepdims=True), sux_ + jnp.sum(u * x, axis=0, keepdims=True)

            nil_ = jnp.zeros((1, 256), F32)
            su_, sux_ = lax.fori_loop(0, 4, u_step, (nil_, nil_))
            put_stats(n, su_, sux_, 256, None)
            t_ = reduce_all(n, None)
            gsx = ln.push(getattr(s, "at%d" % n), out_gs.at[r], xpeer)
            gsn = ln.near(getattr(s, "at%d" % n), out_gs.at[r])
            mu_, mux_ = t_[0:1] / count, t_[1:2] / count

            def d_step(base):
                rows = pl.ds(base, 80)
                x = (prebuf[rows, :] - bnp[0:1]) * bnp[1:2]
                d = mask_at(base, 80, 256) * (bnp[2:3] * bnp[1:2]) * (s.u3[rows, 512:768] - mu_ - x * mux_)
                dst[rows, :] = d.astype(BF16)

            rows_loop(320, 80, d_step)
            return gsx, gsn

        gs2, gs2n = norm_back(4, s.par2, s.pre2, s.bnp2, s.dp2, s.o_gs2)
        spread(s.dp2, s.d3m, 1, 256)
        s.u3[:, 0:512] = conv_back(s.d3m, s.wm, 0)
        s.pas1[...] = s.u3[:, pl.ds(ohalf, 256)].astype(BF16)
        pa1 = ln.push(s.pas1, s.par1, xpeer)
        conv_weight(s.a3, s.d3m, gq, 1)
        gq_c = to_core(gq, s.rcm, True)
        wait([gl_c])
        add_core(gl, s.rcl, False)
        gl_y = to_y(s.rcl, s.ryl, False)
        wait([pa1])
        gs1, gs1n = norm_back(5, s.par1, s.pre1, s.bnp1, s.dp1, s.o_gs1)
        dp_x = ln.push(s.dp1.at[pl.ds(other_rows, 160)], s.dp1r, xpeer)
        gf[...] = dot_first(s.xall[...], s.dp1[...]).astype(BF16).reshape(gf.shape)
        gf_c = to_core(gf, s.rcf, False)
        wait([gq_c])
        add_core(gq, s.rcm, True)
        gq_y = to_y(s.rcm, s.rym, True)
        wait([gf_c])
        add_core(gf, s.rcf, False)
        gf_y = to_y(s.rcf, s.ryf, False)

        wait([gr_y])
        add_y(s.rcr, s.ryr, False)
        gr_z = [
            ln.push(s.ryr.at[lax.rem(zk(k), np.int32(2))], s.rzr.at[k - 1], dev(zk(k), y, c, r),
                    lax.div(zk(k), np.int32(2)) == r)
            for k in (1, 2, 3)
        ]
        wait([gl_y])
        add_y(s.rcl, s.ryl, False)
        gl_z = to_z(s.ryl, s.rzl, False)
        wait([gq_y])
        add_y(s.rcm, s.rym, True)
        gq_z = to_z(s.rym, s.rzm, True)
        wait([gf_y])
        add_y(s.rcf, s.ryf, False)
        gf_z = to_z(s.ryf, s.rzf, False)

        wait([wfo_x])
        wfo_n = ln.near(s.wfo, s.wfov)
        wait([dp_x, ds_x])
        wfo_n.wait()
        mine_d = s.dp1[pl.ds(my_rows, 160), :]
        other_d = s.dp1r[...]
        for q in range(2):
            cols = slice(1024 * q, 1024 * q + 1024)
            wa = s.wf[2 * q : 2 * q + 2].reshape(1024, 256)
            wb = s.wfov[2 * q : 2 * q + 2].reshape(1024, 256)
            s.u3[pl.ds(0, 160), :] = dot_last(mine_d, wa) + dot_last(other_d, wb)

            def img_step(base):
                rows = pl.ds(base, 32)
                m = mask_at(my_rows + base, 32, 1024)
                own_d = s.dsum[pl.ds(my_rows + base, 32), :].astype(F32)
                far_d = s.dsr[rows, :].astype(F32)
                d = jnp.where(r == q, own_d, far_d)
                s.oimg[rows, cols] = ((s.u3[rows, :] + d) * m).astype(BF16)

            rows_loop(160, 32, img_step)
        img_n = ln.near(s.oimg, s.o_img)

        def task_out(got, rm, g, ps, out):
            wait(got)
            for part in range(3):
                cps = [ln.near(rm.at[k, 3 * part : 3 * part + 3], s.zst.at[k]) for k in range(3)]
                for cp in cps:
                    cp.wait()
                for t in range(3):
                    v = g[3 * part + t, z].astype(F32) + s.zst[0, t].astype(F32)
                    v = v + (s.zst[1, t].astype(F32) + s.zst[2, t].astype(F32))
                    ps[3 * part + t] = v.astype(BF16)
            lanes_out = pl.ds(fhalf, 256)
            sent = []
            for i in (1, 2, 3):
                yy = 1 - y if i & 2 else y
                cc = 1 - c if i & 1 else c
                sent.append(ln.push(ps.at[:, yy, cc], out.at[y, :, :, lanes_out], dev(z, yy, cc, r)))
            return sent, ln.near(ps.at[:, y, c], out.at[y, :, :, lanes_out])

        ms, mn = task_out(gm_z, s.rm, s.gm, s.psm, s.o_mess)
        hs, hn = task_out(gh_z, s.rh, s.gh, s.psh, s.o_heads)

        @pl.when(special)
        def _():
            for cp in gg_z:
                cp.wait_recv()
            v = (s.gg[z].astype(F32) + s.rg[0].astype(F32)) + (s.rg[1].astype(F32) + s.rg[2].astype(F32))
            s.pg[...] = v.astype(BF16)

        gx = {}
        for o in offsets:
            rr, yy, cc = peer(*o)
            gx[o] = ln.push(s.pg.at[yy, cc], s.o_gates.at[r, :, pl.ds(fhalf, 256)], dev(z, yy, cc, rr), special)
        gate_near = pltpu.make_async_copy(
            s.pg.at[y, c], s.o_gates.at[r, :, pl.ds(fhalf, 256)], s.near_sems.at[SEMS - 2]
        )
        pl.when(special)(gate_near.start)

        wait(cg)
        v = s.gcls[b].astype(F32)
        for i in range(15):
            v = v + s.rcls[i].astype(F32)
        s.clss[...] = v
        cls_x = ln.push(s.clss, s.clsr, xpeer)

        wait([gr_z[0], gr_z[1], gr_z[2]], owner)

        @pl.when(owner)
        def _():
            v_ = s.ryr[zl].astype(F32) + s.rzr[0].astype(F32)
            s.fnr[...] = (v_ + (s.rzr[1].astype(F32) + s.rzr[2].astype(F32))).astype(BF16)

        gr_x = ln.push(s.fnr, s.o_red, xpeer, owner)
        red_near = pltpu.make_async_copy(s.fnr, s.o_red, s.near_sems.at[SEMS - 3])
        pl.when(owner)(red_near.start)
        wait(gl_z)
        add_z(s.ryl, s.rzl, s.fnl, False)
        gl_x = ln.push(s.fnl, s.o_last.at[:, lastl], xpeer)
        n1 = ln.near(s.fnl, s.o_last.at[:, lastl])
        wait(gq_z)
        add_z(s.rym, s.rzm, s.fnm, True)
        gq_x = ln.push(s.fnm, s.o_mid.at[:, :, pl.ds(half, 256)], xpeer)
        n2 = ln.near(s.fnm, s.o_mid.at[:, :, pl.ds(half, 256)])
        wait(gf_z)
        add_z(s.ryf, s.rzf, s.fnf, False)
        gf_x = ln.push(s.fnf, s.o_first.at[:, pl.ds(half, 256)], xpeer)
        n3 = ln.near(s.fnf, s.o_first.at[:, pl.ds(half, 256)])
        wait([cls_x])
        s.clso[...] = s.clss[...] + s.clsr[...]
        n4 = ln.near(s.clso, s.o_cls)
        wait([gr_x], jnp.logical_not(owner))
        wait([gl_x, gq_x, gf_x, gs1, gs2, gs3])
        wait(ms + hs)
        for o in offsets:
            wait([gx[o]], (r != y) if (o[0] + o[1]) % 2 else special)
        pl.when(special)(gate_near.wait)
        pl.when(owner)(red_near.wait)
        for cp in (gs1n, gs2n, gs3n, img_n, mn, hn, n1, n2, n3, n4):
            cp.wait()
        ln.drain()

    pl.run_scoped(block_back, *[pltpu.VMEM(*v) for v in LATE.values()])


SHAPES["dfs2"] = ((1280, 256), BF16)


LATE = dict(
    u3=((320, 1024), F32),
    dp3=((320, 1024), BF16),
    d3m=((480, 768), BF16),
    dsum=((320, 1024), BF16),
    oimg=((160, 2048), BF16),
    pas1=((320, 256), BF16),
    pas2=((320, 256), BF16),
    dp1=((320, 256), BF16),
    dp2=((320, 256), BF16),
    wfov=((4, 2, 2, 128, 256), BF16),
    gr=((2, 2, 2, 128, 512), BF16),
    gl=((4, 2, 2, 32, 1024), BF16),
    gq=((9, 4, 2, 2, 32, 256), BF16),
    gf=((4, 2, 2, 128, 256), BF16),
)


def fast(args):
    (
        images, crop_height, crop_width, w_first, gain_first, shift_first, w_middle, gain_middle, shift_middle,
        w_last, gain_last, shift_last, w_reduce, w_heads, w_message, w_gates, w_classes, depth_cot, class_cot,
    ) = args
    b, r = lax.axis_index("batch"), lax.axis_index("rows")
    batch = lax.axis_size("batch")
    classes = w_classes.shape[1]

    def placed(vec):
        share = vec.shape[0]
        full = jnp.tile(vec.astype(F32), batch)
        owner = lax.iota(jnp.int32, share * batch) // share
        return lax.dynamic_slice_in_dim(jnp.where(owner == b, full, 0.0), r * (share * batch // 2), share * batch // 2)

    def small(gain, shift):
        zero = jnp.zeros((256,), F32)
        return jnp.stack([zero, zero, placed(gain), placed(shift), zero, zero, zero, zero])

    st3 = jnp.concatenate(
        [jnp.zeros((4, 512), F32), placed(gain_last).reshape(2, 512), placed(shift_last).reshape(2, 512)]
    )
    ins = (
        crop_height, crop_width, images.reshape(160, 2048), w_first, w_middle, w_last, w_reduce, w_gates,
        jnp.pad(w_classes, ((0, 0), (0, 128 - classes))), w_heads, w_message,
        small(gain_first, shift_first), small(gain_middle, shift_middle), st3,
        depth_cot.reshape(160, 512), jnp.pad(class_cot.reshape(160, classes), ((0, 0), (0, 128 - classes))),
    )
    names = list(INS) + list(OUTS) + list(SHAPES) + ["send_sems", "recv_sems", "near_sems"]
    smem, hbm, vmem = (pl.BlockSpec(memory_space=m) for m in (pltpu.SMEM, pl.ANY, pltpu.VMEM))
    spec = {"crop_h": smem, "crop_w": smem, "st1": vmem, "st2": vmem, "st3": vmem}
    outs = pl.pallas_call(
        functools.partial(body, names),
        out_shape=[jax.ShapeDtypeStruct(*v) for v in OUTS.values()],
        in_specs=[spec.get(n, hbm) for n in INS],
        out_specs=[hbm] * len(OUTS),
        scratch_shapes=[pltpu.VMEM(*v) for v in SHAPES.values()]
        + [pltpu.SemaphoreType.DMA((SEMS,)) for _ in range(3)],
        compiler_params=pltpu.CompilerParams(has_side_effects=True, vmem_limit_bytes=64 * 2**20),
        name="residual_distill",
    )(*ins)
    o = dict(zip(OUTS, outs))

    def share_of(v, axis):
        return v.astype(F32)

    def vector(gs, gain):
        per = gs.shape[2] * (gs.shape[1] // 8)
        width = 256 if gs.shape[2] == 256 else 1024
        rows = 1 if width == 256 else 2
        first = gs[:, rows * (1 if gain else 0) : rows * (2 if gain else 1)].reshape(2 * width)
        share = 2 * width // batch
        return lax.dynamic_slice_in_dim(first, b * share, share)

    return (
        o["o_depth"].reshape(1, 2, 80, 512),
        o["o_logits"][:, :classes].reshape(1, 2, 80, classes),
        o["o_img"].astype(F32).reshape(1, 2, 80, 2048),
        o["o_first"].astype(F32),
        vector(o["o_gs1"], True),
        vector(o["o_gs1"], False),
        o["o_mid"].astype(F32),
        vector(o["o_gs2"], True),
        vector(o["o_gs2"], False),
        o["o_last"].astype(F32),
        vector(o["o_gs3"], True),
        vector(o["o_gs3"], False),
        o["o_red"].astype(F32),
        o["o_heads"].astype(F32),
        o["o_mess"].astype(F32),
        o["o_gates"].astype(F32),
        o["o_cls"][:, :classes],
    )


def solution(mesh):
    def step(*args):
        if mesh.shape["batch"] == 16 and mesh.shape["rows"] == 2:
            return fast(args)
        return shards(*args)

    placed = (
        P("batch", "rows", None, None),
        P(),
        P(),
        P("batch", None),
        P("batch"),
        P("batch"),
        P(None, "batch", None),
        P("batch"),
        P("batch"),
        P("batch", None),
        P("batch"),
        P("batch"),
        P("batch", None),
        P("rows", None, "batch", None),
        P("rows", None, "batch", None),
        P(None, "batch", None),
        P("batch", None),
        P("batch", "rows", None, None),
        P("batch", "rows", None, None),
    )
    return jax.shard_map(
        step,
        mesh=mesh,
        in_specs=placed,
        out_specs=(
            P("batch", "rows", None, None),
            P("batch", "rows", None, None),
            P("batch", "rows", None, None),
            P("batch", None),
            P("batch"),
            P("batch"),
            P(None, "batch", None),
            P("batch"),
            P("batch"),
            P("batch", None),
            P("batch"),
            P("batch"),
            P("batch", None),
            P("rows", None, "batch", None),
            P("rows", None, "batch", None),
            P(None, "batch", None),
            P("batch", None),
        ),
        check_vma=False,
    )
```

```python
import functools
from types import SimpleNamespace

import numpy as np
import jax
import jax.numpy as jnp
from jax import lax
from jax.sharding import PartitionSpec as P
from jax.experimental import pallas as pl
from jax.experimental.pallas import tpu as pltpu

EPS = 1e-05
MESH = pl.DeviceIdType.MESH
F32 = jnp.float32
BF16 = jnp.bfloat16
ROOT = 0.7978845608028654
CUBE = 0.044715
SENDS = 240
NEAR = 54


def dot(left, right):
    return jnp.dot(left, right, preferred_element_type=F32)


def dot_last(left, right):
    return lax.dot_general(left, right, (((1,), (1,)), ((), ())), preferred_element_type=F32)


def dot_first(left, right):
    return lax.dot_general(left, right, (((0,), (0,)), ((), ())), preferred_element_type=F32)


def gelu_of(v):
    return 0.5 * v * (1.0 + jnp.tanh(ROOT * (v + CUBE * v * v * v)))


def slope_of(v):
    t = jnp.tanh(ROOT * (v + CUBE * v * v * v))
    return 0.5 * (1.0 + t) + 0.5 * v * (1.0 - t * t) * (ROOT * (1.0 + 3.0 * CUBE * v * v))


def rows_loop(total, chunk, step):
    def body(index, carry):
        step(pl.multiple_of(index * chunk, chunk))
        return carry

    lax.fori_loop(0, total // chunk, body, 0)


class Copy:
    def __init__(self, remote, links, index, like):
        self.remote, self.links, self.index, self.like = remote, links, index, like

    def wait_recv(self):
        if self.like is None:
            self.remote.wait_recv()
        else:
            ref = self.like(1)
            pltpu.make_async_copy(ref, ref, self.links.recv.at[self.index]).wait()

    def wait_send(self):
        if self.like is None:
            self.remote.wait_send()
        else:
            ref = self.like(0)
            pltpu.make_async_copy(ref, ref, self.links.send.at[self.index]).wait()


class Group:
    scoped = True

    def __init__(self, links, index, like):
        self.links, self.index, self.like = links, index, like

    def push(self, src, dst, device, when=None):
        remote = pltpu.make_async_remote_copy(
            src_ref=src,
            dst_ref=dst,
            send_sem=self.links.send.at[self.index],
            recv_sem=self.links.recv.at[self.index],
            device_id=device,
            device_id_type=MESH,
        )
        if when is None:
            remote.start()
        else:
            pl.when(when)(remote.start)

    def wait_recv(self):
        ref = self.like()
        pltpu.make_async_copy(ref, ref, self.links.recv.at[self.index]).wait()

    def wait_send(self):
        ref = self.like()
        pltpu.make_async_copy(ref, ref, self.links.send.at[self.index]).wait()


class Links:
    def __init__(self, send, recv, local):
        self.send, self.recv, self.local = send, recv, local
        self.used, self.local_used = 0, 0
        self.open = []

    def push(self, src, dst, device, when=None, like=None):
        i = self.used
        self.used += 1
        send, recv = self.send.at[i], self.recv.at[i]
        remote = pltpu.make_async_remote_copy(
            src_ref=src, dst_ref=dst, send_sem=send, recv_sem=recv, device_id=device, device_id_type=MESH
        )
        if when is None:
            remote.start()
        else:
            pl.when(when)(remote.start)
        cp = Copy(remote, self, i, like)
        self.open.append((cp, when))
        return cp

    def group(self, like, when=None):
        cp = Group(self, self.used, like)
        self.used += 1
        self.open.append((cp, when))
        return cp

    def near(self, src, dst):
        i = self.local_used
        self.local_used += 1
        cp = pltpu.make_async_copy(src, dst, self.local.at[i])
        cp.start()
        return cp

    def drain(self, scoped=False):
        kept = []
        for cp, when in self.open:
            if scoped and isinstance(cp, Copy) and cp.like is not None:
                kept.append((cp, when))
            elif when is None:
                cp.wait_send()
            else:
                pl.when(when)(cp.wait_send)
        self.open = kept


def wait(copies, when=None):
    def run():
        for cp in copies:
            cp.wait_recv()

    if when is None:
        run()
    else:
        pl.when(when)(run)


def lanes(mask, width):
    return jnp.concatenate([mask] * (width // 128), axis=1) if width > 128 else mask


def padded_2(cells, sides, width):
    for axis, dim in sides:
        count = lax.axis_size(axis)
        ends = count - 1
        head = lax.slice_in_dim(cells, 0, width, axis=dim)
        tail = lax.slice_in_dim(cells, cells.shape[dim] - width, cells.shape[dim], axis=dim)
        cells = jnp.concatenate(
            [
                lax.ppermute(tail, axis, [(i, (i + 1) % count) for i in range(ends)]),
                cells,
                lax.ppermute(head, axis, [((i + 1) % count, i) for i in range(ends)]),
            ],
            axis=dim,
        )
    return cells


def gelu_tanh(values):
    return jax.nn.gelu(values, approximate=True)


def gelu_slope(values, upstream):
    return jax.vjp(gelu_tanh, values)[1](upstream)[0]


def project(values, weight):
    return jnp.einsum("nrcj,jk->nrck", values, weight, preferred_element_type=jnp.float32)


def project_back(upstream, weight):
    return jnp.einsum("nrck,jk->nrcj", upstream, weight, preferred_element_type=jnp.float32)


def outer_sum(values, upstream):
    return jnp.einsum("nrcj,nrck->jk", values, upstream, preferred_element_type=jnp.float32)


def widen(padded):
    return jnp.pad(padded, ((0, 0), (0, 0), (1, 1), (0, 0)))


def halo_value(values):
    return padded_2(values, (("rows", 1),), 1)


def halo_grad(values):
    return padded_2(values, (("rows", 1),), 1)


def conv_apply(padded, kernel):
    row_count = padded.shape[1] - 2
    col_count = padded.shape[2]
    widened = widen(padded)
    running = jnp.zeros((padded.shape[0], row_count, col_count, kernel.shape[2]), jnp.float32)
    for tap_index in range(9):
        shift_down = tap_index // 3
        shift_right = tap_index % 3
        running = running + project(
            widened[
                :, shift_down : shift_down + row_count, shift_right : shift_right + col_count, :
            ],
            kernel[tap_index],
        )
    return running


def conv_kernel_grad(padded, upstream):
    row_count = upstream.shape[1]
    col_count = upstream.shape[2]
    widened = widen(padded)
    return jnp.stack(
        [
            outer_sum(
                widened[
                    :,
                    tap_index // 3 : tap_index // 3 + row_count,
                    tap_index % 3 : tap_index % 3 + col_count,
                    :,
                ],
                upstream,
            )
            for tap_index in range(9)
        ]
    )


def conv_input_grad(padded_grad, kernel):
    row_count = padded_grad.shape[1] - 2
    col_count = padded_grad.shape[2]
    widened = widen(padded_grad)
    running = jnp.zeros((padded_grad.shape[0], row_count, col_count, kernel.shape[1]), jnp.float32)
    for tap_index in range(9):
        shift_down = tap_index // 3
        shift_right = tap_index % 3
        running = running + project_back(
            widened[
                :,
                2 - shift_down : 2 - shift_down + row_count,
                2 - shift_right : 2 - shift_right + col_count,
                :,
            ],
            kernel[tap_index],
        )
    return running


def crop_mask(height, width, first_row, row_count, col_count):
    row_ids = first_row + jnp.arange(row_count, dtype=jnp.int32)
    col_ids = jnp.arange(col_count, dtype=jnp.int32)
    inside = (row_ids[None, :, None] < height[:, None, None]) & (
        col_ids[None, None, :] < width[:, None, None]
    )
    return inside.astype(jnp.float32)[..., None]


def norm_forward(pre_act, pixel_mask, gain_vec, shift_vec, valid_count):
    sums = jnp.sum(pre_act * pixel_mask, axis=(0, 1, 2))
    squares = jnp.sum(pre_act * pre_act * pixel_mask, axis=(0, 1, 2))
    sums, squares = lax.psum((sums, squares), ("batch", "rows"))
    mean_vec = sums / valid_count
    inv_std = lax.rsqrt(squares / valid_count - mean_vec * mean_vec + EPS)
    normal = (pre_act - mean_vec) * inv_std
    return (normal, inv_std, normal * gain_vec + shift_vec)


def norm_backward(upstream, normal, inv_std, gain_vec, pixel_mask, valid_count):
    shift_part = jnp.sum(upstream, axis=(0, 1, 2))
    gain_part = jnp.sum(upstream * normal, axis=(0, 1, 2))
    shift_part, gain_part = lax.psum((shift_part, gain_part), ("batch", "rows"))
    d_pre = (
        pixel_mask
        * gain_vec
        * inv_std
        * (upstream - shift_part / valid_count - normal * gain_part / valid_count)
    )
    return (d_pre, gain_part, shift_part)


def task_forward(padded_in, heads, messages, pixel_mask, pad_rows):
    pre_list = []
    feat_list = []
    padded_feats = []
    message_list = []
    for task in range(heads.shape[0]):
        pre_act = conv_apply(padded_in, heads[task])
        feature = (gelu_tanh(pre_act) * pixel_mask).astype(jnp.bfloat16)
        padded_feat = pad_rows(feature)
        pre_list.append(pre_act)
        feat_list.append(feature)
        padded_feats.append(padded_feat)
        message_list.append(conv_apply(padded_feat, messages[task]).astype(jnp.bfloat16))
    return (pre_list, feat_list, padded_feats, message_list)


def task_backward(
    padded_in,
    heads,
    messages,
    pixel_mask,
    pre_list,
    padded_feats,
    feat_grads,
    message_grads,
    pad_grad,
):
    input_grad = jnp.zeros(
        padded_in.shape[:1] + (padded_in.shape[1] - 2,) + padded_in.shape[2:], jnp.float32
    )
    head_grads = []
    kernel_grads = []
    for task in range(heads.shape[0]):
        low_message = message_grads[task].astype(jnp.bfloat16)
        kernel_grads.append(conv_kernel_grad(padded_feats[task], low_message))
        feat_grad = feat_grads[task] + conv_input_grad(pad_grad(low_message), messages[task])
        low_pre = gelu_slope(pre_list[task], feat_grad * pixel_mask).astype(jnp.bfloat16)
        head_grads.append(conv_kernel_grad(padded_in, low_pre))
        input_grad = input_grad + conv_input_grad(pad_grad(low_pre), heads[task])
    return (input_grad, jnp.stack(head_grads), jnp.stack(kernel_grads))


def streams_forward(features, messages, gates_all, classes_all, pixel_mask):
    gate_depth = jax.nn.sigmoid(project(features[0], gates_all[0]))
    gate_class = jax.nn.sigmoid(project(features[3], gates_all[1]))
    depth_sum = (
        messages[1].astype(jnp.float32)
        + messages[2].astype(jnp.float32)
        + messages[3].astype(jnp.float32)
    )
    class_sum = (
        messages[0].astype(jnp.float32)
        + messages[1].astype(jnp.float32)
        + messages[2].astype(jnp.float32)
    )
    depth_stream = (features[0].astype(jnp.float32) + gate_depth * depth_sum) * pixel_mask
    merged = (features[3].astype(jnp.float32) + gate_class * class_sum).astype(jnp.bfloat16)
    class_logits = project(merged, classes_all) * pixel_mask
    return (depth_stream, class_logits, merged, gate_depth, gate_class, depth_sum, class_sum)


def streams_backward(
    features,
    merged,
    gate_depth,
    gate_class,
    depth_sum,
    class_sum,
    depth_cot,
    class_cot,
    gates_all,
    classes_all,
    pixel_mask,
):
    depth_grad = depth_cot.astype(jnp.float32) * pixel_mask
    logit_grad = (class_cot.astype(jnp.float32) * pixel_mask).astype(jnp.bfloat16)
    grad_classes = outer_sum(merged, logit_grad)
    merged_grad = project_back(logit_grad, classes_all)
    gate_depth_grad = (depth_grad * depth_sum * gate_depth * (1.0 - gate_depth)).astype(
        jnp.bfloat16
    )
    gate_class_grad = (merged_grad * class_sum * gate_class * (1.0 - gate_class)).astype(
        jnp.bfloat16
    )
    grad_gates = jnp.stack(
        [outer_sum(features[0], gate_depth_grad), outer_sum(features[3], gate_class_grad)]
    )
    depth_feat = depth_grad + project_back(gate_depth_grad, gates_all[0])
    class_feat = merged_grad + project_back(gate_class_grad, gates_all[1])
    depth_message = depth_grad * gate_depth
    class_message = merged_grad * gate_class
    nothing = jnp.zeros_like(depth_grad)
    feat_grads = [depth_feat, nothing, nothing, class_feat]
    message_grads = [
        class_message,
        depth_message + class_message,
        depth_message + class_message,
        depth_message,
    ]
    return (feat_grads, message_grads, grad_gates, grad_classes)


def shards(
    images,
    crop_height,
    crop_width,
    w_first,
    gain_first,
    shift_first,
    w_middle,
    gain_middle,
    shift_middle,
    w_last,
    gain_last,
    shift_last,
    w_reduce,
    w_heads,
    w_message,
    w_gates,
    w_classes,
    depth_cot,
    class_cot,
):
    image_index = lax.axis_index("batch")
    batch_count = lax.axis_size("batch")
    row_count = images.shape[1]
    col_count = images.shape[2]
    height = lax.dynamic_slice_in_dim(crop_height, image_index, 1, 0)
    width = lax.dynamic_slice_in_dim(crop_width, image_index, 1, 0)
    pixel_mask = crop_mask(height, width, lax.axis_index("rows") * row_count, row_count, col_count)
    valid_count = jnp.sum(crop_height * crop_width).astype(jnp.float32)
    gathered = (
        lax.all_gather(w_first, "batch", axis=0, tiled=True),
        lax.all_gather(w_middle, "batch", axis=1, tiled=True),
        lax.all_gather(w_last, "batch", axis=0, tiled=True),
        lax.all_gather(w_reduce, "batch", axis=0, tiled=True),
        lax.all_gather(w_gates, "batch", axis=1, tiled=True),
        lax.all_gather(w_classes, "batch", axis=0, tiled=True),
        lax.all_gather(gain_first, "batch", axis=0, tiled=True),
        lax.all_gather(shift_first, "batch", axis=0, tiled=True),
        lax.all_gather(gain_middle, "batch", axis=0, tiled=True),
        lax.all_gather(shift_middle, "batch", axis=0, tiled=True),
        lax.all_gather(gain_last, "batch", axis=0, tiled=True),
        lax.all_gather(shift_last, "batch", axis=0, tiled=True),
        lax.all_gather(w_heads, "batch", axis=2, tiled=True),
        lax.all_gather(w_message, "batch", axis=2, tiled=True),
    )
    first_all = gathered[0]
    middle_all = gathered[1]
    last_all = gathered[2]
    reduce_all = gathered[3]
    gates_all = gathered[4]
    classes_all = gathered[5]
    gain_one = gathered[6].astype(jnp.float32)
    shift_one = gathered[7].astype(jnp.float32)
    gain_two = gathered[8].astype(jnp.float32)
    shift_two = gathered[9].astype(jnp.float32)
    gain_three = gathered[10].astype(jnp.float32)
    shift_three = gathered[11].astype(jnp.float32)
    heads_own = gathered[12]
    message_own = gathered[13]
    masked_in = images.astype(jnp.float32) * pixel_mask
    low_in = masked_in.astype(jnp.bfloat16)
    pre_first = project(low_in, first_all)
    normal_first, std_first, out_first = norm_forward(
        pre_first, pixel_mask, gain_one, shift_one, valid_count
    )
    act_first = (gelu_tanh(out_first) * pixel_mask).astype(jnp.bfloat16)
    padded_first = halo_value(act_first)
    pre_middle = conv_apply(padded_first, middle_all)
    normal_middle, std_middle, out_middle = norm_forward(
        pre_middle, pixel_mask, gain_two, shift_two, valid_count
    )
    act_middle = (gelu_tanh(out_middle) * pixel_mask).astype(jnp.bfloat16)
    pre_last = project(act_middle, last_all)
    normal_last, std_last, out_last = norm_forward(
        pre_last, pixel_mask, gain_three, shift_three, valid_count
    )
    summed = out_last + masked_in
    block_out = (gelu_tanh(summed) * pixel_mask).astype(jnp.bfloat16)
    low_reduced = project(block_out, reduce_all).astype(jnp.bfloat16)
    heads_all, message_all = (
        lax.all_gather(heads_own, "rows", axis=0, tiled=True),
        lax.all_gather(message_own, "rows", axis=0, tiled=True),
    )
    padded_in = halo_value(low_reduced)
    pre_list, feat_list, padded_feats, message_list = task_forward(
        padded_in, heads_all, message_all, pixel_mask, halo_value
    )
    depth_stream, class_logits, merged, gate_depth, gate_class, depth_sum, class_sum = (
        streams_forward(feat_list, message_list, gates_all, classes_all, pixel_mask)
    )
    feat_grads, message_grads, grad_gates, grad_classes = streams_backward(
        feat_list,
        merged,
        gate_depth,
        gate_class,
        depth_sum,
        class_sum,
        depth_cot,
        class_cot,
        gates_all,
        classes_all,
        pixel_mask,
    )
    reduced_grad, grad_heads, grad_message = task_backward(
        padded_in,
        heads_all,
        message_all,
        pixel_mask,
        pre_list,
        padded_feats,
        feat_grads,
        message_grads,
        halo_grad,
    )
    low_reduced_grad = reduced_grad.astype(jnp.bfloat16)
    grad_reduce = outer_sum(block_out, low_reduced_grad)
    block_grad = project_back(low_reduced_grad, reduce_all)
    sum_grad = gelu_slope(summed, block_grad * pixel_mask)
    d_last, gain_grad_three, shift_grad_three = norm_backward(
        sum_grad, normal_last, std_last, gain_three, pixel_mask, valid_count
    )
    low_last = d_last.astype(jnp.bfloat16)
    grad_last = outer_sum(act_middle, low_last)
    middle_grad = project_back(low_last, last_all)
    d_middle, gain_grad_two, shift_grad_two = norm_backward(
        gelu_slope(out_middle, middle_grad * pixel_mask),
        normal_middle,
        std_middle,
        gain_two,
        pixel_mask,
        valid_count,
    )
    low_middle = d_middle.astype(jnp.bfloat16)
    grad_middle = conv_kernel_grad(padded_first, low_middle)
    first_grad = conv_input_grad(halo_grad(low_middle), middle_all)
    d_first, gain_grad_one, shift_grad_one = norm_backward(
        gelu_slope(out_first, first_grad * pixel_mask),
        normal_first,
        std_first,
        gain_one,
        pixel_mask,
        valid_count,
    )
    low_first = d_first.astype(jnp.bfloat16)
    grad_first = outer_sum(low_in, low_first)
    image_grad = (project_back(low_first, first_all) + sum_grad) * pixel_mask
    summed_grads = (
        lax.psum_scatter(grad_first, "batch", scatter_dimension=0, tiled=True),
        lax.psum_scatter(grad_middle, "batch", scatter_dimension=1, tiled=True),
        lax.psum_scatter(grad_last, "batch", scatter_dimension=0, tiled=True),
        lax.psum_scatter(grad_reduce, "batch", scatter_dimension=0, tiled=True),
        lax.psum_scatter(grad_gates, "batch", scatter_dimension=1, tiled=True),
        lax.psum_scatter(grad_classes, "batch", scatter_dimension=0, tiled=True),
        lax.psum_scatter(grad_heads, "batch", scatter_dimension=2, tiled=True),
        lax.psum_scatter(grad_message, "batch", scatter_dimension=2, tiled=True),
    )
    shared = (
        lax.psum(summed_grads[0].astype(jnp.bfloat16), "rows").astype(jnp.float32),
        lax.psum(summed_grads[1].astype(jnp.bfloat16), "rows").astype(jnp.float32),
        lax.psum(summed_grads[2].astype(jnp.bfloat16), "rows").astype(jnp.float32),
        lax.psum(summed_grads[3].astype(jnp.bfloat16), "rows").astype(jnp.float32),
        lax.psum(summed_grads[4].astype(jnp.bfloat16), "rows").astype(jnp.float32),
        lax.psum(summed_grads[5].astype(jnp.bfloat16), "rows").astype(jnp.float32),
    )
    heads_out, message_out = (
        lax.psum_scatter(
            summed_grads[6].astype(jnp.bfloat16), "rows", scatter_dimension=0, tiled=True
        ).astype(jnp.float32),
        lax.psum_scatter(
            summed_grads[7].astype(jnp.bfloat16), "rows", scatter_dimension=0, tiled=True
        ).astype(jnp.float32),
    )

    def own_share(member):
        share = member.shape[0] // batch_count
        return lax.dynamic_slice_in_dim(member, image_index * share, share, 0)

    return (
        depth_stream.astype(jnp.bfloat16),
        class_logits.astype(jnp.bfloat16),
        image_grad,
        shared[0],
        own_share(gain_grad_one),
        own_share(shift_grad_one),
        shared[1],
        own_share(gain_grad_two),
        own_share(shift_grad_two),
        shared[2],
        own_share(gain_grad_three),
        own_share(shift_grad_three),
        shared[3],
        heads_out,
        message_out,
        shared[4],
        shared[5],
    )


SHAPES = dict(
    wf=((4, 2, 2, 128, 256), BF16),
    wm=((9, 4, 2, 2, 32, 256), BF16),
    wl=((4, 2, 2, 32, 1024), BF16),
    wr=((4, 2, 128, 512), BF16),
    wc=((16, 32, 128), BF16),
    wcs=((32, 128), BF16),
    wcv=((32, 40), BF16),
    cct=((2, 40, 80), BF16),
    ctf=((128, 128), F32),
    xh=((320, 1024), BF16),
    wh=((9, 4, 2, 2, 32, 256), BF16),
    wq=((9, 4, 2, 2, 32, 256), BF16),
    wg=((4, 2, 2, 32, 256), BF16),
    xall=((320, 2048), BF16),
    maskp=((1280, 128), F32),
    pre1=((320, 256), F32),
    pre2=((320, 256), F32),
    pre3=((320, 1024), F32),
    bnp1=((8, 256), F32),
    bnp2=((8, 256), F32),
    bnp3=((8, 1024), F32),
    a1=((320, 512), BF16),
    a2=((320, 512), BF16),
    a3=((480, 1536), BF16),
    blk=((320, 1024), BF16),
    rps=((160, 512), BF16),
    rpr=((160, 512), BF16),
    rbuf=((1280, 512), BF16),
    fown=((1280, 256), BF16),
    ffull=((1280, 512), BF16),
    msgb=((1280, 256), BF16),
    gateb=((1280, 256), BF16),
    mrecv=((4, 160, 512), BF16),
    dcotv=((160, 512), BF16),
    ccotv=((160, 128), BF16),
    olt=((2, 40, 80), BF16),
    ods=((160, 512), BF16),
    olg=((160, 128), BF16),
    mrg=((160, 512), BF16),
    fg=((2, 2, 160, 512), BF16),
    dmg=((1280, 256), BF16),
    exg=((2, 1280, 256), BF16),
    gm=((9, 4, 2, 2, 32, 256), BF16),
    gh=((9, 4, 2, 2, 32, 256), BF16),
    gg=((4, 2, 2, 32, 256), BF16),
    rg=((3, 2, 2, 32, 256), BF16),
    hop=((2, 9, 2, 2, 32, 256), BF16),
    gcls=((16, 32, 128), BF16),
    rcls=((15, 32, 128), BF16),
    clsr=((32, 128), F32),
    dfs=((1280, 256), BF16),
    dfr=((1280, 256), BF16),
    drs=((640, 512), BF16),
    drr=((640, 512), BF16),
    dro=((3, 160, 512), BF16),
    dred=((320, 512), BF16),
    dsr=((160, 1024), BF16),
    par2=((320, 256), BF16),
    par1=((320, 256), BF16),
    dp1r=((160, 256), BF16),
    rcr=((4, 2, 128, 512), BF16),
    rcl=((4, 2, 32, 1024), BF16),
    rcm=((9, 4, 2, 32, 256), BF16),
    rcf=((4, 2, 128, 256), BF16),
    ryr=((4, 128, 512), BF16),
    ryl=((4, 32, 1024), BF16),
    rym=((9, 4, 32, 256), BF16),
    ryf=((4, 128, 256), BF16),
    rzr=((3, 128, 512), BF16),
    rzl=((3, 32, 1024), BF16),
    rzm=((3, 9, 32, 256), BF16),
    rzf=((3, 128, 256), BF16),
)
for _i, _w in enumerate((256, 256, 512, 512, 256, 256)):
    SHAPES["am%d" % _i] = ((8, _w), F32)
    SHAPES["as%d" % _i] = ((8, _w), F32)
    SHAPES["at%d" % _i] = ((8, _w), F32)
    SHAPES["ar%d" % _i] = ((3, 8, _w), F32)
    SHAPES["az%d" % _i] = ((3, 8, _w), F32)

INS = (
    "crop_h", "crop_w", "images", "first", "middle", "last", "reduce", "gates",
    "classes", "heads", "messages", "gains", "dcot", "ccot",
)
OUTS = dict(
    o_depth=((160, 512), BF16),
    o_logits=((2, 40, 80), BF16),
    o_img=((160, 2048), BF16),
    o_first=((128, 512), BF16),
    o_gs1=((2, 8, 256), F32),
    o_mid=((9, 32, 512), BF16),
    o_gs2=((2, 8, 256), F32),
    o_last=((2, 32, 1024), BF16),
    o_gs3=((2, 8, 512), F32),
    o_red=((128, 512), BF16),
    o_heads=((2, 9, 32, 512), BF16),
    o_mess=((2, 9, 32, 512), BF16),
    o_gates=((2, 32, 512), BF16),
    o_cls=((32, 128), F32),
    rm=((3, 9, 2, 2, 32, 256), BF16),
    rh=((3, 9, 2, 2, 32, 256), BF16),
    wfo=((4, 2, 2, 128, 256), BF16),
    st_h=((9, 32, 512), BF16),
    st_m=((9, 32, 512), BF16),
)


def shift_columns(v):
    rows, width = v.shape
    col = lax.broadcasted_iota(jnp.int32, (rows, width), 0)
    left = jnp.where(col == 0, 0.0, pltpu.roll(v, 1, 0))
    right = jnp.where(col == rows - 1, 0.0, pltpu.roll(v, rows - 1, 0))
    return left, right


def spread(src, dst, n_img, width):
    zero = jnp.zeros((80, 3 * width), BF16)
    for pad in range(n_img + 1):
        dst[pl.ds(pad * 400, 80), :] = zero

    def body(i, carry):
        v = src[pl.ds(pl.multiple_of(i * 80, 16), 80), :]
        left, right = shift_columns(v.astype(F32))
        row = pl.multiple_of((i + lax.div(i, np.int32(4)) + 1) * 80, 16)
        dst[pl.ds(row, 80), 0:width] = left.astype(BF16)
        dst[pl.ds(row, 80), width : 2 * width] = v
        dst[pl.ds(row, 80), 2 * width : 3 * width] = right.astype(BF16)
        return carry

    lax.fori_loop(0, 4 * n_img, body, 0)


def conv_rows(a3, w, img):
    acc = None
    for a in range(3):
        base = pl.multiple_of((5 * img + a) * 80, 16)
        part = dot(a3[pl.ds(base, 320), :], w[3 * a : 3 * a + 3].reshape(1536, 256))
        acc = part if acc is None else acc + part
    return acc


def conv_back(d3, w, img):
    acc = None
    for a in range(3):
        for q in range(3):
            base = pl.multiple_of((5 * img + a) * 80, 16)
            tap = 3 * (2 - a) + (2 - q)
            part = dot_last(d3[pl.ds(base, 320), 256 * q : 256 * q + 256], w[tap].reshape(512, 256))
            acc = part if acc is None else acc + part
    return acc


def conv_weight(a3, d3, out, n_img, first, last):
    depth = (5 * n_img - 1) * 80

    def body(tap, carry):
        a = lax.div(tap, np.int32(3))
        q = tap - 3 * a
        left = a3[pl.ds(pl.multiple_of(a * 80, 16), depth), pl.ds(pl.multiple_of(q * 512, 128), 512)]
        out[tap] = dot_first(left, d3[pl.ds(80, depth), 256:512]).astype(BF16).reshape(out.shape[1:])
        return carry

    lax.fori_loop(first, last, body, 0)


def body(names, *refs):
    s = SimpleNamespace(**dict(zip(names, refs)))
    b, r = lax.axis_index("batch"), lax.axis_index("rows")
    z = lax.div(b, np.int32(4))
    y = lax.rem(lax.div(b, np.int32(2)), np.int32(2))
    c = lax.rem(b, np.int32(2))
    ln = Links(s.send_sems, s.recv_sems, s.near_sems)
    half, fhalf = 256 * r, 256 * c

    def dev(zz, yy, cc, rr):
        return (4 * zz + 2 * yy + cc, rr)

    def zk(k):
        return lax.rem(z + k, np.int32(4))

    core, ypeer, xpeer = dev(z, y, 1 - c, r), dev(z, 1 - y, c, r), dev(z, y, c, 1 - r)
    special = r == y
    task = 2 * r + y
    img = 2 * y + c
    own_px = pl.multiple_of(320 * img + 160 * r, 16)
    my_rows = pl.multiple_of(160 * r, 16)
    other_rows = pl.multiple_of(160 * (1 - r), 16)
    half = pl.multiple_of(half, 128)
    ohalf = pl.multiple_of(256 * (1 - r), 128)
    fhalf = pl.multiple_of(fhalf, 128)
    offsets = [(dr, dy, dc) for dr in range(2) for dy in range(2) for dc in range(2) if dr + dy + dc]

    def peer(dr, dy, dc):
        rr = 1 - r if dr else r
        yy = 1 - y if dy else y
        cc = 1 - c if dc else c
        return rr, yy, cc

    def px_of(rr, yy, cc):
        return pl.multiple_of(320 * (2 * yy + cc) + 160 * rr, 16)

    ends = (z == 0) | (z == 3)
    inner = jnp.logical_not(ends)
    not_first, not_last = z != 0, z != 3
    far_end = dev(jnp.where(z == 1, 0, 3), y, c, r)
    odd = c == r

    def both(p, q):
        return q if p is None else (p if q is None else p & q)

    def line_start(src, at, when=None):
        got = {q: ln.push(src, at(z), dev(zk(q), y, c, r), when) for q in (1, 3)}
        got[2] = ln.push(src, at(z), dev(zk(2), y, c, r), both(when, ends))
        return got, [ln.push(src, at(z), ypeer, when)]

    def line_relay(state, at, when=None):
        got, ys = state
        wait([got[1], got[3]], when)
        got[0] = ln.push(at(3 - z), at(3 - z), far_end, both(when, inner))
        ys.append(ln.push(at(zk(3)), at(zk(3)), ypeer, when))
        ys.append(ln.push(at(zk(1)), at(zk(1)), ypeer, when))

    def line_last(state, at, col, when=None):
        got, ys = state
        wait([got[2]], both(when, inner))
        wait([got[0]], both(when, ends))
        ys.append(ln.push(at(zk(2)), at(zk(2)), ypeer, when))
        return [ln.push(col(y), col(y), core, when)]

    def line_core(state, col, cores, when=None):
        wait(state[1], when)
        cores.append(ln.push(col(1 - y), col(1 - y), core, when))

    def at_wf(zz):
        return s.wf.at[zz, y, c]

    def at_wm(zz):
        return s.wm.at[:, zz, y, c]

    def at_wl(zz):
        return s.wl.at[zz, y, c]

    def at_wr(zz):
        return s.wr.at[zz, y]

    def col_wf(yy):
        return s.wf.at[:, yy, c]

    def col_wm(yy):
        return s.wm.at[:, :, yy, c]

    def col_wl(yy):
        return s.wl.at[:, yy, c]

    def col_wr(yy):
        return s.wr.at[:, yy]

    near_last = [
        ln.near(s.last.at[:, pl.ds(pl.multiple_of((2 * i + r) * 128, 128), 128)], s.wl.at[z, y, c, :, 128 * i : 128 * i + 128])
        for i in range(8)
    ]
    near_own = ln.near(s.images, s.xall.at[pl.ds(my_rows, 160)])
    near_cls = ln.near(s.classes, s.wcv)
    near_wf = ln.near(s.first.at[:, pl.ds(half, 256)], s.wf.at[z, y, c])
    near_wm = ln.near(s.middle.at[:, :, pl.ds(half, 256)], s.wm.at[:, z, y, c])
    red_local = pltpu.make_async_copy(s.reduce, s.wr.at[z, y], s.near_sems.at[NEAR - 1])
    pl.when(odd)(red_local.start)
    near_late = [
        ln.near(s.dcot, s.dcotv),
        ln.near(s.ccot, s.cct),
        ln.near(s.heads.at[y, :, :, pl.ds(fhalf, 256)], s.wh.at[:, z, y, c]),
        ln.near(s.messages.at[y, :, :, pl.ds(fhalf, 256)], s.wq.at[:, z, y, c]),
        ln.near(s.gates.at[r, :, pl.ds(fhalf, 256)], s.wg.at[z, y, c]),
    ]
    barrier = pltpu.get_barrier_semaphore()
    friends = [
        dev(zk(q), 1 - y if j else y, 1 - c if i else c, r) for q in range(4) for j in range(2) for i in range(2) if q + j + i
    ] + [dev(z, 1 - y if j else y, 1 - c if i else c, 1 - r) for j in range(2) for i in range(2)]
    for friend in friends:
        pl.semaphore_signal(barrier, inc=1, device_id=friend, device_id_type=MESH)
    pl.semaphore_wait(barrier, len(friends))

    go_wf = line_start(s.first.at[:, pl.ds(half, 256)], at_wf)
    img_x = ln.push(s.images, s.xall.at[pl.ds(my_rows, 160)], xpeer)
    go_wm = line_start(s.middle.at[:, :, pl.ds(half, 256)], at_wm)
    for cp in near_last:
        cp.wait()
    got_wl = {q: ln.push(at_wl(z), at_wl(z), dev(zk(q), y, c, r)) for q in (1, 3)}
    got_wl[2] = ln.push(at_wl(z), at_wl(z), dev(zk(2), y, c, r), ends)
    got_wr = {q: ln.push(s.reduce, at_wr(z), dev(zk(q), y, c, r), odd) for q in (1, 3)}
    got_wr[2] = ln.push(s.reduce, at_wr(z), dev(zk(2), y, c, r), odd & ends)

    for i in range(4):
        high, wide = s.crop_h[4 * z + i], s.crop_w[4 * z + i]
        for row in range(4):
            col = lax.broadcasted_iota(jnp.int32, (80, 128), 0)
            inside = (col < wide) & (row < high)
            s.maskp[pl.ds(320 * i + 80 * row, 80), :] = jnp.where(inside, 1.0, 0.0)
    total = s.crop_h[0] * s.crop_w[0]
    for i in range(1, 16):
        total = total + s.crop_h[i] * s.crop_w[i]
    count = total.astype(F32)
    mine = pl.multiple_of(320 * img, 16)

    def mask_at(base, rows, width):
        return lanes(s.maskp[pl.ds(mine + base, rows), :], width)

    near_cls.wait()
    s.wcs[...] = jnp.zeros(s.wcs.shape, BF16)
    s.wcs[:, 0:40] = s.wcv[...]
    s.wc[b] = s.wcs[...]
    near_own.wait()
    near_wf.wait()
    line_relay(go_wf, at_wf)
    cores_wf = line_last(go_wf, at_wf, col_wf)
    near_wm.wait()
    line_relay(go_wm, at_wm)
    line_core(go_wf, col_wf, cores_wf)
    wait([img_x])

    def mask_x(base):
        rows = pl.ds(base, 80)
        v = (s.xall[rows, :].astype(F32) * mask_at(base, 80, 2048)).astype(BF16)
        s.xall[rows, :] = v
        for i in range(8):
            pick = jnp.where(r == 0, v[:, 256 * i : 256 * i + 128].astype(F32), v[:, 256 * i + 128 : 256 * i + 256].astype(F32))
            s.xh[rows, 128 * i : 128 * i + 128] = pick.astype(BF16)

    rows_loop(320, 80, mask_x)
    wait(cores_wf)

    def task_push(src, dst, lo, hi, staged):
        yy = 1 - y if staged else y
        got = {}
        for q in (1, 3, 2, 0):
            def like(q=q):
                return dst.at[lo:hi, 0, 0] if q else dst.at[lo:hi, 0, 0, 0]

            when = ends if q == 2 else None
            got[q] = ln.group(like, when)
            for i in range(2):
                if q + i == 0:
                    continue
                cc = 1 - c if i else c
                got[q].push(
                    src.at[lo:hi, :, pl.ds(pl.multiple_of(256 * cc, 128), 256)],
                    dst.at[lo:hi, z, yy, c],
                    dev(zk(q) if q else z, y, cc, r),
                    when,
                )
        return got, lo, hi, yy

    def task_relay(state, dst):
        got, lo, hi, yy = state
        wait([got[0], got[1], got[3]])
        hand = ln.push(dst.at[lo:hi, 3 - z, yy], dst.at[lo:hi, 3 - z, yy], far_end, inner)
        return got, hand

    def task_ready(state):
        got, hand = state
        wait([got[2]], inner)
        wait([hand], ends)

    def plane_start(n):
        m, ar = (getattr(s, p + str(n)) for p in ("am", "ar"))
        one = ln.group(lambda: ar)
        for i in (1, 2, 3):
            yy = 1 - y if i & 2 else y
            cc = 1 - c if i & 1 else c
            one.push(m, ar.at[i - 1], dev(z, yy, cc, r))
        return one

    def plane_end(n, one):
        m, sm, ar = (getattr(s, p + str(n)) for p in ("am", "as", "ar"))
        wait([one])
        sm[...] = (m[...] + ar[0]) + (ar[1] + ar[2])

    def reduce_plane(n):
        plane_end(n, plane_start(n))

    def reduce_line(n):
        sm, t, az = (getattr(s, p + str(n)) for p in ("as", "at", "az"))
        two = ln.group(lambda: az)
        for q in (1, 2, 3):
            two.push(sm, az.at[q - 1], dev(zk(q), y, c, r))
        wait([two])
        t[...] = (sm[...] + az[0]) + (az[1] + az[2])
        return t[...]

    def stats_of(pre, width, msg):
        m = lanes(s.maskp[pl.ds(mine, 320), :], width)
        v = pre * m
        sums = jnp.sum(v, axis=0, keepdims=True)
        squares = jnp.sum(v * pre, axis=0, keepdims=True)
        return sums, squares

    def norm_terms(n, bnp, width):
        t = reduce_line(n)
        if width == 256:
            rows = [t[i : i + 1] for i in range(4)]
        else:
            rows = [jnp.concatenate([t[2 * i : 2 * i + 1], t[2 * i + 1 : 2 * i + 2]], axis=1) for i in range(4)]
        mean = rows[0] / count
        inv = lax.rsqrt(rows[1] / count - mean * mean + EPS)
        bnp[0:1], bnp[1:2], bnp[2:3], bnp[3:4] = mean, inv, rows[2], rows[3]

    quarter = lax.div(b, np.int32(4))
    spot = 32 * lax.rem(b, np.int32(4))

    def placed(n):
        lane = lax.broadcasted_iota(jnp.int32, (8, 128), 1)
        out = []
        for p in range(2):
            if n < 2:
                v = jnp.broadcast_to(s.gains[0:1, :], (8, 128))
                v = pltpu.roll(v, lax.rem(spot + 128 - 32 * (2 * n + p), np.int32(128)), 1)
                v = jnp.where((lane >= spot) & (lane < spot + 32), v, 0.0)
                out.append(jnp.concatenate([jnp.where(quarter == 2 * r + i, v[0:1], 0.0) for i in range(2)], axis=1))
            else:
                v = s.gains[1 + p : 2 + p, :]
                out.append(
                    [
                        jnp.concatenate(
                            [jnp.where(odd & (lax.div(b, np.int32(2)) == 4 * h + i), v, 0.0) for i in range(4)], axis=1
                        )
                        for h in range(2)
                    ]
                )
        return out

    def put_stats(n, first, second, width, layer):
        m = getattr(s, "am%d" % n)
        m[...] = jnp.zeros(m.shape, F32)
        if width == 256:
            m[0:1], m[1:2] = first, second
            if layer is not None:
                m[2:3], m[3:4] = placed(layer)
        else:
            m[0:1], m[1:2] = first[:, :512], first[:, 512:]
            m[2:3], m[3:4] = second[:, :512], second[:, 512:]
            if layer is not None:
                gain, shift = placed(layer)
                m[4:5], m[5:6] = gain
                m[6:7], m[7:8] = shift

    pre = dot(s.xall[...], s.wf[...].reshape(2048, 256))
    s.pre1[...] = pre
    first_sum, first_sq = stats_of(pre, 256, None)
    put_stats(0, first_sum, first_sq, 256, 0)
    cores_wm = line_last(go_wm, at_wm, col_wm)
    reduce_plane(0)
    go_wl = (got_wl, [ln.push(at_wl(z), at_wl(z), ypeer)])
    go_wr = (got_wr, [ln.push(s.reduce, at_wr(z), ypeer, odd)])
    pl.when(odd)(red_local.wait)
    line_relay(go_wl, at_wl)
    line_relay(go_wr, at_wr, odd)
    norm_terms(0, s.bnp1, 256)
    heads_a = task_push(s.heads.at[y], s.wh, 0, 4, False)

    def act_from(prebuf, bnp, dst):
        def step(base):
            x = (prebuf[pl.ds(base, 80), :] - bnp[0:1]) * bnp[1:2] * bnp[2:3] + bnp[3:4]
            dst[pl.ds(base, 80), pl.ds(half, 256)] = (gelu_of(x) * mask_at(base, 80, 256)).astype(BF16)

        rows_loop(320, 80, step)

    act_from(s.pre1, s.bnp1, s.a1)
    a1_x = ln.push(s.a1.at[:, pl.ds(half, 256)], s.a1.at[:, pl.ds(half, 256)], xpeer)
    line_core(go_wm, col_wm, cores_wm)
    cores_wl = line_last(go_wl, at_wl, col_wl)
    cores_wr = line_last(go_wr, at_wr, col_wr, odd)
    wait(cores_wm)
    wait([a1_x])
    spread(s.a1, s.a3, 1, 512)
    pre = conv_rows(s.a3, s.wm, 0)
    s.pre2[...] = pre
    first_sum, first_sq = stats_of(pre, 256, None)
    put_stats(1, first_sum, first_sq, 256, 1)
    reduce_plane(1)
    over_h = ln.push(s.heads.at[1 - y], s.st_h, ypeer)
    norm_terms(1, s.bnp2, 256)
    relay_a = task_relay(heads_a, s.wh)
    heads_b = task_push(s.heads.at[y], s.wh, 4, 8, False)
    act_from(s.pre2, s.bnp2, s.a2)
    a2_x = ln.push(s.a2.at[:, pl.ds(half, 256)], s.a2.at[:, pl.ds(half, 256)], xpeer)
    line_core(go_wl, col_wl, cores_wl)
    line_core(go_wr, col_wr, cores_wr, odd)
    wait(cores_wl)
    wait([a2_x])
    pre = dot(s.a2[...], s.wl[...].reshape(512, 1024))
    s.pre3[...] = pre
    first_sum, first_sq = stats_of(pre, 1024, None)
    put_stats(2, first_sum, first_sq, 1024, 2)
    reduce_plane(2)
    over_m = ln.push(s.messages.at[1 - y], s.st_m, ypeer)
    norm_terms(2, s.bnp3, 1024)
    relay_b = task_relay(heads_b, s.wh)
    heads_c = task_push(s.heads.at[y], s.wh, 8, 9, False)
    wait([over_h])
    staged_h = ln.near(s.st_h.at[:, :, pl.ds(fhalf, 256)], s.wh.at[:, z, 1 - y, c])
    heads_d = task_push(s.st_h, s.wh, 0, 5, True)
    heads_e = task_push(s.st_h, s.wh, 5, 9, True)
    gate_got = {}
    cls_got = ln.group(lambda: s.wc.at[0:15])
    for q in range(4):
        for j in range(2):
            if q + j:
                gate_got[q, j] = ln.group(lambda: s.wg.at[0, 0], (y == r) if j == 0 else (y != r))
            for i in range(2):
                if q + j + i == 0:
                    continue
                yy = 1 - y if j else y
                cc = 1 - c if i else c
                to = dev(zk(q) if q else z, yy, cc, r)
                cls_got.push(s.wcs, s.wc.at[b], to)
                src = s.gates.at[r, :, pl.ds(pl.multiple_of(256 * cc, 128), 256)]
                if q + j:
                    gate_got[q, j].push(src, s.wg.at[z, y, c], to, (y == r) if j == 0 else (y != r))
                else:
                    gate_got[0, 0] = ln.push(src, s.wg.at[z, y, c], to, y == r)

    def summed_at(base, rows):
        x = (s.pre3[pl.ds(base, rows), :] - s.bnp3[0:1]) * s.bnp3[1:2]
        return x, x * s.bnp3[2:3] + s.bnp3[3:4] + s.xh[pl.ds(base, rows), :].astype(F32)

    def block_step(base):
        _, v = summed_at(base, 32)
        s.blk[pl.ds(base, 32), :] = (gelu_of(v) * mask_at(base, 32, 1024)).astype(BF16)

    rows_loop(320, 32, block_step)
    wait(cores_wr, jnp.logical_not(odd))
    wred = s.wr[...].reshape(1024, 512)
    s.rps[...] = dot(s.blk[pl.ds(other_rows, 160), :], wred).astype(BF16)
    red_x = ln.push(s.rps, s.rpr, xpeer)
    part = dot(s.blk[pl.ds(my_rows, 160), :], wred)
    wait([red_x])
    s.rbuf[pl.ds(own_px, 160), :] = (part + s.rpr[...].astype(F32)).astype(BF16)

    def block_of(rr, yy, cc, lo=0, n=160):
        return s.rbuf.at[pl.ds(pl.multiple_of(px_of(rr, yy, cc) + lo, 16), n)]

    for cp in near_late:
        cp.wait()
    own = block_of(r, y, c)
    g_x = ln.push(own, own, xpeer)
    g_y = ln.push(own, own, ypeer)
    g_c = ln.push(own, own, core)
    relay_c = task_relay(heads_c, s.wh)
    wait([g_x])
    bx = block_of(1 - r, y, c, 0, 80)
    g_xy = ln.push(bx, bx, ypeer)
    wait([g_y])
    by = block_of(r, 1 - y, c, 80, 80)
    g_yx = ln.push(by, by, xpeer)
    bx = block_of(1 - r, y, c)
    g_c1 = ln.push(bx, bx, core)
    by = block_of(r, 1 - y, c)
    g_c2 = ln.push(by, by, core)
    wait([g_xy, g_yx])
    bd = block_of(1 - r, 1 - y, c)
    g_c3 = ln.push(bd, bd, core)
    relay_d = task_relay(heads_d, s.wh)
    wfo_x = ln.push(s.wf, s.wfo, xpeer)
    wait([g_c, g_c1, g_c2, g_c3])

    near_end = dev(jnp.where(z == 0, 1, 2), y, c, r)
    other_end = dev(jnp.where(z == 1, 3, 0), y, c, r)

    def grad_push(n, g, rm, lo, hi):
        def like(slot):
            return lambda side: rm.at[slot, lo:hi] if side else g.at[lo:hi, 0]

        got = {}
        for q in (1, 2, 3):
            direct = {1: not_last, 2: ends, 3: not_first}[q]
            got[q] = ln.push(g.at[lo:hi, zk(q)], rm.at[q - 1, lo:hi], dev(zk(q), y, c, r), direct, like(q - 1))
        hop = s.hop.at[n, lo:hi]
        got[0] = ln.push(
            g.at[lo:hi, 3 - z], hop, near_end, ends, lambda side: s.hop.at[n, lo:hi] if side else g.at[lo:hi, 0]
        )
        return got, n, g, rm, lo, hi

    def grad_hop(state):
        got, n, g, rm, lo, hi = state

        def add():
            got[0].wait_recv()
            far = jnp.where(z == 1, 3, 0)
            for t in range(lo, hi):
                s.hop[n, t] = (s.hop[n, t].astype(F32) + g[t, far].astype(F32)).astype(BF16)

        pl.when(inner)(add)
        got[4] = ln.push(
            s.hop.at[n, lo:hi], rm.at[1, lo:hi], other_end, inner,
            lambda side: rm.at[1, lo:hi] if side else s.hop.at[n, lo:hi],
        )

    def grad_wait(state):
        got = state[0]
        wait([got[1]], not_first)
        wait([got[3]], not_last)
        wait([got[2]], inner)
        wait([got[4]], ends)

    def tasks(r3, f3, d3, preh, dfull):
        spread(s.rbuf, r3, 4, 512)
        relay_e = task_relay(heads_e, s.wh)
        wait([over_m])
        staged_m = ln.near(s.st_m.at[:, :, pl.ds(fhalf, 256)], s.wq.at[:, z, 1 - y, c])

        def mess_push(a):
            return [
                task_push(s.st_m if staged else s.messages.at[y], s.wq, 3 * a, 3 * a + 3, staged) for staged in (False, True)
            ]

        mess = [mess_push(0), mess_push(1)]
        for part in (relay_a, relay_b, relay_c, relay_d, relay_e):
            task_ready(part)
        staged_h.wait()

        def head_step(i, carry):
            v = conv_rows(r3, s.wh, i)
            px = pl.multiple_of(i * 320, 16)
            preh[pl.ds(px, 320), :] = v
            return carry

        lax.fori_loop(0, 4, head_step, 0)

        def feat_step(base):
            m = lanes(s.maskp[pl.ds(base, 80), :], 256)
            s.fown[pl.ds(base, 80), :] = (gelu_of(preh[pl.ds(base, 80), :]) * m).astype(BF16)

        rows_loop(1280, 80, feat_step)
        f_c = ln.push(s.fown, s.ffull.at[:, pl.ds(fhalf, 256)], core)
        f_n = ln.near(s.fown, s.ffull.at[:, pl.ds(fhalf, 256)])

        def seven():
            return s.dmg.at[0:1120]

        def to_owners(src, dst_of, when):
            got = {}
            for o in offsets:
                rr, yy, cc = peer(*o)
                got[o] = ln.push(
                    src.at[pl.ds(px_of(rr, yy, cc), 160)], dst_of().at[:, pl.ds(fhalf, 256)], dev(z, yy, cc, rr), when
                )
            return got

        f_own = to_owners(s.fown, lambda: s.fg.at[r, 0], special)

        def keep(dst, src):
            def run():
                dst[:, pl.ds(fhalf, 256)] = src[pl.ds(own_px, 160), :]

            return run

        pl.when(special)(keep(s.fg.at[r, 0], s.fown))
        f_n.wait()
        wait([f_c])

        def gate_ready():
            for cp in gate_got.values():
                cp.wait_recv()

        pl.when(special)(gate_ready)

        @pl.when(special)
        def _():
            def gate_step(base):
                v = dot(s.ffull[pl.ds(base, 320), :], s.wg[...].reshape(512, 256))
                s.gateb[pl.ds(base, 320), :] = (1.0 / (1.0 + jnp.exp(-v))).astype(BF16)

            rows_loop(1280, 320, gate_step)

        g_own = to_owners(s.gateb, lambda: s.fg.at[r, 1], special)
        pl.when(special)(keep(s.fg.at[r, 1], s.gateb))
        spread(s.ffull, f3, 4, 512)
        relayed = [[task_relay(p, s.wq) for p in mess[0]]]
        mess.append(mess_push(2))
        relayed.append([task_relay(p, s.wq) for p in mess[1]])
        staged_m.wait()
        for a in range(3):
            for p in relayed[a]:
                task_ready(p)
            if a == 0:
                relayed.append(None)

            def mess_step(i, carry, a=a):
                rows = pl.ds(pl.multiple_of(i * 320, 16), 320)
                base = pl.multiple_of((5 * i + a) * 80, 16)
                v = dot(f3[pl.ds(base, 320), :], s.wq[3 * a : 3 * a + 3].reshape(1536, 256))
                if a:
                    v = dfull[rows, 0:256] + v
                if a < 2:
                    dfull[rows, 0:256] = v
                else:
                    s.msgb[rows, :] = v.astype(BF16)
                return carry

            lax.fori_loop(0, 4, mess_step, 0)
            if a == 0:
                relayed[2] = [task_relay(p, s.wq) for p in mess[2]]

        m_own = ln.group(seven)
        for o in offsets:
            rr, yy, cc = peer(*o)
            m_own.push(s.msgb.at[pl.ds(px_of(rr, yy, cc), 160)], s.mrecv.at[task, :, pl.ds(fhalf, 256)], dev(z, yy, cc, rr))
        keep(s.mrecv.at[task], s.msgb)()

        wait([cls_got])
        for i in range(2):
            s.ctf[...] = jnp.zeros((128, 128), F32)
            s.ctf[0:40, 0:80] = s.cct[i].astype(F32)
            turned = s.ctf[...].T
            s.ccotv[80 * i : 80 * i + 80, :] = turned[0:80, :].astype(BF16)
        for o in offsets:
            wait([f_own[o], g_own[o]], (r != y) if (o[0] + o[1]) % 2 else special)

        wait([m_own])

        def stream_step(base):
            rows = pl.ds(base, 32)
            m = lanes(s.maskp[pl.ds(own_px + base, 32), :], 512)
            m0, m1, m2, m3 = (s.mrecv[t, rows, :].astype(F32) for t in range(4))
            f0, f3_ = s.fg[0, 0, rows, :].astype(F32), s.fg[1, 0, rows, :].astype(F32)
            mid = m1 + m2
            sd, sc = mid + m3, m0 + mid
            gd, gc = s.fg[0, 1, rows, :].astype(F32), s.fg[1, 1, rows, :].astype(F32)
            s.ods[rows, :] = ((f0 + gd * sd) * m).astype(BF16)
            merged = (f3_ + gc * sc).astype(BF16)
            s.mrg[rows, :] = merged
            m1l = m[:, :128]
            wcls = s.wc[...].reshape(512, 128)
            s.olg[rows, :] = (dot(merged, wcls) * m1l).astype(BF16)
            dj = (s.ccotv[rows, :].astype(F32) * m1l).astype(BF16)
            s.ccotv[rows, :] = dj
            dd = s.dcotv[rows, :].astype(F32) * m
            dmer = dot_last(dj, wcls)
            s.fg[0, 0, rows, :] = dd.astype(BF16)
            s.fg[1, 0, rows, :] = dmer.astype(BF16)
            s.fg[0, 1, rows, :] = (dd * sd * gd * (1.0 - gd)).astype(BF16)
            s.fg[1, 1, rows, :] = (dmer * sc * gc * (1.0 - gc)).astype(BF16)
            down, up = dd * gd, dmer * gc
            both = (down + up).astype(BF16)
            s.mrecv[0, rows, :] = up.astype(BF16)
            s.mrecv[1, rows, :] = both
            s.mrecv[2, rows, :] = both
            s.mrecv[3, rows, :] = down.astype(BF16)

        rows_loop(160, 32, stream_step)
        e_got = {}
        d_got = ln.group(seven)
        for o in offsets:
            rr, yy, cc = peer(*o)
            ll = pl.ds(pl.multiple_of(256 * cc, 128), 256)
            d_got.push(s.mrecv.at[2 * rr + yy, :, ll], s.dmg.at[pl.ds(own_px, 160)], dev(z, yy, cc, rr))
        for o in offsets:
            rr, yy, cc = peer(*o)
            ll = pl.ds(pl.multiple_of(256 * cc, 128), 256)
            e_got[o] = ln.push(s.fg.at[rr, :, :, ll], s.exg.at[:, pl.ds(own_px, 160)], dev(z, yy, cc, rr), rr == yy)
        s.dmg[pl.ds(own_px, 160), :] = s.mrecv[task, :, pl.ds(fhalf, 256)]

        @pl.when(special)
        def _():
            for e in range(2):
                s.exg[e, pl.ds(own_px, 160), :] = s.fg[r, e, :, pl.ds(fhalf, 256)]

        @pl.when(jnp.logical_not(special))
        def _():
            s.exg[...] = jnp.zeros(s.exg.shape, BF16)

        for i in range(2):
            s.ctf[...] = jnp.zeros((128, 128), F32)
            s.ctf[0:80, :] = s.olg[80 * i : 80 * i + 80, :].astype(F32)
            turned = s.ctf[...].T
            s.olt[i] = turned[0:40, 0:80].astype(BF16)
        out_near = [ln.near(s.ods, s.o_depth), ln.near(s.olt, s.o_logits)]
        s.gcls[...] = dot_first(s.mrg[...], s.ccotv[...]).astype(BF16).reshape(16, 32, 128)
        cg = ln.group(lambda: s.rcls)
        n_cls = 0
        for q in range(4):
            for j in range(2):
                for i in range(2):
                    if q + j + i == 0:
                        continue
                    yy = 1 - y if j else y
                    cc = 1 - c if i else c
                    zz = zk(q) if q else z
                    cg.push(s.gcls.at[4 * zz + 2 * yy + cc], s.rcls.at[n_cls], dev(zz, yy, cc, r))
                    n_cls += 1
        wait([d_got])
        spread(s.dmg, d3, 4, 256)
        gm_z = []
        for a in range(3):
            conv_weight(f3, d3, s.gm, 4, 3 * a, 3 * a + 3)
            gm_z.append(grad_push(0, s.gm, s.rm, 3 * a, 3 * a + 3))
        wait([e_got[o] for o in offsets], special)

        def back_step(i, carry):
            px = pl.multiple_of(i * 320, 16)
            dfull[pl.ds(px, 320), :] = conv_back(d3, s.wq, i)
            return carry

        lax.fori_loop(0, 4, back_step, 0)

        @pl.when(special)
        def _():
            def gate_back(base):
                rows = pl.ds(base, 320)
                dfull[rows, :] = dfull[rows, :] + dot_last(s.exg[1, rows, :], s.wg[...].reshape(512, 256))

            rows_loop(1280, 320, gate_back)

        chalf = pl.ds(pl.multiple_of(256 * (1 - c), 128), 256)

        def give(base):
            rows = pl.ds(base, 80)
            s.dfs[rows, :] = dfull[rows, chalf].astype(BF16)

        rows_loop(1280, 80, give)
        df_c = ln.push(s.dfs, s.dfr, core)

        @pl.when(special)
        def _():
            s.gg[...] = dot_first(s.ffull[...], s.exg[1]).astype(BF16).reshape(s.gg.shape)

        gg_z = [ln.push(s.gg.at[zk(k)], s.rg.at[k - 1], dev(zk(k), y, c, r), special, lambda side, k=k: s.rg.at[k - 1] if side else s.gg.at[0]) for k in (1, 2, 3)]
        wait([df_c])

        def dhead_step(base):
            rows = pl.ds(base, 80)
            m = lanes(s.maskp[rows, :], 256)
            d = dfull[rows, pl.ds(fhalf, 256)] + s.dfr[rows, :].astype(F32) + s.exg[0, rows, :].astype(F32)
            s.dmg[rows, :] = (slope_of(preh[rows, :]) * d * m).astype(BF16)

        rows_loop(1280, 80, dhead_step)
        spread(s.dmg, d3, 4, 256)

        def back_step2(i, carry):
            px = pl.multiple_of(i * 320, 16)
            dfull[pl.ds(px, 320), :] = conv_back(d3, s.wh, i)
            return carry

        lax.fori_loop(0, 4, back_step2, 0)
        for yy in range(2):
            src = pl.multiple_of(320 * (2 * yy) + 320 * (1 - c), 16)
            s.drs[pl.ds(320 * yy, 320), :] = dfull[pl.ds(src, 320), :].astype(BF16)
        dr_c = ln.push(s.drs, s.drr, core)
        wait([dr_c])
        for yy in range(2):
            src = pl.multiple_of(320 * (2 * yy) + 320 * c, 16)
            rows = pl.ds(320 * yy, 320)
            s.drr[rows, :] = (dfull[pl.ds(src, 320), :] + s.drr[rows, :].astype(F32)).astype(BF16)
        ro = []
        for dr, dy in ((1, 0), (0, 1), (1, 1)):
            rr, yy, _ = peer(dr, dy, 0)
            src = s.drr.at[pl.ds(pl.multiple_of(320 * yy + 160 * rr, 16), 160)]
            ro.append(ln.push(src, s.dro.at[len(ro)], dev(z, yy, c, rr)))
        conv_weight(r3, d3, s.gh, 4, 0, 9)
        grad_hop(gm_z[0])
        wait(ro)
        keep_rows = pl.ds(pl.multiple_of(320 * y + 160 * r, 16), 160)
        total_red = s.drr[keep_rows, :].astype(F32)
        for i in range(3):
            total_red = total_red + s.dro[i].astype(F32)
        s.dred[pl.ds(my_rows, 160), :] = total_red.astype(BF16)
        for cp in out_near:
            cp.wait()
        ln.drain(scoped=True)
        return cg, gm_z, gg_z

    state = {}

    def scope_tasks(*scr):
        state["t"] = tasks(*scr)

    pl.run_scoped(
        scope_tasks,
        pltpu.VMEM((1680, 1536), BF16),
        pltpu.VMEM((1680, 1536), BF16),
        pltpu.VMEM((1680, 768), BF16),
        pltpu.VMEM((1280, 256), F32),
        pltpu.VMEM((1280, 512), F32),
    )
    cg, gm_z, gg_z = state["t"]

    dr_x = ln.push(s.dred.at[pl.ds(my_rows, 160)], s.dred.at[pl.ds(my_rows, 160)], xpeer)

    def block_back(*late):
        for name, ref in zip(LATE, late):
            setattr(s, name, ref)
        gr, gl, gq, gf = s.gr, s.gl, s.gq, s.gf

        def to_core(g, rc, lead):
            at = g.at[:, :, :, 1 - c] if lead else g.at[:, :, 1 - c]
            return ln.push(at, rc, core)

        def add_core(g, rc, lead):
            if lead:
                for t in range(9):
                    rc[t] = (rc[t].astype(F32) + g[t, :, :, c].astype(F32)).astype(BF16)
            else:
                for t in range(rc.shape[0]):
                    rc[t] = (rc[t].astype(F32) + g[t, :, c].astype(F32)).astype(BF16)

        def to_y(rc, ry, lead):
            return ln.push(rc.at[:, :, 1 - y] if lead else rc.at[:, 1 - y], ry, ypeer)

        def add_y(rc, ry, lead):
            for t in range(ry.shape[0]):
                mine_y = rc[t, :, y] if lead else rc[t, y]
                ry[t] = (ry[t].astype(F32) + mine_y.astype(F32)).astype(BF16)

        def to_z(ry, rz, lead):
            return [
                ln.push(ry.at[:, zk(k)] if lead else ry.at[zk(k)], rz.at[k - 1], dev(zk(k), y, c, r)) for k in (1, 2, 3)
            ]

        def add_z(ry, rz, fin, lead):
            mine_z = (ry[:, z] if lead else ry[z]).astype(F32)
            fin[...] = ((mine_z + rz[0].astype(F32)) + (rz[1].astype(F32) + rz[2].astype(F32))).astype(BF16)

        def task_out(states, rm, g, ps, out):
            for part in states:
                grad_wait(part)
            loads = [[ln.near(rm.at[q, 3 * part : 3 * part + 3], s.zst.at[part % 2, q]) for q in range(3)] for part in range(2)]
            for part in range(3):
                for cp in loads[part]:
                    cp.wait()
                v0 = s.zst.at[part % 2]
                for t in range(3):
                    first_in = jnp.where(z == 0, 0.0, v0[0, t].astype(F32))
                    third_in = jnp.where(z == 3, 0.0, v0[2, t].astype(F32))
                    v = g[3 * part + t, z].astype(F32) + first_in + (v0[1, t].astype(F32) + third_in)
                    ps[3 * part + t] = v.astype(BF16)
                if part == 0:
                    loads.append([ln.near(rm.at[q, 6:9], s.zst.at[0, q]) for q in range(3)])
            lanes_out = pl.ds(fhalf, 256)
            sent = []
            for i in (1, 2, 3):
                yy = 1 - y if i & 2 else y
                cc = 1 - c if i & 1 else c
                sent.append(ln.push(ps.at[:, yy, cc], out.at[y, :, :, lanes_out], dev(z, yy, cc, r)))
            return sent, ln.near(ps.at[:, y, c], out.at[y, :, :, lanes_out])

        wait([dr_x])

        def d3_step(i, carry):
            su, sux = carry
            rows = pl.ds(pl.multiple_of(i * 32, 16), 32)
            x, v = summed_at(i * 32, 32)
            u = slope_of(v) * s.u3[rows, :] * mask_at(i * 32, 32, 1024)
            s.u3[rows, :] = u
            s.dsum[rows, :] = u.astype(BF16)
            return su + jnp.sum(u, axis=0, keepdims=True), sux + jnp.sum(u * x, axis=0, keepdims=True)

        s.u3[...] = dot_last(s.dred[...], s.wr[...].reshape(1024, 512))
        nil = jnp.zeros((1, 1024), F32)
        su, sux = lax.fori_loop(0, 10, d3_step, (nil, nil))
        put_stats(3, su, sux, 1024, None)
        ar3 = plane_start(3)
        ds_x = ln.push(s.dsum.at[pl.ds(other_rows, 160)], s.dsr, xpeer)
        gr[...] = dot_first(s.blk[...], s.dred[...]).astype(BF16).reshape(gr.shape)
        gr_c = ln.push(gr, s.rcr, core, jnp.logical_not(odd))
        plane_end(3, ar3)
        t = reduce_line(3)
        for part in gm_z[1:]:
            grad_hop(part)
        gh_z = [grad_push(1, s.gh, s.rh, 0, 2)]
        gs3 = ln.push(s.at3, s.o_gs3.at[r], xpeer)
        gs3n = ln.near(s.at3, s.o_gs3.at[r])
        mu = jnp.concatenate([t[0:1], t[1:2]], axis=1) / count
        mux = jnp.concatenate([t[2:3], t[3:4]], axis=1) / count

        def dp3_step(base):
            rows = pl.ds(base, 32)
            x = (s.pre3[rows, :] - s.bnp3[0:1]) * s.bnp3[1:2]
            d = mask_at(base, 32, 1024) * (s.bnp3[2:3] * s.bnp3[1:2]) * (s.u3[rows, :] - mu - x * mux)
            s.dp3[rows, :] = d.astype(BF16)

        rows_loop(320, 32, dp3_step)

        def partial_out(pas, value_of):
            pas[...] = value_of(ohalf).astype(BF16)

        wlast = s.wl
        s.u3[:, 0:512] = dot_last(s.dp3[...], wlast[...].reshape(512, 1024))
        s.pas2[...] = s.u3[:, pl.ds(ohalf, 256)].astype(BF16)
        pa2 = ln.push(s.pas2, s.par2, xpeer)
        gl[...] = dot_first(s.a2[...], s.dp3[...]).astype(BF16).reshape(gl.shape)
        gl_c = to_core(gl, s.rcl, False)
        wait([gr_c], odd)

        @pl.when(odd)
        def _():
            for q in range(4):
                s.rcr[q] = (s.rcr[q].astype(F32) + gr[q].astype(F32)).astype(BF16)

        later = {}

        def after_plane_two():
            later["gr_y"] = ln.push(s.rcr.at[:, 1 - y], s.ryr, ypeer, odd)
            wait([gl_c])
            add_core(gl, s.rcl, False)
            later["gl_y"] = to_y(s.rcl, s.ryl, False)

        def after_plane_one():
            wait([gq_c])
            add_core(gq, s.rcm, True)
            later["gq_y"] = to_y(s.rcm, s.rym, True)

        wait([pa2])

        def norm_back(n, par, prebuf, bnp, dst, out_gs, middle, after):
            def u_step(i, carry):
                su_, sux_ = carry
                base = pl.multiple_of(i * 80, 16)
                rows = pl.ds(base, 80)
                x = (prebuf[rows, :] - bnp[0:1]) * bnp[1:2]
                v = x * bnp[2:3] + bnp[3:4]
                d = s.u3[rows, pl.ds(half, 256)] + par[rows, :].astype(F32)
                u = slope_of(v) * d * mask_at(base, 80, 256)
                s.u3[rows, 512:768] = u
                return su_ + jnp.sum(u, axis=0, keepdims=True), sux_ + jnp.sum(u * x, axis=0, keepdims=True)

            nil_ = jnp.zeros((1, 256), F32)
            su_, sux_ = lax.fori_loop(0, 4, u_step, (nil_, nil_))
            put_stats(n, su_, sux_, 256, None)
            reduce_plane(n)
            middle()
            t_ = reduce_line(n)
            after()
            gsx = ln.push(getattr(s, "at%d" % n), out_gs.at[r], xpeer)
            gsn = ln.near(getattr(s, "at%d" % n), out_gs.at[r])
            mu_, mux_ = t_[0:1] / count, t_[1:2] / count

            def d_step(base):
                rows = pl.ds(base, 80)
                x = (prebuf[rows, :] - bnp[0:1]) * bnp[1:2]
                d = mask_at(base, 80, 256) * (bnp[2:3] * bnp[1:2]) * (s.u3[rows, 512:768] - mu_ - x * mux_)
                dst[rows, :] = d.astype(BF16)

            rows_loop(320, 80, d_step)
            return gsx, gsn

        gs2, gs2n = norm_back(4, s.par2, s.pre2, s.bnp2, s.dp2, s.o_gs2, after_plane_two, lambda: gh_z.append(grad_push(1, s.gh, s.rh, 2, 4)))
        spread(s.dp2, s.d3m, 1, 256)
        s.u3[:, 0:512] = conv_back(s.d3m, s.wm, 0)
        s.pas1[...] = s.u3[:, pl.ds(ohalf, 256)].astype(BF16)
        pa1 = ln.push(s.pas1, s.par1, xpeer)
        conv_weight(s.a3, s.d3m, gq, 1, 0, 9)
        gq_c = to_core(gq, s.rcm, True)
        wait([pa1])
        gs1, gs1n = norm_back(5, s.par1, s.pre1, s.bnp1, s.dp1, s.o_gs1, after_plane_one, lambda: gh_z.append(grad_push(1, s.gh, s.rh, 4, 9)))
        dp_x = ln.push(s.dp1.at[pl.ds(other_rows, 160)], s.dp1r, xpeer)
        gf[...] = dot_first(s.xall[...], s.dp1[...]).astype(BF16).reshape(gf.shape)
        gf_c = to_core(gf, s.rcf, False)
        wait([gf_c])
        add_core(gf, s.rcf, False)
        gf_y = to_y(s.rcf, s.ryf, False)
        gr_y, gl_y, gq_y = later["gr_y"], later["gl_y"], later["gq_y"]
        ms, mn = task_out(gm_z, s.rm, s.gm, s.psm, s.o_mess)

        wait([gr_y], odd)

        @pl.when(odd)
        def _():
            for q in range(4):
                s.ryr[q] = (s.ryr[q].astype(F32) + s.rcr[q, y].astype(F32)).astype(BF16)

        for part in gh_z[:2]:
            grad_hop(part)
        gr_z = [ln.push(s.ryr.at[zk(q)], s.rzr.at[q - 1], dev(zk(q), y, c, r), odd) for q in (1, 2, 3)]
        wait([gl_y])
        add_y(s.rcl, s.ryl, False)
        gl_z = to_z(s.ryl, s.rzl, False)
        wait([gq_y])
        add_y(s.rcm, s.rym, True)
        gq_z = to_z(s.rym, s.rzm, True)
        wait([gf_y])
        add_y(s.rcf, s.ryf, False)
        gf_z = to_z(s.ryf, s.rzf, False)

        wait([wfo_x])
        wfo_n = ln.near(s.wfo, s.wfov)
        wait([dp_x, ds_x])
        wfo_n.wait()
        mine_d = s.dp1[pl.ds(my_rows, 160), :]
        other_d = s.dp1r[...]
        for q in range(2):
            cols = slice(1024 * q, 1024 * q + 1024)
            wa = s.wf[2 * q : 2 * q + 2].reshape(1024, 256)
            wb = s.wfov[2 * q : 2 * q + 2].reshape(1024, 256)
            s.u3[pl.ds(0, 160), :] = dot_last(mine_d, wa) + dot_last(other_d, wb)

            def img_step(base):
                rows = pl.ds(base, 32)
                m = mask_at(my_rows + base, 32, 1024)
                own_d = s.dsum[pl.ds(my_rows + base, 32), 512 * q : 512 * q + 512].astype(F32)
                far_d = s.dsr[rows, 512 * q : 512 * q + 512].astype(F32)
                d = jnp.concatenate(
                    [
                        jnp.where(r == j % 2, own_d[:, 64 * (j - j % 2) :][:, :128], far_d[:, 64 * (j - j % 2) :][:, :128])
                        for j in range(8)
                    ],
                    axis=1,
                )
                s.oimg[rows, cols] = ((s.u3[rows, :] + d) * m).astype(BF16)

            rows_loop(160, 32, img_step)
        img_n = ln.near(s.oimg, s.o_img)

        grad_hop(gh_z[2])
        hs, hn = task_out(gh_z, s.rh, s.gh, s.psh, s.o_heads)

        @pl.when(special)
        def _():
            for cp in gg_z:
                cp.wait_recv()
            v = (s.gg[z].astype(F32) + s.rg[0].astype(F32)) + (s.rg[1].astype(F32) + s.rg[2].astype(F32))
            s.pg[...] = v.astype(BF16)

        gx = {}
        for o in offsets:
            rr, yy, cc = peer(*o)
            gx[o] = ln.push(s.pg.at[yy, cc], s.o_gates.at[r, :, pl.ds(fhalf, 256)], dev(z, yy, cc, rr), special)
        gate_near = pltpu.make_async_copy(
            s.pg.at[y, c], s.o_gates.at[r, :, pl.ds(fhalf, 256)], s.near_sems.at[NEAR - 2]
        )
        pl.when(special)(gate_near.start)

        wait([cg])
        v = s.gcls[b].astype(F32)
        for i in range(15):
            v = v + s.rcls[i].astype(F32)
        s.clss[...] = v
        cls_x = ln.push(s.clss, s.clsr, xpeer)

        wait(gr_z, odd)

        @pl.when(odd)
        def _():
            v_ = s.ryr[z].astype(F32) + s.rzr[0].astype(F32)
            s.fnr[...] = (v_ + (s.rzr[1].astype(F32) + s.rzr[2].astype(F32))).astype(BF16)

        gr_x = ln.push(s.fnr, s.o_red, xpeer, odd)
        red_near = pltpu.make_async_copy(s.fnr, s.o_red, s.near_sems.at[NEAR - 3])
        pl.when(odd)(red_near.start)
        wait(gl_z)
        add_z(s.ryl, s.rzl, s.fnl, False)
        gl_x = ln.push(s.fnl, s.o_last.at[r], xpeer)
        n1 = ln.near(s.fnl, s.o_last.at[r])
        wait(gq_z)
        add_z(s.rym, s.rzm, s.fnm, True)
        gq_x = ln.push(s.fnm, s.o_mid.at[:, :, pl.ds(half, 256)], xpeer)
        n2 = ln.near(s.fnm, s.o_mid.at[:, :, pl.ds(half, 256)])
        wait(gf_z)
        add_z(s.ryf, s.rzf, s.fnf, False)
        gf_x = ln.push(s.fnf, s.o_first.at[:, pl.ds(half, 256)], xpeer)
        n3 = ln.near(s.fnf, s.o_first.at[:, pl.ds(half, 256)])
        wait([cls_x])
        s.clso[...] = s.clss[...] + s.clsr[...]
        n4 = ln.near(s.clso, s.o_cls)
        wait([gr_x], jnp.logical_not(odd))
        wait([gl_x, gq_x, gf_x, gs1, gs2, gs3])
        wait(ms + hs)
        for o in offsets:
            wait([gx[o]], (r != y) if (o[0] + o[1]) % 2 else special)
        pl.when(special)(gate_near.wait)
        pl.when(odd)(red_near.wait)
        for cp in (gs1n, gs2n, gs3n, img_n, mn, hn, n1, n2, n3, n4):
            cp.wait()
        ln.drain()

    pl.run_scoped(block_back, *[pltpu.VMEM(*v) for v in LATE.values()])


LATE = dict(
    zst=((2, 3, 3, 2, 2, 32, 256), BF16),
    psm=((9, 2, 2, 32, 256), BF16),
    psh=((9, 2, 2, 32, 256), BF16),
    fnr=((128, 512), BF16),
    fnl=((32, 1024), BF16),
    fnm=((9, 32, 256), BF16),
    fnf=((128, 256), BF16),
    pg=((2, 2, 32, 256), BF16),
    clss=((32, 128), F32),
    clso=((32, 128), F32),
    u3=((320, 1024), F32),
    dp3=((320, 1024), BF16),
    d3m=((480, 768), BF16),
    dsum=((320, 1024), BF16),
    oimg=((160, 2048), BF16),
    pas1=((320, 256), BF16),
    pas2=((320, 256), BF16),
    dp1=((320, 256), BF16),
    dp2=((320, 256), BF16),
    wfov=((4, 2, 2, 128, 256), BF16),
    gr=((4, 2, 128, 512), BF16),
    gl=((4, 2, 2, 32, 1024), BF16),
    gq=((9, 4, 2, 2, 32, 256), BF16),
    gf=((4, 2, 2, 128, 256), BF16),
)


FINAL = dict(
    depth=((160, 512), BF16),
    logits=((2, 40, 80), BF16),
    img=((160, 2048), F32),
    first=((128, 512), F32),
    gain1=((1, 32), F32),
    shift1=((1, 32), F32),
    mid=((9, 32, 512), F32),
    gain2=((1, 32), F32),
    shift2=((1, 32), F32),
    last=((32, 2048), F32),
    gain3=((1, 128), F32),
    shift3=((1, 128), F32),
    red=((128, 512), F32),
    heads=((2, 9, 32, 512), F32),
    mess=((2, 9, 32, 512), F32),
    gates=((2, 32, 512), F32),
    cls=((32, 40), F32),
)


def widen_out(names, *refs):
    s = SimpleNamespace(**dict(zip(names, refs)))
    b = lax.axis_index("batch")
    used = [0]

    def move(src, dst):
        cp = pltpu.make_async_copy(src, dst, s.sems.at[used[0]])
        used[0] += 1
        cp.start()
        return cp

    done = [move(s.o_depth, s.depth), move(s.o_logits, s.logits)]
    wide = ["mess", "heads", "mid", "img", "last", "red", "first", "gates"]
    loads = {n: move(getattr(s, "o_" + n), getattr(s, "i_" + n)) for n in wide}
    small = [move(getattr(s, "o_" + n), getattr(s, "i_" + n)) for n in ("gs1", "gs2", "gs3", "cls")]
    for n in wide:
        loads[n].wait()
        src, dst = getattr(s, "i_" + n), getattr(s, "v_" + n)
        if n == "last":
            for i in range(8):
                for h in range(2):
                    lane = 128 * (2 * i + h)
                    dst[:, lane : lane + 128] = src[h, :, 128 * i : 128 * i + 128].astype(F32)
        elif n == "img":
            for i in range(0, 160, 32):
                dst[i : i + 32, :] = src[i : i + 32, :].astype(F32)
        elif len(src.shape) > 2:
            for i in range(src.shape[0]):
                dst[i] = src[i].astype(F32)
        else:
            dst[...] = src[...].astype(F32)
        done.append(move(dst, getattr(s, n)))
    for cp in small:
        cp.wait()
    quarter, spot = lax.div(b, np.int32(4)), lax.rem(b, np.int32(4))
    at = pl.ds(pl.multiple_of(128 * lax.rem(quarter, np.int32(2)), 128), 128)
    for n, layer in ((1, s.i_gs1), (2, s.i_gs2)):
        v = pltpu.roll(layer[lax.div(quarter, np.int32(2)), :, at], lax.rem(128 - 32 * spot, np.int32(128)), 1)
        for row, kind in ((1, "gain"), (0, "shift")):
            keep = getattr(s, "v_%s%d" % (kind, n))
            keep[...] = v[row : row + 1, 0:32]
            done.append(move(keep, getattr(s, "%s%d" % (kind, n))))
    block = lax.div(b, np.int32(2))
    at = pl.ds(pl.multiple_of(128 * lax.rem(block, np.int32(4)), 128), 128)
    v = s.i_gs3[lax.rem(b, np.int32(2)), :, at]
    low = lax.div(block, np.int32(4)) == 0
    s.v_shift3[...] = jnp.where(low, v[0:1], v[1:2])
    s.v_gain3[...] = jnp.where(low, v[2:3], v[3:4])
    done.append(move(s.v_shift3, s.shift3))
    done.append(move(s.v_gain3, s.gain3))
    s.v_cls[...] = s.i_cls[:, 0:40]
    done.append(move(s.v_cls, s.cls))
    for cp in done:
        cp.wait()


def fast(args):
    (
        images, crop_height, crop_width, w_first, gain_first, shift_first, w_middle, gain_middle, shift_middle,
        w_last, gain_last, shift_last, w_reduce, w_heads, w_message, w_gates, w_classes, depth_cot, class_cot,
    ) = args
    narrow = jnp.concatenate([gain_first, shift_first, gain_middle, shift_middle])
    gains = jnp.stack([narrow, gain_last, shift_last]).astype(F32)
    ins = (
        crop_height, crop_width, images.reshape(160, 2048), w_first, w_middle, w_last, w_reduce, w_gates, w_classes,
        w_heads, w_message, gains, depth_cot.reshape(160, 512), class_cot.transpose(0, 1, 3, 2).reshape(2, 40, 80),
    )
    names = list(INS) + list(OUTS) + list(SHAPES) + ["send_sems", "recv_sems", "near_sems"]
    smem, hbm, vmem = (pl.BlockSpec(memory_space=m) for m in (pltpu.SMEM, pltpu.HBM, pltpu.VMEM))
    spec = {"crop_h": smem, "crop_w": smem, "gains": vmem}
    outs = pl.pallas_call(
        functools.partial(body, names),
        out_shape=[jax.ShapeDtypeStruct(*v) for v in OUTS.values()],
        in_specs=[spec.get(n, hbm) for n in INS],
        out_specs=[hbm] * len(OUTS),
        scratch_shapes=[pltpu.VMEM(*v) for v in SHAPES.values()]
        + [pltpu.SemaphoreType.DMA((n,)) for n in (SENDS, SENDS, NEAR)],
        compiler_params=pltpu.CompilerParams(has_side_effects=True, collective_id=0, vmem_limit_bytes=64 * 2**20),
        name="residual_distill",
    )(*ins)
    o = dict(zip(OUTS, outs))
    taken = [n for n in OUTS if n.startswith("o_")]
    staged = {"i_" + n[2:]: OUTS[n] for n in taken if n not in ("o_depth", "o_logits")}
    staged.update({"v_" + n: v for n, v in FINAL.items() if n not in ("depth", "logits")})
    final = pl.pallas_call(
        functools.partial(widen_out, taken + list(FINAL) + list(staged) + ["sems"]),
        out_shape=[jax.ShapeDtypeStruct(*v) for v in FINAL.values()],
        in_specs=[hbm] * len(taken),
        out_specs=[hbm] * len(FINAL),
        scratch_shapes=[pltpu.VMEM(*v) for v in staged.values()] + [pltpu.SemaphoreType.DMA((40,))],
        compiler_params=pltpu.CompilerParams(vmem_limit_bytes=32 * 2**20),
        name="widen_out",
    )(*[o[n] for n in taken])
    f = dict(zip(FINAL, final))
    f["depth"] = f["depth"].reshape(1, 2, 80, 512)
    f["logits"] = f["logits"].reshape(1, 2, 40, 80).transpose(0, 1, 3, 2)
    f["img"] = f["img"].reshape(1, 2, 80, 2048)
    for n in ("gain1", "shift1", "gain2", "shift2", "gain3", "shift3"):
        f[n] = f[n].reshape(-1)
    return tuple(f.values())


def solution(mesh):
    def step(*args):
        if mesh.shape["batch"] == 16 and mesh.shape["rows"] == 2:
            return fast(args)
        return shards(*args)

    placed = (
        P("batch", "rows", None, None),
        P(),
        P(),
        P("batch", None),
        P("batch"),
        P("batch"),
        P(None, "batch", None),
        P("batch"),
        P("batch"),
        P("batch", None),
        P("batch"),
        P("batch"),
        P("batch", None),
        P("rows", None, "batch", None),
        P("rows", None, "batch", None),
        P(None, "batch", None),
        P("batch", None),
        P("batch", "rows", None, None),
        P("batch", "rows", None, None),
    )
    return jax.shard_map(
        step,
        mesh=mesh,
        in_specs=placed,
        out_specs=(
            P("batch", "rows", None, None),
            P("batch", "rows", None, None),
            P("batch", "rows", None, None),
            P("batch", None),
            P("batch"),
            P("batch"),
            P(None, "batch", None),
            P("batch"),
            P("batch"),
            P("batch", None),
            P("batch"),
            P("batch"),
            P("batch", None),
            P("rows", None, "batch", None),
            P("rows", None, "batch", None),
            P(None, "batch", None),
            P("batch", None),
        ),
        check_vma=False,
    )
```

```python
import functools
from types import SimpleNamespace

import numpy as np
import jax
import jax.numpy as jnp
from jax import lax
from jax.sharding import PartitionSpec as P
from jax.experimental import pallas as pl
from jax.experimental.pallas import tpu as pltpu

EPS = 1e-05
MESH = pl.DeviceIdType.MESH
F32 = jnp.float32
BF16 = jnp.bfloat16
ROOT = 0.7978845608028654
CUBE = 0.044715
SENDS = 247
NEAR = 54


def dot(left, right):
    return jnp.dot(left, right, preferred_element_type=F32)


def dot_last(left, right):
    return lax.dot_general(left, right, (((1,), (1,)), ((), ())), preferred_element_type=F32)


def dot_first(left, right):
    return lax.dot_general(left, right, (((0,), (0,)), ((), ())), preferred_element_type=F32)


def gelu_of(v):
    return 0.5 * v * (1.0 + jnp.tanh(ROOT * (v + CUBE * v * v * v)))


def slope_of(v):
    t = jnp.tanh(ROOT * (v + CUBE * v * v * v))
    return 0.5 * (1.0 + t) + 0.5 * v * (1.0 - t * t) * (ROOT * (1.0 + 3.0 * CUBE * v * v))


def rows_loop(total, chunk, step):
    def body(index, carry):
        step(pl.multiple_of(index * chunk, chunk))
        return carry

    lax.fori_loop(0, total // chunk, body, 0)


class Copy:
    def __init__(self, remote, links, index, like):
        self.remote, self.links, self.index, self.like = remote, links, index, like

    def wait_recv(self):
        if self.like is None:
            self.remote.wait_recv()
        else:
            ref = self.like(1)
            pltpu.make_async_copy(ref, ref, self.links.recv.at[self.index]).wait()

    def wait_send(self):
        if self.like is None:
            self.remote.wait_send()
        else:
            ref = self.like(0)
            pltpu.make_async_copy(ref, ref, self.links.send.at[self.index]).wait()


class Group:
    scoped = True

    def __init__(self, links, index, like):
        self.links, self.index, self.like = links, index, like

    def push(self, src, dst, device, when=None):
        remote = pltpu.make_async_remote_copy(
            src_ref=src,
            dst_ref=dst,
            send_sem=self.links.send.at[self.index],
            recv_sem=self.links.recv.at[self.index],
            device_id=device,
            device_id_type=MESH,
        )
        if when is None:
            remote.start()
        else:
            pl.when(when)(remote.start)

    def wait_recv(self):
        ref = self.like()
        pltpu.make_async_copy(ref, ref, self.links.recv.at[self.index]).wait()

    def wait_send(self):
        ref = self.like()
        pltpu.make_async_copy(ref, ref, self.links.send.at[self.index]).wait()


class Links:
    def __init__(self, send, recv, local):
        self.send, self.recv, self.local = send, recv, local
        self.used, self.local_used = 0, 0
        self.open = []

    def push(self, src, dst, device, when=None, like=None):
        i = self.used
        self.used += 1
        send, recv = self.send.at[i], self.recv.at[i]
        remote = pltpu.make_async_remote_copy(
            src_ref=src, dst_ref=dst, send_sem=send, recv_sem=recv, device_id=device, device_id_type=MESH
        )
        if when is None:
            remote.start()
        else:
            pl.when(when)(remote.start)
        cp = Copy(remote, self, i, like)
        self.open.append((cp, when))
        return cp

    def group(self, like, when=None):
        cp = Group(self, self.used, like)
        self.used += 1
        self.open.append((cp, when))
        return cp

    def near(self, src, dst):
        i = self.local_used
        self.local_used += 1
        cp = pltpu.make_async_copy(src, dst, self.local.at[i])
        cp.start()
        return cp

    def drain(self, scoped=False):
        kept = []
        for cp, when in self.open:
            if scoped and isinstance(cp, Copy) and cp.like is not None:
                kept.append((cp, when))
            elif when is None:
                cp.wait_send()
            else:
                pl.when(when)(cp.wait_send)
        self.open = kept


def wait(copies, when=None):
    def run():
        for cp in copies:
            cp.wait_recv()

    if when is None:
        run()
    else:
        pl.when(when)(run)


def lanes(mask, width):
    return jnp.concatenate([mask] * (width // 128), axis=1) if width > 128 else mask


def padded_2(cells, sides, width):
    for axis, dim in sides:
        count = lax.axis_size(axis)
        ends = count - 1
        head = lax.slice_in_dim(cells, 0, width, axis=dim)
        tail = lax.slice_in_dim(cells, cells.shape[dim] - width, cells.shape[dim], axis=dim)
        cells = jnp.concatenate(
            [
                lax.ppermute(tail, axis, [(i, (i + 1) % count) for i in range(ends)]),
                cells,
                lax.ppermute(head, axis, [((i + 1) % count, i) for i in range(ends)]),
            ],
            axis=dim,
        )
    return cells


def gelu_tanh(values):
    return jax.nn.gelu(values, approximate=True)


def gelu_slope(values, upstream):
    return jax.vjp(gelu_tanh, values)[1](upstream)[0]


def project(values, weight):
    return jnp.einsum("nrcj,jk->nrck", values, weight, preferred_element_type=jnp.float32)


def project_back(upstream, weight):
    return jnp.einsum("nrck,jk->nrcj", upstream, weight, preferred_element_type=jnp.float32)


def outer_sum(values, upstream):
    return jnp.einsum("nrcj,nrck->jk", values, upstream, preferred_element_type=jnp.float32)


def widen(padded):
    return jnp.pad(padded, ((0, 0), (0, 0), (1, 1), (0, 0)))


def halo_value(values):
    return padded_2(values, (("rows", 1),), 1)


def halo_grad(values):
    return padded_2(values, (("rows", 1),), 1)


def conv_apply(padded, kernel):
    row_count = padded.shape[1] - 2
    col_count = padded.shape[2]
    widened = widen(padded)
    running = jnp.zeros((padded.shape[0], row_count, col_count, kernel.shape[2]), jnp.float32)
    for tap_index in range(9):
        shift_down = tap_index // 3
        shift_right = tap_index % 3
        running = running + project(
            widened[
                :, shift_down : shift_down + row_count, shift_right : shift_right + col_count, :
            ],
            kernel[tap_index],
        )
    return running


def conv_kernel_grad(padded, upstream):
    row_count = upstream.shape[1]
    col_count = upstream.shape[2]
    widened = widen(padded)
    return jnp.stack(
        [
            outer_sum(
                widened[
                    :,
                    tap_index // 3 : tap_index // 3 + row_count,
                    tap_index % 3 : tap_index % 3 + col_count,
                    :,
                ],
                upstream,
            )
            for tap_index in range(9)
        ]
    )


def conv_input_grad(padded_grad, kernel):
    row_count = padded_grad.shape[1] - 2
    col_count = padded_grad.shape[2]
    widened = widen(padded_grad)
    running = jnp.zeros((padded_grad.shape[0], row_count, col_count, kernel.shape[1]), jnp.float32)
    for tap_index in range(9):
        shift_down = tap_index // 3
        shift_right = tap_index % 3
        running = running + project_back(
            widened[
                :,
                2 - shift_down : 2 - shift_down + row_count,
                2 - shift_right : 2 - shift_right + col_count,
                :,
            ],
            kernel[tap_index],
        )
    return running


def crop_mask(height, width, first_row, row_count, col_count):
    row_ids = first_row + jnp.arange(row_count, dtype=jnp.int32)
    col_ids = jnp.arange(col_count, dtype=jnp.int32)
    inside = (row_ids[None, :, None] < height[:, None, None]) & (
        col_ids[None, None, :] < width[:, None, None]
    )
    return inside.astype(jnp.float32)[..., None]


def norm_forward(pre_act, pixel_mask, gain_vec, shift_vec, valid_count):
    sums = jnp.sum(pre_act * pixel_mask, axis=(0, 1, 2))
    squares = jnp.sum(pre_act * pre_act * pixel_mask, axis=(0, 1, 2))
    sums, squares = lax.psum((sums, squares), ("batch", "rows"))
    mean_vec = sums / valid_count
    inv_std = lax.rsqrt(squares / valid_count - mean_vec * mean_vec + EPS)
    normal = (pre_act - mean_vec) * inv_std
    return (normal, inv_std, normal * gain_vec + shift_vec)


def norm_backward(upstream, normal, inv_std, gain_vec, pixel_mask, valid_count):
    shift_part = jnp.sum(upstream, axis=(0, 1, 2))
    gain_part = jnp.sum(upstream * normal, axis=(0, 1, 2))
    shift_part, gain_part = lax.psum((shift_part, gain_part), ("batch", "rows"))
    d_pre = (
        pixel_mask
        * gain_vec
        * inv_std
        * (upstream - shift_part / valid_count - normal * gain_part / valid_count)
    )
    return (d_pre, gain_part, shift_part)


def task_forward(padded_in, heads, messages, pixel_mask, pad_rows):
    pre_list = []
    feat_list = []
    padded_feats = []
    message_list = []
    for task in range(heads.shape[0]):
        pre_act = conv_apply(padded_in, heads[task])
        feature = (gelu_tanh(pre_act) * pixel_mask).astype(jnp.bfloat16)
        padded_feat = pad_rows(feature)
        pre_list.append(pre_act)
        feat_list.append(feature)
        padded_feats.append(padded_feat)
        message_list.append(conv_apply(padded_feat, messages[task]).astype(jnp.bfloat16))
    return (pre_list, feat_list, padded_feats, message_list)


def task_backward(
    padded_in,
    heads,
    messages,
    pixel_mask,
    pre_list,
    padded_feats,
    feat_grads,
    message_grads,
    pad_grad,
):
    input_grad = jnp.zeros(
        padded_in.shape[:1] + (padded_in.shape[1] - 2,) + padded_in.shape[2:], jnp.float32
    )
    head_grads = []
    kernel_grads = []
    for task in range(heads.shape[0]):
        low_message = message_grads[task].astype(jnp.bfloat16)
        kernel_grads.append(conv_kernel_grad(padded_feats[task], low_message))
        feat_grad = feat_grads[task] + conv_input_grad(pad_grad(low_message), messages[task])
        low_pre = gelu_slope(pre_list[task], feat_grad * pixel_mask).astype(jnp.bfloat16)
        head_grads.append(conv_kernel_grad(padded_in, low_pre))
        input_grad = input_grad + conv_input_grad(pad_grad(low_pre), heads[task])
    return (input_grad, jnp.stack(head_grads), jnp.stack(kernel_grads))


def streams_forward(features, messages, gates_all, classes_all, pixel_mask):
    gate_depth = jax.nn.sigmoid(project(features[0], gates_all[0]))
    gate_class = jax.nn.sigmoid(project(features[3], gates_all[1]))
    depth_sum = (
        messages[1].astype(jnp.float32)
        + messages[2].astype(jnp.float32)
        + messages[3].astype(jnp.float32)
    )
    class_sum = (
        messages[0].astype(jnp.float32)
        + messages[1].astype(jnp.float32)
        + messages[2].astype(jnp.float32)
    )
    depth_stream = (features[0].astype(jnp.float32) + gate_depth * depth_sum) * pixel_mask
    merged = (features[3].astype(jnp.float32) + gate_class * class_sum).astype(jnp.bfloat16)
    class_logits = project(merged, classes_all) * pixel_mask
    return (depth_stream, class_logits, merged, gate_depth, gate_class, depth_sum, class_sum)


def streams_backward(
    features,
    merged,
    gate_depth,
    gate_class,
    depth_sum,
    class_sum,
    depth_cot,
    class_cot,
    gates_all,
    classes_all,
    pixel_mask,
):
    depth_grad = depth_cot.astype(jnp.float32) * pixel_mask
    logit_grad = (class_cot.astype(jnp.float32) * pixel_mask).astype(jnp.bfloat16)
    grad_classes = outer_sum(merged, logit_grad)
    merged_grad = project_back(logit_grad, classes_all)
    gate_depth_grad = (depth_grad * depth_sum * gate_depth * (1.0 - gate_depth)).astype(
        jnp.bfloat16
    )
    gate_class_grad = (merged_grad * class_sum * gate_class * (1.0 - gate_class)).astype(
        jnp.bfloat16
    )
    grad_gates = jnp.stack(
        [outer_sum(features[0], gate_depth_grad), outer_sum(features[3], gate_class_grad)]
    )
    depth_feat = depth_grad + project_back(gate_depth_grad, gates_all[0])
    class_feat = merged_grad + project_back(gate_class_grad, gates_all[1])
    depth_message = depth_grad * gate_depth
    class_message = merged_grad * gate_class
    nothing = jnp.zeros_like(depth_grad)
    feat_grads = [depth_feat, nothing, nothing, class_feat]
    message_grads = [
        class_message,
        depth_message + class_message,
        depth_message + class_message,
        depth_message,
    ]
    return (feat_grads, message_grads, grad_gates, grad_classes)


def shards(
    images,
    crop_height,
    crop_width,
    w_first,
    gain_first,
    shift_first,
    w_middle,
    gain_middle,
    shift_middle,
    w_last,
    gain_last,
    shift_last,
    w_reduce,
    w_heads,
    w_message,
    w_gates,
    w_classes,
    depth_cot,
    class_cot,
):
    image_index = lax.axis_index("batch")
    batch_count = lax.axis_size("batch")
    row_count = images.shape[1]
    col_count = images.shape[2]
    height = lax.dynamic_slice_in_dim(crop_height, image_index, 1, 0)
    width = lax.dynamic_slice_in_dim(crop_width, image_index, 1, 0)
    pixel_mask = crop_mask(height, width, lax.axis_index("rows") * row_count, row_count, col_count)
    valid_count = jnp.sum(crop_height * crop_width).astype(jnp.float32)
    gathered = (
        lax.all_gather(w_first, "batch", axis=0, tiled=True),
        lax.all_gather(w_middle, "batch", axis=1, tiled=True),
        lax.all_gather(w_last, "batch", axis=0, tiled=True),
        lax.all_gather(w_reduce, "batch", axis=0, tiled=True),
        lax.all_gather(w_gates, "batch", axis=1, tiled=True),
        lax.all_gather(w_classes, "batch", axis=0, tiled=True),
        lax.all_gather(gain_first, "batch", axis=0, tiled=True),
        lax.all_gather(shift_first, "batch", axis=0, tiled=True),
        lax.all_gather(gain_middle, "batch", axis=0, tiled=True),
        lax.all_gather(shift_middle, "batch", axis=0, tiled=True),
        lax.all_gather(gain_last, "batch", axis=0, tiled=True),
        lax.all_gather(shift_last, "batch", axis=0, tiled=True),
        lax.all_gather(w_heads, "batch", axis=2, tiled=True),
        lax.all_gather(w_message, "batch", axis=2, tiled=True),
    )
    first_all = gathered[0]
    middle_all = gathered[1]
    last_all = gathered[2]
    reduce_all = gathered[3]
    gates_all = gathered[4]
    classes_all = gathered[5]
    gain_one = gathered[6].astype(jnp.float32)
    shift_one = gathered[7].astype(jnp.float32)
    gain_two = gathered[8].astype(jnp.float32)
    shift_two = gathered[9].astype(jnp.float32)
    gain_three = gathered[10].astype(jnp.float32)
    shift_three = gathered[11].astype(jnp.float32)
    heads_own = gathered[12]
    message_own = gathered[13]
    masked_in = images.astype(jnp.float32) * pixel_mask
    low_in = masked_in.astype(jnp.bfloat16)
    pre_first = project(low_in, first_all)
    normal_first, std_first, out_first = norm_forward(
        pre_first, pixel_mask, gain_one, shift_one, valid_count
    )
    act_first = (gelu_tanh(out_first) * pixel_mask).astype(jnp.bfloat16)
    padded_first = halo_value(act_first)
    pre_middle = conv_apply(padded_first, middle_all)
    normal_middle, std_middle, out_middle = norm_forward(
        pre_middle, pixel_mask, gain_two, shift_two, valid_count
    )
    act_middle = (gelu_tanh(out_middle) * pixel_mask).astype(jnp.bfloat16)
    pre_last = project(act_middle, last_all)
    normal_last, std_last, out_last = norm_forward(
        pre_last, pixel_mask, gain_three, shift_three, valid_count
    )
    summed = out_last + masked_in
    block_out = (gelu_tanh(summed) * pixel_mask).astype(jnp.bfloat16)
    low_reduced = project(block_out, reduce_all).astype(jnp.bfloat16)
    heads_all, message_all = (
        lax.all_gather(heads_own, "rows", axis=0, tiled=True),
        lax.all_gather(message_own, "rows", axis=0, tiled=True),
    )
    padded_in = halo_value(low_reduced)
    pre_list, feat_list, padded_feats, message_list = task_forward(
        padded_in, heads_all, message_all, pixel_mask, halo_value
    )
    depth_stream, class_logits, merged, gate_depth, gate_class, depth_sum, class_sum = (
        streams_forward(feat_list, message_list, gates_all, classes_all, pixel_mask)
    )
    feat_grads, message_grads, grad_gates, grad_classes = streams_backward(
        feat_list,
        merged,
        gate_depth,
        gate_class,
        depth_sum,
        class_sum,
        depth_cot,
        class_cot,
        gates_all,
        classes_all,
        pixel_mask,
    )
    reduced_grad, grad_heads, grad_message = task_backward(
        padded_in,
        heads_all,
        message_all,
        pixel_mask,
        pre_list,
        padded_feats,
        feat_grads,
        message_grads,
        halo_grad,
    )
    low_reduced_grad = reduced_grad.astype(jnp.bfloat16)
    grad_reduce = outer_sum(block_out, low_reduced_grad)
    block_grad = project_back(low_reduced_grad, reduce_all)
    sum_grad = gelu_slope(summed, block_grad * pixel_mask)
    d_last, gain_grad_three, shift_grad_three = norm_backward(
        sum_grad, normal_last, std_last, gain_three, pixel_mask, valid_count
    )
    low_last = d_last.astype(jnp.bfloat16)
    grad_last = outer_sum(act_middle, low_last)
    middle_grad = project_back(low_last, last_all)
    d_middle, gain_grad_two, shift_grad_two = norm_backward(
        gelu_slope(out_middle, middle_grad * pixel_mask),
        normal_middle,
        std_middle,
        gain_two,
        pixel_mask,
        valid_count,
    )
    low_middle = d_middle.astype(jnp.bfloat16)
    grad_middle = conv_kernel_grad(padded_first, low_middle)
    first_grad = conv_input_grad(halo_grad(low_middle), middle_all)
    d_first, gain_grad_one, shift_grad_one = norm_backward(
        gelu_slope(out_first, first_grad * pixel_mask),
        normal_first,
        std_first,
        gain_one,
        pixel_mask,
        valid_count,
    )
    low_first = d_first.astype(jnp.bfloat16)
    grad_first = outer_sum(low_in, low_first)
    image_grad = (project_back(low_first, first_all) + sum_grad) * pixel_mask
    summed_grads = (
        lax.psum_scatter(grad_first, "batch", scatter_dimension=0, tiled=True),
        lax.psum_scatter(grad_middle, "batch", scatter_dimension=1, tiled=True),
        lax.psum_scatter(grad_last, "batch", scatter_dimension=0, tiled=True),
        lax.psum_scatter(grad_reduce, "batch", scatter_dimension=0, tiled=True),
        lax.psum_scatter(grad_gates, "batch", scatter_dimension=1, tiled=True),
        lax.psum_scatter(grad_classes, "batch", scatter_dimension=0, tiled=True),
        lax.psum_scatter(grad_heads, "batch", scatter_dimension=2, tiled=True),
        lax.psum_scatter(grad_message, "batch", scatter_dimension=2, tiled=True),
    )
    shared = (
        lax.psum(summed_grads[0].astype(jnp.bfloat16), "rows").astype(jnp.float32),
        lax.psum(summed_grads[1].astype(jnp.bfloat16), "rows").astype(jnp.float32),
        lax.psum(summed_grads[2].astype(jnp.bfloat16), "rows").astype(jnp.float32),
        lax.psum(summed_grads[3].astype(jnp.bfloat16), "rows").astype(jnp.float32),
        lax.psum(summed_grads[4].astype(jnp.bfloat16), "rows").astype(jnp.float32),
        lax.psum(summed_grads[5].astype(jnp.bfloat16), "rows").astype(jnp.float32),
    )
    heads_out, message_out = (
        lax.psum_scatter(
            summed_grads[6].astype(jnp.bfloat16), "rows", scatter_dimension=0, tiled=True
        ).astype(jnp.float32),
        lax.psum_scatter(
            summed_grads[7].astype(jnp.bfloat16), "rows", scatter_dimension=0, tiled=True
        ).astype(jnp.float32),
    )

    def own_share(member):
        share = member.shape[0] // batch_count
        return lax.dynamic_slice_in_dim(member, image_index * share, share, 0)

    return (
        depth_stream.astype(jnp.bfloat16),
        class_logits.astype(jnp.bfloat16),
        image_grad,
        shared[0],
        own_share(gain_grad_one),
        own_share(shift_grad_one),
        shared[1],
        own_share(gain_grad_two),
        own_share(shift_grad_two),
        shared[2],
        own_share(gain_grad_three),
        own_share(shift_grad_three),
        shared[3],
        heads_out,
        message_out,
        shared[4],
        shared[5],
    )


SHAPES = dict(
    wf=((4, 2, 2, 128, 256), BF16),
    wm=((9, 4, 2, 2, 32, 256), BF16),
    wl=((4, 2, 2, 32, 1024), BF16),
    wr=((4, 2, 128, 512), BF16),
    wc=((16, 32, 128), BF16),
    wcs=((32, 128), BF16),
    wcv=((32, 40), BF16),
    cct=((2, 40, 80), BF16),
    ctf=((128, 128), F32),
    xh=((320, 1024), BF16),
    wh=((9, 4, 2, 2, 32, 256), BF16),
    wq=((9, 4, 2, 2, 32, 256), BF16),
    wg=((4, 2, 2, 32, 256), BF16),
    xall=((320, 2048), BF16),
    maskp=((1280, 128), F32),
    pre1=((320, 256), F32),
    pre2=((320, 256), F32),
    pre3=((320, 1024), F32),
    bnp1=((8, 256), F32),
    bnp2=((8, 256), F32),
    bnp3=((8, 1024), F32),
    a1=((320, 512), BF16),
    a2=((320, 512), BF16),
    a3=((480, 1536), BF16),
    blk=((320, 1024), BF16),
    rps=((160, 512), BF16),
    rpr=((160, 512), BF16),
    rbuf=((1280, 512), BF16),
    fown=((1280, 256), BF16),
    ffull=((1280, 512), BF16),
    msgb=((1280, 256), BF16),
    gateb=((1280, 256), BF16),
    mrecv=((4, 160, 512), BF16),
    dm=((4, 160, 512), BF16),
    eu=((2, 160, 512), BF16),
    dcotv=((160, 512), BF16),
    ccotv=((160, 128), BF16),
    olt=((2, 40, 80), BF16),
    ods=((160, 512), BF16),
    olg=((160, 128), BF16),
    mrg=((160, 512), BF16),
    fg=((2, 2, 160, 512), BF16),
    dmg=((1280, 256), BF16),
    exg=((2, 1280, 256), BF16),
    gm=((9, 4, 2, 2, 32, 256), BF16),
    gh=((9, 4, 2, 2, 32, 256), BF16),
    gg=((4, 2, 2, 32, 256), BF16),
    rg=((3, 2, 2, 32, 256), BF16),
    hop=((2, 9, 2, 2, 32, 256), BF16),
    gcls=((16, 32, 128), BF16),
    rcls=((15, 32, 128), BF16),
    clsr=((32, 128), F32),
    dfs=((1280, 256), BF16),
    dfr=((1280, 256), BF16),
    drs=((640, 512), BF16),
    drr=((640, 512), BF16),
    dro=((3, 160, 512), BF16),
    dred=((320, 512), BF16),
    dsr=((160, 1024), BF16),
    par2=((320, 256), BF16),
    par1=((320, 256), BF16),
    dp1r=((160, 256), BF16),
    rcr=((4, 2, 128, 512), BF16),
    rcl=((4, 2, 32, 1024), BF16),
    rcm=((9, 4, 2, 32, 256), BF16),
    rcf=((4, 2, 128, 256), BF16),
    ryr=((4, 128, 512), BF16),
    ryl=((4, 32, 1024), BF16),
    rym=((9, 4, 32, 256), BF16),
    ryf=((4, 128, 256), BF16),
    rzr=((3, 128, 512), BF16),
    rzl=((3, 32, 1024), BF16),
    rzm=((3, 9, 32, 256), BF16),
    rzf=((3, 128, 256), BF16),
)
for _i, _w in enumerate((256, 256, 512, 512, 256, 256)):
    SHAPES["am%d" % _i] = ((8, _w), F32)
    SHAPES["as%d" % _i] = ((8, _w), F32)
    SHAPES["at%d" % _i] = ((8, _w), F32)
    SHAPES["ar%d" % _i] = ((3, 8, _w), F32)
    SHAPES["az%d" % _i] = ((3, 8, _w), F32)

INS = (
    "crop_h", "crop_w", "images", "first", "middle", "last", "reduce", "gates",
    "classes", "heads", "messages", "gains", "dcot", "ccot",
)
OUTS = dict(
    o_depth=((160, 512), BF16),
    o_logits=((2, 40, 80), BF16),
    o_img=((160, 2048), BF16),
    o_first=((128, 512), BF16),
    o_gs1=((2, 8, 256), F32),
    o_mid=((9, 32, 512), BF16),
    o_gs2=((2, 8, 256), F32),
    o_last=((2, 32, 1024), BF16),
    o_gs3=((2, 8, 512), F32),
    o_red=((128, 512), BF16),
    o_heads=((2, 9, 32, 512), BF16),
    o_mess=((2, 9, 32, 512), BF16),
    o_gates=((2, 32, 512), BF16),
    o_cls=((32, 128), F32),
    rm=((3, 9, 2, 2, 32, 256), BF16),
    rh=((3, 9, 2, 2, 32, 256), BF16),
    wfo=((4, 2, 2, 128, 256), BF16),
    st_h=((9, 32, 512), BF16),
    st_m=((9, 32, 512), BF16),
)


def shift_columns(v):
    rows, width = v.shape
    col = lax.broadcasted_iota(jnp.int32, (rows, width), 0)
    left = jnp.where(col == 0, 0.0, pltpu.roll(v, 1, 0))
    right = jnp.where(col == rows - 1, 0.0, pltpu.roll(v, rows - 1, 0))
    return left, right


def spread(src, dst, n_img, width):
    zero = jnp.zeros((80, 3 * width), BF16)
    for pad in range(n_img + 1):
        dst[pl.ds(pad * 400, 80), :] = zero

    def body(i, carry):
        v = src[pl.ds(pl.multiple_of(i * 80, 16), 80), :]
        left, right = shift_columns(v.astype(F32))
        row = pl.multiple_of((i + lax.div(i, np.int32(4)) + 1) * 80, 16)
        dst[pl.ds(row, 80), 0:width] = left.astype(BF16)
        dst[pl.ds(row, 80), width : 2 * width] = v
        dst[pl.ds(row, 80), 2 * width : 3 * width] = right.astype(BF16)
        return carry

    lax.fori_loop(0, 4 * n_img, body, 0)


def conv_rows(a3, w, img):
    acc = None
    for a in range(3):
        base = pl.multiple_of((5 * img + a) * 80, 16)
        part = dot(a3[pl.ds(base, 320), :], w[3 * a : 3 * a + 3].reshape(1536, 256))
        acc = part if acc is None else acc + part
    return acc


def conv_back(d3, w, img):
    acc = None
    for a in range(3):
        for q in range(3):
            base = pl.multiple_of((5 * img + a) * 80, 16)
            tap = 3 * (2 - a) + (2 - q)
            part = dot_last(d3[pl.ds(base, 320), 256 * q : 256 * q + 256], w[tap].reshape(512, 256))
            acc = part if acc is None else acc + part
    return acc


def conv_weight(a3, d3, out, n_img, first, last):
    depth = (5 * n_img - 1) * 80

    def body(tap, carry):
        a = lax.div(tap, np.int32(3))
        q = tap - 3 * a
        left = a3[pl.ds(pl.multiple_of(a * 80, 16), depth), pl.ds(pl.multiple_of(q * 512, 128), 512)]
        out[tap] = dot_first(left, d3[pl.ds(80, depth), 256:512]).astype(BF16).reshape(out.shape[1:])
        return carry

    lax.fori_loop(first, last, body, 0)


def body(names, *refs):
    s = SimpleNamespace(**dict(zip(names, refs)))
    b, r = lax.axis_index("batch"), lax.axis_index("rows")
    z = lax.div(b, np.int32(4))
    y = lax.rem(lax.div(b, np.int32(2)), np.int32(2))
    c = lax.rem(b, np.int32(2))
    ln = Links(s.send_sems, s.recv_sems, s.near_sems)
    half, fhalf = 256 * r, 256 * c

    def dev(zz, yy, cc, rr):
        return (4 * zz + 2 * yy + cc, rr)

    def zk(k):
        return lax.rem(z + k, np.int32(4))

    core, ypeer, xpeer = dev(z, y, 1 - c, r), dev(z, 1 - y, c, r), dev(z, y, c, 1 - r)
    special = r == y
    task = 2 * r + y
    img = 2 * y + c
    own_px = pl.multiple_of(320 * img + 160 * r, 16)
    my_rows = pl.multiple_of(160 * r, 16)
    other_rows = pl.multiple_of(160 * (1 - r), 16)
    half = pl.multiple_of(half, 128)
    ohalf = pl.multiple_of(256 * (1 - r), 128)
    fhalf = pl.multiple_of(fhalf, 128)
    offsets = [(dr, dy, dc) for dr in range(2) for dy in range(2) for dc in range(2) if dr + dy + dc]

    def peer(dr, dy, dc):
        rr = 1 - r if dr else r
        yy = 1 - y if dy else y
        cc = 1 - c if dc else c
        return rr, yy, cc

    def px_of(rr, yy, cc):
        return pl.multiple_of(320 * (2 * yy + cc) + 160 * rr, 16)

    ends = (z == 0) | (z == 3)
    inner = jnp.logical_not(ends)
    not_first, not_last = z != 0, z != 3
    far_end = dev(jnp.where(z == 1, 0, 3), y, c, r)
    odd = c == r

    def both(p, q):
        return q if p is None else (p if q is None else p & q)

    def line_start(src, at, when=None):
        got = {q: ln.push(src, at(z), dev(zk(q), y, c, r), when) for q in (1, 3)}
        got[2] = ln.push(src, at(z), dev(zk(2), y, c, r), both(when, ends))
        return got, [ln.push(src, at(z), ypeer, when)]

    def line_relay(state, at, when=None):
        got, ys = state
        wait([got[1], got[3]], when)
        got[0] = ln.push(at(3 - z), at(3 - z), far_end, both(when, inner))
        ys.append(ln.push(at(zk(3)), at(zk(3)), ypeer, when))
        ys.append(ln.push(at(zk(1)), at(zk(1)), ypeer, when))

    def line_last(state, at, col, when=None):
        got, ys = state
        wait([got[2]], both(when, inner))
        wait([got[0]], both(when, ends))
        ys.append(ln.push(at(zk(2)), at(zk(2)), ypeer, when))
        return [ln.push(col(y), col(y), core, when)]

    def line_core(state, col, cores, when=None):
        wait(state[1], when)
        cores.append(ln.push(col(1 - y), col(1 - y), core, when))

    def at_wf(zz):
        return s.wf.at[zz, y, c]

    def at_wm(zz):
        return s.wm.at[:, zz, y, c]

    def at_wl(zz):
        return s.wl.at[zz, y, c]

    def at_wr(zz):
        return s.wr.at[zz, y]

    def col_wf(yy):
        return s.wf.at[:, yy, c]

    def col_wm(yy):
        return s.wm.at[:, :, yy, c]

    def col_wl(yy):
        return s.wl.at[:, yy, c]

    def col_wr(yy):
        return s.wr.at[:, yy]

    near_last = [
        ln.near(s.last.at[:, pl.ds(pl.multiple_of((2 * i + r) * 128, 128), 128)], s.wl.at[z, y, c, :, 128 * i : 128 * i + 128])
        for i in range(8)
    ]
    near_own = ln.near(s.images, s.xall.at[pl.ds(my_rows, 160)])
    near_cls = ln.near(s.classes, s.wcv)
    near_wf = ln.near(s.first.at[:, pl.ds(half, 256)], s.wf.at[z, y, c])
    near_wm = ln.near(s.middle.at[:, :, pl.ds(half, 256)], s.wm.at[:, z, y, c])
    red_local = pltpu.make_async_copy(s.reduce, s.wr.at[z, y], s.near_sems.at[NEAR - 1])
    pl.when(odd)(red_local.start)
    near_late = [
        ln.near(s.dcot, s.dcotv),
        ln.near(s.ccot, s.cct),
        ln.near(s.heads.at[y, :, :, pl.ds(fhalf, 256)], s.wh.at[:, z, y, c]),
        ln.near(s.messages.at[y, :, :, pl.ds(fhalf, 256)], s.wq.at[:, z, y, c]),
        ln.near(s.gates.at[r, :, pl.ds(fhalf, 256)], s.wg.at[z, y, c]),
    ]
    barrier = pltpu.get_barrier_semaphore()
    friends = [
        dev(zk(q), 1 - y if j else y, 1 - c if i else c, r) for q in range(4) for j in range(2) for i in range(2) if q + j + i
    ] + [dev(z, 1 - y if j else y, 1 - c if i else c, 1 - r) for j in range(2) for i in range(2)]
    for friend in friends:
        pl.semaphore_signal(barrier, inc=1, device_id=friend, device_id_type=MESH)
    pl.semaphore_wait(barrier, len(friends))

    go_wf = line_start(s.first.at[:, pl.ds(half, 256)], at_wf)
    img_x = ln.push(s.images, s.xall.at[pl.ds(my_rows, 160)], xpeer)
    go_wm = line_start(s.middle.at[:, :, pl.ds(half, 256)], at_wm)
    for cp in near_last:
        cp.wait()
    got_wl = {q: ln.push(at_wl(z), at_wl(z), dev(zk(q), y, c, r)) for q in (1, 3)}
    got_wl[2] = ln.push(at_wl(z), at_wl(z), dev(zk(2), y, c, r), ends)
    got_wr = {q: ln.push(s.reduce, at_wr(z), dev(zk(q), y, c, r), odd) for q in (1, 3)}
    got_wr[2] = ln.push(s.reduce, at_wr(z), dev(zk(2), y, c, r), odd & ends)

    for i in range(4):
        high, wide = s.crop_h[4 * z + i], s.crop_w[4 * z + i]
        for row in range(4):
            col = lax.broadcasted_iota(jnp.int32, (80, 128), 0)
            inside = (col < wide) & (row < high)
            s.maskp[pl.ds(320 * i + 80 * row, 80), :] = jnp.where(inside, 1.0, 0.0)
    total = s.crop_h[0] * s.crop_w[0]
    for i in range(1, 16):
        total = total + s.crop_h[i] * s.crop_w[i]
    count = total.astype(F32)
    mine = pl.multiple_of(320 * img, 16)

    def mask_at(base, rows, width):
        return lanes(s.maskp[pl.ds(mine + base, rows), :], width)

    near_cls.wait()
    s.wcs[...] = jnp.zeros(s.wcs.shape, BF16)
    s.wcs[:, 0:40] = s.wcv[...]
    s.wc[b] = s.wcs[...]
    near_own.wait()
    near_wf.wait()
    line_relay(go_wf, at_wf)
    cores_wf = line_last(go_wf, at_wf, col_wf)
    near_wm.wait()
    line_relay(go_wm, at_wm)
    line_core(go_wf, col_wf, cores_wf)
    wait([img_x])

    def mask_x(base):
        rows = pl.ds(base, 80)
        v = (s.xall[rows, :].astype(F32) * mask_at(base, 80, 2048)).astype(BF16)
        s.xall[rows, :] = v
        for i in range(8):
            pick = jnp.where(r == 0, v[:, 256 * i : 256 * i + 128].astype(F32), v[:, 256 * i + 128 : 256 * i + 256].astype(F32))
            s.xh[rows, 128 * i : 128 * i + 128] = pick.astype(BF16)

    rows_loop(320, 80, mask_x)
    wait(cores_wf)

    def task_push(src, dst, lo, hi, staged):
        yy = 1 - y if staged else y
        got = {}
        for q in (1, 3, 2, 0):
            def like(q=q):
                return dst.at[lo:hi, 0, 0] if q else dst.at[lo:hi, 0, 0, 0]

            when = ends if q == 2 else None
            got[q] = ln.group(like, when)
            for i in range(2):
                if q + i == 0:
                    continue
                cc = 1 - c if i else c
                got[q].push(
                    src.at[lo:hi, :, pl.ds(pl.multiple_of(256 * cc, 128), 256)],
                    dst.at[lo:hi, z, yy, c],
                    dev(zk(q) if q else z, y, cc, r),
                    when,
                )
        return got, lo, hi, yy

    def task_relay(state, dst):
        got, lo, hi, yy = state
        wait([got[0], got[1], got[3]])
        hand = ln.push(dst.at[lo:hi, 3 - z, yy], dst.at[lo:hi, 3 - z, yy], far_end, inner)
        return got, hand

    def task_ready(state):
        got, hand = state
        wait([got[2]], inner)
        wait([hand], ends)

    def plane_start(n):
        m, ar = (getattr(s, p + str(n)) for p in ("am", "ar"))
        one = ln.group(lambda: ar)
        for i in (1, 2, 3):
            yy = 1 - y if i & 2 else y
            cc = 1 - c if i & 1 else c
            one.push(m, ar.at[i - 1], dev(z, yy, cc, r))
        return one

    def plane_end(n, one):
        m, sm, ar = (getattr(s, p + str(n)) for p in ("am", "as", "ar"))
        wait([one])
        sm[...] = (m[...] + ar[0]) + (ar[1] + ar[2])

    def reduce_plane(n):
        plane_end(n, plane_start(n))

    def reduce_line(n):
        sm, t, az = (getattr(s, p + str(n)) for p in ("as", "at", "az"))
        two = ln.group(lambda: az)
        for q in (1, 2, 3):
            two.push(sm, az.at[q - 1], dev(zk(q), y, c, r))
        wait([two])
        t[...] = (sm[...] + az[0]) + (az[1] + az[2])
        return t[...]

    def stats_of(pre, width, msg):
        m = lanes(s.maskp[pl.ds(mine, 320), :], width)
        v = pre * m
        sums = jnp.sum(v, axis=0, keepdims=True)
        squares = jnp.sum(v * pre, axis=0, keepdims=True)
        return sums, squares

    def norm_terms(n, bnp, width):
        t = reduce_line(n)
        if width == 256:
            rows = [t[i : i + 1] for i in range(4)]
        else:
            rows = [jnp.concatenate([t[2 * i : 2 * i + 1], t[2 * i + 1 : 2 * i + 2]], axis=1) for i in range(4)]
        mean = rows[0] / count
        inv = lax.rsqrt(rows[1] / count - mean * mean + EPS)
        bnp[0:1], bnp[1:2], bnp[2:3], bnp[3:4] = mean, inv, rows[2], rows[3]

    quarter = lax.div(b, np.int32(4))
    spot = 32 * lax.rem(b, np.int32(4))

    def placed(n):
        lane = lax.broadcasted_iota(jnp.int32, (8, 128), 1)
        out = []
        for p in range(2):
            if n < 2:
                v = jnp.broadcast_to(s.gains[0:1, :], (8, 128))
                v = pltpu.roll(v, lax.rem(spot + 128 - 32 * (2 * n + p), np.int32(128)), 1)
                v = jnp.where((lane >= spot) & (lane < spot + 32), v, 0.0)
                out.append(jnp.concatenate([jnp.where(quarter == 2 * r + i, v[0:1], 0.0) for i in range(2)], axis=1))
            else:
                v = s.gains[1 + p : 2 + p, :]
                out.append(
                    [
                        jnp.concatenate(
                            [jnp.where(odd & (lax.div(b, np.int32(2)) == 4 * h + i), v, 0.0) for i in range(4)], axis=1
                        )
                        for h in range(2)
                    ]
                )
        return out

    def put_stats(n, first, second, width, layer):
        m = getattr(s, "am%d" % n)
        m[...] = jnp.zeros(m.shape, F32)
        if width == 256:
            m[0:1], m[1:2] = first, second
            if layer is not None:
                m[2:3], m[3:4] = placed(layer)
        else:
            m[0:1], m[1:2] = first[:, :512], first[:, 512:]
            m[2:3], m[3:4] = second[:, :512], second[:, 512:]
            if layer is not None:
                gain, shift = placed(layer)
                m[4:5], m[5:6] = gain
                m[6:7], m[7:8] = shift

    pre = dot(s.xall[...], s.wf[...].reshape(2048, 256))
    s.pre1[...] = pre
    first_sum, first_sq = stats_of(pre, 256, None)
    put_stats(0, first_sum, first_sq, 256, 0)
    cores_wm = line_last(go_wm, at_wm, col_wm)
    reduce_plane(0)
    go_wl = (got_wl, [ln.push(at_wl(z), at_wl(z), ypeer)])
    go_wr = (got_wr, [ln.push(s.reduce, at_wr(z), ypeer, odd)])
    pl.when(odd)(red_local.wait)
    line_relay(go_wl, at_wl)
    line_relay(go_wr, at_wr, odd)
    norm_terms(0, s.bnp1, 256)
    heads_a = task_push(s.heads.at[y], s.wh, 0, 5, False)

    def act_from(prebuf, bnp, dst):
        def step(base):
            x = (prebuf[pl.ds(base, 80), :] - bnp[0:1]) * bnp[1:2] * bnp[2:3] + bnp[3:4]
            dst[pl.ds(base, 80), pl.ds(half, 256)] = (gelu_of(x) * mask_at(base, 80, 256)).astype(BF16)

        rows_loop(320, 80, step)

    act_from(s.pre1, s.bnp1, s.a1)
    a1_x = ln.push(s.a1.at[:, pl.ds(half, 256)], s.a1.at[:, pl.ds(half, 256)], xpeer)
    line_core(go_wm, col_wm, cores_wm)
    cores_wl = line_last(go_wl, at_wl, col_wl)
    cores_wr = line_last(go_wr, at_wr, col_wr, odd)
    wait(cores_wm)
    wait([a1_x])
    spread(s.a1, s.a3, 1, 512)
    pre = conv_rows(s.a3, s.wm, 0)
    s.pre2[...] = pre
    first_sum, first_sq = stats_of(pre, 256, None)
    put_stats(1, first_sum, first_sq, 256, 1)
    reduce_plane(1)
    over_h = ln.push(s.heads.at[1 - y], s.st_h, ypeer)
    norm_terms(1, s.bnp2, 256)
    relay_a = task_relay(heads_a, s.wh)
    heads_b = task_push(s.heads.at[y], s.wh, 5, 9, False)
    act_from(s.pre2, s.bnp2, s.a2)
    a2_x = ln.push(s.a2.at[:, pl.ds(half, 256)], s.a2.at[:, pl.ds(half, 256)], xpeer)
    line_core(go_wl, col_wl, cores_wl)
    line_core(go_wr, col_wr, cores_wr, odd)
    wait(cores_wl)
    wait([a2_x])
    pre = dot(s.a2[...], s.wl[...].reshape(512, 1024))
    s.pre3[...] = pre
    first_sum, first_sq = stats_of(pre, 1024, None)
    put_stats(2, first_sum, first_sq, 1024, 2)
    reduce_plane(2)
    over_m = ln.push(s.messages.at[1 - y], s.st_m, ypeer)
    norm_terms(2, s.bnp3, 1024)
    relay_b = task_relay(heads_b, s.wh)
    wait([over_h])
    staged_h = ln.near(s.st_h.at[:, :, pl.ds(fhalf, 256)], s.wh.at[:, z, 1 - y, c])
    heads_d = task_push(s.st_h, s.wh, 0, 5, True)
    heads_e = task_push(s.st_h, s.wh, 5, 9, True)
    gate_got = {}
    cls_got = ln.group(lambda: s.wc.at[0:15])
    for q in range(4):
        for j in range(2):
            if q + j:
                gate_got[q, j] = ln.group(lambda: s.wg.at[0, 0], (y == r) if j == 0 else (y != r))
            for i in range(2):
                if q + j + i == 0:
                    continue
                yy = 1 - y if j else y
                cc = 1 - c if i else c
                to = dev(zk(q) if q else z, yy, cc, r)
                cls_got.push(s.wcs, s.wc.at[b], to)
                src = s.gates.at[r, :, pl.ds(pl.multiple_of(256 * cc, 128), 256)]
                if q + j:
                    gate_got[q, j].push(src, s.wg.at[z, y, c], to, (y == r) if j == 0 else (y != r))
                else:
                    gate_got[0, 0] = ln.push(src, s.wg.at[z, y, c], to, y == r)

    def summed_at(base, rows):
        x = (s.pre3[pl.ds(base, rows), :] - s.bnp3[0:1]) * s.bnp3[1:2]
        return x, x * s.bnp3[2:3] + s.bnp3[3:4] + s.xh[pl.ds(base, rows), :].astype(F32)

    def block_step(base):
        _, v = summed_at(base, 32)
        s.blk[pl.ds(base, 32), :] = (gelu_of(v) * mask_at(base, 32, 1024)).astype(BF16)

    rows_loop(320, 32, block_step)
    wait(cores_wr, jnp.logical_not(odd))
    wred = s.wr[...].reshape(1024, 512)
    s.rps[...] = dot(s.blk[pl.ds(other_rows, 160), :], wred).astype(BF16)
    red_x = ln.push(s.rps, s.rpr, xpeer)
    part = dot(s.blk[pl.ds(my_rows, 160), :], wred)
    wait([red_x])
    s.rbuf[pl.ds(own_px, 160), :] = (part + s.rpr[...].astype(F32)).astype(BF16)

    def block_of(rr, yy, cc, lo=0, n=160):
        return s.rbuf.at[pl.ds(pl.multiple_of(px_of(rr, yy, cc) + lo, 16), n)]

    for cp in near_late:
        cp.wait()
    own = block_of(r, y, c)
    g_x = ln.push(own, own, xpeer)
    g_y = ln.push(own, own, ypeer)
    g_c = ln.push(own, own, core)
    wait([g_x])
    bx = block_of(1 - r, y, c, 0, 80)
    g_xy = ln.push(bx, bx, ypeer)
    wait([g_y])
    by = block_of(r, 1 - y, c, 80, 80)
    g_yx = ln.push(by, by, xpeer)
    bx = block_of(1 - r, y, c)
    g_c1 = ln.push(bx, bx, core)
    by = block_of(r, 1 - y, c)
    g_c2 = ln.push(by, by, core)
    wait([g_xy, g_yx])
    bd = block_of(1 - r, 1 - y, c)
    g_c3 = ln.push(bd, bd, core)
    relay_d = task_relay(heads_d, s.wh)
    wfo_x = ln.push(s.wf, s.wfo, xpeer)
    wait([g_c, g_c1, g_c2, g_c3])

    near_end = dev(jnp.where(z == 0, 1, 2), y, c, r)
    other_end = dev(jnp.where(z == 1, 3, 0), y, c, r)

    def grad_push(n, g, rm, lo, hi):
        def like(slot):
            return lambda side: rm.at[slot, lo:hi] if side else g.at[lo:hi, 0]

        got = {}
        for q in (1, 2, 3):
            direct = {1: not_last, 2: ends, 3: not_first}[q]
            got[q] = ln.push(g.at[lo:hi, zk(q)], rm.at[q - 1, lo:hi], dev(zk(q), y, c, r), direct, like(q - 1))
        hop = s.hop.at[n, lo:hi]
        got[0] = ln.push(
            g.at[lo:hi, 3 - z], hop, near_end, ends, lambda side: s.hop.at[n, lo:hi] if side else g.at[lo:hi, 0]
        )
        return got, n, g, rm, lo, hi

    def grad_hop(state):
        got, n, g, rm, lo, hi = state

        def add():
            got[0].wait_recv()
            far = jnp.where(z == 1, 3, 0)
            for t in range(lo, hi):
                s.hop[n, t] = (s.hop[n, t].astype(F32) + g[t, far].astype(F32)).astype(BF16)

        pl.when(inner)(add)
        got[4] = ln.push(
            s.hop.at[n, lo:hi], rm.at[1, lo:hi], other_end, inner,
            lambda side: rm.at[1, lo:hi] if side else s.hop.at[n, lo:hi],
        )

    def grad_wait(state):
        got = state[0]
        wait([got[1]], not_first)
        wait([got[3]], not_last)
        wait([got[2]], inner)
        wait([got[4]], ends)

    def tasks(r3, f3, d3, preh, dfull):
        spread(s.rbuf, r3, 4, 512)
        relay_e = task_relay(heads_e, s.wh)
        wait([over_m])
        staged_m = ln.near(s.st_m.at[:, :, pl.ds(fhalf, 256)], s.wq.at[:, z, 1 - y, c])

        def mess_push(a):
            return [
                task_push(s.st_m if staged else s.messages.at[y], s.wq, 3 * a, 3 * a + 3, staged) for staged in (False, True)
            ]

        mess = [mess_push(0), mess_push(1)]
        for part in (relay_a, relay_b, relay_d, relay_e):
            task_ready(part)
        staged_h.wait()

        def head_step(i, carry):
            v = conv_rows(r3, s.wh, i)
            px = pl.multiple_of(i * 320, 16)
            preh[pl.ds(px, 320), :] = v
            return carry

        lax.fori_loop(0, 4, head_step, 0)

        def feat_step(base):
            m = lanes(s.maskp[pl.ds(base, 80), :], 256)
            s.fown[pl.ds(base, 80), :] = (gelu_of(preh[pl.ds(base, 80), :]) * m).astype(BF16)

        rows_loop(1280, 80, feat_step)
        f_c = ln.push(s.fown, s.ffull.at[:, pl.ds(fhalf, 256)], core)
        f_n = ln.near(s.fown, s.ffull.at[:, pl.ds(fhalf, 256)])

        def seven():
            return s.dmg.at[0:1120]

        def to_owners(src, dst_of, when):
            got = {}
            for o in offsets:
                rr, yy, cc = peer(*o)
                got[o] = ln.push(
                    src.at[pl.ds(px_of(rr, yy, cc), 160)], dst_of().at[:, pl.ds(fhalf, 256)], dev(z, yy, cc, rr), when
                )
            return got

        f_own = to_owners(s.fown, lambda: s.fg.at[r, 0], special)

        def keep(dst, src):
            def run():
                dst[:, pl.ds(fhalf, 256)] = src[pl.ds(own_px, 160), :]

            return run

        pl.when(special)(keep(s.fg.at[r, 0], s.fown))
        f_n.wait()
        wait([f_c])

        def gate_ready():
            for cp in gate_got.values():
                cp.wait_recv()

        pl.when(special)(gate_ready)

        @pl.when(special)
        def _():
            def gate_step(base):
                v = dot(s.ffull[pl.ds(base, 320), :], s.wg[...].reshape(512, 256))
                s.gateb[pl.ds(base, 320), :] = (1.0 / (1.0 + jnp.exp(-v))).astype(BF16)

            rows_loop(1280, 320, gate_step)

        g_own = to_owners(s.gateb, lambda: s.fg.at[r, 1], special)
        pl.when(special)(keep(s.fg.at[r, 1], s.gateb))
        relayed = [[task_relay(p, s.wq) for p in mess[0]]]
        mess.append(mess_push(2))
        spread(s.ffull, f3, 4, 512)

        wait([cls_got])
        for i in range(2):
            s.ctf[...] = jnp.zeros((128, 128), F32)
            s.ctf[0:40, 0:80] = s.cct[i].astype(F32)
            turned = s.ctf[...].T
            s.ccotv[80 * i : 80 * i + 80, :] = turned[0:80, :].astype(BF16)
        for o in offsets:
            wait([g_own[o]], (r != y) if (o[0] + o[1]) % 2 else special)

        def early_step(base):
            rows = pl.ds(base, 32)
            m = lanes(s.maskp[pl.ds(own_px + base, 32), :], 512)
            gd, gc = s.fg[0, 1, rows, :].astype(F32), s.fg[1, 1, rows, :].astype(F32)
            dj = (s.ccotv[rows, :].astype(F32) * m[:, :128]).astype(BF16)
            s.ccotv[rows, :] = dj
            dd = s.dcotv[rows, :].astype(F32) * m
            dmer = dot_last(dj, s.wc[...].reshape(512, 128))
            s.eu[0, rows, :] = dd.astype(BF16)
            s.eu[1, rows, :] = dmer.astype(BF16)
            down, up = dd * gd, dmer * gc
            both = (down + up).astype(BF16)
            s.dm[0, rows, :] = up.astype(BF16)
            s.dm[1, rows, :] = both
            s.dm[2, rows, :] = both
            s.dm[3, rows, :] = down.astype(BF16)

        rows_loop(160, 32, early_step)
        d_got = ln.group(seven)
        for o in offsets:
            rr, yy, cc = peer(*o)
            ll = pl.ds(pl.multiple_of(256 * cc, 128), 256)
            d_got.push(s.dm.at[2 * rr + yy, :, ll], s.dmg.at[pl.ds(own_px, 160)], dev(z, yy, cc, rr))
        u_got = {}
        for o in offsets:
            rr, yy, cc = peer(*o)
            ll = pl.ds(pl.multiple_of(256 * cc, 128), 256)
            u_got[o] = ln.push(s.eu.at[rr, :, ll], s.exg.at[0, pl.ds(own_px, 160)], dev(z, yy, cc, rr), rr == yy)
        s.dmg[pl.ds(own_px, 160), :] = s.dm[task, :, pl.ds(fhalf, 256)]

        @pl.when(special)
        def _():
            s.exg[0, pl.ds(own_px, 160), :] = s.eu[r, :, pl.ds(fhalf, 256)]

        @pl.when(jnp.logical_not(special))
        def _():
            s.exg[0] = jnp.zeros(s.exg.shape[1:], BF16)

        relayed.append([task_relay(p, s.wq) for p in mess[1]])
        wait([d_got])
        spread(s.dmg, d3, 4, 256)
        conv_weight(f3, d3, s.gm, 4, 0, 9)
        staged_m.wait()
        gm_z = []
        for a in range(3):
            if a == 2:
                relayed.append([task_relay(p, s.wq) for p in mess[2]])
                for part in range(3):
                    gm_z.append(grad_push(0, s.gm, s.rm, 3 * part, 3 * part + 3))
            for p in relayed[a]:
                task_ready(p)

            def mess_step(i, carry, a=a):
                rows = pl.ds(pl.multiple_of(i * 320, 16), 320)
                base = pl.multiple_of((5 * i + a) * 80, 16)
                v = dot(f3[pl.ds(base, 320), :], s.wq[3 * a : 3 * a + 3].reshape(1536, 256))
                if a:
                    v = dfull[rows, 0:256] + v
                if a < 2:
                    dfull[rows, 0:256] = v
                else:
                    s.msgb[rows, :] = v.astype(BF16)
                return carry

            lax.fori_loop(0, 4, mess_step, 0)

        m_own = ln.group(seven)
        for o in offsets:
            rr, yy, cc = peer(*o)
            m_own.push(s.msgb.at[pl.ds(px_of(rr, yy, cc), 160)], s.mrecv.at[task, :, pl.ds(fhalf, 256)], dev(z, yy, cc, rr))
        keep(s.mrecv.at[task], s.msgb)()

        def back_step(i, carry):
            px = pl.multiple_of(i * 320, 16)
            dfull[pl.ds(px, 320), :] = conv_back(d3, s.wq, i)
            return carry

        lax.fori_loop(0, 4, back_step, 0)

        for o in offsets:
            wait([f_own[o]], (r != y) if (o[0] + o[1]) % 2 else special)
        wait([m_own])

        def stream_step(base):
            rows = pl.ds(base, 32)
            m = lanes(s.maskp[pl.ds(own_px + base, 32), :], 512)
            m0, m1, m2, m3 = (s.mrecv[t, rows, :].astype(F32) for t in range(4))
            f0, f3_ = s.fg[0, 0, rows, :].astype(F32), s.fg[1, 0, rows, :].astype(F32)
            mid = m1 + m2
            sd, sc = mid + m3, m0 + mid
            gd, gc = s.fg[0, 1, rows, :].astype(F32), s.fg[1, 1, rows, :].astype(F32)
            s.ods[rows, :] = ((f0 + gd * sd) * m).astype(BF16)
            merged = (f3_ + gc * sc).astype(BF16)
            s.mrg[rows, :] = merged
            s.olg[rows, :] = (dot(merged, s.wc[...].reshape(512, 128)) * m[:, :128]).astype(BF16)
            dd, dmer = s.eu[0, rows, :].astype(F32), s.eu[1, rows, :].astype(F32)
            s.fg[0, 1, rows, :] = (dd * sd * gd * (1.0 - gd)).astype(BF16)
            s.fg[1, 1, rows, :] = (dmer * sc * gc * (1.0 - gc)).astype(BF16)

        rows_loop(160, 32, stream_step)
        e_got = {}
        for o in offsets:
            rr, yy, cc = peer(*o)
            ll = pl.ds(pl.multiple_of(256 * cc, 128), 256)
            e_got[o] = ln.push(s.fg.at[rr, 1, :, ll], s.exg.at[1, pl.ds(own_px, 160)], dev(z, yy, cc, rr), rr == yy)

        @pl.when(special)
        def _():
            s.exg[1, pl.ds(own_px, 160), :] = s.fg[r, 1, :, pl.ds(fhalf, 256)]

        for i in range(2):
            s.ctf[...] = jnp.zeros((128, 128), F32)
            s.ctf[0:80, :] = s.olg[80 * i : 80 * i + 80, :].astype(F32)
            turned = s.ctf[...].T
            s.olt[i] = turned[0:40, 0:80].astype(BF16)
        out_near = [ln.near(s.ods, s.o_depth), ln.near(s.olt, s.o_logits)]
        s.gcls[...] = dot_first(s.mrg[...], s.ccotv[...]).astype(BF16).reshape(16, 32, 128)
        wait([u_got[o] for o in offsets], special)
        wait([e_got[o] for o in offsets], special)

        @pl.when(special)
        def _():
            def gate_back(base):
                rows = pl.ds(base, 320)
                dfull[rows, :] = dfull[rows, :] + dot_last(s.exg[1, rows, :], s.wg[...].reshape(512, 256))

            rows_loop(1280, 320, gate_back)

        chalf = pl.ds(pl.multiple_of(256 * (1 - c), 128), 256)

        def give(base):
            rows = pl.ds(base, 80)
            s.dfs[rows, :] = dfull[rows, chalf].astype(BF16)

        rows_loop(1280, 80, give)
        df_c = ln.push(s.dfs, s.dfr, core)

        @pl.when(special)
        def _():
            s.gg[...] = dot_first(s.ffull[...], s.exg[1]).astype(BF16).reshape(s.gg.shape)

        gg_z = [ln.push(s.gg.at[zk(k)], s.rg.at[k - 1], dev(zk(k), y, c, r), special, lambda side, k=k: s.rg.at[k - 1] if side else s.gg.at[0]) for k in (1, 2, 3)]
        cg = ln.group(lambda: s.rcls)
        n_cls = 0
        for q in range(4):
            for j in range(2):
                for i in range(2):
                    if q + j + i == 0:
                        continue
                    yy = 1 - y if j else y
                    cc = 1 - c if i else c
                    zz = zk(q) if q else z
                    cg.push(s.gcls.at[4 * zz + 2 * yy + cc], s.rcls.at[n_cls], dev(zz, yy, cc, r))
                    n_cls += 1
        wait([df_c])

        def dhead_step(base):
            rows = pl.ds(base, 80)
            m = lanes(s.maskp[rows, :], 256)
            d = dfull[rows, pl.ds(fhalf, 256)] + s.dfr[rows, :].astype(F32) + s.exg[0, rows, :].astype(F32)
            s.dmg[rows, :] = (slope_of(preh[rows, :]) * d * m).astype(BF16)

        rows_loop(1280, 80, dhead_step)
        spread(s.dmg, d3, 4, 256)

        def back_step2(i, carry):
            px = pl.multiple_of(i * 320, 16)
            dfull[pl.ds(px, 320), :] = conv_back(d3, s.wh, i)
            return carry

        lax.fori_loop(0, 4, back_step2, 0)
        for yy in range(2):
            src = pl.multiple_of(320 * (2 * yy) + 320 * (1 - c), 16)
            s.drs[pl.ds(320 * yy, 320), :] = dfull[pl.ds(src, 320), :].astype(BF16)
        dr_c = ln.push(s.drs, s.drr, core)
        wait([dr_c])
        for yy in range(2):
            src = pl.multiple_of(320 * (2 * yy) + 320 * c, 16)
            rows = pl.ds(320 * yy, 320)
            s.drr[rows, :] = (dfull[pl.ds(src, 320), :] + s.drr[rows, :].astype(F32)).astype(BF16)
        ro = []
        for dr, dy in ((1, 0), (0, 1), (1, 1)):
            rr, yy, _ = peer(dr, dy, 0)
            src = s.drr.at[pl.ds(pl.multiple_of(320 * yy + 160 * rr, 16), 160)]
            ro.append(ln.push(src, s.dro.at[len(ro)], dev(z, yy, c, rr)))
        gh_z = []
        conv_weight(r3, d3, s.gh, 4, 0, 2)
        grad_hop(gm_z[0])
        gh_z.append(grad_push(1, s.gh, s.rh, 0, 2))
        conv_weight(r3, d3, s.gh, 4, 2, 9)
        grad_hop(gm_z[1])
        wait(ro)
        keep_rows = pl.ds(pl.multiple_of(320 * y + 160 * r, 16), 160)
        total_red = s.drr[keep_rows, :].astype(F32)
        for i in range(3):
            total_red = total_red + s.dro[i].astype(F32)
        s.dred[pl.ds(my_rows, 160), :] = total_red.astype(BF16)
        for cp in out_near:
            cp.wait()
        ln.drain(scoped=True)
        return cg, gm_z, gg_z, gh_z

    state = {}

    def scope_tasks(*scr):
        state["t"] = tasks(*scr)

    pl.run_scoped(
        scope_tasks,
        pltpu.VMEM((1680, 1536), BF16),
        pltpu.VMEM((1680, 1536), BF16),
        pltpu.VMEM((1680, 768), BF16),
        pltpu.VMEM((1280, 256), F32),
        pltpu.VMEM((1280, 512), F32),
    )
    cg, gm_z, gg_z, gh_z = state["t"]

    dr_x = ln.push(s.dred.at[pl.ds(my_rows, 160)], s.dred.at[pl.ds(my_rows, 160)], xpeer)

    def block_back(*late):
        for name, ref in zip(LATE, late):
            setattr(s, name, ref)
        gr, gl, gq, gf = s.gr, s.gl, s.gq, s.gf

        def to_core(g, rc, lead):
            at = g.at[:, :, :, 1 - c] if lead else g.at[:, :, 1 - c]
            return ln.push(at, rc, core)

        def add_core(g, rc, lead):
            if lead:
                for t in range(9):
                    rc[t] = (rc[t].astype(F32) + g[t, :, :, c].astype(F32)).astype(BF16)
            else:
                for t in range(rc.shape[0]):
                    rc[t] = (rc[t].astype(F32) + g[t, :, c].astype(F32)).astype(BF16)

        def to_y(rc, ry, lead):
            return ln.push(rc.at[:, :, 1 - y] if lead else rc.at[:, 1 - y], ry, ypeer)

        def add_y(rc, ry, lead):
            for t in range(ry.shape[0]):
                mine_y = rc[t, :, y] if lead else rc[t, y]
                ry[t] = (ry[t].astype(F32) + mine_y.astype(F32)).astype(BF16)

        def to_z(ry, rz, lead):
            return [
                ln.push(ry.at[:, zk(k)] if lead else ry.at[zk(k)], rz.at[k - 1], dev(zk(k), y, c, r)) for k in (1, 2, 3)
            ]

        def add_z(ry, rz, fin, lead):
            mine_z = (ry[:, z] if lead else ry[z]).astype(F32)
            fin[...] = ((mine_z + rz[0].astype(F32)) + (rz[1].astype(F32) + rz[2].astype(F32))).astype(BF16)

        def task_out(states, rm, g, ps, out):
            for part in states:
                grad_wait(part)
            loads = [[ln.near(rm.at[q, 3 * part : 3 * part + 3], s.zst.at[part % 2, q]) for q in range(3)] for part in range(2)]
            for part in range(3):
                for cp in loads[part]:
                    cp.wait()
                v0 = s.zst.at[part % 2]
                for t in range(3):
                    first_in = jnp.where(z == 0, 0.0, v0[0, t].astype(F32))
                    third_in = jnp.where(z == 3, 0.0, v0[2, t].astype(F32))
                    v = g[3 * part + t, z].astype(F32) + first_in + (v0[1, t].astype(F32) + third_in)
                    ps[3 * part + t] = v.astype(BF16)
                if part == 0:
                    loads.append([ln.near(rm.at[q, 6:9], s.zst.at[0, q]) for q in range(3)])
            lanes_out = pl.ds(fhalf, 256)
            sent = []
            for i in (1, 2, 3):
                yy = 1 - y if i & 2 else y
                cc = 1 - c if i & 1 else c
                sent.append(ln.push(ps.at[:, yy, cc], out.at[y, :, :, lanes_out], dev(z, yy, cc, r)))
            return sent, ln.near(ps.at[:, y, c], out.at[y, :, :, lanes_out])

        wait([dr_x])

        def d3_step(i, carry):
            su, sux = carry
            rows = pl.ds(pl.multiple_of(i * 32, 16), 32)
            x, v = summed_at(i * 32, 32)
            u = slope_of(v) * s.u3[rows, :] * mask_at(i * 32, 32, 1024)
            s.u3[rows, :] = u
            s.dsum[rows, :] = u.astype(BF16)
            return su + jnp.sum(u, axis=0, keepdims=True), sux + jnp.sum(u * x, axis=0, keepdims=True)

        s.u3[...] = dot_last(s.dred[...], s.wr[...].reshape(1024, 512))
        nil = jnp.zeros((1, 1024), F32)
        su, sux = lax.fori_loop(0, 10, d3_step, (nil, nil))
        put_stats(3, su, sux, 1024, None)
        ar3 = plane_start(3)
        ds_x = ln.push(s.dsum.at[pl.ds(other_rows, 160)], s.dsr, xpeer)
        gr[...] = dot_first(s.blk[...], s.dred[...]).astype(BF16).reshape(gr.shape)
        gr_c = ln.push(gr, s.rcr, core, jnp.logical_not(odd))
        plane_end(3, ar3)
        grad_hop(gm_z[2])
        t = reduce_line(3)
        gh_z.append(grad_push(1, s.gh, s.rh, 2, 5))
        gs3 = ln.push(s.at3, s.o_gs3.at[r], xpeer)
        gs3n = ln.near(s.at3, s.o_gs3.at[r])
        mu = jnp.concatenate([t[0:1], t[1:2]], axis=1) / count
        mux = jnp.concatenate([t[2:3], t[3:4]], axis=1) / count

        def dp3_step(base):
            rows = pl.ds(base, 32)
            x = (s.pre3[rows, :] - s.bnp3[0:1]) * s.bnp3[1:2]
            d = mask_at(base, 32, 1024) * (s.bnp3[2:3] * s.bnp3[1:2]) * (s.u3[rows, :] - mu - x * mux)
            s.dp3[rows, :] = d.astype(BF16)

        rows_loop(320, 32, dp3_step)

        def partial_out(pas, value_of):
            pas[...] = value_of(ohalf).astype(BF16)

        wlast = s.wl
        s.u3[:, 0:512] = dot_last(s.dp3[...], wlast[...].reshape(512, 1024))
        s.pas2[...] = s.u3[:, pl.ds(ohalf, 256)].astype(BF16)
        pa2 = ln.push(s.pas2, s.par2, xpeer)
        gl[...] = dot_first(s.a2[...], s.dp3[...]).astype(BF16).reshape(gl.shape)
        gl_c = to_core(gl, s.rcl, False)
        wait([gr_c], odd)

        @pl.when(odd)
        def _():
            for q in range(4):
                s.rcr[q] = (s.rcr[q].astype(F32) + gr[q].astype(F32)).astype(BF16)

        later = {}

        def after_plane_two():
            later["gr_y"] = ln.push(s.rcr.at[:, 1 - y], s.ryr, ypeer, odd)
            wait([gl_c])
            add_core(gl, s.rcl, False)
            later["gl_y"] = to_y(s.rcl, s.ryl, False)

        def after_plane_one():
            wait([gq_c])
            add_core(gq, s.rcm, True)
            later["gq_y"] = to_y(s.rcm, s.rym, True)

        wait([pa2])

        def norm_back(n, par, prebuf, bnp, dst, out_gs, middle, after):
            def u_step(i, carry):
                su_, sux_ = carry
                base = pl.multiple_of(i * 80, 16)
                rows = pl.ds(base, 80)
                x = (prebuf[rows, :] - bnp[0:1]) * bnp[1:2]
                v = x * bnp[2:3] + bnp[3:4]
                d = s.u3[rows, pl.ds(half, 256)] + par[rows, :].astype(F32)
                u = slope_of(v) * d * mask_at(base, 80, 256)
                s.u3[rows, 512:768] = u
                return su_ + jnp.sum(u, axis=0, keepdims=True), sux_ + jnp.sum(u * x, axis=0, keepdims=True)

            nil_ = jnp.zeros((1, 256), F32)
            su_, sux_ = lax.fori_loop(0, 4, u_step, (nil_, nil_))
            put_stats(n, su_, sux_, 256, None)
            reduce_plane(n)
            middle()
            t_ = reduce_line(n)
            after()
            gsx = ln.push(getattr(s, "at%d" % n), out_gs.at[r], xpeer)
            gsn = ln.near(getattr(s, "at%d" % n), out_gs.at[r])
            mu_, mux_ = t_[0:1] / count, t_[1:2] / count

            def d_step(base):
                rows = pl.ds(base, 80)
                x = (prebuf[rows, :] - bnp[0:1]) * bnp[1:2]
                d = mask_at(base, 80, 256) * (bnp[2:3] * bnp[1:2]) * (s.u3[rows, 512:768] - mu_ - x * mux_)
                dst[rows, :] = d.astype(BF16)

            rows_loop(320, 80, d_step)
            return gsx, gsn

        def window_two():
            grad_hop(gh_z[0])
            gh_z.append(grad_push(1, s.gh, s.rh, 5, 8))
            grad_hop(gh_z[1])

        def window_one():
            gh_z.append(grad_push(1, s.gh, s.rh, 8, 9))
            grad_hop(gh_z[2])

        gs2, gs2n = norm_back(4, s.par2, s.pre2, s.bnp2, s.dp2, s.o_gs2, after_plane_two, window_two)
        spread(s.dp2, s.d3m, 1, 256)
        s.u3[:, 0:512] = conv_back(s.d3m, s.wm, 0)
        s.pas1[...] = s.u3[:, pl.ds(ohalf, 256)].astype(BF16)
        pa1 = ln.push(s.pas1, s.par1, xpeer)
        conv_weight(s.a3, s.d3m, gq, 1, 0, 9)
        gq_c = to_core(gq, s.rcm, True)
        wait([pa1])
        gs1, gs1n = norm_back(5, s.par1, s.pre1, s.bnp1, s.dp1, s.o_gs1, after_plane_one, window_one)
        dp_x = ln.push(s.dp1.at[pl.ds(other_rows, 160)], s.dp1r, xpeer)
        gf[...] = dot_first(s.xall[...], s.dp1[...]).astype(BF16).reshape(gf.shape)
        gf_c = to_core(gf, s.rcf, False)
        wait([gf_c])
        add_core(gf, s.rcf, False)
        gf_y = to_y(s.rcf, s.ryf, False)
        gr_y, gl_y, gq_y = later["gr_y"], later["gl_y"], later["gq_y"]
        ms, mn = task_out(gm_z, s.rm, s.gm, s.psm, s.o_mess)

        wait([gr_y], odd)

        @pl.when(odd)
        def _():
            for q in range(4):
                s.ryr[q] = (s.ryr[q].astype(F32) + s.rcr[q, y].astype(F32)).astype(BF16)

        grad_hop(gh_z[3])
        gr_z = [ln.push(s.ryr.at[zk(q)], s.rzr.at[q - 1], dev(zk(q), y, c, r), odd) for q in (1, 2, 3)]
        wait([gl_y])
        add_y(s.rcl, s.ryl, False)
        gl_z = to_z(s.ryl, s.rzl, False)
        wait([gq_y])
        add_y(s.rcm, s.rym, True)
        gq_z = to_z(s.rym, s.rzm, True)
        wait([gf_y])
        add_y(s.rcf, s.ryf, False)
        gf_z = to_z(s.ryf, s.rzf, False)

        wait([wfo_x])
        wfo_n = ln.near(s.wfo, s.wfov)
        wait([dp_x, ds_x])
        wfo_n.wait()
        mine_d = s.dp1[pl.ds(my_rows, 160), :]
        other_d = s.dp1r[...]
        for q in range(2):
            cols = slice(1024 * q, 1024 * q + 1024)
            wa = s.wf[2 * q : 2 * q + 2].reshape(1024, 256)
            wb = s.wfov[2 * q : 2 * q + 2].reshape(1024, 256)
            s.u3[pl.ds(0, 160), :] = dot_last(mine_d, wa) + dot_last(other_d, wb)

            def img_step(base):
                rows = pl.ds(base, 32)
                m = mask_at(my_rows + base, 32, 1024)
                own_d = s.dsum[pl.ds(my_rows + base, 32), 512 * q : 512 * q + 512].astype(F32)
                far_d = s.dsr[rows, 512 * q : 512 * q + 512].astype(F32)
                d = jnp.concatenate(
                    [
                        jnp.where(r == j % 2, own_d[:, 64 * (j - j % 2) :][:, :128], far_d[:, 64 * (j - j % 2) :][:, :128])
                        for j in range(8)
                    ],
                    axis=1,
                )
                s.oimg[rows, cols] = ((s.u3[rows, :] + d) * m).astype(BF16)

            rows_loop(160, 32, img_step)
        img_n = ln.near(s.oimg, s.o_img)

        hs, hn = task_out(gh_z, s.rh, s.gh, s.psh, s.o_heads)

        @pl.when(special)
        def _():
            for cp in gg_z:
                cp.wait_recv()
            v = (s.gg[z].astype(F32) + s.rg[0].astype(F32)) + (s.rg[1].astype(F32) + s.rg[2].astype(F32))
            s.pg[...] = v.astype(BF16)

        gx = {}
        for o in offsets:
            rr, yy, cc = peer(*o)
            gx[o] = ln.push(s.pg.at[yy, cc], s.o_gates.at[r, :, pl.ds(fhalf, 256)], dev(z, yy, cc, rr), special)
        gate_near = pltpu.make_async_copy(
            s.pg.at[y, c], s.o_gates.at[r, :, pl.ds(fhalf, 256)], s.near_sems.at[NEAR - 2]
        )
        pl.when(special)(gate_near.start)

        wait([cg])
        v = s.gcls[b].astype(F32)
        for i in range(15):
            v = v + s.rcls[i].astype(F32)
        s.clss[...] = v
        cls_x = ln.push(s.clss, s.clsr, xpeer)

        wait(gr_z, odd)

        @pl.when(odd)
        def _():
            v_ = s.ryr[z].astype(F32) + s.rzr[0].astype(F32)
            s.fnr[...] = (v_ + (s.rzr[1].astype(F32) + s.rzr[2].astype(F32))).astype(BF16)

        gr_x = ln.push(s.fnr, s.o_red, xpeer, odd)
        red_near = pltpu.make_async_copy(s.fnr, s.o_red, s.near_sems.at[NEAR - 3])
        pl.when(odd)(red_near.start)
        wait(gl_z)
        add_z(s.ryl, s.rzl, s.fnl, False)
        gl_x = ln.push(s.fnl, s.o_last.at[r], xpeer)
        n1 = ln.near(s.fnl, s.o_last.at[r])
        wait(gq_z)
        add_z(s.rym, s.rzm, s.fnm, True)
        gq_x = ln.push(s.fnm, s.o_mid.at[:, :, pl.ds(half, 256)], xpeer)
        n2 = ln.near(s.fnm, s.o_mid.at[:, :, pl.ds(half, 256)])
        wait(gf_z)
        add_z(s.ryf, s.rzf, s.fnf, False)
        gf_x = ln.push(s.fnf, s.o_first.at[:, pl.ds(half, 256)], xpeer)
        n3 = ln.near(s.fnf, s.o_first.at[:, pl.ds(half, 256)])
        wait([cls_x])
        s.clso[...] = s.clss[...] + s.clsr[...]
        n4 = ln.near(s.clso, s.o_cls)
        wait([gr_x], jnp.logical_not(odd))
        wait([gl_x, gq_x, gf_x, gs1, gs2, gs3])
        wait(ms + hs)
        for o in offsets:
            wait([gx[o]], (r != y) if (o[0] + o[1]) % 2 else special)
        pl.when(special)(gate_near.wait)
        pl.when(odd)(red_near.wait)
        for cp in (gs1n, gs2n, gs3n, img_n, mn, hn, n1, n2, n3, n4):
            cp.wait()
        ln.drain()

    pl.run_scoped(block_back, *[pltpu.VMEM(*v) for v in LATE.values()])


LATE = dict(
    zst=((2, 3, 3, 2, 2, 32, 256), BF16),
    psm=((9, 2, 2, 32, 256), BF16),
    psh=((9, 2, 2, 32, 256), BF16),
    fnr=((128, 512), BF16),
    fnl=((32, 1024), BF16),
    fnm=((9, 32, 256), BF16),
    fnf=((128, 256), BF16),
    pg=((2, 2, 32, 256), BF16),
    clss=((32, 128), F32),
    clso=((32, 128), F32),
    u3=((320, 1024), F32),
    dp3=((320, 1024), BF16),
    d3m=((480, 768), BF16),
    dsum=((320, 1024), BF16),
    oimg=((160, 2048), BF16),
    pas1=((320, 256), BF16),
    pas2=((320, 256), BF16),
    dp1=((320, 256), BF16),
    dp2=((320, 256), BF16),
    wfov=((4, 2, 2, 128, 256), BF16),
    gr=((4, 2, 128, 512), BF16),
    gl=((4, 2, 2, 32, 1024), BF16),
    gq=((9, 4, 2, 2, 32, 256), BF16),
    gf=((4, 2, 2, 128, 256), BF16),
)


FINAL = dict(
    depth=((160, 512), BF16),
    logits=((2, 40, 80), BF16),
    img=((160, 2048), F32),
    first=((128, 512), F32),
    gain1=((1, 32), F32),
    shift1=((1, 32), F32),
    mid=((9, 32, 512), F32),
    gain2=((1, 32), F32),
    shift2=((1, 32), F32),
    last=((32, 2048), F32),
    gain3=((1, 128), F32),
    shift3=((1, 128), F32),
    red=((128, 512), F32),
    heads=((2, 9, 32, 512), F32),
    mess=((2, 9, 32, 512), F32),
    gates=((2, 32, 512), F32),
    cls=((32, 40), F32),
)


def widen_out(names, *refs):
    s = SimpleNamespace(**dict(zip(names, refs)))
    b = lax.axis_index("batch")
    used = [0]

    def move(src, dst):
        cp = pltpu.make_async_copy(src, dst, s.sems.at[used[0]])
        used[0] += 1
        cp.start()
        return cp

    done = [move(s.o_depth, s.depth), move(s.o_logits, s.logits)]
    wide = ["mess", "heads", "mid", "img", "last", "red", "first", "gates"]
    loads = {n: move(getattr(s, "o_" + n), getattr(s, "i_" + n)) for n in wide}
    small = [move(getattr(s, "o_" + n), getattr(s, "i_" + n)) for n in ("gs1", "gs2", "gs3", "cls")]
    for n in wide:
        loads[n].wait()
        src, dst = getattr(s, "i_" + n), getattr(s, "v_" + n)
        if n == "last":
            for i in range(8):
                for h in range(2):
                    lane = 128 * (2 * i + h)
                    dst[:, lane : lane + 128] = src[h, :, 128 * i : 128 * i + 128].astype(F32)
        elif n == "img":
            for i in range(0, 160, 32):
                dst[i : i + 32, :] = src[i : i + 32, :].astype(F32)
        elif len(src.shape) > 2:
            for i in range(src.shape[0]):
                dst[i] = src[i].astype(F32)
        else:
            dst[...] = src[...].astype(F32)
        done.append(move(dst, getattr(s, n)))
    for cp in small:
        cp.wait()
    quarter, spot = lax.div(b, np.int32(4)), lax.rem(b, np.int32(4))
    at = pl.ds(pl.multiple_of(128 * lax.rem(quarter, np.int32(2)), 128), 128)
    for n, layer in ((1, s.i_gs1), (2, s.i_gs2)):
        v = pltpu.roll(layer[lax.div(quarter, np.int32(2)), :, at], lax.rem(128 - 32 * spot, np.int32(128)), 1)
        for row, kind in ((1, "gain"), (0, "shift")):
            keep = getattr(s, "v_%s%d" % (kind, n))
            keep[...] = v[row : row + 1, 0:32]
            done.append(move(keep, getattr(s, "%s%d" % (kind, n))))
    block = lax.div(b, np.int32(2))
    at = pl.ds(pl.multiple_of(128 * lax.rem(block, np.int32(4)), 128), 128)
    v = s.i_gs3[lax.rem(b, np.int32(2)), :, at]
    low = lax.div(block, np.int32(4)) == 0
    s.v_shift3[...] = jnp.where(low, v[0:1], v[1:2])
    s.v_gain3[...] = jnp.where(low, v[2:3], v[3:4])
    done.append(move(s.v_shift3, s.shift3))
    done.append(move(s.v_gain3, s.gain3))
    s.v_cls[...] = s.i_cls[:, 0:40]
    done.append(move(s.v_cls, s.cls))
    for cp in done:
        cp.wait()


def fast(args):
    (
        images, crop_height, crop_width, w_first, gain_first, shift_first, w_middle, gain_middle, shift_middle,
        w_last, gain_last, shift_last, w_reduce, w_heads, w_message, w_gates, w_classes, depth_cot, class_cot,
    ) = args
    narrow = jnp.concatenate([gain_first, shift_first, gain_middle, shift_middle])
    gains = jnp.stack([narrow, gain_last, shift_last]).astype(F32)
    ins = (
        crop_height, crop_width, images.reshape(160, 2048), w_first, w_middle, w_last, w_reduce, w_gates, w_classes,
        w_heads, w_message, gains, depth_cot.reshape(160, 512), class_cot.transpose(0, 1, 3, 2).reshape(2, 40, 80),
    )
    names = list(INS) + list(OUTS) + list(SHAPES) + ["send_sems", "recv_sems", "near_sems"]
    smem, hbm, vmem = (pl.BlockSpec(memory_space=m) for m in (pltpu.SMEM, pltpu.HBM, pltpu.VMEM))
    spec = {"crop_h": smem, "crop_w": smem, "gains": vmem}
    outs = pl.pallas_call(
        functools.partial(body, names),
        out_shape=[jax.ShapeDtypeStruct(*v) for v in OUTS.values()],
        in_specs=[spec.get(n, hbm) for n in INS],
        out_specs=[hbm] * len(OUTS),
        scratch_shapes=[pltpu.VMEM(*v) for v in SHAPES.values()]
        + [pltpu.SemaphoreType.DMA((n,)) for n in (SENDS, SENDS, NEAR)],
        compiler_params=pltpu.CompilerParams(has_side_effects=True, collective_id=0, vmem_limit_bytes=64 * 2**20),
        name="residual_distill",
    )(*ins)
    o = dict(zip(OUTS, outs))
    taken = [n for n in OUTS if n.startswith("o_")]
    staged = {"i_" + n[2:]: OUTS[n] for n in taken if n not in ("o_depth", "o_logits")}
    staged.update({"v_" + n: v for n, v in FINAL.items() if n not in ("depth", "logits")})
    final = pl.pallas_call(
        functools.partial(widen_out, taken + list(FINAL) + list(staged) + ["sems"]),
        out_shape=[jax.ShapeDtypeStruct(*v) for v in FINAL.values()],
        in_specs=[hbm] * len(taken),
        out_specs=[hbm] * len(FINAL),
        scratch_shapes=[pltpu.VMEM(*v) for v in staged.values()] + [pltpu.SemaphoreType.DMA((40,))],
        compiler_params=pltpu.CompilerParams(vmem_limit_bytes=64 * 2**20),
        name="widen_out",
    )(*[o[n] for n in taken])
    f = dict(zip(FINAL, final))
    f["depth"] = f["depth"].reshape(1, 2, 80, 512)
    f["logits"] = f["logits"].reshape(1, 2, 40, 80).transpose(0, 1, 3, 2)
    f["img"] = f["img"].reshape(1, 2, 80, 2048)
    for n in ("gain1", "shift1", "gain2", "shift2", "gain3", "shift3"):
        f[n] = f[n].reshape(-1)
    return tuple(f.values())


def solution(mesh):
    def step(*args):
        if mesh.shape["batch"] == 16 and mesh.shape["rows"] == 2:
            return fast(args)
        return shards(*args)

    placed = (
        P("batch", "rows", None, None),
        P(),
        P(),
        P("batch", None),
        P("batch"),
        P("batch"),
        P(None, "batch", None),
        P("batch"),
        P("batch"),
        P("batch", None),
        P("batch"),
        P("batch"),
        P("batch", None),
        P("rows", None, "batch", None),
        P("rows", None, "batch", None),
        P(None, "batch", None),
        P("batch", None),
        P("batch", "rows", None, None),
        P("batch", "rows", None, None),
    )
    return jax.shard_map(
        step,
        mesh=mesh,
        in_specs=placed,
        out_specs=(
            P("batch", "rows", None, None),
            P("batch", "rows", None, None),
            P("batch", "rows", None, None),
            P("batch", None),
            P("batch"),
            P("batch"),
            P(None, "batch", None),
            P("batch"),
            P("batch"),
            P("batch", None),
            P("batch"),
            P("batch"),
            P("batch", None),
            P("rows", None, "batch", None),
            P("rows", None, "batch", None),
            P(None, "batch", None),
            P("batch", None),
        ),
        check_vma=False,
    )
```

```python
import functools
from types import SimpleNamespace

import numpy as np
import jax
import jax.numpy as jnp
from jax import lax
from jax.sharding import PartitionSpec as P
from jax.experimental import pallas as pl
from jax.experimental.pallas import tpu as pltpu

EPS = 1e-05
MESH = pl.DeviceIdType.MESH
F32 = jnp.float32
BF16 = jnp.bfloat16
ROOT = 0.7978845608028654
CUBE = 0.044715
SENDS = 118
RECVS = 183
NEAR = 21


def dot(left, right):
    return jnp.dot(left, right, preferred_element_type=F32)


def dot_last(left, right):
    return lax.dot_general(left, right, (((1,), (1,)), ((), ())), preferred_element_type=F32)


def dot_first(left, right):
    return lax.dot_general(left, right, (((0,), (0,)), ((), ())), preferred_element_type=F32)


def gelu_of(v):
    return 0.5 * v * (1.0 + jnp.tanh(ROOT * (v + CUBE * v * v * v)))


def slope_of(v):
    t = jnp.tanh(ROOT * (v + CUBE * v * v * v))
    return 0.5 * (1.0 + t) + 0.5 * v * (1.0 - t * t) * (ROOT * (1.0 + 3.0 * CUBE * v * v))


def rows_loop(total, chunk, step):
    def body(index, carry):
        step(pl.multiple_of(index * chunk, chunk))
        return carry

    lax.fori_loop(0, total // chunk, body, 0)


class Copy:
    def __init__(self, remote, links, send, recv, like):
        self.remote, self.links, self.send, self.recv, self.like = remote, links, send, recv, like
        self.scoped = like is None

    def wait_recv(self):
        if self.like is None:
            self.remote.wait_recv()
        else:
            ref = self.like(1)
            pltpu.make_async_copy(ref, ref, self.links.recv.at[self.recv]).wait()

    def wait_send(self):
        if self.like is None:
            self.remote.wait_send()
        else:
            ref = self.like(0)
            pltpu.make_async_copy(ref, ref, self.links.send.at[self.send]).wait()


class Group:
    scoped = True

    def __init__(self, links, send, recv, like):
        self.links, self.send, self.recv, self.like = links, send, recv, like

    def push(self, src, dst, device, when=None):
        self.links.start(src, dst, device, self.send, self.recv, when)

    def wait_recv(self):
        ref = self.like()
        pltpu.make_async_copy(ref, ref, self.links.recv.at[self.recv]).wait()

    def wait_send(self):
        ref = self.like()
        pltpu.make_async_copy(ref, ref, self.links.send.at[self.send]).wait()


class Near:
    def __init__(self, links, src, dst):
        self.links, self.index = links, links.local_free.pop(0)
        self.copy = pltpu.make_async_copy(src, dst, links.local.at[self.index])
        self.copy.start()

    def wait(self):
        self.copy.wait()
        self.links.local_free.insert(0, self.index)


class Links:
    def __init__(self, send, recv, local):
        self.send, self.recv, self.local = send, recv, local
        self.used = 0
        self.send_free = list(range(SENDS))
        self.local_free = list(range(NEAR - 4))
        self.open = []

    def start(self, src, dst, device, send, recv, when):
        remote = pltpu.make_async_remote_copy(
            src_ref=src,
            dst_ref=dst,
            send_sem=self.send.at[send],
            recv_sem=self.recv.at[recv],
            device_id=device,
            device_id_type=MESH,
        )
        if when is None:
            remote.start()
        else:
            pl.when(when)(remote.start)
        return remote

    def pair(self):
        self.used += 1
        return self.send_free.pop(0), self.used - 1

    def push(self, src, dst, device, when=None, like=None):
        send, recv = self.pair()
        cp = Copy(self.start(src, dst, device, send, recv, when), self, send, recv, like)
        self.open.append((cp, when))
        return cp

    def group(self, like, when=None):
        cp = Group(self, *self.pair(), like)
        self.open.append((cp, when))
        return cp

    def near(self, src, dst):
        return Near(self, src, dst)

    def drain(self, scoped=False):
        kept = []
        for cp, when in self.open:
            if scoped and not cp.scoped:
                kept.append((cp, when))
                continue
            if when is None:
                cp.wait_send()
            else:
                pl.when(when)(cp.wait_send)
            self.send_free.insert(0, cp.send)
        self.open = kept


def wait(copies, when=None):
    def run():
        for cp in copies:
            cp.wait_recv()

    if when is None:
        run()
    else:
        pl.when(when)(run)


def lanes(mask, width):
    return jnp.concatenate([mask] * (width // 128), axis=1) if width > 128 else mask


def padded_2(cells, sides, width):
    for axis, dim in sides:
        count = lax.axis_size(axis)
        ends = count - 1
        head = lax.slice_in_dim(cells, 0, width, axis=dim)
        tail = lax.slice_in_dim(cells, cells.shape[dim] - width, cells.shape[dim], axis=dim)
        cells = jnp.concatenate(
            [
                lax.ppermute(tail, axis, [(i, (i + 1) % count) for i in range(ends)]),
                cells,
                lax.ppermute(head, axis, [((i + 1) % count, i) for i in range(ends)]),
            ],
            axis=dim,
        )
    return cells


def gelu_tanh(values):
    return jax.nn.gelu(values, approximate=True)


def gelu_slope(values, upstream):
    return jax.vjp(gelu_tanh, values)[1](upstream)[0]


def project(values, weight):
    return jnp.einsum("nrcj,jk->nrck", values, weight, preferred_element_type=jnp.float32)


def project_back(upstream, weight):
    return jnp.einsum("nrck,jk->nrcj", upstream, weight, preferred_element_type=jnp.float32)


def outer_sum(values, upstream):
    return jnp.einsum("nrcj,nrck->jk", values, upstream, preferred_element_type=jnp.float32)


def widen(padded):
    return jnp.pad(padded, ((0, 0), (0, 0), (1, 1), (0, 0)))


def halo_value(values):
    return padded_2(values, (("rows", 1),), 1)


def halo_grad(values):
    return padded_2(values, (("rows", 1),), 1)


def conv_apply(padded, kernel):
    row_count = padded.shape[1] - 2
    col_count = padded.shape[2]
    widened = widen(padded)
    running = jnp.zeros((padded.shape[0], row_count, col_count, kernel.shape[2]), jnp.float32)
    for tap_index in range(9):
        shift_down = tap_index // 3
        shift_right = tap_index % 3
        running = running + project(
            widened[
                :, shift_down : shift_down + row_count, shift_right : shift_right + col_count, :
            ],
            kernel[tap_index],
        )
    return running


def conv_kernel_grad(padded, upstream):
    row_count = upstream.shape[1]
    col_count = upstream.shape[2]
    widened = widen(padded)
    return jnp.stack(
        [
            outer_sum(
                widened[
                    :,
                    tap_index // 3 : tap_index // 3 + row_count,
                    tap_index % 3 : tap_index % 3 + col_count,
                    :,
                ],
                upstream,
            )
            for tap_index in range(9)
        ]
    )


def conv_input_grad(padded_grad, kernel):
    row_count = padded_grad.shape[1] - 2
    col_count = padded_grad.shape[2]
    widened = widen(padded_grad)
    running = jnp.zeros((padded_grad.shape[0], row_count, col_count, kernel.shape[1]), jnp.float32)
    for tap_index in range(9):
        shift_down = tap_index // 3
        shift_right = tap_index % 3
        running = running + project_back(
            widened[
                :,
                2 - shift_down : 2 - shift_down + row_count,
                2 - shift_right : 2 - shift_right + col_count,
                :,
            ],
            kernel[tap_index],
        )
    return running


def crop_mask(height, width, first_row, row_count, col_count):
    row_ids = first_row + jnp.arange(row_count, dtype=jnp.int32)
    col_ids = jnp.arange(col_count, dtype=jnp.int32)
    inside = (row_ids[None, :, None] < height[:, None, None]) & (
        col_ids[None, None, :] < width[:, None, None]
    )
    return inside.astype(jnp.float32)[..., None]


def norm_forward(pre_act, pixel_mask, gain_vec, shift_vec, valid_count):
    sums = jnp.sum(pre_act * pixel_mask, axis=(0, 1, 2))
    squares = jnp.sum(pre_act * pre_act * pixel_mask, axis=(0, 1, 2))
    sums, squares = lax.psum((sums, squares), ("batch", "rows"))
    mean_vec = sums / valid_count
    inv_std = lax.rsqrt(squares / valid_count - mean_vec * mean_vec + EPS)
    normal = (pre_act - mean_vec) * inv_std
    return (normal, inv_std, normal * gain_vec + shift_vec)


def norm_backward(upstream, normal, inv_std, gain_vec, pixel_mask, valid_count):
    shift_part = jnp.sum(upstream, axis=(0, 1, 2))
    gain_part = jnp.sum(upstream * normal, axis=(0, 1, 2))
    shift_part, gain_part = lax.psum((shift_part, gain_part), ("batch", "rows"))
    d_pre = (
        pixel_mask
        * gain_vec
        * inv_std
        * (upstream - shift_part / valid_count - normal * gain_part / valid_count)
    )
    return (d_pre, gain_part, shift_part)


def task_forward(padded_in, heads, messages, pixel_mask, pad_rows):
    pre_list = []
    feat_list = []
    padded_feats = []
    message_list = []
    for task in range(heads.shape[0]):
        pre_act = conv_apply(padded_in, heads[task])
        feature = (gelu_tanh(pre_act) * pixel_mask).astype(jnp.bfloat16)
        padded_feat = pad_rows(feature)
        pre_list.append(pre_act)
        feat_list.append(feature)
        padded_feats.append(padded_feat)
        message_list.append(conv_apply(padded_feat, messages[task]).astype(jnp.bfloat16))
    return (pre_list, feat_list, padded_feats, message_list)


def task_backward(
    padded_in,
    heads,
    messages,
    pixel_mask,
    pre_list,
    padded_feats,
    feat_grads,
    message_grads,
    pad_grad,
):
    input_grad = jnp.zeros(
        padded_in.shape[:1] + (padded_in.shape[1] - 2,) + padded_in.shape[2:], jnp.float32
    )
    head_grads = []
    kernel_grads = []
    for task in range(heads.shape[0]):
        low_message = message_grads[task].astype(jnp.bfloat16)
        kernel_grads.append(conv_kernel_grad(padded_feats[task], low_message))
        feat_grad = feat_grads[task] + conv_input_grad(pad_grad(low_message), messages[task])
        low_pre = gelu_slope(pre_list[task], feat_grad * pixel_mask).astype(jnp.bfloat16)
        head_grads.append(conv_kernel_grad(padded_in, low_pre))
        input_grad = input_grad + conv_input_grad(pad_grad(low_pre), heads[task])
    return (input_grad, jnp.stack(head_grads), jnp.stack(kernel_grads))


def streams_forward(features, messages, gates_all, classes_all, pixel_mask):
    gate_depth = jax.nn.sigmoid(project(features[0], gates_all[0]))
    gate_class = jax.nn.sigmoid(project(features[3], gates_all[1]))
    depth_sum = (
        messages[1].astype(jnp.float32)
        + messages[2].astype(jnp.float32)
        + messages[3].astype(jnp.float32)
    )
    class_sum = (
        messages[0].astype(jnp.float32)
        + messages[1].astype(jnp.float32)
        + messages[2].astype(jnp.float32)
    )
    depth_stream = (features[0].astype(jnp.float32) + gate_depth * depth_sum) * pixel_mask
    merged = (features[3].astype(jnp.float32) + gate_class * class_sum).astype(jnp.bfloat16)
    class_logits = project(merged, classes_all) * pixel_mask
    return (depth_stream, class_logits, merged, gate_depth, gate_class, depth_sum, class_sum)


def streams_backward(
    features,
    merged,
    gate_depth,
    gate_class,
    depth_sum,
    class_sum,
    depth_cot,
    class_cot,
    gates_all,
    classes_all,
    pixel_mask,
):
    depth_grad = depth_cot.astype(jnp.float32) * pixel_mask
    logit_grad = (class_cot.astype(jnp.float32) * pixel_mask).astype(jnp.bfloat16)
    grad_classes = outer_sum(merged, logit_grad)
    merged_grad = project_back(logit_grad, classes_all)
    gate_depth_grad = (depth_grad * depth_sum * gate_depth * (1.0 - gate_depth)).astype(
        jnp.bfloat16
    )
    gate_class_grad = (merged_grad * class_sum * gate_class * (1.0 - gate_class)).astype(
        jnp.bfloat16
    )
    grad_gates = jnp.stack(
        [outer_sum(features[0], gate_depth_grad), outer_sum(features[3], gate_class_grad)]
    )
    depth_feat = depth_grad + project_back(gate_depth_grad, gates_all[0])
    class_feat = merged_grad + project_back(gate_class_grad, gates_all[1])
    depth_message = depth_grad * gate_depth
    class_message = merged_grad * gate_class
    nothing = jnp.zeros_like(depth_grad)
    feat_grads = [depth_feat, nothing, nothing, class_feat]
    message_grads = [
        class_message,
        depth_message + class_message,
        depth_message + class_message,
        depth_message,
    ]
    return (feat_grads, message_grads, grad_gates, grad_classes)


def shards(
    images,
    crop_height,
    crop_width,
    w_first,
    gain_first,
    shift_first,
    w_middle,
    gain_middle,
    shift_middle,
    w_last,
    gain_last,
    shift_last,
    w_reduce,
    w_heads,
    w_message,
    w_gates,
    w_classes,
    depth_cot,
    class_cot,
):
    image_index = lax.axis_index("batch")
    batch_count = lax.axis_size("batch")
    row_count = images.shape[1]
    col_count = images.shape[2]
    height = lax.dynamic_slice_in_dim(crop_height, image_index, 1, 0)
    width = lax.dynamic_slice_in_dim(crop_width, image_index, 1, 0)
    pixel_mask = crop_mask(height, width, lax.axis_index("rows") * row_count, row_count, col_count)
    valid_count = jnp.sum(crop_height * crop_width).astype(jnp.float32)
    gathered = (
        lax.all_gather(w_first, "batch", axis=0, tiled=True),
        lax.all_gather(w_middle, "batch", axis=1, tiled=True),
        lax.all_gather(w_last, "batch", axis=0, tiled=True),
        lax.all_gather(w_reduce, "batch", axis=0, tiled=True),
        lax.all_gather(w_gates, "batch", axis=1, tiled=True),
        lax.all_gather(w_classes, "batch", axis=0, tiled=True),
        lax.all_gather(gain_first, "batch", axis=0, tiled=True),
        lax.all_gather(shift_first, "batch", axis=0, tiled=True),
        lax.all_gather(gain_middle, "batch", axis=0, tiled=True),
        lax.all_gather(shift_middle, "batch", axis=0, tiled=True),
        lax.all_gather(gain_last, "batch", axis=0, tiled=True),
        lax.all_gather(shift_last, "batch", axis=0, tiled=True),
        lax.all_gather(w_heads, "batch", axis=2, tiled=True),
        lax.all_gather(w_message, "batch", axis=2, tiled=True),
    )
    first_all = gathered[0]
    middle_all = gathered[1]
    last_all = gathered[2]
    reduce_all = gathered[3]
    gates_all = gathered[4]
    classes_all = gathered[5]
    gain_one = gathered[6].astype(jnp.float32)
    shift_one = gathered[7].astype(jnp.float32)
    gain_two = gathered[8].astype(jnp.float32)
    shift_two = gathered[9].astype(jnp.float32)
    gain_three = gathered[10].astype(jnp.float32)
    shift_three = gathered[11].astype(jnp.float32)
    heads_own = gathered[12]
    message_own = gathered[13]
    masked_in = images.astype(jnp.float32) * pixel_mask
    low_in = masked_in.astype(jnp.bfloat16)
    pre_first = project(low_in, first_all)
    normal_first, std_first, out_first = norm_forward(
        pre_first, pixel_mask, gain_one, shift_one, valid_count
    )
    act_first = (gelu_tanh(out_first) * pixel_mask).astype(jnp.bfloat16)
    padded_first = halo_value(act_first)
    pre_middle = conv_apply(padded_first, middle_all)
    normal_middle, std_middle, out_middle = norm_forward(
        pre_middle, pixel_mask, gain_two, shift_two, valid_count
    )
    act_middle = (gelu_tanh(out_middle) * pixel_mask).astype(jnp.bfloat16)
    pre_last = project(act_middle, last_all)
    normal_last, std_last, out_last = norm_forward(
        pre_last, pixel_mask, gain_three, shift_three, valid_count
    )
    summed = out_last + masked_in
    block_out = (gelu_tanh(summed) * pixel_mask).astype(jnp.bfloat16)
    low_reduced = project(block_out, reduce_all).astype(jnp.bfloat16)
    heads_all, message_all = (
        lax.all_gather(heads_own, "rows", axis=0, tiled=True),
        lax.all_gather(message_own, "rows", axis=0, tiled=True),
    )
    padded_in = halo_value(low_reduced)
    pre_list, feat_list, padded_feats, message_list = task_forward(
        padded_in, heads_all, message_all, pixel_mask, halo_value
    )
    depth_stream, class_logits, merged, gate_depth, gate_class, depth_sum, class_sum = (
        streams_forward(feat_list, message_list, gates_all, classes_all, pixel_mask)
    )
    feat_grads, message_grads, grad_gates, grad_classes = streams_backward(
        feat_list,
        merged,
        gate_depth,
        gate_class,
        depth_sum,
        class_sum,
        depth_cot,
        class_cot,
        gates_all,
        classes_all,
        pixel_mask,
    )
    reduced_grad, grad_heads, grad_message = task_backward(
        padded_in,
        heads_all,
        message_all,
        pixel_mask,
        pre_list,
        padded_feats,
        feat_grads,
        message_grads,
        halo_grad,
    )
    low_reduced_grad = reduced_grad.astype(jnp.bfloat16)
    grad_reduce = outer_sum(block_out, low_reduced_grad)
    block_grad = project_back(low_reduced_grad, reduce_all)
    sum_grad = gelu_slope(summed, block_grad * pixel_mask)
    d_last, gain_grad_three, shift_grad_three = norm_backward(
        sum_grad, normal_last, std_last, gain_three, pixel_mask, valid_count
    )
    low_last = d_last.astype(jnp.bfloat16)
    grad_last = outer_sum(act_middle, low_last)
    middle_grad = project_back(low_last, last_all)
    d_middle, gain_grad_two, shift_grad_two = norm_backward(
        gelu_slope(out_middle, middle_grad * pixel_mask),
        normal_middle,
        std_middle,
        gain_two,
        pixel_mask,
        valid_count,
    )
    low_middle = d_middle.astype(jnp.bfloat16)
    grad_middle = conv_kernel_grad(padded_first, low_middle)
    first_grad = conv_input_grad(halo_grad(low_middle), middle_all)
    d_first, gain_grad_one, shift_grad_one = norm_backward(
        gelu_slope(out_first, first_grad * pixel_mask),
        normal_first,
        std_first,
        gain_one,
        pixel_mask,
        valid_count,
    )
    low_first = d_first.astype(jnp.bfloat16)
    grad_first = outer_sum(low_in, low_first)
    image_grad = (project_back(low_first, first_all) + sum_grad) * pixel_mask
    summed_grads = (
        lax.psum_scatter(grad_first, "batch", scatter_dimension=0, tiled=True),
        lax.psum_scatter(grad_middle, "batch", scatter_dimension=1, tiled=True),
        lax.psum_scatter(grad_last, "batch", scatter_dimension=0, tiled=True),
        lax.psum_scatter(grad_reduce, "batch", scatter_dimension=0, tiled=True),
        lax.psum_scatter(grad_gates, "batch", scatter_dimension=1, tiled=True),
        lax.psum_scatter(grad_classes, "batch", scatter_dimension=0, tiled=True),
        lax.psum_scatter(grad_heads, "batch", scatter_dimension=2, tiled=True),
        lax.psum_scatter(grad_message, "batch", scatter_dimension=2, tiled=True),
    )
    shared = (
        lax.psum(summed_grads[0].astype(jnp.bfloat16), "rows").astype(jnp.float32),
        lax.psum(summed_grads[1].astype(jnp.bfloat16), "rows").astype(jnp.float32),
        lax.psum(summed_grads[2].astype(jnp.bfloat16), "rows").astype(jnp.float32),
        lax.psum(summed_grads[3].astype(jnp.bfloat16), "rows").astype(jnp.float32),
        lax.psum(summed_grads[4].astype(jnp.bfloat16), "rows").astype(jnp.float32),
        lax.psum(summed_grads[5].astype(jnp.bfloat16), "rows").astype(jnp.float32),
    )
    heads_out, message_out = (
        lax.psum_scatter(
            summed_grads[6].astype(jnp.bfloat16), "rows", scatter_dimension=0, tiled=True
        ).astype(jnp.float32),
        lax.psum_scatter(
            summed_grads[7].astype(jnp.bfloat16), "rows", scatter_dimension=0, tiled=True
        ).astype(jnp.float32),
    )

    def own_share(member):
        share = member.shape[0] // batch_count
        return lax.dynamic_slice_in_dim(member, image_index * share, share, 0)

    return (
        depth_stream.astype(jnp.bfloat16),
        class_logits.astype(jnp.bfloat16),
        image_grad,
        shared[0],
        own_share(gain_grad_one),
        own_share(shift_grad_one),
        shared[1],
        own_share(gain_grad_two),
        own_share(shift_grad_two),
        shared[2],
        own_share(gain_grad_three),
        own_share(shift_grad_three),
        shared[3],
        heads_out,
        message_out,
        shared[4],
        shared[5],
    )


SHAPES = dict(
    wf=((4, 2, 2, 128, 256), BF16),
    wm=((9, 4, 2, 2, 32, 256), BF16),
    wl=((4, 2, 2, 32, 1024), BF16),
    wr=((4, 2, 128, 512), BF16),
    wc=((16, 32, 128), BF16),
    wcs=((32, 128), BF16),
    wcv=((32, 40), BF16),
    cct=((2, 40, 80), BF16),
    ctf=((128, 128), F32),
    xh=((320, 1024), BF16),
    wh=((9, 4, 2, 2, 32, 256), BF16),
    wq=((9, 4, 2, 2, 32, 256), BF16),
    wg=((4, 2, 2, 32, 256), BF16),
    xall=((320, 2048), BF16),
    maskp=((1280, 128), F32),
    pre1=((320, 256), F32),
    pre2=((320, 256), F32),
    pre3=((320, 1024), F32),
    bnp1=((8, 256), F32),
    bnp2=((8, 256), F32),
    bnp3=((8, 1024), F32),
    a1=((320, 512), BF16),
    a2=((320, 512), BF16),
    a3=((480, 1536), BF16),
    blk=((320, 1024), BF16),
    rps=((160, 512), BF16),
    rpr=((160, 512), BF16),
    rbuf=((1280, 512), BF16),
    fown=((1280, 256), BF16),
    ffull=((1280, 512), BF16),
    msgb=((1280, 256), BF16),
    gateb=((1280, 256), BF16),
    mrecv=((4, 160, 512), BF16),
    dm=((4, 160, 512), BF16),
    eu=((2, 160, 512), BF16),
    dcotv=((160, 512), BF16),
    ccotv=((160, 128), BF16),
    olt=((2, 40, 80), BF16),
    ods=((160, 512), BF16),
    olg=((160, 128), BF16),
    mrg=((160, 512), BF16),
    fg=((2, 2, 160, 512), BF16),
    dmg=((1280, 256), BF16),
    exg=((2, 1280, 256), BF16),
    gm=((9, 4, 2, 2, 32, 256), BF16),
    gh=((9, 4, 2, 2, 32, 256), BF16),
    gg=((4, 2, 2, 32, 256), BF16),
    rg=((3, 2, 2, 32, 256), BF16),
    hop=((2, 9, 2, 2, 32, 256), BF16),
    gcls=((16, 32, 128), BF16),
    rcls=((15, 32, 128), BF16),
    clsr=((32, 128), F32),
    dfs=((1280, 256), BF16),
    dfr=((1280, 256), BF16),
    drs=((640, 512), BF16),
    drr=((640, 512), BF16),
    dro=((3, 160, 512), BF16),
    dred=((320, 512), BF16),
    dsr=((160, 1024), BF16),
    par2=((320, 256), BF16),
    par1=((320, 256), BF16),
    dp1r=((160, 256), BF16),
    rcr=((4, 2, 128, 512), BF16),
    rcl=((4, 2, 32, 1024), BF16),
    rcm=((9, 4, 2, 32, 256), BF16),
    rcf=((4, 2, 128, 256), BF16),
    ryr=((4, 128, 512), BF16),
    hpr=((128, 512), BF16),
    hpl=((32, 1024), BF16),
    ryl=((4, 32, 1024), BF16),
    rym=((9, 4, 32, 256), BF16),
    ryf=((4, 128, 256), BF16),
    rzr=((3, 128, 512), BF16),
    rzl=((3, 32, 1024), BF16),
    rzm=((3, 9, 32, 256), BF16),
    rzf=((3, 128, 256), BF16),
)
for _i, _w in enumerate((256, 256, 512, 512, 256, 256)):
    SHAPES["am%d" % _i] = ((8, _w), F32)
    SHAPES["as%d" % _i] = ((8, _w), F32)
    SHAPES["at%d" % _i] = ((8, _w), F32)
    SHAPES["ar%d" % _i] = ((3, 8, _w), F32)
    SHAPES["az%d" % _i] = ((3, 8, _w), F32)

INS = (
    "crop_h", "crop_w", "images", "first", "middle", "last", "reduce", "gates",
    "classes", "heads", "messages", "gains", "dcot", "ccot",
)
OUTS = dict(
    o_depth=((160, 512), BF16),
    o_logits=((2, 40, 80), BF16),
    o_img=((160, 2048), BF16),
    o_first=((128, 512), BF16),
    o_gs1=((2, 8, 256), F32),
    o_mid=((9, 32, 512), BF16),
    o_gs2=((2, 8, 256), F32),
    o_last=((2, 32, 1024), BF16),
    o_gs3=((2, 8, 512), F32),
    o_red=((128, 512), BF16),
    o_heads=((2, 9, 32, 512), BF16),
    o_mess=((2, 9, 32, 512), BF16),
    o_gates=((2, 32, 512), BF16),
    o_cls=((32, 128), F32),
    rm=((3, 9, 2, 2, 32, 256), BF16),
    rh=((3, 9, 2, 2, 32, 256), BF16),
    wfo=((4, 2, 2, 128, 256), BF16),
    st_h=((9, 32, 512), BF16),
    st_m=((9, 32, 512), BF16),
)


def shift_columns(v):
    rows, width = v.shape
    col = lax.broadcasted_iota(jnp.int32, (rows, width), 0)
    left = jnp.where(col == 0, 0.0, pltpu.roll(v, 1, 0))
    right = jnp.where(col == rows - 1, 0.0, pltpu.roll(v, rows - 1, 0))
    return left, right


def spread(src, dst, n_img, width):
    zero = jnp.zeros((80, 3 * width), BF16)
    for pad in range(n_img + 1):
        dst[pl.ds(pad * 400, 80), :] = zero

    def body(i, carry):
        v = src[pl.ds(pl.multiple_of(i * 80, 16), 80), :]
        left, right = shift_columns(v.astype(F32))
        row = pl.multiple_of((i + lax.div(i, np.int32(4)) + 1) * 80, 16)
        dst[pl.ds(row, 80), 0:width] = left.astype(BF16)
        dst[pl.ds(row, 80), width : 2 * width] = v
        dst[pl.ds(row, 80), 2 * width : 3 * width] = right.astype(BF16)
        return carry

    lax.fori_loop(0, 4 * n_img, body, 0)


def conv_rows(a3, w, img):
    acc = None
    for a in range(3):
        base = pl.multiple_of((5 * img + a) * 80, 16)
        part = dot(a3[pl.ds(base, 320), :], w[3 * a : 3 * a + 3].reshape(1536, 256))
        acc = part if acc is None else acc + part
    return acc


def conv_back(d3, w, img):
    acc = None
    for a in range(3):
        for q in range(3):
            base = pl.multiple_of((5 * img + a) * 80, 16)
            tap = 3 * (2 - a) + (2 - q)
            part = dot_last(d3[pl.ds(base, 320), 256 * q : 256 * q + 256], w[tap].reshape(512, 256))
            acc = part if acc is None else acc + part
    return acc


def conv_weight(a3, d3, out, n_img, first, last):
    depth = (5 * n_img - 1) * 80

    def body(tap, carry):
        a = lax.div(tap, np.int32(3))
        q = tap - 3 * a
        left = a3[pl.ds(pl.multiple_of(a * 80, 16), depth), pl.ds(pl.multiple_of(q * 512, 128), 512)]
        out[tap] = dot_first(left, d3[pl.ds(80, depth), 256:512]).astype(BF16).reshape(out.shape[1:])
        return carry

    lax.fori_loop(first, last, body, 0)


def body(names, *refs):
    s = SimpleNamespace(**dict(zip(names, refs)))
    b, r = lax.axis_index("batch"), lax.axis_index("rows")
    z = lax.div(b, np.int32(4))
    y = lax.rem(lax.div(b, np.int32(2)), np.int32(2))
    c = lax.rem(b, np.int32(2))
    ln = Links(s.send_sems, s.recv_sems, s.near_sems)
    half, fhalf = 256 * r, 256 * c

    def dev(zz, yy, cc, rr):
        return (4 * zz + 2 * yy + cc, rr)

    def zk(k):
        return lax.rem(z + k, np.int32(4))

    core, ypeer, xpeer = dev(z, y, 1 - c, r), dev(z, 1 - y, c, r), dev(z, y, c, 1 - r)
    special = r == y
    plain = r != y
    task = 2 * r + y
    img = 2 * y + c
    own_px = pl.multiple_of(320 * img + 160 * r, 16)
    my_rows = pl.multiple_of(160 * r, 16)
    other_rows = pl.multiple_of(160 * (1 - r), 16)
    half = pl.multiple_of(half, 128)
    ohalf = pl.multiple_of(256 * (1 - r), 128)
    fhalf = pl.multiple_of(fhalf, 128)
    offsets = [(dr, dy, dc) for dr in range(2) for dy in range(2) for dc in range(2) if dr + dy + dc]

    def peer(dr, dy, dc):
        rr = 1 - r if dr else r
        yy = 1 - y if dy else y
        cc = 1 - c if dc else c
        return rr, yy, cc

    def px_of(rr, yy, cc):
        return pl.multiple_of(320 * (2 * yy + cc) + 160 * rr, 16)

    ends = (z == 0) | (z == 3)
    inner = jnp.logical_not(ends)
    not_first, not_last = z != 0, z != 3
    far_end = dev(jnp.where(z == 1, 0, 3), y, c, r)
    odd = c == r

    def both(p, q):
        return q if p is None else (p if q is None else p & q)

    def line_start(src, at, pair, when=None, relay=True):
        sides = ln.group(pair, when)
        for q in (1, 3):
            sides.push(src, at(z), dev(zk(q), y, c, r), when)
        across = ln.push(src, at(z), dev(zk(2), y, c, r), both(when, ends) if relay else when)
        return [sides, across, relay, None, None]

    def line_y(state, src, at, four, when=None):
        state[4] = ln.group(four, when)
        state[4].push(src, at(z), ypeer, when)

    def line_relay(state, at, when=None):
        sides, _, relay = state[:3]
        wait([sides], when)
        if relay:
            state[3] = ln.push(at(3 - z), at(3 - z), far_end, both(when, inner))

    def line_sides(state, at, when=None):
        ys = state[4]
        ys.push(at(zk(3)), at(zk(3)), ypeer, when)
        ys.push(at(zk(1)), at(zk(1)), ypeer, when)

    def line_last(state, at, col, when=None):
        _, across, relay, hand, ys = state
        if relay:
            wait([across], both(when, inner))
            wait([hand], both(when, ends))
        else:
            wait([across], when)
        ys.push(at(zk(2)), at(zk(2)), ypeer, when)
        return [ln.push(col(y), col(y), core, when)]

    def line_core(state, col, cores, when=None):
        wait([state[4]], when)
        cores.append(ln.push(col(1 - y), col(1 - y), core, when))

    def at_wf(zz):
        return s.wf.at[zz, y, c]

    def at_wm(zz):
        return s.wm.at[:, zz, y, c]

    def at_wl(zz):
        return s.wl.at[zz, y, c]

    def at_wr(zz):
        return s.wr.at[zz, y]

    def col_wf(yy):
        return s.wf.at[:, yy, c]

    def col_wm(yy):
        return s.wm.at[:, :, yy, c]

    def col_wl(yy):
        return s.wl.at[:, yy, c]

    def col_wr(yy):
        return s.wr.at[:, yy]

    near_last = [
        ln.near(s.last.at[:, pl.ds(pl.multiple_of((2 * i + r) * 128, 128), 128)], s.wl.at[z, y, c, :, 128 * i : 128 * i + 128])
        for i in range(8)
    ]
    near_own = ln.near(s.images, s.xall.at[pl.ds(my_rows, 160)])
    near_cls = ln.near(s.classes, s.wcv)
    near_wf = ln.near(s.first.at[:, pl.ds(half, 256)], s.wf.at[z, y, c])
    near_wm = ln.near(s.middle.at[:, :, pl.ds(half, 256)], s.wm.at[:, z, y, c])
    red_local = pltpu.make_async_copy(s.reduce, s.wr.at[z, y], s.near_sems.at[NEAR - 1])
    pl.when(odd)(red_local.start)
    near_late = [
        ln.near(s.dcot, s.dcotv),
        ln.near(s.ccot, s.cct),
        ln.near(s.heads.at[y, :, :, pl.ds(fhalf, 256)], s.wh.at[:, z, y, c]),
        ln.near(s.messages.at[y, :, :, pl.ds(fhalf, 256)], s.wq.at[:, z, y, c]),
        ln.near(s.gates.at[r, :, pl.ds(fhalf, 256)], s.wg.at[z, y, c]),
    ]
    barrier = pltpu.get_barrier_semaphore()
    friends = [
        dev(zk(q), 1 - y if j else y, 1 - c if i else c, r) for q in range(4) for j in range(2) for i in range(2) if q + j + i
    ] + [dev(z, 1 - y if j else y, 1 - c if i else c, 1 - r) for j in range(2) for i in range(2)]
    for friend in friends:
        pl.semaphore_signal(barrier, inc=1, device_id=friend, device_id_type=MESH)
    pl.semaphore_wait(barrier, len(friends))

    src_wf, src_wm = s.first.at[:, pl.ds(half, 256)], s.middle.at[:, :, pl.ds(half, 256)]
    go_wf = line_start(src_wf, at_wf, lambda: s.wf.at[0, 0], relay=False)
    line_y(go_wf, src_wf, at_wf, lambda: s.wf.at[:, 0, 0])
    img_x = ln.push(s.images, s.xall.at[pl.ds(my_rows, 160)], xpeer)
    go_wm = line_start(src_wm, at_wm, lambda: s.wm.at[:, 0, 0])
    line_y(go_wm, src_wm, at_wm, lambda: s.wm.at[:, :, 0, 0])
    for cp in near_last:
        cp.wait()
    go_wl = line_start(at_wl(z), at_wl, lambda: s.wl.at[0, 0])
    go_wr = line_start(s.reduce, at_wr, lambda: s.wr.at[0], odd)

    for i in range(4):
        high, wide = s.crop_h[4 * z + i], s.crop_w[4 * z + i]
        for row in range(4):
            col = lax.broadcasted_iota(jnp.int32, (80, 128), 0)
            inside = (col < wide) & (row < high)
            s.maskp[pl.ds(320 * i + 80 * row, 80), :] = jnp.where(inside, 1.0, 0.0)
    total = s.crop_h[0] * s.crop_w[0]
    for i in range(1, 16):
        total = total + s.crop_h[i] * s.crop_w[i]
    count = total.astype(F32)
    mine = pl.multiple_of(320 * img, 16)

    def mask_at(base, rows, width):
        return lanes(s.maskp[pl.ds(mine + base, rows), :], width)

    near_cls.wait()
    s.wcs[...] = jnp.zeros(s.wcs.shape, BF16)
    s.wcs[:, 0:40] = s.wcv[...]
    s.wc[b] = s.wcs[...]
    near_own.wait()
    near_wf.wait()
    line_relay(go_wf, at_wf)
    line_sides(go_wf, at_wf)
    cores_wf = line_last(go_wf, at_wf, col_wf)
    near_wm.wait()
    line_relay(go_wm, at_wm)
    line_core(go_wf, col_wf, cores_wf)
    wait([img_x])

    def mask_x(base):
        rows = pl.ds(base, 80)
        v = (s.xall[rows, :].astype(F32) * mask_at(base, 80, 2048)).astype(BF16)
        s.xall[rows, :] = v
        for i in range(8):
            pick = jnp.where(r == 0, v[:, 256 * i : 256 * i + 128].astype(F32), v[:, 256 * i + 128 : 256 * i + 256].astype(F32))
            s.xh[rows, 128 * i : 128 * i + 128] = pick.astype(BF16)

    rows_loop(320, 80, mask_x)
    wait(cores_wf)
    wfo_x = ln.group(lambda: s.wf)
    for zz in (0, 1):
        wfo_x.push(s.wf.at[zz], s.wfo.at[zz], xpeer)

    def task_push(src, dst, lo, hi, staged):
        yy = 1 - y if staged else y
        taps = hi - lo
        sides = ln.group(lambda: s.rbuf.at[0 : 80 * taps])
        across = ln.group(lambda: dst.at[lo:hi, 0, 0], ends)
        for q in (1, 3, 2, 0):
            for i in range(2):
                if q + i == 0:
                    continue
                cc = 1 - c if i else c
                (across if q == 2 else sides).push(
                    src.at[lo:hi, :, pl.ds(pl.multiple_of(256 * cc, 128), 256)],
                    dst.at[lo:hi, z, yy, c],
                    dev(zk(q) if q else z, y, cc, r),
                    ends if q == 2 else None,
                )
        return sides, across, lo, hi, yy

    def task_relay(state, dst):
        sides, across, lo, hi, yy = state
        wait([sides])
        hand = ln.push(dst.at[lo:hi, 3 - z, yy], dst.at[lo:hi, 3 - z, yy], far_end, inner)
        return across, hand

    def task_ready(state):
        across, hand = state
        wait([across], inner)
        wait([hand], ends)

    def plane_start(n):
        m, ar = (getattr(s, p + str(n)) for p in ("am", "ar"))
        one = ln.group(lambda: ar)
        for i in (1, 2, 3):
            yy = 1 - y if i & 2 else y
            cc = 1 - c if i & 1 else c
            one.push(m, ar.at[i - 1], dev(z, yy, cc, r))
        return one

    def plane_end(n, one):
        m, sm, ar = (getattr(s, p + str(n)) for p in ("am", "as", "ar"))
        wait([one])
        sm[...] = (m[...] + ar[0]) + (ar[1] + ar[2])

    def reduce_plane(n):
        plane_end(n, plane_start(n))

    def reduce_line(n, bulk=None):
        sm, t, az = (getattr(s, p + str(n)) for p in ("as", "at", "az"))
        two = ln.group(lambda: az)
        for q in (1, 2, 3):
            two.push(sm, az.at[q - 1], dev(zk(q), y, c, r))
        if bulk is not None:
            bulk()
        wait([two])
        t[...] = (sm[...] + az[0]) + (az[1] + az[2])
        return t[...]

    def stats_of(pre, width, msg):
        m = lanes(s.maskp[pl.ds(mine, 320), :], width)
        v = pre * m
        sums = jnp.sum(v, axis=0, keepdims=True)
        squares = jnp.sum(v * pre, axis=0, keepdims=True)
        return sums, squares

    def norm_terms(n, bnp, width, bulk=None):
        t = reduce_line(n, bulk)
        if width == 256:
            rows = [t[i : i + 1] for i in range(4)]
        else:
            rows = [jnp.concatenate([t[2 * i : 2 * i + 1], t[2 * i + 1 : 2 * i + 2]], axis=1) for i in range(4)]
        mean = rows[0] / count
        inv = lax.rsqrt(rows[1] / count - mean * mean + EPS)
        bnp[0:1], bnp[1:2], bnp[2:3], bnp[3:4] = mean, inv, rows[2], rows[3]

    quarter = lax.div(b, np.int32(4))
    spot = 32 * lax.rem(b, np.int32(4))

    def placed(n):
        lane = lax.broadcasted_iota(jnp.int32, (8, 128), 1)
        out = []
        for p in range(2):
            if n < 2:
                v = jnp.broadcast_to(s.gains[0:1, :], (8, 128))
                v = pltpu.roll(v, lax.rem(spot + 128 - 32 * (2 * n + p), np.int32(128)), 1)
                v = jnp.where((lane >= spot) & (lane < spot + 32), v, 0.0)
                out.append(jnp.concatenate([jnp.where(quarter == 2 * r + i, v[0:1], 0.0) for i in range(2)], axis=1))
            else:
                v = s.gains[1 + p : 2 + p, :]
                out.append(
                    [
                        jnp.concatenate(
                            [jnp.where(odd & (lax.div(b, np.int32(2)) == 4 * h + i), v, 0.0) for i in range(4)], axis=1
                        )
                        for h in range(2)
                    ]
                )
        return out

    def put_stats(n, first, second, width, layer):
        m = getattr(s, "am%d" % n)
        m[...] = jnp.zeros(m.shape, F32)
        if width == 256:
            m[0:1], m[1:2] = first, second
            if layer is not None:
                m[2:3], m[3:4] = placed(layer)
        else:
            m[0:1], m[1:2] = first[:, :512], first[:, 512:]
            m[2:3], m[3:4] = second[:, :512], second[:, 512:]
            if layer is not None:
                gain, shift = placed(layer)
                m[4:5], m[5:6] = gain
                m[6:7], m[7:8] = shift

    pre = dot(s.xall[...], s.wf[...].reshape(2048, 256))
    s.pre1[...] = pre
    first_sum, first_sq = stats_of(pre, 256, None)
    put_stats(0, first_sum, first_sq, 256, 0)
    plane_one = plane_start(0)
    line_sides(go_wm, at_wm)
    cores_wm = line_last(go_wm, at_wm, col_wm)
    plane_end(0, plane_one)
    line_y(go_wl, at_wl(z), at_wl, lambda: s.wl.at[:, 0, 0])
    pl.when(odd)(red_local.wait)
    line_relay(go_wl, at_wl)
    line_relay(go_wr, at_wr, odd)
    line_sides(go_wl, at_wl)
    heads = []
    norm_terms(0, s.bnp1, 256, lambda: heads.append(task_push(s.heads.at[y], s.wh, 0, 9, False)))

    def act_from(prebuf, bnp, dst):
        def step(base):
            x = (prebuf[pl.ds(base, 80), :] - bnp[0:1]) * bnp[1:2] * bnp[2:3] + bnp[3:4]
            dst[pl.ds(base, 80), pl.ds(half, 256)] = (gelu_of(x) * mask_at(base, 80, 256)).astype(BF16)

        rows_loop(320, 80, step)

    act_from(s.pre1, s.bnp1, s.a1)
    a1_x = ln.push(s.a1.at[:, pl.ds(half, 256)], s.a1.at[:, pl.ds(half, 256)], xpeer)
    line_core(go_wm, col_wm, cores_wm)
    cores_wl = line_last(go_wl, at_wl, col_wl)
    over_h = ln.push(s.heads.at[1 - y], s.st_h, ypeer)
    wait(cores_wm)
    wait([a1_x])
    wfo_x.push(s.wf.at[2], s.wfo.at[2], xpeer)
    spread(s.a1, s.a3, 1, 512)
    pre = conv_rows(s.a3, s.wm, 0)
    s.pre2[...] = pre
    first_sum, first_sq = stats_of(pre, 256, None)
    put_stats(1, first_sum, first_sq, 256, 1)
    reduce_plane(1)
    line_y(go_wr, s.reduce, at_wr, lambda: s.wr.at[:, 0], odd)
    line_sides(go_wr, at_wr, odd)
    cores_wr = line_last(go_wr, at_wr, col_wr, odd)
    relayed_h = []

    def bulk_two():
        relayed_h.append(task_relay(heads[0], s.wh))
        wait([over_h])
        heads.append(task_push(s.st_h, s.wh, 0, 5, True))

    norm_terms(1, s.bnp2, 256, bulk_two)
    act_from(s.pre2, s.bnp2, s.a2)
    a2_x = ln.push(s.a2.at[:, pl.ds(half, 256)], s.a2.at[:, pl.ds(half, 256)], xpeer)
    line_core(go_wl, col_wl, cores_wl)
    wait(cores_wl)
    wait([a2_x])
    wfo_x.push(s.wf.at[3], s.wfo.at[3], xpeer)
    pre = dot(s.a2[...], s.wl[...].reshape(512, 1024))
    s.pre3[...] = pre
    first_sum, first_sq = stats_of(pre, 1024, None)
    put_stats(2, first_sum, first_sq, 1024, 2)
    reduce_plane(2)
    over_m = ln.push(s.messages.at[1 - y], s.st_m, ypeer)
    mess = []

    def mess_push(a, staged):
        return task_push(s.st_m if staged else s.messages.at[y], s.wq, 3 * a, 3 * a + 3, staged)

    def bulk_three():
        heads.append(task_push(s.st_h, s.wh, 5, 9, True))
        mess.extend([[mess_push(a, False)] for a in range(2)])

    norm_terms(2, s.bnp3, 1024, bulk_three)
    staged_h = ln.near(s.st_h.at[:, :, pl.ds(fhalf, 256)], s.wh.at[:, z, 1 - y, c])
    gate_got = {}
    cls_got = ln.group(lambda: s.wc.at[0:15])
    for q in range(4):
        for j in range(2):
            if q + j:
                gate_got[q, j] = ln.group(lambda: s.wg.at[0, 0], (y == r) if j == 0 else (y != r))
            for i in range(2):
                if q + j + i == 0:
                    continue
                yy = 1 - y if j else y
                cc = 1 - c if i else c
                to = dev(zk(q) if q else z, yy, cc, r)
                cls_got.push(s.wcs, s.wc.at[b], to)
                src = s.gates.at[r, :, pl.ds(pl.multiple_of(256 * cc, 128), 256)]
                if q + j:
                    gate_got[q, j].push(src, s.wg.at[z, y, c], to, (y == r) if j == 0 else (y != r))
                else:
                    gate_got[0, 0] = ln.push(src, s.wg.at[z, y, c], to, y == r)

    def summed_at(base, rows):
        x = (s.pre3[pl.ds(base, rows), :] - s.bnp3[0:1]) * s.bnp3[1:2]
        return x, x * s.bnp3[2:3] + s.bnp3[3:4] + s.xh[pl.ds(base, rows), :].astype(F32)

    def block_step(base):
        _, v = summed_at(base, 32)
        s.blk[pl.ds(base, 32), :] = (gelu_of(v) * mask_at(base, 32, 1024)).astype(BF16)

    rows_loop(320, 32, block_step)
    relayed_h.append(task_relay(heads[1], s.wh))
    line_core(go_wr, col_wr, cores_wr, odd)
    wait(cores_wr, jnp.logical_not(odd))
    wred = s.wr[...].reshape(1024, 512)
    s.rps[...] = dot(s.blk[pl.ds(other_rows, 160), :], wred).astype(BF16)
    red_x = ln.push(s.rps, s.rpr, xpeer)
    part = dot(s.blk[pl.ds(my_rows, 160), :], wred)
    wait([red_x])
    s.rbuf[pl.ds(own_px, 160), :] = (part + s.rpr[...].astype(F32)).astype(BF16)

    def block_of(rr, yy, cc, lo=0, n=160):
        return s.rbuf.at[pl.ds(pl.multiple_of(px_of(rr, yy, cc) + lo, 16), n)]

    for cp in near_late:
        cp.wait()
    own = block_of(r, y, c)
    g_x = ln.push(own, own, xpeer)
    g_y = ln.push(own, own, ypeer)
    g_c = ln.push(own, own, core)
    wait([g_x])
    bx = block_of(1 - r, y, c, 0, 80)
    g_xy = ln.push(bx, bx, ypeer)
    wait([g_y])
    by = block_of(r, 1 - y, c, 80, 80)
    g_yx = ln.push(by, by, xpeer)
    bx = block_of(1 - r, y, c)
    g_c1 = ln.push(bx, bx, core)
    by = block_of(r, 1 - y, c)
    g_c2 = ln.push(by, by, core)
    wait([g_xy, g_yx])
    bd = block_of(1 - r, 1 - y, c)
    g_c3 = ln.push(bd, bd, core)
    relayed_h.append(task_relay(heads[2], s.wh))
    wait([over_m])
    staged_m = ln.near(s.st_m.at[:, :, pl.ds(fhalf, 256)], s.wq.at[:, z, 1 - y, c])
    mess[0].append(mess_push(0, True))
    mess[1].append(mess_push(1, True))
    mess.append([mess_push(2, False)])
    wait([g_c, g_c1, g_c2, g_c3])

    near_end = dev(jnp.where(z == 0, 1, 2), y, c, r)
    other_end = dev(jnp.where(z == 1, 3, 0), y, c, r)

    def grad_push(n, g, rm, lo, hi):
        def like(slot):
            return lambda side: rm.at[slot, lo:hi] if side else g.at[lo:hi, 0]

        got = {}
        for q in (1, 2, 3):
            direct = {1: not_last, 2: ends, 3: not_first}[q]
            got[q] = ln.push(g.at[lo:hi, zk(q)], rm.at[q - 1, lo:hi], dev(zk(q), y, c, r), direct, like(q - 1))
        hop = s.hop.at[n, lo:hi]
        got[0] = ln.push(
            g.at[lo:hi, 3 - z], hop, near_end, ends, lambda side: s.hop.at[n, lo:hi] if side else g.at[lo:hi, 0]
        )
        return got, n, g, rm, lo, hi

    def grad_hop(state):
        got, n, g, rm, lo, hi = state

        def add():
            got[0].wait_recv()
            far = jnp.where(z == 1, 3, 0)
            for t in range(lo, hi):
                s.hop[n, t] = (s.hop[n, t].astype(F32) + g[t, far].astype(F32)).astype(BF16)

        pl.when(inner)(add)
        got[4] = ln.push(
            s.hop.at[n, lo:hi], rm.at[1, lo:hi], other_end, inner,
            lambda side: rm.at[1, lo:hi] if side else s.hop.at[n, lo:hi],
        )

    def grad_wait(state):
        got = state[0]
        wait([got[1]], not_first)
        wait([got[3]], not_last)
        wait([got[2]], inner)
        wait([got[4]], ends)

    def tasks(r3, f3, d3, preh, dfull):
        spread(s.rbuf, r3, 4, 512)
        for part in relayed_h:
            task_ready(part)
        staged_h.wait()

        def head_step(i, carry):
            v = conv_rows(r3, s.wh, i)
            px = pl.multiple_of(i * 320, 16)
            preh[pl.ds(px, 320), :] = v
            return carry

        lax.fori_loop(0, 4, head_step, 0)

        def feat_step(base):
            m = lanes(s.maskp[pl.ds(base, 80), :], 256)
            s.fown[pl.ds(base, 80), :] = (gelu_of(preh[pl.ds(base, 80), :]) * m).astype(BF16)

        rows_loop(1280, 80, feat_step)
        f_c = ln.push(s.fown, s.ffull.at[:, pl.ds(fhalf, 256)], core)
        f_n = ln.near(s.fown, s.ffull.at[:, pl.ds(fhalf, 256)])

        def seven():
            return s.dmg.at[0:1120]

        def pieces(n):
            return lambda: s.dmg.at[0 : 160 * n]

        even = [o for o in offsets if (o[0] + o[1]) % 2 == 0]
        uneven = [o for o in offsets if (o[0] + o[1]) % 2]

        def to_owners(src, dst_of):
            got = [ln.group(pieces(len(o)), special) for o in (even, uneven)]
            for g, group in zip(got, (even, uneven)):
                for o in group:
                    rr, yy, cc = peer(*o)
                    g.push(src.at[pl.ds(px_of(rr, yy, cc), 160)], dst_of().at[:, pl.ds(fhalf, 256)], dev(z, yy, cc, rr), special)
            return got

        def from_tasks(got):
            wait([got[0]], special)
            wait([got[1]], plain)

        def to_tasks(src_of, dst):
            got = [ln.group(pieces(len(o)), w) for o, w in ((even, special), (uneven, plain))]
            for g, group, w in zip(got, (even, uneven), (special, plain)):
                for o in group:
                    rr, yy, cc = peer(*o)
                    ll = pl.ds(pl.multiple_of(256 * cc, 128), 256)
                    g.push(src_of(rr).at[:, ll], dst.at[pl.ds(own_px, 160)], dev(z, yy, cc, rr), w)
            return got

        def keep(dst, src):
            def run():
                dst[:, pl.ds(fhalf, 256)] = src[pl.ds(own_px, 160), :]

            return run

        pl.when(special)(keep(s.fg.at[r, 0], s.fown))
        f_n.wait()
        wait([f_c])

        def gate_ready():
            for cp in gate_got.values():
                cp.wait_recv()

        pl.when(special)(gate_ready)

        @pl.when(special)
        def _():
            def gate_step(base):
                v = dot(s.ffull[pl.ds(base, 320), :], s.wg[...].reshape(512, 256))
                s.gateb[pl.ds(base, 320), :] = (1.0 / (1.0 + jnp.exp(-v))).astype(BF16)

            rows_loop(1280, 320, gate_step)

        g_own = to_owners(s.gateb, lambda: s.fg.at[r, 1])
        pl.when(special)(keep(s.fg.at[r, 1], s.gateb))
        f_own = to_owners(s.fown, lambda: s.fg.at[r, 0])

        relayed = [[task_relay(p, s.wq) for p in mess[0]]]
        mess[2].append(mess_push(2, True))
        spread(s.ffull, f3, 4, 512)

        wait([cls_got])
        for i in range(2):
            s.ctf[...] = jnp.zeros((128, 128), F32)
            s.ctf[0:40, 0:80] = s.cct[i].astype(F32)
            turned = s.ctf[...].T
            s.ccotv[80 * i : 80 * i + 80, :] = turned[0:80, :].astype(BF16)
        from_tasks(g_own)

        def early_step(base):
            rows = pl.ds(base, 32)
            m = lanes(s.maskp[pl.ds(own_px + base, 32), :], 512)
            gd, gc = s.fg[0, 1, rows, :].astype(F32), s.fg[1, 1, rows, :].astype(F32)
            dj = (s.ccotv[rows, :].astype(F32) * m[:, :128]).astype(BF16)
            s.ccotv[rows, :] = dj
            dd = s.dcotv[rows, :].astype(F32) * m
            dmer = dot_last(dj, s.wc[...].reshape(512, 128))
            s.eu[0, rows, :] = dd.astype(BF16)
            s.eu[1, rows, :] = dmer.astype(BF16)
            down, up = dd * gd, dmer * gc
            both = (down + up).astype(BF16)
            s.dm[0, rows, :] = up.astype(BF16)
            s.dm[1, rows, :] = both
            s.dm[2, rows, :] = both
            s.dm[3, rows, :] = down.astype(BF16)

        rows_loop(160, 32, early_step)
        d_got = ln.group(seven)
        for o in offsets:
            rr, yy, cc = peer(*o)
            ll = pl.ds(pl.multiple_of(256 * cc, 128), 256)
            d_got.push(s.dm.at[2 * rr + yy, :, ll], s.dmg.at[pl.ds(own_px, 160)], dev(z, yy, cc, rr))
        u_got = to_tasks(lambda rr: s.eu.at[rr], s.exg.at[0])
        s.dmg[pl.ds(own_px, 160), :] = s.dm[task, :, pl.ds(fhalf, 256)]

        @pl.when(special)
        def _():
            s.exg[0, pl.ds(own_px, 160), :] = s.eu[r, :, pl.ds(fhalf, 256)]

        @pl.when(jnp.logical_not(special))
        def _():
            s.exg[0] = jnp.zeros(s.exg.shape[1:], BF16)

        relayed.append([task_relay(p, s.wq) for p in mess[1]])
        relayed.append([task_relay(p, s.wq) for p in mess[2]])
        wait([d_got])
        spread(s.dmg, d3, 4, 256)
        conv_weight(f3, d3, s.gm, 4, 0, 9)
        staged_m.wait()
        gm_z = []
        for a in range(3):
            if a == 0:
                for part in range(3):
                    gm_z.append(grad_push(0, s.gm, s.rm, 3 * part, 3 * part + 3))
            for p in relayed[a]:
                task_ready(p)

            def mess_step(i, carry, a=a):
                rows = pl.ds(pl.multiple_of(i * 320, 16), 320)
                base = pl.multiple_of((5 * i + a) * 80, 16)
                v = dot(f3[pl.ds(base, 320), :], s.wq[3 * a : 3 * a + 3].reshape(1536, 256))
                if a:
                    v = dfull[rows, 0:256] + v
                if a < 2:
                    dfull[rows, 0:256] = v
                else:
                    s.msgb[rows, :] = v.astype(BF16)
                return carry

            lax.fori_loop(0, 4, mess_step, 0)

        m_own = ln.group(seven)
        for o in offsets:
            rr, yy, cc = peer(*o)
            m_own.push(s.msgb.at[pl.ds(px_of(rr, yy, cc), 160)], s.mrecv.at[task, :, pl.ds(fhalf, 256)], dev(z, yy, cc, rr))
        keep(s.mrecv.at[task], s.msgb)()

        def back_step(i, carry):
            px = pl.multiple_of(i * 320, 16)
            dfull[pl.ds(px, 320), :] = conv_back(d3, s.wq, i)
            return carry

        lax.fori_loop(0, 4, back_step, 0)

        from_tasks(f_own)
        wait([m_own])

        def stream_step(base):
            rows = pl.ds(base, 32)
            m = lanes(s.maskp[pl.ds(own_px + base, 32), :], 512)
            m0, m1, m2, m3 = (s.mrecv[t, rows, :].astype(F32) for t in range(4))
            f0, f3_ = s.fg[0, 0, rows, :].astype(F32), s.fg[1, 0, rows, :].astype(F32)
            mid = m1 + m2
            sd, sc = mid + m3, m0 + mid
            gd, gc = s.fg[0, 1, rows, :].astype(F32), s.fg[1, 1, rows, :].astype(F32)
            s.ods[rows, :] = ((f0 + gd * sd) * m).astype(BF16)
            merged = (f3_ + gc * sc).astype(BF16)
            s.mrg[rows, :] = merged
            s.olg[rows, :] = (dot(merged, s.wc[...].reshape(512, 128)) * m[:, :128]).astype(BF16)
            dd, dmer = s.eu[0, rows, :].astype(F32), s.eu[1, rows, :].astype(F32)
            s.fg[0, 1, rows, :] = (dd * sd * gd * (1.0 - gd)).astype(BF16)
            s.fg[1, 1, rows, :] = (dmer * sc * gc * (1.0 - gc)).astype(BF16)

        rows_loop(160, 32, stream_step)
        e_got = to_tasks(lambda rr: s.fg.at[rr, 1], s.exg.at[1])

        @pl.when(special)
        def _():
            s.exg[1, pl.ds(own_px, 160), :] = s.fg[r, 1, :, pl.ds(fhalf, 256)]

        for i in range(2):
            s.ctf[...] = jnp.zeros((128, 128), F32)
            s.ctf[0:80, :] = s.olg[80 * i : 80 * i + 80, :].astype(F32)
            turned = s.ctf[...].T
            s.olt[i] = turned[0:40, 0:80].astype(BF16)
        out_near = [ln.near(s.ods, s.o_depth), ln.near(s.olt, s.o_logits)]
        s.gcls[...] = dot_first(s.mrg[...], s.ccotv[...]).astype(BF16).reshape(16, 32, 128)
        grad_hop(gm_z[0])
        wait(u_got + e_got, special)

        @pl.when(special)
        def _():
            def gate_back(base):
                rows = pl.ds(base, 320)
                dfull[rows, :] = dfull[rows, :] + dot_last(s.exg[1, rows, :], s.wg[...].reshape(512, 256))

            rows_loop(1280, 320, gate_back)

        chalf = pl.ds(pl.multiple_of(256 * (1 - c), 128), 256)

        def give(base):
            rows = pl.ds(base, 80)
            s.dfs[rows, :] = dfull[rows, chalf].astype(BF16)

        rows_loop(1280, 80, give)
        df_c = ln.push(s.dfs, s.dfr, core)

        @pl.when(special)
        def _():
            s.gg[...] = dot_first(s.ffull[...], s.exg[1]).astype(BF16).reshape(s.gg.shape)

        gg_z = [ln.push(s.gg.at[zk(k)], s.rg.at[k - 1], dev(zk(k), y, c, r), special, lambda side, k=k: s.rg.at[k - 1] if side else s.gg.at[0]) for k in (1, 2, 3)]
        cg = ln.group(lambda: s.rcls)
        n_cls = 0
        for q in range(4):
            for j in range(2):
                for i in range(2):
                    if q + j + i == 0:
                        continue
                    yy = 1 - y if j else y
                    cc = 1 - c if i else c
                    zz = zk(q) if q else z
                    cg.push(s.gcls.at[4 * zz + 2 * yy + cc], s.rcls.at[n_cls], dev(zz, yy, cc, r))
                    n_cls += 1
        wait([df_c])

        def dhead_step(base):
            rows = pl.ds(base, 80)
            m = lanes(s.maskp[rows, :], 256)
            d = dfull[rows, pl.ds(fhalf, 256)] + s.dfr[rows, :].astype(F32) + s.exg[0, rows, :].astype(F32)
            s.dmg[rows, :] = (slope_of(preh[rows, :]) * d * m).astype(BF16)

        rows_loop(1280, 80, dhead_step)
        spread(s.dmg, d3, 4, 256)

        def back_step2(i, carry):
            px = pl.multiple_of(i * 320, 16)
            dfull[pl.ds(px, 320), :] = conv_back(d3, s.wh, i)
            return carry

        lax.fori_loop(0, 4, back_step2, 0)
        for yy in range(2):
            src = pl.multiple_of(320 * (2 * yy) + 320 * (1 - c), 16)
            s.drs[pl.ds(320 * yy, 320), :] = dfull[pl.ds(src, 320), :].astype(BF16)
        dr_c = ln.push(s.drs, s.drr, core)
        grad_hop(gm_z[1])
        wait([dr_c])
        for yy in range(2):
            src = pl.multiple_of(320 * (2 * yy) + 320 * c, 16)
            rows = pl.ds(320 * yy, 320)
            s.drr[rows, :] = (dfull[pl.ds(src, 320), :] + s.drr[rows, :].astype(F32)).astype(BF16)
        ro = []
        for dr, dy in ((1, 0), (0, 1), (1, 1)):
            rr, yy, _ = peer(dr, dy, 0)
            src = s.drr.at[pl.ds(pl.multiple_of(320 * yy + 160 * rr, 16), 160)]
            ro.append(ln.push(src, s.dro.at[len(ro)], dev(z, yy, c, rr)))
        gh_z = []
        conv_weight(r3, d3, s.gh, 4, 0, 3)
        gh_z.append(grad_push(1, s.gh, s.rh, 0, 3))
        conv_weight(r3, d3, s.gh, 4, 3, 9)
        wait(ro)
        keep_rows = pl.ds(pl.multiple_of(320 * y + 160 * r, 16), 160)
        total_red = s.drr[keep_rows, :].astype(F32)
        for i in range(3):
            total_red = total_red + s.dro[i].astype(F32)
        s.dred[pl.ds(my_rows, 160), :] = total_red.astype(BF16)
        for cp in out_near:
            cp.wait()
        ln.drain(scoped=True)
        return cg, gm_z, gg_z, gh_z

    state = {}

    def scope_tasks(*scr):
        state["t"] = tasks(*scr)

    pl.run_scoped(
        scope_tasks,
        pltpu.VMEM((1680, 1536), BF16),
        pltpu.VMEM((1680, 1536), BF16),
        pltpu.VMEM((1680, 768), BF16),
        pltpu.VMEM((1280, 256), F32),
        pltpu.VMEM((1280, 512), F32),
    )
    cg, gm_z, gg_z, gh_z = state["t"]

    dr_x = ln.push(s.dred.at[pl.ds(my_rows, 160)], s.dred.at[pl.ds(my_rows, 160)], xpeer)

    def block_back(*late):
        for name, ref in zip(LATE, late):
            setattr(s, name, ref)
        gr, gl, gq, gf = s.gr, s.gl, s.gq, s.gf

        def to_core(g, rc, lead):
            at = g.at[:, :, :, 1 - c] if lead else g.at[:, :, 1 - c]
            return ln.push(at, rc, core)

        def add_core(g, rc, lead):
            if lead:
                for t in range(9):
                    rc[t] = (rc[t].astype(F32) + g[t, :, :, c].astype(F32)).astype(BF16)
            else:
                for t in range(rc.shape[0]):
                    rc[t] = (rc[t].astype(F32) + g[t, :, c].astype(F32)).astype(BF16)

        def to_y(rc, ry, lead):
            return ln.push(rc.at[:, :, 1 - y] if lead else rc.at[:, 1 - y], ry, ypeer)

        def add_y(rc, ry, lead):
            for t in range(ry.shape[0]):
                mine_y = rc[t, :, y] if lead else rc[t, y]
                ry[t] = (ry[t].astype(F32) + mine_y.astype(F32)).astype(BF16)

        def to_z(ry, rz, lead, when=None, hop=None):
            def part(zz):
                return ry.at[:, zz] if lead else ry.at[zz]

            got = {}
            for q in (1, 2, 3):
                direct = None if hop is None else {1: not_last, 2: ends, 3: not_first}[q]
                got[q] = ln.push(part(zk(q)), rz.at[q - 1], dev(zk(q), y, c, r), both(when, direct))
            if hop is not None:
                got[0] = ln.push(part(3 - z), hop, near_end, both(when, ends))
            return got, part, rz, hop, when

        def hop_z(state):
            got, part, rz, hop, when = state

            def add():
                got[0].wait_recv()
                hop[...] = (hop[...].astype(F32) + part(jnp.where(z == 1, 3, 0))[...].astype(F32)).astype(BF16)

            pl.when(both(when, inner))(add)
            got[4] = ln.push(hop, rz.at[1], other_end, both(when, inner))

        def wait_z(state):
            got, _, _, hop, when = state
            if hop is None:
                wait([got[1], got[2], got[3]], when)
            else:
                wait([got[1]], both(when, not_first))
                wait([got[3]], both(when, not_last))
                wait([got[2]], both(when, inner))
                wait([got[4]], both(when, ends))

        def add_z(ry, rz, fin, lead, hop=True):
            mine_z = (ry[:, z] if lead else ry[z]).astype(F32)
            v0, v2 = rz[0].astype(F32), rz[2].astype(F32)
            if hop:
                v0, v2 = jnp.where(z == 0, 0.0, v0), jnp.where(z == 3, 0.0, v2)
            fin[...] = ((mine_z + v0) + (rz[1].astype(F32) + v2)).astype(BF16)

        def task_out(states, rm, g, ps, out):
            for part in states:
                grad_wait(part)
            loads = [[ln.near(rm.at[q, 3 * part : 3 * part + 3], s.zst.at[part % 2, q]) for q in range(3)] for part in range(2)]
            for part in range(3):
                for cp in loads[part]:
                    cp.wait()
                v0 = s.zst.at[part % 2]
                for t in range(3):
                    first_in = jnp.where(z == 0, 0.0, v0[0, t].astype(F32))
                    third_in = jnp.where(z == 3, 0.0, v0[2, t].astype(F32))
                    v = g[3 * part + t, z].astype(F32) + first_in + (v0[1, t].astype(F32) + third_in)
                    ps[3 * part + t] = v.astype(BF16)
                if part == 0:
                    loads.append([ln.near(rm.at[q, 6:9], s.zst.at[0, q]) for q in range(3)])
            lanes_out = pl.ds(fhalf, 256)
            sent = []
            for i in (1, 2, 3):
                yy = 1 - y if i & 2 else y
                cc = 1 - c if i & 1 else c
                sent.append(ln.push(ps.at[:, yy, cc], out.at[y, :, :, lanes_out], dev(z, yy, cc, r)))
            return sent, ln.near(ps.at[:, y, c], out.at[y, :, :, lanes_out])

        wait([dr_x])

        def d3_step(i, carry):
            su, sux = carry
            rows = pl.ds(pl.multiple_of(i * 32, 16), 32)
            x, v = summed_at(i * 32, 32)
            u = slope_of(v) * s.u3[rows, :] * mask_at(i * 32, 32, 1024)
            s.u3[rows, :] = u
            s.dsum[rows, :] = u.astype(BF16)
            return su + jnp.sum(u, axis=0, keepdims=True), sux + jnp.sum(u * x, axis=0, keepdims=True)

        s.u3[...] = dot_last(s.dred[...], s.wr[...].reshape(1024, 512))
        nil = jnp.zeros((1, 1024), F32)
        su, sux = lax.fori_loop(0, 10, d3_step, (nil, nil))
        put_stats(3, su, sux, 1024, None)
        ar3 = plane_start(3)
        ds_x = ln.push(s.dsum.at[pl.ds(other_rows, 160)], s.dsr, xpeer)
        grad_hop(gm_z[2])
        gr[...] = dot_first(s.blk[...], s.dred[...]).astype(BF16).reshape(gr.shape)
        gr_c = ln.push(gr, s.rcr, core, jnp.logical_not(odd))
        plane_end(3, ar3)
        t = reduce_line(3, lambda: gh_z.append(grad_push(1, s.gh, s.rh, 3, 6)))
        gs3 = ln.push(s.at3, s.o_gs3.at[r], xpeer)
        gs3n = ln.near(s.at3, s.o_gs3.at[r])
        mu = jnp.concatenate([t[0:1], t[1:2]], axis=1) / count
        mux = jnp.concatenate([t[2:3], t[3:4]], axis=1) / count

        def dp3_step(base):
            rows = pl.ds(base, 32)
            x = (s.pre3[rows, :] - s.bnp3[0:1]) * s.bnp3[1:2]
            d = mask_at(base, 32, 1024) * (s.bnp3[2:3] * s.bnp3[1:2]) * (s.u3[rows, :] - mu - x * mux)
            s.dp3[rows, :] = d.astype(BF16)

        rows_loop(320, 32, dp3_step)

        def partial_out(pas, value_of):
            pas[...] = value_of(ohalf).astype(BF16)

        wlast = s.wl
        s.u3[:, 0:512] = dot_last(s.dp3[...], wlast[...].reshape(512, 1024))
        s.pas2[...] = s.u3[:, pl.ds(ohalf, 256)].astype(BF16)
        pa2 = ln.push(s.pas2, s.par2, xpeer)
        gl[...] = dot_first(s.a2[...], s.dp3[...]).astype(BF16).reshape(gl.shape)
        gl_c = to_core(gl, s.rcl, False)
        wait([gr_c], odd)

        @pl.when(odd)
        def _():
            for q in range(4):
                s.rcr[q] = (s.rcr[q].astype(F32) + gr[q].astype(F32)).astype(BF16)

        later = {"gr_y": ln.push(s.rcr.at[:, 1 - y], s.ryr, ypeer, odd)}

        def after_plane_two():
            wait([gl_c])
            add_core(gl, s.rcl, False)
            later["gl_y"] = to_y(s.rcl, s.ryl, False)

        def after_plane_one():
            wait([gq_c])
            add_core(gq, s.rcm, True)
            later["gq_y"] = [
                ln.push(s.rcm.at[3 * a : 3 * a + 3, :, 1 - y], s.rym.at[3 * a : 3 * a + 3], ypeer) for a in range(3)
            ]

        wait([pa2])

        def norm_back(n, par, prebuf, bnp, dst, out_gs, middle, after):
            def u_step(i, carry):
                su_, sux_ = carry
                base = pl.multiple_of(i * 80, 16)
                rows = pl.ds(base, 80)
                x = (prebuf[rows, :] - bnp[0:1]) * bnp[1:2]
                v = x * bnp[2:3] + bnp[3:4]
                d = s.u3[rows, pl.ds(half, 256)] + par[rows, :].astype(F32)
                u = slope_of(v) * d * mask_at(base, 80, 256)
                s.u3[rows, 512:768] = u
                return su_ + jnp.sum(u, axis=0, keepdims=True), sux_ + jnp.sum(u * x, axis=0, keepdims=True)

            nil_ = jnp.zeros((1, 256), F32)
            su_, sux_ = lax.fori_loop(0, 4, u_step, (nil_, nil_))
            put_stats(n, su_, sux_, 256, None)
            reduce_plane(n)
            middle()
            t_ = reduce_line(n, after)
            gsx = ln.push(getattr(s, "at%d" % n), out_gs.at[r], xpeer)
            gsn = ln.near(getattr(s, "at%d" % n), out_gs.at[r])
            mu_, mux_ = t_[0:1] / count, t_[1:2] / count

            def d_step(base):
                rows = pl.ds(base, 80)
                x = (prebuf[rows, :] - bnp[0:1]) * bnp[1:2]
                d = mask_at(base, 80, 256) * (bnp[2:3] * bnp[1:2]) * (s.u3[rows, 512:768] - mu_ - x * mux_)
                dst[rows, :] = d.astype(BF16)

            rows_loop(320, 80, d_step)
            return gsx, gsn

        def window_two():
            grad_hop(gh_z[0])
            gh_z.append(grad_push(1, s.gh, s.rh, 6, 9))
            later["mess"] = task_out(gm_z, s.rm, s.gm, s.psm, s.o_mess)

        def window_one():
            grad_hop(gh_z[1])
            wait([later["gr_y"]], odd)

            @pl.when(odd)
            def _():
                for q in range(4):
                    s.ryr[q] = (s.ryr[q].astype(F32) + s.rcr[q, y].astype(F32)).astype(BF16)

            later["gr_z"] = to_z(s.ryr, s.rzr, False, odd, s.hpr)
            wait([later["gl_y"]])
            add_y(s.rcl, s.ryl, False)
            later["gl_z"] = to_z(s.ryl, s.rzl, False, None, s.hpl)

        gs2, gs2n = norm_back(4, s.par2, s.pre2, s.bnp2, s.dp2, s.o_gs2, after_plane_two, window_two)
        spread(s.dp2, s.d3m, 1, 256)
        s.u3[:, 0:512] = conv_back(s.d3m, s.wm, 0)
        s.pas1[...] = s.u3[:, pl.ds(ohalf, 256)].astype(BF16)
        pa1 = ln.push(s.pas1, s.par1, xpeer)
        conv_weight(s.a3, s.d3m, gq, 1, 0, 9)
        gq_c = to_core(gq, s.rcm, True)
        wait([pa1])
        gs1, gs1n = norm_back(5, s.par1, s.pre1, s.bnp1, s.dp1, s.o_gs1, after_plane_one, window_one)
        dp_x = ln.push(s.dp1.at[pl.ds(other_rows, 160)], s.dp1r, xpeer)
        gf[...] = dot_first(s.xall[...], s.dp1[...]).astype(BF16).reshape(gf.shape)
        gf_c = to_core(gf, s.rcf, False)
        wait([gf_c])
        add_core(gf, s.rcf, False)
        gf_y = to_y(s.rcf, s.ryf, False)
        ms, mn = later["mess"]
        gr_z, gl_z = later["gr_z"], later["gl_z"]
        grad_hop(gh_z[2])
        gq_z = []
        for a in range(3):
            wait([later["gq_y"][a]])
            for t in range(3 * a, 3 * a + 3):
                s.rym[t] = (s.rym[t].astype(F32) + s.rcm[t, :, y].astype(F32)).astype(BF16)
            g = ln.group(lambda a=a: s.rzm.at[:, 3 * a : 3 * a + 3])
            for q in (1, 2, 3):
                g.push(s.rym.at[3 * a : 3 * a + 3, zk(q)], s.rzm.at[q - 1, 3 * a : 3 * a + 3], dev(zk(q), y, c, r))
            gq_z.append(g)
            if a == 0:
                hop_z(gr_z)
                hop_z(gl_z)
        wait([gf_y])
        add_y(s.rcf, s.ryf, False)
        gf_z = to_z(s.ryf, s.rzf, False)

        wait([wfo_x])
        wfo_n = ln.near(s.wfo, s.wfov)
        wait([dp_x, ds_x])
        wfo_n.wait()
        mine_d = s.dp1[pl.ds(my_rows, 160), :]
        other_d = s.dp1r[...]
        for q in range(2):
            cols = slice(1024 * q, 1024 * q + 1024)
            wa = s.wf[2 * q : 2 * q + 2].reshape(1024, 256)
            wb = s.wfov[2 * q : 2 * q + 2].reshape(1024, 256)
            s.u3[pl.ds(0, 160), :] = dot_last(mine_d, wa) + dot_last(other_d, wb)

            def img_step(base):
                rows = pl.ds(base, 32)
                m = mask_at(my_rows + base, 32, 1024)
                own_d = s.dsum[pl.ds(my_rows + base, 32), 512 * q : 512 * q + 512].astype(F32)
                far_d = s.dsr[rows, 512 * q : 512 * q + 512].astype(F32)
                d = jnp.concatenate(
                    [
                        jnp.where(r == j % 2, own_d[:, 64 * (j - j % 2) :][:, :128], far_d[:, 64 * (j - j % 2) :][:, :128])
                        for j in range(8)
                    ],
                    axis=1,
                )
                s.oimg[rows, cols] = ((s.u3[rows, :] + d) * m).astype(BF16)

            rows_loop(160, 32, img_step)
        img_n = ln.near(s.oimg, s.o_img)

        hs, hn = task_out(gh_z, s.rh, s.gh, s.psh, s.o_heads)

        @pl.when(special)
        def _():
            for cp in gg_z:
                cp.wait_recv()
            v = (s.gg[z].astype(F32) + s.rg[0].astype(F32)) + (s.rg[1].astype(F32) + s.rg[2].astype(F32))
            s.pg[...] = v.astype(BF16)

        gx = [ln.group(lambda n=n: s.wg.at[0:3, 0, 0] if n == 3 else s.wg.at[0:4, 0, 0], special) for n in (3, 4)]
        for g, odd_one in zip(gx, (0, 1)):
            for o in offsets:
                if (o[0] + o[1]) % 2 == odd_one:
                    rr, yy, cc = peer(*o)
                    g.push(s.pg.at[yy, cc], s.o_gates.at[r, :, pl.ds(fhalf, 256)], dev(z, yy, cc, rr), special)
        gate_near = pltpu.make_async_copy(
            s.pg.at[y, c], s.o_gates.at[r, :, pl.ds(fhalf, 256)], s.near_sems.at[NEAR - 2]
        )
        pl.when(special)(gate_near.start)

        wait([cg])
        v = s.gcls[b].astype(F32)
        for i in range(15):
            v = v + s.rcls[i].astype(F32)
        s.clss[...] = v
        cls_x = ln.push(s.clss, s.clsr, xpeer)

        wait_z(gr_z)
        pl.when(odd)(lambda: add_z(s.ryr, s.rzr, s.fnr, False))
        gr_x = ln.push(s.fnr, s.o_red, xpeer, odd)
        red_near = pltpu.make_async_copy(s.fnr, s.o_red, s.near_sems.at[NEAR - 3])
        pl.when(odd)(red_near.start)
        wait_z(gl_z)
        add_z(s.ryl, s.rzl, s.fnl, False)
        gl_x = ln.push(s.fnl, s.o_last.at[r], xpeer)
        n1 = ln.near(s.fnl, s.o_last.at[r])
        wait(gq_z)
        add_z(s.rym, s.rzm, s.fnm, True, False)
        gq_x = ln.push(s.fnm, s.o_mid.at[:, :, pl.ds(half, 256)], xpeer)
        n2 = ln.near(s.fnm, s.o_mid.at[:, :, pl.ds(half, 256)])
        wait_z(gf_z)
        add_z(s.ryf, s.rzf, s.fnf, False, False)
        gf_x = ln.push(s.fnf, s.o_first.at[:, pl.ds(half, 256)], xpeer)
        n3 = ln.near(s.fnf, s.o_first.at[:, pl.ds(half, 256)])
        wait([cls_x])
        s.clso[...] = s.clss[...] + s.clsr[...]
        n4 = ln.near(s.clso, s.o_cls)
        wait([gr_x], jnp.logical_not(odd))
        wait([gl_x, gq_x, gf_x, gs1, gs2, gs3])
        wait(ms + hs)
        wait([gx[0]], special)
        wait([gx[1]], plain)
        pl.when(special)(gate_near.wait)
        pl.when(odd)(red_near.wait)
        for cp in (gs1n, gs2n, gs3n, img_n, mn, hn, n1, n2, n3, n4):
            cp.wait()
        ln.drain()

    pl.run_scoped(block_back, *[pltpu.VMEM(*v) for v in LATE.values()])


LATE = dict(
    zst=((2, 3, 3, 2, 2, 32, 256), BF16),
    psm=((9, 2, 2, 32, 256), BF16),
    psh=((9, 2, 2, 32, 256), BF16),
    fnr=((128, 512), BF16),
    fnl=((32, 1024), BF16),
    fnm=((9, 32, 256), BF16),
    fnf=((128, 256), BF16),
    pg=((2, 2, 32, 256), BF16),
    clss=((32, 128), F32),
    clso=((32, 128), F32),
    u3=((320, 1024), F32),
    dp3=((320, 1024), BF16),
    d3m=((480, 768), BF16),
    dsum=((320, 1024), BF16),
    oimg=((160, 2048), BF16),
    pas1=((320, 256), BF16),
    pas2=((320, 256), BF16),
    dp1=((320, 256), BF16),
    dp2=((320, 256), BF16),
    wfov=((4, 2, 2, 128, 256), BF16),
    gr=((4, 2, 128, 512), BF16),
    gl=((4, 2, 2, 32, 1024), BF16),
    gq=((9, 4, 2, 2, 32, 256), BF16),
    gf=((4, 2, 2, 128, 256), BF16),
)


FINAL = dict(
    depth=((160, 512), BF16),
    logits=((2, 40, 80), BF16),
    img=((160, 2048), F32),
    first=((128, 512), F32),
    gain1=((1, 32), F32),
    shift1=((1, 32), F32),
    mid=((9, 32, 512), F32),
    gain2=((1, 32), F32),
    shift2=((1, 32), F32),
    last=((32, 2048), F32),
    gain3=((1, 128), F32),
    shift3=((1, 128), F32),
    red=((128, 512), F32),
    heads=((2, 9, 32, 512), F32),
    mess=((2, 9, 32, 512), F32),
    gates=((2, 32, 512), F32),
    cls=((32, 40), F32),
)


def widen_out(names, *refs):
    s = SimpleNamespace(**dict(zip(names, refs)))
    b = lax.axis_index("batch")
    used = [0]

    def move(src, dst):
        cp = pltpu.make_async_copy(src, dst, s.sems.at[used[0]])
        used[0] += 1
        cp.start()
        return cp

    done = [move(s.o_depth, s.depth), move(s.o_logits, s.logits)]
    wide = ["mess", "heads", "mid", "img", "last", "red", "first", "gates"]
    loads = {n: move(getattr(s, "o_" + n), getattr(s, "i_" + n)) for n in wide}
    small = [move(getattr(s, "o_" + n), getattr(s, "i_" + n)) for n in ("gs1", "gs2", "gs3", "cls")]
    for n in wide:
        loads[n].wait()
        src, dst = getattr(s, "i_" + n), getattr(s, "v_" + n)
        if n == "last":
            for i in range(8):
                for h in range(2):
                    lane = 128 * (2 * i + h)
                    dst[:, lane : lane + 128] = src[h, :, 128 * i : 128 * i + 128].astype(F32)
        elif n == "img":
            for i in range(0, 160, 32):
                dst[i : i + 32, :] = src[i : i + 32, :].astype(F32)
        elif len(src.shape) > 2:
            for i in range(src.shape[0]):
                dst[i] = src[i].astype(F32)
        else:
            dst[...] = src[...].astype(F32)
        done.append(move(dst, getattr(s, n)))
    for cp in small:
        cp.wait()
    quarter, spot = lax.div(b, np.int32(4)), lax.rem(b, np.int32(4))
    at = pl.ds(pl.multiple_of(128 * lax.rem(quarter, np.int32(2)), 128), 128)
    for n, layer in ((1, s.i_gs1), (2, s.i_gs2)):
        v = pltpu.roll(layer[lax.div(quarter, np.int32(2)), :, at], lax.rem(128 - 32 * spot, np.int32(128)), 1)
        for row, kind in ((1, "gain"), (0, "shift")):
            keep = getattr(s, "v_%s%d" % (kind, n))
            keep[...] = v[row : row + 1, 0:32]
            done.append(move(keep, getattr(s, "%s%d" % (kind, n))))
    block = lax.div(b, np.int32(2))
    at = pl.ds(pl.multiple_of(128 * lax.rem(block, np.int32(4)), 128), 128)
    v = s.i_gs3[lax.rem(b, np.int32(2)), :, at]
    low = lax.div(block, np.int32(4)) == 0
    s.v_shift3[...] = jnp.where(low, v[0:1], v[1:2])
    s.v_gain3[...] = jnp.where(low, v[2:3], v[3:4])
    done.append(move(s.v_shift3, s.shift3))
    done.append(move(s.v_gain3, s.gain3))
    s.v_cls[...] = s.i_cls[:, 0:40]
    done.append(move(s.v_cls, s.cls))
    for cp in done:
        cp.wait()


def fast(args):
    (
        images, crop_height, crop_width, w_first, gain_first, shift_first, w_middle, gain_middle, shift_middle,
        w_last, gain_last, shift_last, w_reduce, w_heads, w_message, w_gates, w_classes, depth_cot, class_cot,
    ) = args
    narrow = jnp.concatenate([gain_first, shift_first, gain_middle, shift_middle])
    gains = jnp.stack([narrow, gain_last, shift_last]).astype(F32)
    ins = (
        crop_height, crop_width, images.reshape(160, 2048), w_first, w_middle, w_last, w_reduce, w_gates, w_classes,
        w_heads, w_message, gains, depth_cot.reshape(160, 512), class_cot.transpose(0, 1, 3, 2).reshape(2, 40, 80),
    )
    names = list(INS) + list(OUTS) + list(SHAPES) + ["send_sems", "recv_sems", "near_sems"]
    smem, hbm, vmem = (pl.BlockSpec(memory_space=m) for m in (pltpu.SMEM, pltpu.HBM, pltpu.VMEM))
    spec = {"crop_h": smem, "crop_w": smem, "gains": vmem}
    outs = pl.pallas_call(
        functools.partial(body, names),
        out_shape=[jax.ShapeDtypeStruct(*v) for v in OUTS.values()],
        in_specs=[spec.get(n, hbm) for n in INS],
        out_specs=[hbm] * len(OUTS),
        scratch_shapes=[pltpu.VMEM(*v) for v in SHAPES.values()]
        + [pltpu.SemaphoreType.DMA((n,)) for n in (SENDS, RECVS, NEAR)],
        compiler_params=pltpu.CompilerParams(has_side_effects=True, collective_id=0, vmem_limit_bytes=64 * 2**20),
        name="residual_distill",
    )(*ins)
    o = dict(zip(OUTS, outs))
    taken = [n for n in OUTS if n.startswith("o_")]
    staged = {"i_" + n[2:]: OUTS[n] for n in taken if n not in ("o_depth", "o_logits")}
    staged.update({"v_" + n: v for n, v in FINAL.items() if n not in ("depth", "logits")})
    final = pl.pallas_call(
        functools.partial(widen_out, taken + list(FINAL) + list(staged) + ["sems"]),
        out_shape=[jax.ShapeDtypeStruct(*v) for v in FINAL.values()],
        in_specs=[hbm] * len(taken),
        out_specs=[hbm] * len(FINAL),
        scratch_shapes=[pltpu.VMEM(*v) for v in staged.values()] + [pltpu.SemaphoreType.DMA((40,))],
        compiler_params=pltpu.CompilerParams(vmem_limit_bytes=64 * 2**20),
        name="widen_out",
    )(*[o[n] for n in taken])
    f = dict(zip(FINAL, final))
    f["depth"] = f["depth"].reshape(1, 2, 80, 512)
    f["logits"] = f["logits"].reshape(1, 2, 40, 80).transpose(0, 1, 3, 2)
    f["img"] = f["img"].reshape(1, 2, 80, 2048)
    for n in ("gain1", "shift1", "gain2", "shift2", "gain3", "shift3"):
        f[n] = f[n].reshape(-1)
    return tuple(f.values())


def solution(mesh):
    def step(*args):
        if mesh.shape["batch"] == 16 and mesh.shape["rows"] == 2:
            return fast(args)
        return shards(*args)

    placed = (
        P("batch", "rows", None, None),
        P(),
        P(),
        P("batch", None),
        P("batch"),
        P("batch"),
        P(None, "batch", None),
        P("batch"),
        P("batch"),
        P("batch", None),
        P("batch"),
        P("batch"),
        P("batch", None),
        P("rows", None, "batch", None),
        P("rows", None, "batch", None),
        P(None, "batch", None),
        P("batch", None),
        P("batch", "rows", None, None),
        P("batch", "rows", None, None),
    )
    return jax.shard_map(
        step,
        mesh=mesh,
        in_specs=placed,
        out_specs=(
            P("batch", "rows", None, None),
            P("batch", "rows", None, None),
            P("batch", "rows", None, None),
            P("batch", None),
            P("batch"),
            P("batch"),
            P(None, "batch", None),
            P("batch"),
            P("batch"),
            P("batch", None),
            P("batch"),
            P("batch"),
            P("batch", None),
            P("rows", None, "batch", None),
            P("rows", None, "batch", None),
            P(None, "batch", None),
            P("batch", None),
        ),
        check_vma=False,
    )
```

```python
import functools
from types import SimpleNamespace

import numpy as np
import jax
import jax.numpy as jnp
from jax import lax
from jax.sharding import PartitionSpec as P
from jax.experimental import pallas as pl
from jax.experimental.pallas import tpu as pltpu

EPS = 1e-05
MESH = pl.DeviceIdType.MESH
F32 = jnp.float32
BF16 = jnp.bfloat16
ROOT = 0.7978845608028654
CUBE = 0.044715
SENDS = 121
RECVS = 196
NEAR = 21


def dot(left, right):
    return jnp.dot(left, right, preferred_element_type=F32)


def dot_last(left, right):
    return lax.dot_general(left, right, (((1,), (1,)), ((), ())), preferred_element_type=F32)


def dot_first(left, right):
    return lax.dot_general(left, right, (((0,), (0,)), ((), ())), preferred_element_type=F32)


def gelu_of(v):
    return 0.5 * v * (1.0 + jnp.tanh(ROOT * (v + CUBE * v * v * v)))


def slope_of(v):
    t = jnp.tanh(ROOT * (v + CUBE * v * v * v))
    return 0.5 * (1.0 + t) + 0.5 * v * (1.0 - t * t) * (ROOT * (1.0 + 3.0 * CUBE * v * v))


def rows_loop(total, chunk, step):
    def body(index, carry):
        step(pl.multiple_of(index * chunk, chunk))
        return carry

    lax.fori_loop(0, total // chunk, body, 0)


class Copy:
    def __init__(self, remote, links, send, recv, like):
        self.remote, self.links, self.send, self.recv, self.like = remote, links, send, recv, like
        self.scoped = like is None

    def wait_recv(self):
        if self.like is None:
            self.remote.wait_recv()
        else:
            ref = self.like(1)
            pltpu.make_async_copy(ref, ref, self.links.recv.at[self.recv]).wait()

    def wait_send(self):
        if self.like is None:
            self.remote.wait_send()
        else:
            ref = self.like(0)
            pltpu.make_async_copy(ref, ref, self.links.send.at[self.send]).wait()


class Group:
    scoped = True

    def __init__(self, links, send, recv, like):
        self.links, self.send, self.recv, self.like = links, send, recv, like

    def push(self, src, dst, device, when=None):
        self.links.start(src, dst, device, self.send, self.recv, when)

    def wait_recv(self):
        ref = self.like()
        pltpu.make_async_copy(ref, ref, self.links.recv.at[self.recv]).wait()

    def wait_send(self):
        ref = self.like()
        pltpu.make_async_copy(ref, ref, self.links.send.at[self.send]).wait()


class Near:
    def __init__(self, links, src, dst):
        self.links, self.index = links, links.local_free.pop(0)
        self.copy = pltpu.make_async_copy(src, dst, links.local.at[self.index])
        self.copy.start()

    def wait(self):
        self.copy.wait()
        self.links.local_free.insert(0, self.index)


class Links:
    def __init__(self, send, recv, local):
        self.send, self.recv, self.local = send, recv, local
        self.used = 0
        self.send_free = list(range(SENDS))
        self.local_free = list(range(NEAR - 4))
        self.open = []

    def start(self, src, dst, device, send, recv, when):
        remote = pltpu.make_async_remote_copy(
            src_ref=src,
            dst_ref=dst,
            send_sem=self.send.at[send],
            recv_sem=self.recv.at[recv],
            device_id=device,
            device_id_type=MESH,
        )
        if when is None:
            remote.start()
        else:
            pl.when(when)(remote.start)
        return remote

    def pair(self):
        self.used += 1
        return self.send_free.pop(0), self.used - 1

    def push(self, src, dst, device, when=None, like=None):
        send, recv = self.pair()
        cp = Copy(self.start(src, dst, device, send, recv, when), self, send, recv, like)
        self.open.append((cp, when))
        return cp

    def group(self, like, when=None):
        cp = Group(self, *self.pair(), like)
        self.open.append((cp, when))
        return cp

    def near(self, src, dst):
        return Near(self, src, dst)

    def drain(self, scoped=False):
        kept = []
        for cp, when in self.open:
            if scoped and not cp.scoped:
                kept.append((cp, when))
                continue
            if when is None:
                cp.wait_send()
            else:
                pl.when(when)(cp.wait_send)
            self.send_free.insert(0, cp.send)
        self.open = kept


def wait(copies, when=None):
    def run():
        for cp in copies:
            cp.wait_recv()

    if when is None:
        run()
    else:
        pl.when(when)(run)


def lanes(mask, width):
    return jnp.concatenate([mask] * (width // 128), axis=1) if width > 128 else mask


def padded_2(cells, sides, width):
    for axis, dim in sides:
        count = lax.axis_size(axis)
        ends = count - 1
        head = lax.slice_in_dim(cells, 0, width, axis=dim)
        tail = lax.slice_in_dim(cells, cells.shape[dim] - width, cells.shape[dim], axis=dim)
        cells = jnp.concatenate(
            [
                lax.ppermute(tail, axis, [(i, (i + 1) % count) for i in range(ends)]),
                cells,
                lax.ppermute(head, axis, [((i + 1) % count, i) for i in range(ends)]),
            ],
            axis=dim,
        )
    return cells


def gelu_tanh(values):
    return jax.nn.gelu(values, approximate=True)


def gelu_slope(values, upstream):
    return jax.vjp(gelu_tanh, values)[1](upstream)[0]


def project(values, weight):
    return jnp.einsum("nrcj,jk->nrck", values, weight, preferred_element_type=jnp.float32)


def project_back(upstream, weight):
    return jnp.einsum("nrck,jk->nrcj", upstream, weight, preferred_element_type=jnp.float32)


def outer_sum(values, upstream):
    return jnp.einsum("nrcj,nrck->jk", values, upstream, preferred_element_type=jnp.float32)


def widen(padded):
    return jnp.pad(padded, ((0, 0), (0, 0), (1, 1), (0, 0)))


def halo_value(values):
    return padded_2(values, (("rows", 1),), 1)


def halo_grad(values):
    return padded_2(values, (("rows", 1),), 1)


def conv_apply(padded, kernel):
    row_count = padded.shape[1] - 2
    col_count = padded.shape[2]
    widened = widen(padded)
    running = jnp.zeros((padded.shape[0], row_count, col_count, kernel.shape[2]), jnp.float32)
    for tap_index in range(9):
        shift_down = tap_index // 3
        shift_right = tap_index % 3
        running = running + project(
            widened[
                :, shift_down : shift_down + row_count, shift_right : shift_right + col_count, :
            ],
            kernel[tap_index],
        )
    return running


def conv_kernel_grad(padded, upstream):
    row_count = upstream.shape[1]
    col_count = upstream.shape[2]
    widened = widen(padded)
    return jnp.stack(
        [
            outer_sum(
                widened[
                    :,
                    tap_index // 3 : tap_index // 3 + row_count,
                    tap_index % 3 : tap_index % 3 + col_count,
                    :,
                ],
                upstream,
            )
            for tap_index in range(9)
        ]
    )


def conv_input_grad(padded_grad, kernel):
    row_count = padded_grad.shape[1] - 2
    col_count = padded_grad.shape[2]
    widened = widen(padded_grad)
    running = jnp.zeros((padded_grad.shape[0], row_count, col_count, kernel.shape[1]), jnp.float32)
    for tap_index in range(9):
        shift_down = tap_index // 3
        shift_right = tap_index % 3
        running = running + project_back(
            widened[
                :,
                2 - shift_down : 2 - shift_down + row_count,
                2 - shift_right : 2 - shift_right + col_count,
                :,
            ],
            kernel[tap_index],
        )
    return running


def crop_mask(height, width, first_row, row_count, col_count):
    row_ids = first_row + jnp.arange(row_count, dtype=jnp.int32)
    col_ids = jnp.arange(col_count, dtype=jnp.int32)
    inside = (row_ids[None, :, None] < height[:, None, None]) & (
        col_ids[None, None, :] < width[:, None, None]
    )
    return inside.astype(jnp.float32)[..., None]


def norm_forward(pre_act, pixel_mask, gain_vec, shift_vec, valid_count):
    sums = jnp.sum(pre_act * pixel_mask, axis=(0, 1, 2))
    squares = jnp.sum(pre_act * pre_act * pixel_mask, axis=(0, 1, 2))
    sums, squares = lax.psum((sums, squares), ("batch", "rows"))
    mean_vec = sums / valid_count
    inv_std = lax.rsqrt(squares / valid_count - mean_vec * mean_vec + EPS)
    normal = (pre_act - mean_vec) * inv_std
    return (normal, inv_std, normal * gain_vec + shift_vec)


def norm_backward(upstream, normal, inv_std, gain_vec, pixel_mask, valid_count):
    shift_part = jnp.sum(upstream, axis=(0, 1, 2))
    gain_part = jnp.sum(upstream * normal, axis=(0, 1, 2))
    shift_part, gain_part = lax.psum((shift_part, gain_part), ("batch", "rows"))
    d_pre = (
        pixel_mask
        * gain_vec
        * inv_std
        * (upstream - shift_part / valid_count - normal * gain_part / valid_count)
    )
    return (d_pre, gain_part, shift_part)


def task_forward(padded_in, heads, messages, pixel_mask, pad_rows):
    pre_list = []
    feat_list = []
    padded_feats = []
    message_list = []
    for task in range(heads.shape[0]):
        pre_act = conv_apply(padded_in, heads[task])
        feature = (gelu_tanh(pre_act) * pixel_mask).astype(jnp.bfloat16)
        padded_feat = pad_rows(feature)
        pre_list.append(pre_act)
        feat_list.append(feature)
        padded_feats.append(padded_feat)
        message_list.append(conv_apply(padded_feat, messages[task]).astype(jnp.bfloat16))
    return (pre_list, feat_list, padded_feats, message_list)


def task_backward(
    padded_in,
    heads,
    messages,
    pixel_mask,
    pre_list,
    padded_feats,
    feat_grads,
    message_grads,
    pad_grad,
):
    input_grad = jnp.zeros(
        padded_in.shape[:1] + (padded_in.shape[1] - 2,) + padded_in.shape[2:], jnp.float32
    )
    head_grads = []
    kernel_grads = []
    for task in range(heads.shape[0]):
        low_message = message_grads[task].astype(jnp.bfloat16)
        kernel_grads.append(conv_kernel_grad(padded_feats[task], low_message))
        feat_grad = feat_grads[task] + conv_input_grad(pad_grad(low_message), messages[task])
        low_pre = gelu_slope(pre_list[task], feat_grad * pixel_mask).astype(jnp.bfloat16)
        head_grads.append(conv_kernel_grad(padded_in, low_pre))
        input_grad = input_grad + conv_input_grad(pad_grad(low_pre), heads[task])
    return (input_grad, jnp.stack(head_grads), jnp.stack(kernel_grads))


def streams_forward(features, messages, gates_all, classes_all, pixel_mask):
    gate_depth = jax.nn.sigmoid(project(features[0], gates_all[0]))
    gate_class = jax.nn.sigmoid(project(features[3], gates_all[1]))
    depth_sum = (
        messages[1].astype(jnp.float32)
        + messages[2].astype(jnp.float32)
        + messages[3].astype(jnp.float32)
    )
    class_sum = (
        messages[0].astype(jnp.float32)
        + messages[1].astype(jnp.float32)
        + messages[2].astype(jnp.float32)
    )
    depth_stream = (features[0].astype(jnp.float32) + gate_depth * depth_sum) * pixel_mask
    merged = (features[3].astype(jnp.float32) + gate_class * class_sum).astype(jnp.bfloat16)
    class_logits = project(merged, classes_all) * pixel_mask
    return (depth_stream, class_logits, merged, gate_depth, gate_class, depth_sum, class_sum)


def streams_backward(
    features,
    merged,
    gate_depth,
    gate_class,
    depth_sum,
    class_sum,
    depth_cot,
    class_cot,
    gates_all,
    classes_all,
    pixel_mask,
):
    depth_grad = depth_cot.astype(jnp.float32) * pixel_mask
    logit_grad = (class_cot.astype(jnp.float32) * pixel_mask).astype(jnp.bfloat16)
    grad_classes = outer_sum(merged, logit_grad)
    merged_grad = project_back(logit_grad, classes_all)
    gate_depth_grad = (depth_grad * depth_sum * gate_depth * (1.0 - gate_depth)).astype(
        jnp.bfloat16
    )
    gate_class_grad = (merged_grad * class_sum * gate_class * (1.0 - gate_class)).astype(
        jnp.bfloat16
    )
    grad_gates = jnp.stack(
        [outer_sum(features[0], gate_depth_grad), outer_sum(features[3], gate_class_grad)]
    )
    depth_feat = depth_grad + project_back(gate_depth_grad, gates_all[0])
    class_feat = merged_grad + project_back(gate_class_grad, gates_all[1])
    depth_message = depth_grad * gate_depth
    class_message = merged_grad * gate_class
    nothing = jnp.zeros_like(depth_grad)
    feat_grads = [depth_feat, nothing, nothing, class_feat]
    message_grads = [
        class_message,
        depth_message + class_message,
        depth_message + class_message,
        depth_message,
    ]
    return (feat_grads, message_grads, grad_gates, grad_classes)


def shards(
    images,
    crop_height,
    crop_width,
    w_first,
    gain_first,
    shift_first,
    w_middle,
    gain_middle,
    shift_middle,
    w_last,
    gain_last,
    shift_last,
    w_reduce,
    w_heads,
    w_message,
    w_gates,
    w_classes,
    depth_cot,
    class_cot,
):
    image_index = lax.axis_index("batch")
    batch_count = lax.axis_size("batch")
    row_count = images.shape[1]
    col_count = images.shape[2]
    height = lax.dynamic_slice_in_dim(crop_height, image_index, 1, 0)
    width = lax.dynamic_slice_in_dim(crop_width, image_index, 1, 0)
    pixel_mask = crop_mask(height, width, lax.axis_index("rows") * row_count, row_count, col_count)
    valid_count = jnp.sum(crop_height * crop_width).astype(jnp.float32)
    gathered = (
        lax.all_gather(w_first, "batch", axis=0, tiled=True),
        lax.all_gather(w_middle, "batch", axis=1, tiled=True),
        lax.all_gather(w_last, "batch", axis=0, tiled=True),
        lax.all_gather(w_reduce, "batch", axis=0, tiled=True),
        lax.all_gather(w_gates, "batch", axis=1, tiled=True),
        lax.all_gather(w_classes, "batch", axis=0, tiled=True),
        lax.all_gather(gain_first, "batch", axis=0, tiled=True),
        lax.all_gather(shift_first, "batch", axis=0, tiled=True),
        lax.all_gather(gain_middle, "batch", axis=0, tiled=True),
        lax.all_gather(shift_middle, "batch", axis=0, tiled=True),
        lax.all_gather(gain_last, "batch", axis=0, tiled=True),
        lax.all_gather(shift_last, "batch", axis=0, tiled=True),
        lax.all_gather(w_heads, "batch", axis=2, tiled=True),
        lax.all_gather(w_message, "batch", axis=2, tiled=True),
    )
    first_all = gathered[0]
    middle_all = gathered[1]
    last_all = gathered[2]
    reduce_all = gathered[3]
    gates_all = gathered[4]
    classes_all = gathered[5]
    gain_one = gathered[6].astype(jnp.float32)
    shift_one = gathered[7].astype(jnp.float32)
    gain_two = gathered[8].astype(jnp.float32)
    shift_two = gathered[9].astype(jnp.float32)
    gain_three = gathered[10].astype(jnp.float32)
    shift_three = gathered[11].astype(jnp.float32)
    heads_own = gathered[12]
    message_own = gathered[13]
    masked_in = images.astype(jnp.float32) * pixel_mask
    low_in = masked_in.astype(jnp.bfloat16)
    pre_first = project(low_in, first_all)
    normal_first, std_first, out_first = norm_forward(
        pre_first, pixel_mask, gain_one, shift_one, valid_count
    )
    act_first = (gelu_tanh(out_first) * pixel_mask).astype(jnp.bfloat16)
    padded_first = halo_value(act_first)
    pre_middle = conv_apply(padded_first, middle_all)
    normal_middle, std_middle, out_middle = norm_forward(
        pre_middle, pixel_mask, gain_two, shift_two, valid_count
    )
    act_middle = (gelu_tanh(out_middle) * pixel_mask).astype(jnp.bfloat16)
    pre_last = project(act_middle, last_all)
    normal_last, std_last, out_last = norm_forward(
        pre_last, pixel_mask, gain_three, shift_three, valid_count
    )
    summed = out_last + masked_in
    block_out = (gelu_tanh(summed) * pixel_mask).astype(jnp.bfloat16)
    low_reduced = project(block_out, reduce_all).astype(jnp.bfloat16)
    heads_all, message_all = (
        lax.all_gather(heads_own, "rows", axis=0, tiled=True),
        lax.all_gather(message_own, "rows", axis=0, tiled=True),
    )
    padded_in = halo_value(low_reduced)
    pre_list, feat_list, padded_feats, message_list = task_forward(
        padded_in, heads_all, message_all, pixel_mask, halo_value
    )
    depth_stream, class_logits, merged, gate_depth, gate_class, depth_sum, class_sum = (
        streams_forward(feat_list, message_list, gates_all, classes_all, pixel_mask)
    )
    feat_grads, message_grads, grad_gates, grad_classes = streams_backward(
        feat_list,
        merged,
        gate_depth,
        gate_class,
        depth_sum,
        class_sum,
        depth_cot,
        class_cot,
        gates_all,
        classes_all,
        pixel_mask,
    )
    reduced_grad, grad_heads, grad_message = task_backward(
        padded_in,
        heads_all,
        message_all,
        pixel_mask,
        pre_list,
        padded_feats,
        feat_grads,
        message_grads,
        halo_grad,
    )
    low_reduced_grad = reduced_grad.astype(jnp.bfloat16)
    grad_reduce = outer_sum(block_out, low_reduced_grad)
    block_grad = project_back(low_reduced_grad, reduce_all)
    sum_grad = gelu_slope(summed, block_grad * pixel_mask)
    d_last, gain_grad_three, shift_grad_three = norm_backward(
        sum_grad, normal_last, std_last, gain_three, pixel_mask, valid_count
    )
    low_last = d_last.astype(jnp.bfloat16)
    grad_last = outer_sum(act_middle, low_last)
    middle_grad = project_back(low_last, last_all)
    d_middle, gain_grad_two, shift_grad_two = norm_backward(
        gelu_slope(out_middle, middle_grad * pixel_mask),
        normal_middle,
        std_middle,
        gain_two,
        pixel_mask,
        valid_count,
    )
    low_middle = d_middle.astype(jnp.bfloat16)
    grad_middle = conv_kernel_grad(padded_first, low_middle)
    first_grad = conv_input_grad(halo_grad(low_middle), middle_all)
    d_first, gain_grad_one, shift_grad_one = norm_backward(
        gelu_slope(out_first, first_grad * pixel_mask),
        normal_first,
        std_first,
        gain_one,
        pixel_mask,
        valid_count,
    )
    low_first = d_first.astype(jnp.bfloat16)
    grad_first = outer_sum(low_in, low_first)
    image_grad = (project_back(low_first, first_all) + sum_grad) * pixel_mask
    summed_grads = (
        lax.psum_scatter(grad_first, "batch", scatter_dimension=0, tiled=True),
        lax.psum_scatter(grad_middle, "batch", scatter_dimension=1, tiled=True),
        lax.psum_scatter(grad_last, "batch", scatter_dimension=0, tiled=True),
        lax.psum_scatter(grad_reduce, "batch", scatter_dimension=0, tiled=True),
        lax.psum_scatter(grad_gates, "batch", scatter_dimension=1, tiled=True),
        lax.psum_scatter(grad_classes, "batch", scatter_dimension=0, tiled=True),
        lax.psum_scatter(grad_heads, "batch", scatter_dimension=2, tiled=True),
        lax.psum_scatter(grad_message, "batch", scatter_dimension=2, tiled=True),
    )
    shared = (
        lax.psum(summed_grads[0].astype(jnp.bfloat16), "rows").astype(jnp.float32),
        lax.psum(summed_grads[1].astype(jnp.bfloat16), "rows").astype(jnp.float32),
        lax.psum(summed_grads[2].astype(jnp.bfloat16), "rows").astype(jnp.float32),
        lax.psum(summed_grads[3].astype(jnp.bfloat16), "rows").astype(jnp.float32),
        lax.psum(summed_grads[4].astype(jnp.bfloat16), "rows").astype(jnp.float32),
        lax.psum(summed_grads[5].astype(jnp.bfloat16), "rows").astype(jnp.float32),
    )
    heads_out, message_out = (
        lax.psum_scatter(
            summed_grads[6].astype(jnp.bfloat16), "rows", scatter_dimension=0, tiled=True
        ).astype(jnp.float32),
        lax.psum_scatter(
            summed_grads[7].astype(jnp.bfloat16), "rows", scatter_dimension=0, tiled=True
        ).astype(jnp.float32),
    )

    def own_share(member):
        share = member.shape[0] // batch_count
        return lax.dynamic_slice_in_dim(member, image_index * share, share, 0)

    return (
        depth_stream.astype(jnp.bfloat16),
        class_logits.astype(jnp.bfloat16),
        image_grad,
        shared[0],
        own_share(gain_grad_one),
        own_share(shift_grad_one),
        shared[1],
        own_share(gain_grad_two),
        own_share(shift_grad_two),
        shared[2],
        own_share(gain_grad_three),
        own_share(shift_grad_three),
        shared[3],
        heads_out,
        message_out,
        shared[4],
        shared[5],
    )


BEHIND = (0, 1, 2, 3, 4, 5, )

SHAPES = dict(
    wf=((4, 2, 2, 128, 256), BF16),
    wm=((9, 4, 2, 2, 32, 256), BF16),
    wl=((4, 2, 2, 32, 1024), BF16),
    wr=((4, 2, 128, 512), BF16),
    wc=((16, 32, 128), BF16),
    wcs=((32, 128), BF16),
    gains=((8, 128), F32),
    wcv=((32, 40), BF16),
    cct=((2, 40, 80), BF16),
    ctf=((128, 128), F32),
    xh=((320, 1024), BF16),
    wh=((9, 4, 2, 2, 32, 256), BF16),
    wq=((9, 4, 2, 2, 32, 256), BF16),
    wg=((4, 2, 2, 32, 256), BF16),
    xall=((320, 2048), BF16),
    maskp=((1280, 128), F32),
    pre1=((320, 256), F32),
    pre2=((320, 256), F32),
    pre3=((320, 1024), F32),
    bnp1=((8, 256), F32),
    bnp2=((8, 256), F32),
    bnp3=((8, 1024), F32),
    a1=((320, 512), BF16),
    a2=((320, 512), BF16),
    a3=((480, 1536), BF16),
    blk=((320, 1024), BF16),
    rps=((160, 512), BF16),
    rpr=((160, 512), BF16),
    rbuf=((1280, 512), BF16),
    fown=((1280, 256), BF16),
    ffull=((1280, 512), BF16),
    msgb=((1280, 256), BF16),
    gateb=((1280, 256), BF16),
    mrecv=((4, 160, 512), BF16),
    dm=((4, 160, 512), BF16),
    eu=((2, 160, 512), BF16),
    dcotv=((160, 512), BF16),
    ccotv=((160, 128), BF16),
    olt=((2, 40, 80), BF16),
    ods=((160, 512), BF16),
    olg=((160, 128), BF16),
    mrg=((160, 512), BF16),
    fg=((2, 2, 160, 512), BF16),
    dmg=((1280, 256), BF16),
    exg=((2, 1280, 256), BF16),
    gm=((9, 4, 2, 2, 32, 256), BF16),
    gh=((9, 4, 2, 2, 32, 256), BF16),
    gg=((4, 2, 2, 32, 256), BF16),
    rg=((3, 2, 2, 32, 256), BF16),
    hop=((2, 9, 2, 2, 32, 256), BF16),
    gcls=((16, 32, 128), BF16),
    rcls=((15, 32, 128), BF16),
    clsr=((32, 128), F32),
    dfs=((1280, 256), BF16),
    dfr=((1280, 256), BF16),
    drs=((640, 512), BF16),
    drr=((640, 512), BF16),
    dro=((3, 160, 512), BF16),
    dred=((320, 512), BF16),
    dsr=((160, 1024), BF16),
    par2=((320, 256), BF16),
    par1=((320, 256), BF16),
    dp1r=((160, 256), BF16),
    rcr=((4, 2, 128, 512), BF16),
    rcl=((4, 2, 32, 1024), BF16),
    rcm=((9, 4, 2, 32, 256), BF16),
    rcf=((4, 2, 128, 256), BF16),
    ryr=((4, 128, 512), BF16),
    hpr=((128, 512), BF16),
    hpl=((32, 1024), BF16),
    hpm=((9, 32, 256), BF16),
    ryl=((4, 32, 1024), BF16),
    rym=((9, 4, 32, 256), BF16),
    ryf=((4, 128, 256), BF16),
    rzr=((3, 128, 512), BF16),
    rzl=((3, 32, 1024), BF16),
    rzm=((3, 9, 32, 256), BF16),
    rzf=((3, 128, 256), BF16),
)
for _i, _w in enumerate((256, 256, 512, 512, 256, 256)):
    SHAPES["am%d" % _i] = ((8, _w), F32)
    SHAPES["as%d" % _i] = ((8, _w), F32)
    SHAPES["at%d" % _i] = ((8, _w), F32)
    SHAPES["ar%d" % _i] = ((3, 8, _w), F32)
    SHAPES["az%d" % _i] = ((3, 8, _w), F32)

INS = (
    "crop_h", "crop_w", "images", "first", "middle", "last", "reduce", "gates",
    "classes", "heads", "messages", "gain1", "shift1", "gain2", "shift2", "gain3", "shift3", "dcot", "ccot",
)
OUTS = dict(
    o_depth=((160, 512), BF16),
    o_logits=((2, 40, 80), BF16),
    o_img=((160, 2048), BF16),
    o_first=((128, 512), BF16),
    o_gs1=((2, 8, 256), F32),
    o_mid=((9, 32, 512), BF16),
    o_gs2=((2, 8, 256), F32),
    o_last=((2, 32, 1024), BF16),
    o_gs3=((2, 8, 512), F32),
    o_red=((128, 512), BF16),
    o_heads=((2, 9, 32, 512), BF16),
    o_mess=((2, 9, 32, 512), BF16),
    o_gates=((2, 32, 512), BF16),
    o_cls=((32, 128), F32),
    rm=((3, 9, 2, 2, 32, 256), BF16),
    rh=((3, 9, 2, 2, 32, 256), BF16),
    wfo=((4, 2, 2, 128, 256), BF16),
    st_h=((9, 32, 512), BF16),
    st_m=((9, 32, 512), BF16),
)


def shift_columns(v):
    rows, width = v.shape
    col = lax.broadcasted_iota(jnp.int32, (rows, width), 0)
    left = jnp.where(col == 0, 0.0, pltpu.roll(v, 1, 0))
    right = jnp.where(col == rows - 1, 0.0, pltpu.roll(v, rows - 1, 0))
    return left, right


def spread(src, dst, n_img, width):
    zero = jnp.zeros((80, 3 * width), BF16)
    for pad in range(n_img + 1):
        dst[pl.ds(pad * 400, 80), :] = zero

    def body(i, carry):
        v = src[pl.ds(pl.multiple_of(i * 80, 16), 80), :]
        left, right = shift_columns(v.astype(F32))
        row = pl.multiple_of((i + lax.div(i, np.int32(4)) + 1) * 80, 16)
        dst[pl.ds(row, 80), 0:width] = left.astype(BF16)
        dst[pl.ds(row, 80), width : 2 * width] = v
        dst[pl.ds(row, 80), 2 * width : 3 * width] = right.astype(BF16)
        return carry

    lax.fori_loop(0, 4 * n_img, body, 0)


def conv_rows(a3, w, img):
    acc = None
    for a in range(3):
        base = pl.multiple_of((5 * img + a) * 80, 16)
        part = dot(a3[pl.ds(base, 320), :], w[3 * a : 3 * a + 3].reshape(1536, 256))
        acc = part if acc is None else acc + part
    return acc


def conv_back(d3, w, img):
    acc = None
    for a in range(3):
        for q in range(3):
            base = pl.multiple_of((5 * img + a) * 80, 16)
            tap = 3 * (2 - a) + (2 - q)
            part = dot_last(d3[pl.ds(base, 320), 256 * q : 256 * q + 256], w[tap].reshape(512, 256))
            acc = part if acc is None else acc + part
    return acc


def conv_weight(a3, d3, out, n_img, first, last):
    depth = (5 * n_img - 1) * 80

    def body(tap, carry):
        a = lax.div(tap, np.int32(3))
        q = tap - 3 * a
        left = a3[pl.ds(pl.multiple_of(a * 80, 16), depth), pl.ds(pl.multiple_of(q * 512, 128), 512)]
        out[tap] = dot_first(left, d3[pl.ds(80, depth), 256:512]).astype(BF16).reshape(out.shape[1:])
        return carry

    lax.fori_loop(first, last, body, 0)


def body(names, *refs):
    s = SimpleNamespace(**dict(zip(names, refs)))
    b, r = lax.axis_index("batch"), lax.axis_index("rows")
    z = lax.div(b, np.int32(4))
    y = lax.rem(lax.div(b, np.int32(2)), np.int32(2))
    c = lax.rem(b, np.int32(2))
    ln = Links(s.send_sems, s.recv_sems, s.near_sems)
    half, fhalf = 256 * r, 256 * c

    def dev(zz, yy, cc, rr):
        return (4 * zz + 2 * yy + cc, rr)

    def zk(k):
        return lax.rem(z + k, np.int32(4))

    core, ypeer, xpeer = dev(z, y, 1 - c, r), dev(z, 1 - y, c, r), dev(z, y, c, 1 - r)
    special = r == y
    plain = r != y
    task = 2 * r + y
    img = 2 * y + c
    own_px = pl.multiple_of(320 * img + 160 * r, 16)
    my_rows = pl.multiple_of(160 * r, 16)
    other_rows = pl.multiple_of(160 * (1 - r), 16)
    half = pl.multiple_of(half, 128)
    ohalf = pl.multiple_of(256 * (1 - r), 128)
    fhalf = pl.multiple_of(fhalf, 128)
    offsets = [(dr, dy, dc) for dr in range(2) for dy in range(2) for dc in range(2) if dr + dy + dc]

    def peer(dr, dy, dc):
        rr = 1 - r if dr else r
        yy = 1 - y if dy else y
        cc = 1 - c if dc else c
        return rr, yy, cc

    def px_of(rr, yy, cc):
        return pl.multiple_of(320 * (2 * yy + cc) + 160 * rr, 16)

    ends = (z == 0) | (z == 3)
    inner = jnp.logical_not(ends)
    not_first, not_last = z != 0, z != 3
    far_end = dev(jnp.where(z == 1, 0, 3), y, c, r)
    odd = c == r

    def both(p, q):
        return q if p is None else (p if q is None else p & q)

    def line_start(src, at, pair, when=None, relay=True):
        sides = ln.group(pair, when)
        for q in (1, 3):
            sides.push(src, at(z), dev(zk(q), y, c, r), when)
        across = ln.push(src, at(z), dev(zk(2), y, c, r), both(when, ends) if relay else when)
        return [sides, across, relay, None, None]

    def line_y(state, src, at, four, when=None):
        state[4] = ln.group(four, when)
        state[4].push(src, at(z), ypeer, when)

    def line_relay(state, at, when=None):
        sides, _, relay = state[:3]
        wait([sides], when)
        if relay:
            state[3] = ln.push(at(3 - z), at(3 - z), far_end, both(when, inner))

    def line_sides(state, at, when=None):
        ys = state[4]
        ys.push(at(zk(3)), at(zk(3)), ypeer, when)
        ys.push(at(zk(1)), at(zk(1)), ypeer, when)

    def line_last(state, at, col, when=None):
        _, across, relay, hand, ys = state
        if relay:
            wait([across], both(when, inner))
            wait([hand], both(when, ends))
        else:
            wait([across], when)
        ys.push(at(zk(2)), at(zk(2)), ypeer, when)
        return [ln.push(col(y), col(y), core, when)]

    def line_core(state, col, cores, when=None):
        wait([state[4]], when)
        cores.append(ln.push(col(1 - y), col(1 - y), core, when))

    def at_wf(zz):
        return s.wf.at[zz, y, c]

    def at_wm(zz):
        return s.wm.at[:, zz, y, c]

    def at_wl(zz):
        return s.wl.at[zz, y, c]

    def at_wr(zz):
        return s.wr.at[zz, y]

    def col_wf(yy):
        return s.wf.at[:, yy, c]

    def col_wm(yy):
        return s.wm.at[:, :, yy, c]

    def col_wl(yy):
        return s.wl.at[:, yy, c]

    def col_wr(yy):
        return s.wr.at[:, yy]

    near_last = [
        ln.near(s.last.at[:, pl.ds(pl.multiple_of((2 * i + r) * 128, 128), 128)], s.wl.at[z, y, c, :, 128 * i : 128 * i + 128])
        for i in range(8)
    ]
    near_own = ln.near(s.images, s.xall.at[pl.ds(my_rows, 160)])
    near_cls = ln.near(s.classes, s.wcv)
    near_wf = ln.near(s.first.at[:, pl.ds(half, 256)], s.wf.at[z, y, c])
    near_wm = ln.near(s.middle.at[:, :, pl.ds(half, 256)], s.wm.at[:, z, y, c])
    red_local = pltpu.make_async_copy(s.reduce, s.wr.at[z, y], s.near_sems.at[NEAR - 1])
    pl.when(odd)(red_local.start)
    near_late = [
        ln.near(s.dcot, s.dcotv),
        ln.near(s.ccot, s.cct),
        ln.near(s.heads.at[y, :, :, pl.ds(fhalf, 256)], s.wh.at[:, z, y, c]),
        ln.near(s.messages.at[y, :, :, pl.ds(fhalf, 256)], s.wq.at[:, z, y, c]),
        ln.near(s.gates.at[r, :, pl.ds(fhalf, 256)], s.wg.at[z, y, c]),
    ]
    barrier = pltpu.get_barrier_semaphore()
    friends = [
        dev(zk(q), 1 - y if j else y, 1 - c if i else c, r) for q in range(4) for j in range(2) for i in range(2) if q + j + i
    ] + [dev(z, 1 - y if j else y, 1 - c if i else c, 1 - r) for j in range(2) for i in range(2)]
    for friend in friends:
        pl.semaphore_signal(barrier, inc=1, device_id=friend, device_id_type=MESH)
    pl.semaphore_wait(barrier, len(friends))

    src_wf, src_wm = s.first.at[:, pl.ds(half, 256)], s.middle.at[:, :, pl.ds(half, 256)]
    go_wf = line_start(src_wf, at_wf, lambda: s.wf.at[0, 0], relay=False)
    line_y(go_wf, src_wf, at_wf, lambda: s.wf.at[:, 0, 0])
    img_x = ln.push(s.images, s.xall.at[pl.ds(my_rows, 160)], xpeer)
    go_wm = line_start(src_wm, at_wm, lambda: s.wm.at[:, 0, 0])
    line_y(go_wm, src_wm, at_wm, lambda: s.wm.at[:, :, 0, 0])
    for cp in near_last:
        cp.wait()

    for i in range(4):
        high, wide = s.crop_h[4 * z + i], s.crop_w[4 * z + i]
        for row in range(4):
            col = lax.broadcasted_iota(jnp.int32, (80, 128), 0)
            inside = (col < wide) & (row < high)
            s.maskp[pl.ds(320 * i + 80 * row, 80), :] = jnp.where(inside, 1.0, 0.0)
    total = s.crop_h[0] * s.crop_w[0]
    for i in range(1, 16):
        total = total + s.crop_h[i] * s.crop_w[i]
    count = total.astype(F32)
    mine = pl.multiple_of(320 * img, 16)

    def mask_at(base, rows, width):
        return lanes(s.maskp[pl.ds(mine + base, rows), :], width)

    s.gains[...] = jnp.zeros((8, 128), F32)
    for i, ref in enumerate((s.gain1, s.shift1, s.gain2, s.shift2)):
        s.gains[i : i + 1, 0:32] = ref[...].astype(F32)
    s.gains[4:5, :] = s.gain3[...].astype(F32)
    s.gains[5:6, :] = s.shift3[...].astype(F32)
    near_cls.wait()
    s.wcs[...] = jnp.zeros(s.wcs.shape, BF16)
    s.wcs[:, 0:40] = s.wcv[...]
    s.wc[b] = s.wcs[...]
    near_own.wait()
    near_wf.wait()
    line_relay(go_wf, at_wf)
    line_sides(go_wf, at_wf)
    cores_wf = line_last(go_wf, at_wf, col_wf)
    near_wm.wait()
    line_relay(go_wm, at_wm)
    go_wl = line_start(at_wl(z), at_wl, lambda: s.wl.at[0, 0])
    line_core(go_wf, col_wf, cores_wf)
    wait([img_x])

    def mask_x(base):
        rows = pl.ds(base, 80)
        v = (s.xall[rows, :].astype(F32) * mask_at(base, 80, 2048)).astype(BF16)
        s.xall[rows, :] = v
        for i in range(8):
            pick = jnp.where(r == 0, v[:, 256 * i : 256 * i + 128].astype(F32), v[:, 256 * i + 128 : 256 * i + 256].astype(F32))
            s.xh[rows, 128 * i : 128 * i + 128] = pick.astype(BF16)

    rows_loop(320, 80, mask_x)
    wait(cores_wf)
    wfo_x = ln.group(lambda: s.wf)
    for zz in (0, 1):
        wfo_x.push(s.wf.at[zz], s.wfo.at[zz], xpeer)

    def task_push(src, dst, lo, hi, staged):
        yy = 1 - y if staged else y
        taps = hi - lo
        sides = ln.group(lambda: s.rbuf.at[0 : 80 * taps])
        across = ln.group(lambda: dst.at[lo:hi, 0, 0], ends)
        for q in (1, 3, 2, 0):
            for i in range(2):
                if q + i == 0:
                    continue
                cc = 1 - c if i else c
                (across if q == 2 else sides).push(
                    src.at[lo:hi, :, pl.ds(pl.multiple_of(256 * cc, 128), 256)],
                    dst.at[lo:hi, z, yy, c],
                    dev(zk(q) if q else z, y, cc, r),
                    ends if q == 2 else None,
                )
        return sides, across, lo, hi, yy

    def task_relay(state, dst):
        sides, across, lo, hi, yy = state
        wait([sides])
        hand = ln.push(dst.at[lo:hi, 3 - z, yy], dst.at[lo:hi, 3 - z, yy], far_end, inner)
        return across, hand

    def task_ready(state):
        across, hand = state
        wait([across], inner)
        wait([hand], ends)

    def plane_start(n):
        m, ar = (getattr(s, p + str(n)) for p in ("am", "ar"))
        one = ln.group(lambda: ar)
        for i in (1, 2, 3):
            yy = 1 - y if i & 2 else y
            cc = 1 - c if i & 1 else c
            one.push(m, ar.at[i - 1], dev(z, yy, cc, r))
        return one

    def plane_end(n, one):
        m, sm, ar = (getattr(s, p + str(n)) for p in ("am", "as", "ar"))
        wait([one])
        sm[...] = (m[...] + ar[0]) + (ar[1] + ar[2])

    def reduce_plane(n):
        plane_end(n, plane_start(n))

    def reduce_line(n, bulk=None):
        sm, t, az = (getattr(s, p + str(n)) for p in ("as", "at", "az"))
        two = ln.group(lambda: az)
        for q in (1, 2, 3):
            two.push(sm, az.at[q - 1], dev(zk(q), y, c, r))
        if bulk is not None and n in BEHIND:
            bulk()
        wait([two])
        if bulk is not None and n not in BEHIND:
            bulk()
        t[...] = (sm[...] + az[0]) + (az[1] + az[2])
        return t[...]

    def stats_of(pre, width, msg):
        m = lanes(s.maskp[pl.ds(mine, 320), :], width)
        v = pre * m
        sums = jnp.sum(v, axis=0, keepdims=True)
        squares = jnp.sum(v * pre, axis=0, keepdims=True)
        return sums, squares

    def norm_terms(n, bnp, width, bulk=None):
        t = reduce_line(n, bulk)
        if width == 256:
            rows = [t[i : i + 1] for i in range(4)]
        else:
            rows = [jnp.concatenate([t[2 * i : 2 * i + 1], t[2 * i + 1 : 2 * i + 2]], axis=1) for i in range(4)]
        mean = rows[0] / count
        inv = lax.rsqrt(rows[1] / count - mean * mean + EPS)
        bnp[0:1], bnp[1:2], bnp[2:3], bnp[3:4] = mean, inv, rows[2], rows[3]

    quarter = lax.div(b, np.int32(4))
    spot = 32 * lax.rem(b, np.int32(4))

    def placed(n):
        lane = lax.broadcasted_iota(jnp.int32, (8, 128), 1)
        out = []
        for p in range(2):
            if n < 2:
                v = jnp.broadcast_to(s.gains[2 * n + p : 2 * n + p + 1, :], (8, 128))
                v = pltpu.roll(v, spot, 1)
                v = jnp.where((lane >= spot) & (lane < spot + 32), v, 0.0)
                out.append(jnp.concatenate([jnp.where(quarter == 2 * r + i, v[0:1], 0.0) for i in range(2)], axis=1))
            else:
                v = s.gains[4 + p : 5 + p, :]
                out.append(
                    [
                        jnp.concatenate(
                            [jnp.where(odd & (lax.div(b, np.int32(2)) == 4 * h + i), v, 0.0) for i in range(4)], axis=1
                        )
                        for h in range(2)
                    ]
                )
        return out

    def put_stats(n, first, second, width, layer):
        m = getattr(s, "am%d" % n)
        m[...] = jnp.zeros(m.shape, F32)
        if width == 256:
            m[0:1], m[1:2] = first, second
            if layer is not None:
                m[2:3], m[3:4] = placed(layer)
        else:
            m[0:1], m[1:2] = first[:, :512], first[:, 512:]
            m[2:3], m[3:4] = second[:, :512], second[:, 512:]
            if layer is not None:
                gain, shift = placed(layer)
                m[4:5], m[5:6] = gain
                m[6:7], m[7:8] = shift

    pre = dot(s.xall[...], s.wf[...].reshape(2048, 256))
    s.pre1[...] = pre
    first_sum, first_sq = stats_of(pre, 256, None)
    put_stats(0, first_sum, first_sq, 256, 0)
    plane_one = plane_start(0)
    line_sides(go_wm, at_wm)
    cores_wm = line_last(go_wm, at_wm, col_wm)
    plane_end(0, plane_one)
    line_y(go_wl, at_wl(z), at_wl, lambda: s.wl.at[:, 0, 0])
    pl.when(odd)(red_local.wait)
    heads = []
    late_wr = []

    def bulk_one():
        line_relay(go_wl, at_wl)
        line_sides(go_wl, at_wl)
        late_wr.append(line_start(s.reduce, at_wr, lambda: s.wr.at[0], odd))
        heads.append(task_push(s.heads.at[y], s.wh, 0, 7, False))

    norm_terms(0, s.bnp1, 256, bulk_one)
    go_wr = late_wr[0]

    def act_from(prebuf, bnp, dst):
        def step(base):
            x = (prebuf[pl.ds(base, 80), :] - bnp[0:1]) * bnp[1:2] * bnp[2:3] + bnp[3:4]
            dst[pl.ds(base, 80), pl.ds(half, 256)] = (gelu_of(x) * mask_at(base, 80, 256)).astype(BF16)

        rows_loop(320, 80, step)

    act_from(s.pre1, s.bnp1, s.a1)
    a1_x = ln.push(s.a1.at[:, pl.ds(half, 256)], s.a1.at[:, pl.ds(half, 256)], xpeer)
    line_core(go_wm, col_wm, cores_wm)
    cores_wl = line_last(go_wl, at_wl, col_wl)
    wait(cores_wm)
    wait([a1_x])
    wfo_x.push(s.wf.at[2], s.wfo.at[2], xpeer)
    spread(s.a1, s.a3, 1, 512)
    pre = conv_rows(s.a3, s.wm, 0)
    s.pre2[...] = pre
    first_sum, first_sq = stats_of(pre, 256, None)
    put_stats(1, first_sum, first_sq, 256, 1)
    plane_two = plane_start(1)
    over_h = ln.push(s.heads.at[1 - y], s.st_h, ypeer)
    plane_end(1, plane_two)
    relayed_h = []
    mess = []

    def mess_push(a, staged):
        return task_push(s.st_m if staged else s.messages.at[y], s.wq, 3 * a, 3 * a + 3, staged)

    def bulk_two():
        line_relay(go_wr, at_wr, odd)
        relayed_h.append(task_relay(heads[0], s.wh))
        heads.append(task_push(s.heads.at[y], s.wh, 7, 9, False))
        mess.append([mess_push(0, False)])

    norm_terms(1, s.bnp2, 256, bulk_two)
    line_y(go_wr, s.reduce, at_wr, lambda: s.wr.at[:, 0], odd)
    line_sides(go_wr, at_wr, odd)
    act_from(s.pre2, s.bnp2, s.a2)
    a2_x = ln.push(s.a2.at[:, pl.ds(half, 256)], s.a2.at[:, pl.ds(half, 256)], xpeer)
    line_core(go_wl, col_wl, cores_wl)
    cores_wr = line_last(go_wr, at_wr, col_wr, odd)
    wait(cores_wl)
    wait([a2_x])
    wfo_x.push(s.wf.at[3], s.wfo.at[3], xpeer)
    pre = dot(s.a2[...], s.wl[...].reshape(512, 1024))
    s.pre3[...] = pre
    first_sum, first_sq = stats_of(pre, 1024, None)
    put_stats(2, first_sum, first_sq, 1024, 2)
    plane_three = plane_start(2)
    over_m = ln.push(s.messages.at[1 - y], s.st_m, ypeer)
    plane_end(2, plane_three)
    def bulk_three():
        relayed_h.append(task_relay(heads[1], s.wh))
        heads.append(task_push(s.st_h, s.wh, 0, 5, True))
        heads.append(task_push(s.st_h, s.wh, 5, 9, True))

    wait([over_h])
    norm_terms(2, s.bnp3, 1024, bulk_three)
    staged_h = ln.near(s.st_h.at[:, :, pl.ds(fhalf, 256)], s.wh.at[:, z, 1 - y, c])
    gate_got = {}
    cls_got = ln.group(lambda: s.wc.at[0:15])
    for q in range(4):
        for j in range(2):
            if q + j:
                gate_got[q, j] = ln.group(lambda: s.wg.at[0, 0], (y == r) if j == 0 else (y != r))
            for i in range(2):
                if q + j + i == 0:
                    continue
                yy = 1 - y if j else y
                cc = 1 - c if i else c
                to = dev(zk(q) if q else z, yy, cc, r)
                cls_got.push(s.wcs, s.wc.at[b], to)
                src = s.gates.at[r, :, pl.ds(pl.multiple_of(256 * cc, 128), 256)]
                if q + j:
                    gate_got[q, j].push(src, s.wg.at[z, y, c], to, (y == r) if j == 0 else (y != r))
                else:
                    gate_got[0, 0] = ln.push(src, s.wg.at[z, y, c], to, y == r)

    def summed_at(base, rows):
        x = (s.pre3[pl.ds(base, rows), :] - s.bnp3[0:1]) * s.bnp3[1:2]
        return x, x * s.bnp3[2:3] + s.bnp3[3:4] + s.xh[pl.ds(base, rows), :].astype(F32)

    def block_step(base):
        _, v = summed_at(base, 32)
        s.blk[pl.ds(base, 32), :] = (gelu_of(v) * mask_at(base, 32, 1024)).astype(BF16)

    rows_loop(320, 32, block_step)
    line_core(go_wr, col_wr, cores_wr, odd)
    wait(cores_wr, jnp.logical_not(odd))
    wred = s.wr[...].reshape(1024, 512)
    s.rps[...] = dot(s.blk[pl.ds(other_rows, 160), :], wred).astype(BF16)
    red_x = ln.push(s.rps, s.rpr, xpeer)
    part = dot(s.blk[pl.ds(my_rows, 160), :], wred)
    wait([red_x])
    s.rbuf[pl.ds(own_px, 160), :] = (part + s.rpr[...].astype(F32)).astype(BF16)

    def block_of(rr, yy, cc, lo=0, n=160):
        return s.rbuf.at[pl.ds(pl.multiple_of(px_of(rr, yy, cc) + lo, 16), n)]

    for cp in near_late:
        cp.wait()
    own = block_of(r, y, c)
    g_x = ln.push(own, own, xpeer)
    g_y = ln.push(own, own, ypeer)
    g_c = ln.push(own, own, core)
    wait([g_x])
    relayed_h.append(task_relay(heads[2], s.wh))
    bx = block_of(1 - r, y, c, 0, 80)
    g_xy = ln.push(bx, bx, ypeer)
    wait([g_y])
    by = block_of(r, 1 - y, c, 80, 80)
    g_yx = ln.push(by, by, xpeer)
    bx = block_of(1 - r, y, c)
    g_c1 = ln.push(bx, bx, core)
    by = block_of(r, 1 - y, c)
    g_c2 = ln.push(by, by, core)
    relayed_h.append(task_relay(heads[3], s.wh))
    wait([g_xy, g_yx])
    bd = block_of(1 - r, 1 - y, c)
    g_c3 = ln.push(bd, bd, core)
    wait([over_m])
    staged_m = ln.near(s.st_m.at[:, :, pl.ds(fhalf, 256)], s.wq.at[:, z, 1 - y, c])
    mess[0].append(mess_push(0, True))
    mess.append([mess_push(1, False), mess_push(1, True)])
    mess.append([mess_push(2, False)])
    wait([g_c, g_c1, g_c2, g_c3])

    near_end = dev(jnp.where(z == 0, 1, 2), y, c, r)
    other_end = dev(jnp.where(z == 1, 3, 0), y, c, r)

    def grad_push(n, g, rm, lo, hi):
        def like(slot):
            return lambda side: rm.at[slot, lo:hi] if side else g.at[lo:hi, 0]

        got = {}
        for q in (1, 2, 3):
            direct = {1: not_last, 2: ends, 3: not_first}[q]
            got[q] = ln.push(g.at[lo:hi, zk(q)], rm.at[q - 1, lo:hi], dev(zk(q), y, c, r), direct, like(q - 1))
        hop = s.hop.at[n, lo:hi]
        got[0] = ln.push(
            g.at[lo:hi, 3 - z], hop, near_end, ends, lambda side: s.hop.at[n, lo:hi] if side else g.at[lo:hi, 0]
        )
        return got, n, g, rm, lo, hi

    def grad_hop(state):
        got, n, g, rm, lo, hi = state

        def add():
            got[0].wait_recv()
            far = jnp.where(z == 1, 3, 0)
            for t in range(lo, hi):
                s.hop[n, t] = (s.hop[n, t].astype(F32) + g[t, far].astype(F32)).astype(BF16)

        pl.when(inner)(add)
        got[4] = ln.push(
            s.hop.at[n, lo:hi], rm.at[1, lo:hi], other_end, inner,
            lambda side: rm.at[1, lo:hi] if side else s.hop.at[n, lo:hi],
        )

    def grad_wait(state):
        got = state[0]
        wait([got[1]], not_first)
        wait([got[3]], not_last)
        wait([got[2]], inner)
        wait([got[4]], ends)

    def tasks(r3, f3, d3, preh, dfull):
        spread(s.rbuf, r3, 4, 512)
        for part in relayed_h:
            task_ready(part)
        staged_h.wait()

        def head_step(i, carry):
            v = conv_rows(r3, s.wh, i)
            px = pl.multiple_of(i * 320, 16)
            preh[pl.ds(px, 320), :] = v
            return carry

        lax.fori_loop(0, 4, head_step, 0)

        def feat_step(base):
            m = lanes(s.maskp[pl.ds(base, 80), :], 256)
            s.fown[pl.ds(base, 80), :] = (gelu_of(preh[pl.ds(base, 80), :]) * m).astype(BF16)

        rows_loop(1280, 80, feat_step)
        f_c = ln.push(s.fown, s.ffull.at[:, pl.ds(fhalf, 256)], core)
        f_n = ln.near(s.fown, s.ffull.at[:, pl.ds(fhalf, 256)])

        def seven():
            return s.dmg.at[0:1120]

        def pieces(n):
            return lambda: s.dmg.at[0 : 160 * n]

        even = [o for o in offsets if (o[0] + o[1]) % 2 == 0]
        uneven = [o for o in offsets if (o[0] + o[1]) % 2]

        def to_owners(src, dst_of):
            got = [ln.group(pieces(len(o)), special) for o in (even, uneven)]
            for g, group in zip(got, (even, uneven)):
                for o in group:
                    rr, yy, cc = peer(*o)
                    g.push(src.at[pl.ds(px_of(rr, yy, cc), 160)], dst_of().at[:, pl.ds(fhalf, 256)], dev(z, yy, cc, rr), special)
            return got

        def from_tasks(got):
            wait([got[0]], special)
            wait([got[1]], plain)

        def to_tasks(src_of, dst):
            got = [ln.group(pieces(len(o)), w) for o, w in ((even, special), (uneven, plain))]
            for g, group, w in zip(got, (even, uneven), (special, plain)):
                for o in group:
                    rr, yy, cc = peer(*o)
                    ll = pl.ds(pl.multiple_of(256 * cc, 128), 256)
                    g.push(src_of(rr).at[:, ll], dst.at[pl.ds(own_px, 160)], dev(z, yy, cc, rr), w)
            return got

        def keep(dst, src):
            def run():
                dst[:, pl.ds(fhalf, 256)] = src[pl.ds(own_px, 160), :]

            return run

        pl.when(special)(keep(s.fg.at[r, 0], s.fown))
        f_n.wait()
        wait([f_c])

        def gate_ready():
            for cp in gate_got.values():
                cp.wait_recv()

        pl.when(special)(gate_ready)

        @pl.when(special)
        def _():
            def gate_step(base):
                v = dot(s.ffull[pl.ds(base, 320), :], s.wg[...].reshape(512, 256))
                s.gateb[pl.ds(base, 320), :] = (1.0 / (1.0 + jnp.exp(-v))).astype(BF16)

            rows_loop(1280, 320, gate_step)

        g_own = to_owners(s.gateb, lambda: s.fg.at[r, 1])
        pl.when(special)(keep(s.fg.at[r, 1], s.gateb))

        relayed = [[task_relay(p, s.wq) for p in mess[0]]]
        mess[2].append(mess_push(2, True))
        spread(s.ffull, f3, 4, 512)

        wait([cls_got])
        for i in range(2):
            s.ctf[...] = jnp.zeros((128, 128), F32)
            s.ctf[0:40, 0:80] = s.cct[i].astype(F32)
            turned = s.ctf[...].T
            s.ccotv[80 * i : 80 * i + 80, :] = turned[0:80, :].astype(BF16)
        from_tasks(g_own)

        def early_step(base):
            rows = pl.ds(base, 32)
            m = lanes(s.maskp[pl.ds(own_px + base, 32), :], 512)
            gd, gc = s.fg[0, 1, rows, :].astype(F32), s.fg[1, 1, rows, :].astype(F32)
            dj = (s.ccotv[rows, :].astype(F32) * m[:, :128]).astype(BF16)
            s.ccotv[rows, :] = dj
            dd = s.dcotv[rows, :].astype(F32) * m
            dmer = dot_last(dj, s.wc[...].reshape(512, 128))
            s.eu[0, rows, :] = dd.astype(BF16)
            s.eu[1, rows, :] = dmer.astype(BF16)
            down, up = dd * gd, dmer * gc
            both = (down + up).astype(BF16)
            s.dm[0, rows, :] = up.astype(BF16)
            s.dm[1, rows, :] = both
            s.dm[2, rows, :] = both
            s.dm[3, rows, :] = down.astype(BF16)

        rows_loop(160, 32, early_step)
        d_got = ln.group(seven)
        for o in offsets:
            rr, yy, cc = peer(*o)
            ll = pl.ds(pl.multiple_of(256 * cc, 128), 256)
            d_got.push(s.dm.at[2 * rr + yy, :, ll], s.dmg.at[pl.ds(own_px, 160)], dev(z, yy, cc, rr))
        s.dmg[pl.ds(own_px, 160), :] = s.dm[task, :, pl.ds(fhalf, 256)]

        @pl.when(special)
        def _():
            s.exg[0, pl.ds(own_px, 160), :] = s.eu[r, :, pl.ds(fhalf, 256)]

        @pl.when(jnp.logical_not(special))
        def _():
            s.exg[0] = jnp.zeros(s.exg.shape[1:], BF16)

        relayed.append([task_relay(p, s.wq) for p in mess[1]])

        def mess_conv(a):
            for p in relayed[a]:
                task_ready(p)

            def mess_step(i, carry):
                rows = pl.ds(pl.multiple_of(i * 320, 16), 320)
                base = pl.multiple_of((5 * i + a) * 80, 16)
                v = dot(f3[pl.ds(base, 320), :], s.wq[3 * a : 3 * a + 3].reshape(1536, 256))
                if a:
                    v = dfull[rows, 0:256] + v
                if a < 2:
                    dfull[rows, 0:256] = v
                else:
                    s.msgb[rows, :] = v.astype(BF16)
                return carry

            lax.fori_loop(0, 4, mess_step, 0)

        staged_m.wait()
        mess_conv(0)
        wait([d_got])
        f_own = to_owners(s.fown, lambda: s.fg.at[r, 0])
        u_got = to_tasks(lambda rr: s.eu.at[rr], s.exg.at[0])
        spread(s.dmg, d3, 4, 256)
        conv_weight(f3, d3, s.gm, 4, 0, 6)
        relayed.append([task_relay(p, s.wq) for p in mess[2]])
        gm_z = [grad_push(0, s.gm, s.rm, 0, 3), grad_push(0, s.gm, s.rm, 3, 6)]
        mess_conv(1)
        conv_weight(f3, d3, s.gm, 4, 6, 9)
        gm_z.append(grad_push(0, s.gm, s.rm, 6, 9))
        mess_conv(2)
        m_own = ln.group(seven)
        for o in offsets:
            rr, yy, cc = peer(*o)
            m_own.push(s.msgb.at[pl.ds(px_of(rr, yy, cc), 160)], s.mrecv.at[task, :, pl.ds(fhalf, 256)], dev(z, yy, cc, rr))
        keep(s.mrecv.at[task], s.msgb)()

        def back_step(i, carry):
            px = pl.multiple_of(i * 320, 16)
            dfull[pl.ds(px, 320), :] = conv_back(d3, s.wq, i)
            return carry

        lax.fori_loop(0, 4, back_step, 0)

        from_tasks(f_own)
        wait([m_own])

        def stream_step(base):
            rows = pl.ds(base, 32)
            m = lanes(s.maskp[pl.ds(own_px + base, 32), :], 512)
            m0, m1, m2, m3 = (s.mrecv[t, rows, :].astype(F32) for t in range(4))
            f0, f3_ = s.fg[0, 0, rows, :].astype(F32), s.fg[1, 0, rows, :].astype(F32)
            mid = m1 + m2
            sd, sc = mid + m3, m0 + mid
            gd, gc = s.fg[0, 1, rows, :].astype(F32), s.fg[1, 1, rows, :].astype(F32)
            s.ods[rows, :] = ((f0 + gd * sd) * m).astype(BF16)
            merged = (f3_ + gc * sc).astype(BF16)
            s.mrg[rows, :] = merged
            s.olg[rows, :] = (dot(merged, s.wc[...].reshape(512, 128)) * m[:, :128]).astype(BF16)
            dd, dmer = s.eu[0, rows, :].astype(F32), s.eu[1, rows, :].astype(F32)
            s.fg[0, 1, rows, :] = (dd * sd * gd * (1.0 - gd)).astype(BF16)
            s.fg[1, 1, rows, :] = (dmer * sc * gc * (1.0 - gc)).astype(BF16)

        rows_loop(160, 32, stream_step)
        e_got = to_tasks(lambda rr: s.fg.at[rr, 1], s.exg.at[1])

        @pl.when(special)
        def _():
            s.exg[1, pl.ds(own_px, 160), :] = s.fg[r, 1, :, pl.ds(fhalf, 256)]

        for i in range(2):
            s.ctf[...] = jnp.zeros((128, 128), F32)
            s.ctf[0:80, :] = s.olg[80 * i : 80 * i + 80, :].astype(F32)
            turned = s.ctf[...].T
            s.olt[i] = turned[0:40, 0:80].astype(BF16)
        out_near = [ln.near(s.ods, s.o_depth), ln.near(s.olt, s.o_logits)]
        s.gcls[...] = dot_first(s.mrg[...], s.ccotv[...]).astype(BF16).reshape(16, 32, 128)
        grad_hop(gm_z[0])
        wait(u_got + e_got, special)

        @pl.when(special)
        def _():
            def gate_back(base):
                rows = pl.ds(base, 320)
                dfull[rows, :] = dfull[rows, :] + dot_last(s.exg[1, rows, :], s.wg[...].reshape(512, 256))

            rows_loop(1280, 320, gate_back)

        chalf = pl.ds(pl.multiple_of(256 * (1 - c), 128), 256)

        def give(base):
            rows = pl.ds(base, 80)
            s.dfs[rows, :] = dfull[rows, chalf].astype(BF16)

        rows_loop(1280, 80, give)
        df_c = ln.push(s.dfs, s.dfr, core)

        @pl.when(special)
        def _():
            s.gg[...] = dot_first(s.ffull[...], s.exg[1]).astype(BF16).reshape(s.gg.shape)

        gg_z = [ln.push(s.gg.at[zk(k)], s.rg.at[k - 1], dev(zk(k), y, c, r), special, lambda side, k=k: s.rg.at[k - 1] if side else s.gg.at[0]) for k in (1, 2, 3)]
        cg = ln.group(lambda: s.rcls)
        n_cls = 0
        for q in range(4):
            for j in range(2):
                for i in range(2):
                    if q + j + i == 0:
                        continue
                    yy = 1 - y if j else y
                    cc = 1 - c if i else c
                    zz = zk(q) if q else z
                    cg.push(s.gcls.at[4 * zz + 2 * yy + cc], s.rcls.at[n_cls], dev(zz, yy, cc, r))
                    n_cls += 1
        wait([df_c])

        def dhead_step(base):
            rows = pl.ds(base, 80)
            m = lanes(s.maskp[rows, :], 256)
            d = dfull[rows, pl.ds(fhalf, 256)] + s.dfr[rows, :].astype(F32) + s.exg[0, rows, :].astype(F32)
            s.dmg[rows, :] = (slope_of(preh[rows, :]) * d * m).astype(BF16)

        rows_loop(1280, 80, dhead_step)
        spread(s.dmg, d3, 4, 256)

        def back_step2(i, carry):
            px = pl.multiple_of(i * 320, 16)
            dfull[pl.ds(px, 320), :] = conv_back(d3, s.wh, i)
            return carry

        lax.fori_loop(0, 4, back_step2, 0)
        for yy in range(2):
            src = pl.multiple_of(320 * (2 * yy) + 320 * (1 - c), 16)
            s.drs[pl.ds(320 * yy, 320), :] = dfull[pl.ds(src, 320), :].astype(BF16)
        dr_c = ln.push(s.drs, s.drr, core)
        grad_hop(gm_z[1])
        wait([dr_c])
        for yy in range(2):
            src = pl.multiple_of(320 * (2 * yy) + 320 * c, 16)
            rows = pl.ds(320 * yy, 320)
            s.drr[rows, :] = (dfull[pl.ds(src, 320), :] + s.drr[rows, :].astype(F32)).astype(BF16)
        ro = []
        for dr, dy in ((1, 0), (0, 1), (1, 1)):
            rr, yy, _ = peer(dr, dy, 0)
            src = s.drr.at[pl.ds(pl.multiple_of(320 * yy + 160 * rr, 16), 160)]
            ro.append(ln.push(src, s.dro.at[len(ro)], dev(z, yy, c, rr)))
        gh_z = []
        conv_weight(r3, d3, s.gh, 4, 0, 3)
        gh_z.append(grad_push(1, s.gh, s.rh, 0, 3))
        conv_weight(r3, d3, s.gh, 4, 3, 9)
        wait(ro)
        keep_rows = pl.ds(pl.multiple_of(320 * y + 160 * r, 16), 160)
        total_red = s.drr[keep_rows, :].astype(F32)
        for i in range(3):
            total_red = total_red + s.dro[i].astype(F32)
        s.dred[pl.ds(my_rows, 160), :] = total_red.astype(BF16)
        for cp in out_near:
            cp.wait()
        ln.drain(scoped=True)
        return cg, gm_z, gg_z, gh_z

    state = {}

    def scope_tasks(*scr):
        state["t"] = tasks(*scr)

    pl.run_scoped(
        scope_tasks,
        pltpu.VMEM((1680, 1536), BF16),
        pltpu.VMEM((1680, 1536), BF16),
        pltpu.VMEM((1680, 768), BF16),
        pltpu.VMEM((1280, 256), F32),
        pltpu.VMEM((1280, 512), F32),
    )
    cg, gm_z, gg_z, gh_z = state["t"]

    dr_x = ln.push(s.dred.at[pl.ds(my_rows, 160)], s.dred.at[pl.ds(my_rows, 160)], xpeer)

    def block_back(*late):
        for name, ref in zip(LATE, late):
            setattr(s, name, ref)
        gr, gl, gq, gf = s.gr, s.gl, s.gq, s.gf

        def to_core(g, rc, lead):
            at = g.at[:, :, :, 1 - c] if lead else g.at[:, :, 1 - c]
            return ln.push(at, rc, core)

        def add_core(g, rc, lead):
            if lead:
                for t in range(9):
                    rc[t] = (rc[t].astype(F32) + g[t, :, :, c].astype(F32)).astype(BF16)
            else:
                for t in range(rc.shape[0]):
                    rc[t] = (rc[t].astype(F32) + g[t, :, c].astype(F32)).astype(BF16)

        def to_y(rc, ry, lead):
            return ln.push(rc.at[:, :, 1 - y] if lead else rc.at[:, 1 - y], ry, ypeer)

        def add_y(rc, ry, lead):
            for t in range(ry.shape[0]):
                mine_y = rc[t, :, y] if lead else rc[t, y]
                ry[t] = (ry[t].astype(F32) + mine_y.astype(F32)).astype(BF16)

        def to_z(ry, rz, lead, when=None, hop=None):
            def part(zz):
                return ry.at[:, zz] if lead else ry.at[zz]

            got = {}
            for q in (1, 2, 3):
                direct = None if hop is None else {1: not_last, 2: ends, 3: not_first}[q]
                got[q] = ln.push(part(zk(q)), rz.at[q - 1], dev(zk(q), y, c, r), both(when, direct))
            if hop is not None:
                got[0] = ln.push(part(3 - z), hop, near_end, both(when, ends))
            return got, part, rz, hop, when

        def hop_z(state):
            got, part, rz, hop, when = state

            def add():
                got[0].wait_recv()
                hop[...] = (hop[...].astype(F32) + part(jnp.where(z == 1, 3, 0))[...].astype(F32)).astype(BF16)

            pl.when(both(when, inner))(add)
            got[4] = ln.push(hop, rz.at[1], other_end, both(when, inner))

        def wait_z(state):
            got, _, _, hop, when = state
            if hop is None:
                wait([got[1], got[2], got[3]], when)
            else:
                wait([got[1]], both(when, not_first))
                wait([got[3]], both(when, not_last))
                wait([got[2]], both(when, inner))
                wait([got[4]], both(when, ends))

        def add_z(ry, rz, fin, lead, hop=True):
            mine_z = (ry[:, z] if lead else ry[z]).astype(F32)
            v0, v2 = rz[0].astype(F32), rz[2].astype(F32)
            if hop:
                v0, v2 = jnp.where(z == 0, 0.0, v0), jnp.where(z == 3, 0.0, v2)
            fin[...] = ((mine_z + v0) + (rz[1].astype(F32) + v2)).astype(BF16)

        def task_out(states, rm, g, ps, out):
            for part in states:
                grad_wait(part)
            loads = [[ln.near(rm.at[q, 3 * part : 3 * part + 3], s.zst.at[part % 2, q]) for q in range(3)] for part in range(2)]
            for part in range(3):
                for cp in loads[part]:
                    cp.wait()
                v0 = s.zst.at[part % 2]
                for t in range(3):
                    first_in = jnp.where(z == 0, 0.0, v0[0, t].astype(F32))
                    third_in = jnp.where(z == 3, 0.0, v0[2, t].astype(F32))
                    v = g[3 * part + t, z].astype(F32) + first_in + (v0[1, t].astype(F32) + third_in)
                    ps[3 * part + t] = v.astype(BF16)
                if part == 0:
                    loads.append([ln.near(rm.at[q, 6:9], s.zst.at[0, q]) for q in range(3)])
            lanes_out = pl.ds(fhalf, 256)
            sent = []
            for i in (1, 2, 3):
                yy = 1 - y if i & 2 else y
                cc = 1 - c if i & 1 else c
                sent.append(ln.push(ps.at[:, yy, cc], out.at[y, :, :, lanes_out], dev(z, yy, cc, r)))
            return sent, ln.near(ps.at[:, y, c], out.at[y, :, :, lanes_out])

        wait([dr_x])

        def d3_step(i, carry):
            su, sux = carry
            rows = pl.ds(pl.multiple_of(i * 32, 16), 32)
            x, v = summed_at(i * 32, 32)
            u = slope_of(v) * s.u3[rows, :] * mask_at(i * 32, 32, 1024)
            s.u3[rows, :] = u
            s.dsum[rows, :] = u.astype(BF16)
            return su + jnp.sum(u, axis=0, keepdims=True), sux + jnp.sum(u * x, axis=0, keepdims=True)

        s.u3[...] = dot_last(s.dred[...], s.wr[...].reshape(1024, 512))
        nil = jnp.zeros((1, 1024), F32)
        su, sux = lax.fori_loop(0, 10, d3_step, (nil, nil))
        put_stats(3, su, sux, 1024, None)
        ar3 = plane_start(3)
        ds_x = ln.push(s.dsum.at[pl.ds(other_rows, 160)], s.dsr, xpeer)
        grad_hop(gm_z[2])
        gr[...] = dot_first(s.blk[...], s.dred[...]).astype(BF16).reshape(gr.shape)
        gr_c = ln.push(gr, s.rcr, core, jnp.logical_not(odd))
        plane_end(3, ar3)
        t = reduce_line(3, lambda: gh_z.append(grad_push(1, s.gh, s.rh, 3, 6)))
        gs3 = ln.push(s.at3, s.o_gs3.at[r], xpeer)
        gs3n = ln.near(s.at3, s.o_gs3.at[r])
        mu = jnp.concatenate([t[0:1], t[1:2]], axis=1) / count
        mux = jnp.concatenate([t[2:3], t[3:4]], axis=1) / count

        def dp3_step(base):
            rows = pl.ds(base, 32)
            x = (s.pre3[rows, :] - s.bnp3[0:1]) * s.bnp3[1:2]
            d = mask_at(base, 32, 1024) * (s.bnp3[2:3] * s.bnp3[1:2]) * (s.u3[rows, :] - mu - x * mux)
            s.dp3[rows, :] = d.astype(BF16)

        rows_loop(320, 32, dp3_step)

        def partial_out(pas, value_of):
            pas[...] = value_of(ohalf).astype(BF16)

        wlast = s.wl
        s.u3[:, 0:512] = dot_last(s.dp3[...], wlast[...].reshape(512, 1024))
        s.pas2[...] = s.u3[:, pl.ds(ohalf, 256)].astype(BF16)
        pa2 = ln.push(s.pas2, s.par2, xpeer)
        gl[...] = dot_first(s.a2[...], s.dp3[...]).astype(BF16).reshape(gl.shape)
        gl_c = to_core(gl, s.rcl, False)
        wait([gr_c], odd)

        @pl.when(odd)
        def _():
            for q in range(4):
                s.rcr[q] = (s.rcr[q].astype(F32) + gr[q].astype(F32)).astype(BF16)

        later = {"gr_y": ln.push(s.rcr.at[:, 1 - y], s.ryr, ypeer, odd)}

        def after_plane_two():
            wait([gl_c])
            add_core(gl, s.rcl, False)
            later["gl_y"] = to_y(s.rcl, s.ryl, False)

        def after_plane_one():
            wait([gq_c])
            add_core(gq, s.rcm, True)
            later["gq_y"] = [
                ln.push(s.rcm.at[3 * a : 3 * a + 3, :, 1 - y], s.rym.at[3 * a : 3 * a + 3], ypeer) for a in range(3)
            ]

        wait([pa2])

        def norm_back(n, par, prebuf, bnp, dst, out_gs, middle, after):
            def u_step(i, carry):
                su_, sux_ = carry
                base = pl.multiple_of(i * 80, 16)
                rows = pl.ds(base, 80)
                x = (prebuf[rows, :] - bnp[0:1]) * bnp[1:2]
                v = x * bnp[2:3] + bnp[3:4]
                d = s.u3[rows, pl.ds(half, 256)] + par[rows, :].astype(F32)
                u = slope_of(v) * d * mask_at(base, 80, 256)
                s.u3[rows, 512:768] = u
                return su_ + jnp.sum(u, axis=0, keepdims=True), sux_ + jnp.sum(u * x, axis=0, keepdims=True)

            nil_ = jnp.zeros((1, 256), F32)
            su_, sux_ = lax.fori_loop(0, 4, u_step, (nil_, nil_))
            put_stats(n, su_, sux_, 256, None)
            reduce_plane(n)

            def bulk():
                middle()
                after()

            t_ = reduce_line(n, bulk)
            gsx = ln.push(getattr(s, "at%d" % n), out_gs.at[r], xpeer)
            gsn = ln.near(getattr(s, "at%d" % n), out_gs.at[r])
            mu_, mux_ = t_[0:1] / count, t_[1:2] / count

            def d_step(base):
                rows = pl.ds(base, 80)
                x = (prebuf[rows, :] - bnp[0:1]) * bnp[1:2]
                d = mask_at(base, 80, 256) * (bnp[2:3] * bnp[1:2]) * (s.u3[rows, 512:768] - mu_ - x * mux_)
                dst[rows, :] = d.astype(BF16)

            rows_loop(320, 80, d_step)
            return gsx, gsn

        def window_two():
            grad_hop(gh_z[0])
            gh_z.append(grad_push(1, s.gh, s.rh, 6, 9))
            later["mess"] = task_out(gm_z, s.rm, s.gm, s.psm, s.o_mess)

        def window_one():
            grad_hop(gh_z[1])
            wait([later["gr_y"]], odd)

            @pl.when(odd)
            def _():
                for q in range(4):
                    s.ryr[q] = (s.ryr[q].astype(F32) + s.rcr[q, y].astype(F32)).astype(BF16)

            later["gr_z"] = to_z(s.ryr, s.rzr, False, odd, s.hpr)
            wait([later["gl_y"]])
            add_y(s.rcl, s.ryl, False)
            later["gl_z"] = to_z(s.ryl, s.rzl, False, None, s.hpl)

        gs2, gs2n = norm_back(4, s.par2, s.pre2, s.bnp2, s.dp2, s.o_gs2, after_plane_two, window_two)
        spread(s.dp2, s.d3m, 1, 256)
        s.u3[:, 0:512] = conv_back(s.d3m, s.wm, 0)
        s.pas1[...] = s.u3[:, pl.ds(ohalf, 256)].astype(BF16)
        pa1 = ln.push(s.pas1, s.par1, xpeer)
        conv_weight(s.a3, s.d3m, gq, 1, 0, 9)
        gq_c = to_core(gq, s.rcm, True)
        wait([pa1])
        gs1, gs1n = norm_back(5, s.par1, s.pre1, s.bnp1, s.dp1, s.o_gs1, after_plane_one, window_one)
        dp_x = ln.push(s.dp1.at[pl.ds(other_rows, 160)], s.dp1r, xpeer)
        gf[...] = dot_first(s.xall[...], s.dp1[...]).astype(BF16).reshape(gf.shape)
        gf_c = to_core(gf, s.rcf, False)
        wait([gf_c])
        add_core(gf, s.rcf, False)
        gf_y = to_y(s.rcf, s.ryf, False)
        ms, mn = later["mess"]
        gr_z, gl_z = later["gr_z"], later["gl_z"]
        grad_hop(gh_z[2])
        gq_z = []
        for a in range(3):
            wait([later["gq_y"][a]])
            for t in range(3 * a, 3 * a + 3):
                s.rym[t] = (s.rym[t].astype(F32) + s.rcm[t, :, y].astype(F32)).astype(BF16)
            lead = slice(3 * a, 3 * a + 3)
            rz = SimpleNamespace(at=[s.rzm.at[q, lead] for q in range(3)])
            gq_z.append(to_z(s.rym.at[lead], rz, True, None, s.hpm.at[lead] if a < 2 else None))
            if a == 0:
                hop_z(gr_z)
                hop_z(gl_z)
            else:
                hop_z(gq_z[a - 1])
        wait([gf_y])
        add_y(s.rcf, s.ryf, False)
        gf_z = to_z(s.ryf, s.rzf, False)

        wait([wfo_x])
        wfo_n = ln.near(s.wfo, s.wfov)
        wait([dp_x, ds_x])
        wfo_n.wait()
        mine_d = s.dp1[pl.ds(my_rows, 160), :]
        other_d = s.dp1r[...]
        for q in range(2):
            cols = slice(1024 * q, 1024 * q + 1024)
            wa = s.wf[2 * q : 2 * q + 2].reshape(1024, 256)
            wb = s.wfov[2 * q : 2 * q + 2].reshape(1024, 256)
            s.u3[pl.ds(0, 160), :] = dot_last(mine_d, wa) + dot_last(other_d, wb)

            def img_step(base):
                rows = pl.ds(base, 32)
                m = mask_at(my_rows + base, 32, 1024)
                own_d = s.dsum[pl.ds(my_rows + base, 32), 512 * q : 512 * q + 512].astype(F32)
                far_d = s.dsr[rows, 512 * q : 512 * q + 512].astype(F32)
                d = jnp.concatenate(
                    [
                        jnp.where(r == j % 2, own_d[:, 64 * (j - j % 2) :][:, :128], far_d[:, 64 * (j - j % 2) :][:, :128])
                        for j in range(8)
                    ],
                    axis=1,
                )
                s.oimg[rows, cols] = ((s.u3[rows, :] + d) * m).astype(BF16)

            rows_loop(160, 32, img_step)
        img_n = ln.near(s.oimg, s.o_img)

        hs, hn = task_out(gh_z, s.rh, s.gh, s.psh, s.o_heads)

        @pl.when(special)
        def _():
            for cp in gg_z:
                cp.wait_recv()
            v = (s.gg[z].astype(F32) + s.rg[0].astype(F32)) + (s.rg[1].astype(F32) + s.rg[2].astype(F32))
            s.pg[...] = v.astype(BF16)

        gx = [ln.group(lambda n=n: s.wg.at[0:3, 0, 0] if n == 3 else s.wg.at[0:4, 0, 0], special) for n in (3, 4)]
        for g, odd_one in zip(gx, (0, 1)):
            for o in offsets:
                if (o[0] + o[1]) % 2 == odd_one:
                    rr, yy, cc = peer(*o)
                    g.push(s.pg.at[yy, cc], s.o_gates.at[r, :, pl.ds(fhalf, 256)], dev(z, yy, cc, rr), special)
        gate_near = pltpu.make_async_copy(
            s.pg.at[y, c], s.o_gates.at[r, :, pl.ds(fhalf, 256)], s.near_sems.at[NEAR - 2]
        )
        pl.when(special)(gate_near.start)

        wait([cg])
        v = s.gcls[b].astype(F32)
        for i in range(15):
            v = v + s.rcls[i].astype(F32)
        s.clss[...] = v
        cls_x = ln.push(s.clss, s.clsr, xpeer)

        wait_z(gr_z)
        pl.when(odd)(lambda: add_z(s.ryr, s.rzr, s.fnr, False))
        gr_x = ln.push(s.fnr, s.o_red, xpeer, odd)
        red_near = pltpu.make_async_copy(s.fnr, s.o_red, s.near_sems.at[NEAR - 3])
        pl.when(odd)(red_near.start)
        wait_z(gl_z)
        add_z(s.ryl, s.rzl, s.fnl, False)
        gl_x = ln.push(s.fnl, s.o_last.at[r], xpeer)
        n1 = ln.near(s.fnl, s.o_last.at[r])
        for a in range(3):
            wait_z(gq_z[a])
            lead = slice(3 * a, 3 * a + 3)
            add_z(s.rym.at[lead], s.rzm.at[:, lead], s.fnm.at[lead], True, a < 2)
        gq_x = ln.push(s.fnm, s.o_mid.at[:, :, pl.ds(half, 256)], xpeer)
        n2 = ln.near(s.fnm, s.o_mid.at[:, :, pl.ds(half, 256)])
        wait_z(gf_z)
        add_z(s.ryf, s.rzf, s.fnf, False, False)
        gf_x = ln.push(s.fnf, s.o_first.at[:, pl.ds(half, 256)], xpeer)
        n3 = ln.near(s.fnf, s.o_first.at[:, pl.ds(half, 256)])
        wait([cls_x])
        s.clso[...] = s.clss[...] + s.clsr[...]
        n4 = ln.near(s.clso, s.o_cls)
        wait([gr_x], jnp.logical_not(odd))
        wait([gl_x, gq_x, gf_x, gs1, gs2, gs3])
        wait(ms + hs)
        wait([gx[0]], special)
        wait([gx[1]], plain)
        pl.when(special)(gate_near.wait)
        pl.when(odd)(red_near.wait)
        for cp in (gs1n, gs2n, gs3n, img_n, mn, hn, n1, n2, n3, n4):
            cp.wait()
        ln.drain()

    pl.run_scoped(block_back, *[pltpu.VMEM(*v) for v in LATE.values()])


LATE = dict(
    zst=((2, 3, 3, 2, 2, 32, 256), BF16),
    psm=((9, 2, 2, 32, 256), BF16),
    psh=((9, 2, 2, 32, 256), BF16),
    fnr=((128, 512), BF16),
    fnl=((32, 1024), BF16),
    fnm=((9, 32, 256), BF16),
    fnf=((128, 256), BF16),
    pg=((2, 2, 32, 256), BF16),
    clss=((32, 128), F32),
    clso=((32, 128), F32),
    u3=((320, 1024), F32),
    dp3=((320, 1024), BF16),
    d3m=((480, 768), BF16),
    dsum=((320, 1024), BF16),
    oimg=((160, 2048), BF16),
    pas1=((320, 256), BF16),
    pas2=((320, 256), BF16),
    dp1=((320, 256), BF16),
    dp2=((320, 256), BF16),
    wfov=((4, 2, 2, 128, 256), BF16),
    gr=((4, 2, 128, 512), BF16),
    gl=((4, 2, 2, 32, 1024), BF16),
    gq=((9, 4, 2, 2, 32, 256), BF16),
    gf=((4, 2, 2, 128, 256), BF16),
)


FINAL = dict(
    depth=((160, 512), BF16),
    logits=((2, 40, 80), BF16),
    img=((160, 2048), F32),
    first=((128, 512), F32),
    gain1=((1, 32), F32),
    shift1=((1, 32), F32),
    mid=((9, 32, 512), F32),
    gain2=((1, 32), F32),
    shift2=((1, 32), F32),
    last=((32, 2048), F32),
    gain3=((1, 128), F32),
    shift3=((1, 128), F32),
    red=((128, 512), F32),
    heads=((2, 9, 32, 512), F32),
    mess=((2, 9, 32, 512), F32),
    gates=((2, 32, 512), F32),
    cls=((32, 40), F32),
)


def widen_out(names, *refs):
    s = SimpleNamespace(**dict(zip(names, refs)))
    b = lax.axis_index("batch")
    used = [0]

    def move(src, dst):
        cp = pltpu.make_async_copy(src, dst, s.sems.at[used[0]])
        used[0] += 1
        cp.start()
        return cp

    wide = [("img", slice(lo, lo + n)) for lo, n in ((0, 64), (64, 48), (112, 48))]
    wide += [(n, slice(i, i + 1)) for n in ("mess", "heads") for i in range(2)]
    wide += [("mid", slice(0, 9)), ("red", slice(0, 128)), ("first", slice(0, 128)), ("last", slice(0, 2)), ("gates", slice(0, 2))]
    loads = [move(getattr(s, "o_" + n).at[at], getattr(s, "i_" + n).at[at]) for n, at in wide]
    small = [move(getattr(s, "o_" + n), getattr(s, "i_" + n)) for n in ("gs1", "gs2", "gs3", "cls")]
    done = []
    narrow = [move(s.o_depth, s.i_depth), move(s.o_logits, s.i_logits)]
    for (n, at), cp in zip(wide, loads):
        cp.wait()
        src, dst = getattr(s, "i_" + n), getattr(s, "v_" + n)
        if n == "last":
            for i in range(8):
                for h in range(2):
                    lane = 128 * (2 * i + h)
                    dst[:, lane : lane + 128] = src[h, :, 128 * i : 128 * i + 128].astype(F32)
            done.append(move(dst, s.last))
            continue
        if n in ("mess", "heads"):
            for t in range(9):
                dst[at.start, t] = src[at.start, t].astype(F32)
        elif len(src.shape) > 2:
            for t in range(at.start, at.stop):
                dst[t] = src[t].astype(F32)
        else:
            dst[at] = src[at].astype(F32)
        done.append(move(dst.at[at], getattr(s, n).at[at]))
    for cp in narrow:
        cp.wait()
    done += [move(s.i_depth, s.depth), move(s.i_logits, s.logits)]
    for cp in small:
        cp.wait()
    quarter, spot = lax.div(b, np.int32(4)), lax.rem(b, np.int32(4))
    at = pl.ds(pl.multiple_of(128 * lax.rem(quarter, np.int32(2)), 128), 128)
    for n, layer in ((1, s.i_gs1), (2, s.i_gs2)):
        v = pltpu.roll(layer[lax.div(quarter, np.int32(2)), :, at], lax.rem(128 - 32 * spot, np.int32(128)), 1)
        for row, kind in ((1, "gain"), (0, "shift")):
            keep = getattr(s, "v_%s%d" % (kind, n))
            keep[...] = v[row : row + 1, 0:32]
            done.append(move(keep, getattr(s, "%s%d" % (kind, n))))
    block = lax.div(b, np.int32(2))
    at = pl.ds(pl.multiple_of(128 * lax.rem(block, np.int32(4)), 128), 128)
    v = s.i_gs3[lax.rem(b, np.int32(2)), :, at]
    low = lax.div(block, np.int32(4)) == 0
    s.v_shift3[...] = jnp.where(low, v[0:1], v[1:2])
    s.v_gain3[...] = jnp.where(low, v[2:3], v[3:4])
    done.append(move(s.v_shift3, s.shift3))
    done.append(move(s.v_gain3, s.gain3))
    s.v_cls[...] = s.i_cls[:, 0:40]
    done.append(move(s.v_cls, s.cls))
    for cp in done:
        cp.wait()


def fast(args):
    (
        images, crop_height, crop_width, w_first, gain_first, shift_first, w_middle, gain_middle, shift_middle,
        w_last, gain_last, shift_last, w_reduce, w_heads, w_message, w_gates, w_classes, depth_cot, class_cot,
    ) = args
    ins = (
        crop_height, crop_width, images.reshape(160, 2048), w_first, w_middle, w_last, w_reduce, w_gates, w_classes,
        w_heads, w_message, *(v.reshape(1, -1) for v in (gain_first, shift_first, gain_middle, shift_middle, gain_last, shift_last)), depth_cot.reshape(160, 512), class_cot.transpose(0, 1, 3, 2).reshape(2, 40, 80),
    )
    names = list(INS) + list(OUTS) + list(SHAPES) + ["send_sems", "recv_sems", "near_sems"]
    smem, hbm, vmem = (pl.BlockSpec(memory_space=m) for m in (pltpu.SMEM, pltpu.HBM, pltpu.VMEM))
    spec = {"crop_h": smem, "crop_w": smem}
    spec.update({n: vmem for n in INS if n[:4] in ("gain", "shif")})
    outs = pl.pallas_call(
        functools.partial(body, names),
        out_shape=[jax.ShapeDtypeStruct(*v) for v in OUTS.values()],
        in_specs=[spec.get(n, hbm) for n in INS],
        out_specs=[hbm] * len(OUTS),
        scratch_shapes=[pltpu.VMEM(*v) for v in SHAPES.values()]
        + [pltpu.SemaphoreType.DMA((n,)) for n in (SENDS, RECVS, NEAR)],
        compiler_params=pltpu.CompilerParams(has_side_effects=True, collective_id=0, vmem_limit_bytes=64 * 2**20),
        name="residual_distill",
    )(*ins)
    o = dict(zip(OUTS, outs))
    taken = [n for n in OUTS if n.startswith("o_")]
    staged = {"i_" + n[2:]: OUTS[n] for n in taken}
    staged.update({"v_" + n: v for n, v in FINAL.items() if n not in ("depth", "logits")})
    final = pl.pallas_call(
        functools.partial(widen_out, taken + list(FINAL) + list(staged) + ["sems"]),
        out_shape=[jax.ShapeDtypeStruct(*v) for v in FINAL.values()],
        in_specs=[hbm] * len(taken),
        out_specs=[hbm] * len(FINAL),
        scratch_shapes=[pltpu.VMEM(*v) for v in staged.values()] + [pltpu.SemaphoreType.DMA((41,))],
        compiler_params=pltpu.CompilerParams(vmem_limit_bytes=64 * 2**20),
        name="widen_out",
    )(*[o[n] for n in taken])
    f = dict(zip(FINAL, final))
    f["depth"] = f["depth"].reshape(1, 2, 80, 512)
    f["logits"] = f["logits"].reshape(1, 2, 40, 80).transpose(0, 1, 3, 2)
    f["img"] = f["img"].reshape(1, 2, 80, 2048)
    for n in ("gain1", "shift1", "gain2", "shift2", "gain3", "shift3"):
        f[n] = f[n].reshape(-1)
    return tuple(f.values())


def solution(mesh):
    def step(*args):
        if mesh.shape["batch"] == 16 and mesh.shape["rows"] == 2:
            return fast(args)
        return shards(*args)

    placed = (
        P("batch", "rows", None, None),
        P(),
        P(),
        P("batch", None),
        P("batch"),
        P("batch"),
        P(None, "batch", None),
        P("batch"),
        P("batch"),
        P("batch", None),
        P("batch"),
        P("batch"),
        P("batch", None),
        P("rows", None, "batch", None),
        P("rows", None, "batch", None),
        P(None, "batch", None),
        P("batch", None),
        P("batch", "rows", None, None),
        P("batch", "rows", None, None),
    )
    return jax.shard_map(
        step,
        mesh=mesh,
        in_specs=placed,
        out_specs=(
            P("batch", "rows", None, None),
            P("batch", "rows", None, None),
            P("batch", "rows", None, None),
            P("batch", None),
            P("batch"),
            P("batch"),
            P(None, "batch", None),
            P("batch"),
            P("batch"),
            P("batch", None),
            P("batch"),
            P("batch"),
            P("batch", None),
            P("rows", None, "batch", None),
            P("rows", None, "batch", None),
            P(None, "batch", None),
            P("batch", None),
        ),
        check_vma=False,
    )
```

```python
import functools
from types import SimpleNamespace

import numpy as np
import jax
import jax.numpy as jnp
from jax import lax
from jax.sharding import PartitionSpec as P
from jax.experimental import pallas as pl
from jax.experimental.pallas import tpu as pltpu

EPS = 1e-05
MESH = pl.DeviceIdType.MESH
F32 = jnp.float32
BF16 = jnp.bfloat16
ROOT = 0.7978845608028654
CUBE = 0.044715
SENDS = 121
RECVS = 200
NEAR = 21


def dot(left, right):
    return jnp.dot(left, right, preferred_element_type=F32)


def dot_last(left, right):
    return lax.dot_general(left, right, (((1,), (1,)), ((), ())), preferred_element_type=F32)


def dot_first(left, right):
    return lax.dot_general(left, right, (((0,), (0,)), ((), ())), preferred_element_type=F32)


def gelu_of(v):
    return 0.5 * v * (1.0 + jnp.tanh(ROOT * (v + CUBE * v * v * v)))


def slope_of(v):
    t = jnp.tanh(ROOT * (v + CUBE * v * v * v))
    return 0.5 * (1.0 + t) + 0.5 * v * (1.0 - t * t) * (ROOT * (1.0 + 3.0 * CUBE * v * v))


def rows_loop(total, chunk, step):
    def body(index, carry):
        step(pl.multiple_of(index * chunk, chunk))
        return carry

    lax.fori_loop(0, total // chunk, body, 0)


class Copy:
    def __init__(self, remote, links, send, recv, like):
        self.remote, self.links, self.send, self.recv, self.like = remote, links, send, recv, like
        self.scoped = like is None

    def wait_recv(self):
        if self.like is None:
            self.remote.wait_recv()
        else:
            ref = self.like(1)
            pltpu.make_async_copy(ref, ref, self.links.recv.at[self.recv]).wait()

    def wait_send(self):
        if self.like is None:
            self.remote.wait_send()
        else:
            ref = self.like(0)
            pltpu.make_async_copy(ref, ref, self.links.send.at[self.send]).wait()


class Group:
    scoped = True

    def __init__(self, links, send, recv, like):
        self.links, self.send, self.recv, self.like = links, send, recv, like

    def push(self, src, dst, device, when=None):
        self.links.start(src, dst, device, self.send, self.recv, when)

    def wait_recv(self):
        ref = self.like()
        pltpu.make_async_copy(ref, ref, self.links.recv.at[self.recv]).wait()

    def wait_send(self):
        ref = self.like()
        pltpu.make_async_copy(ref, ref, self.links.send.at[self.send]).wait()


class Near:
    def __init__(self, links, src, dst):
        self.links, self.index = links, links.local_free.pop(0)
        self.copy = pltpu.make_async_copy(src, dst, links.local.at[self.index])
        self.copy.start()

    def wait(self):
        self.copy.wait()
        self.links.local_free.insert(0, self.index)


class Links:
    def __init__(self, send, recv, local):
        self.send, self.recv, self.local = send, recv, local
        self.used = 0
        self.send_free = list(range(SENDS))
        self.local_free = list(range(NEAR - 4))
        self.open = []

    def start(self, src, dst, device, send, recv, when):
        remote = pltpu.make_async_remote_copy(
            src_ref=src,
            dst_ref=dst,
            send_sem=self.send.at[send],
            recv_sem=self.recv.at[recv],
            device_id=device,
            device_id_type=MESH,
        )
        if when is None:
            remote.start()
        else:
            pl.when(when)(remote.start)
        return remote

    def pair(self):
        self.used += 1
        return self.send_free.pop(0), self.used - 1

    def push(self, src, dst, device, when=None, like=None):
        send, recv = self.pair()
        cp = Copy(self.start(src, dst, device, send, recv, when), self, send, recv, like)
        self.open.append((cp, when))
        return cp

    def group(self, like, when=None):
        cp = Group(self, *self.pair(), like)
        self.open.append((cp, when))
        return cp

    def near(self, src, dst):
        return Near(self, src, dst)

    def drain(self, scoped=False):
        kept = []
        for cp, when in self.open:
            if scoped and not cp.scoped:
                kept.append((cp, when))
                continue
            if when is None:
                cp.wait_send()
            else:
                pl.when(when)(cp.wait_send)
            self.send_free.insert(0, cp.send)
        self.open = kept


def wait(copies, when=None):
    def run():
        for cp in copies:
            cp.wait_recv()

    if when is None:
        run()
    else:
        pl.when(when)(run)


def lanes(mask, width):
    return jnp.concatenate([mask] * (width // 128), axis=1) if width > 128 else mask


def padded_2(cells, sides, width):
    for axis, dim in sides:
        count = lax.axis_size(axis)
        ends = count - 1
        head = lax.slice_in_dim(cells, 0, width, axis=dim)
        tail = lax.slice_in_dim(cells, cells.shape[dim] - width, cells.shape[dim], axis=dim)
        cells = jnp.concatenate(
            [
                lax.ppermute(tail, axis, [(i, (i + 1) % count) for i in range(ends)]),
                cells,
                lax.ppermute(head, axis, [((i + 1) % count, i) for i in range(ends)]),
            ],
            axis=dim,
        )
    return cells


def gelu_tanh(values):
    return jax.nn.gelu(values, approximate=True)


def gelu_slope(values, upstream):
    return jax.vjp(gelu_tanh, values)[1](upstream)[0]


def project(values, weight):
    return jnp.einsum("nrcj,jk->nrck", values, weight, preferred_element_type=jnp.float32)


def project_back(upstream, weight):
    return jnp.einsum("nrck,jk->nrcj", upstream, weight, preferred_element_type=jnp.float32)


def outer_sum(values, upstream):
    return jnp.einsum("nrcj,nrck->jk", values, upstream, preferred_element_type=jnp.float32)


def widen(padded):
    return jnp.pad(padded, ((0, 0), (0, 0), (1, 1), (0, 0)))


def halo_value(values):
    return padded_2(values, (("rows", 1),), 1)


def halo_grad(values):
    return padded_2(values, (("rows", 1),), 1)


def conv_apply(padded, kernel):
    row_count = padded.shape[1] - 2
    col_count = padded.shape[2]
    widened = widen(padded)
    running = jnp.zeros((padded.shape[0], row_count, col_count, kernel.shape[2]), jnp.float32)
    for tap_index in range(9):
        shift_down = tap_index // 3
        shift_right = tap_index % 3
        running = running + project(
            widened[
                :, shift_down : shift_down + row_count, shift_right : shift_right + col_count, :
            ],
            kernel[tap_index],
        )
    return running


def conv_kernel_grad(padded, upstream):
    row_count = upstream.shape[1]
    col_count = upstream.shape[2]
    widened = widen(padded)
    return jnp.stack(
        [
            outer_sum(
                widened[
                    :,
                    tap_index // 3 : tap_index // 3 + row_count,
                    tap_index % 3 : tap_index % 3 + col_count,
                    :,
                ],
                upstream,
            )
            for tap_index in range(9)
        ]
    )


def conv_input_grad(padded_grad, kernel):
    row_count = padded_grad.shape[1] - 2
    col_count = padded_grad.shape[2]
    widened = widen(padded_grad)
    running = jnp.zeros((padded_grad.shape[0], row_count, col_count, kernel.shape[1]), jnp.float32)
    for tap_index in range(9):
        shift_down = tap_index // 3
        shift_right = tap_index % 3
        running = running + project_back(
            widened[
                :,
                2 - shift_down : 2 - shift_down + row_count,
                2 - shift_right : 2 - shift_right + col_count,
                :,
            ],
            kernel[tap_index],
        )
    return running


def crop_mask(height, width, first_row, row_count, col_count):
    row_ids = first_row + jnp.arange(row_count, dtype=jnp.int32)
    col_ids = jnp.arange(col_count, dtype=jnp.int32)
    inside = (row_ids[None, :, None] < height[:, None, None]) & (
        col_ids[None, None, :] < width[:, None, None]
    )
    return inside.astype(jnp.float32)[..., None]


def norm_forward(pre_act, pixel_mask, gain_vec, shift_vec, valid_count):
    sums = jnp.sum(pre_act * pixel_mask, axis=(0, 1, 2))
    squares = jnp.sum(pre_act * pre_act * pixel_mask, axis=(0, 1, 2))
    sums, squares = lax.psum((sums, squares), ("batch", "rows"))
    mean_vec = sums / valid_count
    inv_std = lax.rsqrt(squares / valid_count - mean_vec * mean_vec + EPS)
    normal = (pre_act - mean_vec) * inv_std
    return (normal, inv_std, normal * gain_vec + shift_vec)


def norm_backward(upstream, normal, inv_std, gain_vec, pixel_mask, valid_count):
    shift_part = jnp.sum(upstream, axis=(0, 1, 2))
    gain_part = jnp.sum(upstream * normal, axis=(0, 1, 2))
    shift_part, gain_part = lax.psum((shift_part, gain_part), ("batch", "rows"))
    d_pre = (
        pixel_mask
        * gain_vec
        * inv_std
        * (upstream - shift_part / valid_count - normal * gain_part / valid_count)
    )
    return (d_pre, gain_part, shift_part)


def task_forward(padded_in, heads, messages, pixel_mask, pad_rows):
    pre_list = []
    feat_list = []
    padded_feats = []
    message_list = []
    for task in range(heads.shape[0]):
        pre_act = conv_apply(padded_in, heads[task])
        feature = (gelu_tanh(pre_act) * pixel_mask).astype(jnp.bfloat16)
        padded_feat = pad_rows(feature)
        pre_list.append(pre_act)
        feat_list.append(feature)
        padded_feats.append(padded_feat)
        message_list.append(conv_apply(padded_feat, messages[task]).astype(jnp.bfloat16))
    return (pre_list, feat_list, padded_feats, message_list)


def task_backward(
    padded_in,
    heads,
    messages,
    pixel_mask,
    pre_list,
    padded_feats,
    feat_grads,
    message_grads,
    pad_grad,
):
    input_grad = jnp.zeros(
        padded_in.shape[:1] + (padded_in.shape[1] - 2,) + padded_in.shape[2:], jnp.float32
    )
    head_grads = []
    kernel_grads = []
    for task in range(heads.shape[0]):
        low_message = message_grads[task].astype(jnp.bfloat16)
        kernel_grads.append(conv_kernel_grad(padded_feats[task], low_message))
        feat_grad = feat_grads[task] + conv_input_grad(pad_grad(low_message), messages[task])
        low_pre = gelu_slope(pre_list[task], feat_grad * pixel_mask).astype(jnp.bfloat16)
        head_grads.append(conv_kernel_grad(padded_in, low_pre))
        input_grad = input_grad + conv_input_grad(pad_grad(low_pre), heads[task])
    return (input_grad, jnp.stack(head_grads), jnp.stack(kernel_grads))


def streams_forward(features, messages, gates_all, classes_all, pixel_mask):
    gate_depth = jax.nn.sigmoid(project(features[0], gates_all[0]))
    gate_class = jax.nn.sigmoid(project(features[3], gates_all[1]))
    depth_sum = (
        messages[1].astype(jnp.float32)
        + messages[2].astype(jnp.float32)
        + messages[3].astype(jnp.float32)
    )
    class_sum = (
        messages[0].astype(jnp.float32)
        + messages[1].astype(jnp.float32)
        + messages[2].astype(jnp.float32)
    )
    depth_stream = (features[0].astype(jnp.float32) + gate_depth * depth_sum) * pixel_mask
    merged = (features[3].astype(jnp.float32) + gate_class * class_sum).astype(jnp.bfloat16)
    class_logits = project(merged, classes_all) * pixel_mask
    return (depth_stream, class_logits, merged, gate_depth, gate_class, depth_sum, class_sum)


def streams_backward(
    features,
    merged,
    gate_depth,
    gate_class,
    depth_sum,
    class_sum,
    depth_cot,
    class_cot,
    gates_all,
    classes_all,
    pixel_mask,
):
    depth_grad = depth_cot.astype(jnp.float32) * pixel_mask
    logit_grad = (class_cot.astype(jnp.float32) * pixel_mask).astype(jnp.bfloat16)
    grad_classes = outer_sum(merged, logit_grad)
    merged_grad = project_back(logit_grad, classes_all)
    gate_depth_grad = (depth_grad * depth_sum * gate_depth * (1.0 - gate_depth)).astype(
        jnp.bfloat16
    )
    gate_class_grad = (merged_grad * class_sum * gate_class * (1.0 - gate_class)).astype(
        jnp.bfloat16
    )
    grad_gates = jnp.stack(
        [outer_sum(features[0], gate_depth_grad), outer_sum(features[3], gate_class_grad)]
    )
    depth_feat = depth_grad + project_back(gate_depth_grad, gates_all[0])
    class_feat = merged_grad + project_back(gate_class_grad, gates_all[1])
    depth_message = depth_grad * gate_depth
    class_message = merged_grad * gate_class
    nothing = jnp.zeros_like(depth_grad)
    feat_grads = [depth_feat, nothing, nothing, class_feat]
    message_grads = [
        class_message,
        depth_message + class_message,
        depth_message + class_message,
        depth_message,
    ]
    return (feat_grads, message_grads, grad_gates, grad_classes)


def shards(
    images,
    crop_height,
    crop_width,
    w_first,
    gain_first,
    shift_first,
    w_middle,
    gain_middle,
    shift_middle,
    w_last,
    gain_last,
    shift_last,
    w_reduce,
    w_heads,
    w_message,
    w_gates,
    w_classes,
    depth_cot,
    class_cot,
):
    image_index = lax.axis_index("batch")
    batch_count = lax.axis_size("batch")
    row_count = images.shape[1]
    col_count = images.shape[2]
    height = lax.dynamic_slice_in_dim(crop_height, image_index, 1, 0)
    width = lax.dynamic_slice_in_dim(crop_width, image_index, 1, 0)
    pixel_mask = crop_mask(height, width, lax.axis_index("rows") * row_count, row_count, col_count)
    valid_count = jnp.sum(crop_height * crop_width).astype(jnp.float32)
    gathered = (
        lax.all_gather(w_first, "batch", axis=0, tiled=True),
        lax.all_gather(w_middle, "batch", axis=1, tiled=True),
        lax.all_gather(w_last, "batch", axis=0, tiled=True),
        lax.all_gather(w_reduce, "batch", axis=0, tiled=True),
        lax.all_gather(w_gates, "batch", axis=1, tiled=True),
        lax.all_gather(w_classes, "batch", axis=0, tiled=True),
        lax.all_gather(gain_first, "batch", axis=0, tiled=True),
        lax.all_gather(shift_first, "batch", axis=0, tiled=True),
        lax.all_gather(gain_middle, "batch", axis=0, tiled=True),
        lax.all_gather(shift_middle, "batch", axis=0, tiled=True),
        lax.all_gather(gain_last, "batch", axis=0, tiled=True),
        lax.all_gather(shift_last, "batch", axis=0, tiled=True),
        lax.all_gather(w_heads, "batch", axis=2, tiled=True),
        lax.all_gather(w_message, "batch", axis=2, tiled=True),
    )
    first_all = gathered[0]
    middle_all = gathered[1]
    last_all = gathered[2]
    reduce_all = gathered[3]
    gates_all = gathered[4]
    classes_all = gathered[5]
    gain_one = gathered[6].astype(jnp.float32)
    shift_one = gathered[7].astype(jnp.float32)
    gain_two = gathered[8].astype(jnp.float32)
    shift_two = gathered[9].astype(jnp.float32)
    gain_three = gathered[10].astype(jnp.float32)
    shift_three = gathered[11].astype(jnp.float32)
    heads_own = gathered[12]
    message_own = gathered[13]
    masked_in = images.astype(jnp.float32) * pixel_mask
    low_in = masked_in.astype(jnp.bfloat16)
    pre_first = project(low_in, first_all)
    normal_first, std_first, out_first = norm_forward(
        pre_first, pixel_mask, gain_one, shift_one, valid_count
    )
    act_first = (gelu_tanh(out_first) * pixel_mask).astype(jnp.bfloat16)
    padded_first = halo_value(act_first)
    pre_middle = conv_apply(padded_first, middle_all)
    normal_middle, std_middle, out_middle = norm_forward(
        pre_middle, pixel_mask, gain_two, shift_two, valid_count
    )
    act_middle = (gelu_tanh(out_middle) * pixel_mask).astype(jnp.bfloat16)
    pre_last = project(act_middle, last_all)
    normal_last, std_last, out_last = norm_forward(
        pre_last, pixel_mask, gain_three, shift_three, valid_count
    )
    summed = out_last + masked_in
    block_out = (gelu_tanh(summed) * pixel_mask).astype(jnp.bfloat16)
    low_reduced = project(block_out, reduce_all).astype(jnp.bfloat16)
    heads_all, message_all = (
        lax.all_gather(heads_own, "rows", axis=0, tiled=True),
        lax.all_gather(message_own, "rows", axis=0, tiled=True),
    )
    padded_in = halo_value(low_reduced)
    pre_list, feat_list, padded_feats, message_list = task_forward(
        padded_in, heads_all, message_all, pixel_mask, halo_value
    )
    depth_stream, class_logits, merged, gate_depth, gate_class, depth_sum, class_sum = (
        streams_forward(feat_list, message_list, gates_all, classes_all, pixel_mask)
    )
    feat_grads, message_grads, grad_gates, grad_classes = streams_backward(
        feat_list,
        merged,
        gate_depth,
        gate_class,
        depth_sum,
        class_sum,
        depth_cot,
        class_cot,
        gates_all,
        classes_all,
        pixel_mask,
    )
    reduced_grad, grad_heads, grad_message = task_backward(
        padded_in,
        heads_all,
        message_all,
        pixel_mask,
        pre_list,
        padded_feats,
        feat_grads,
        message_grads,
        halo_grad,
    )
    low_reduced_grad = reduced_grad.astype(jnp.bfloat16)
    grad_reduce = outer_sum(block_out, low_reduced_grad)
    block_grad = project_back(low_reduced_grad, reduce_all)
    sum_grad = gelu_slope(summed, block_grad * pixel_mask)
    d_last, gain_grad_three, shift_grad_three = norm_backward(
        sum_grad, normal_last, std_last, gain_three, pixel_mask, valid_count
    )
    low_last = d_last.astype(jnp.bfloat16)
    grad_last = outer_sum(act_middle, low_last)
    middle_grad = project_back(low_last, last_all)
    d_middle, gain_grad_two, shift_grad_two = norm_backward(
        gelu_slope(out_middle, middle_grad * pixel_mask),
        normal_middle,
        std_middle,
        gain_two,
        pixel_mask,
        valid_count,
    )
    low_middle = d_middle.astype(jnp.bfloat16)
    grad_middle = conv_kernel_grad(padded_first, low_middle)
    first_grad = conv_input_grad(halo_grad(low_middle), middle_all)
    d_first, gain_grad_one, shift_grad_one = norm_backward(
        gelu_slope(out_first, first_grad * pixel_mask),
        normal_first,
        std_first,
        gain_one,
        pixel_mask,
        valid_count,
    )
    low_first = d_first.astype(jnp.bfloat16)
    grad_first = outer_sum(low_in, low_first)
    image_grad = (project_back(low_first, first_all) + sum_grad) * pixel_mask
    summed_grads = (
        lax.psum_scatter(grad_first, "batch", scatter_dimension=0, tiled=True),
        lax.psum_scatter(grad_middle, "batch", scatter_dimension=1, tiled=True),
        lax.psum_scatter(grad_last, "batch", scatter_dimension=0, tiled=True),
        lax.psum_scatter(grad_reduce, "batch", scatter_dimension=0, tiled=True),
        lax.psum_scatter(grad_gates, "batch", scatter_dimension=1, tiled=True),
        lax.psum_scatter(grad_classes, "batch", scatter_dimension=0, tiled=True),
        lax.psum_scatter(grad_heads, "batch", scatter_dimension=2, tiled=True),
        lax.psum_scatter(grad_message, "batch", scatter_dimension=2, tiled=True),
    )
    shared = (
        lax.psum(summed_grads[0].astype(jnp.bfloat16), "rows").astype(jnp.float32),
        lax.psum(summed_grads[1].astype(jnp.bfloat16), "rows").astype(jnp.float32),
        lax.psum(summed_grads[2].astype(jnp.bfloat16), "rows").astype(jnp.float32),
        lax.psum(summed_grads[3].astype(jnp.bfloat16), "rows").astype(jnp.float32),
        lax.psum(summed_grads[4].astype(jnp.bfloat16), "rows").astype(jnp.float32),
        lax.psum(summed_grads[5].astype(jnp.bfloat16), "rows").astype(jnp.float32),
    )
    heads_out, message_out = (
        lax.psum_scatter(
            summed_grads[6].astype(jnp.bfloat16), "rows", scatter_dimension=0, tiled=True
        ).astype(jnp.float32),
        lax.psum_scatter(
            summed_grads[7].astype(jnp.bfloat16), "rows", scatter_dimension=0, tiled=True
        ).astype(jnp.float32),
    )

    def own_share(member):
        share = member.shape[0] // batch_count
        return lax.dynamic_slice_in_dim(member, image_index * share, share, 0)

    return (
        depth_stream.astype(jnp.bfloat16),
        class_logits.astype(jnp.bfloat16),
        image_grad,
        shared[0],
        own_share(gain_grad_one),
        own_share(shift_grad_one),
        shared[1],
        own_share(gain_grad_two),
        own_share(shift_grad_two),
        shared[2],
        own_share(gain_grad_three),
        own_share(shift_grad_three),
        shared[3],
        heads_out,
        message_out,
        shared[4],
        shared[5],
    )


BEHIND = (0, 1, 2, 3, 4, 5, )

SHAPES = dict(
    wf=((4, 2, 2, 128, 256), BF16),
    wm=((9, 4, 2, 2, 32, 256), BF16),
    wl=((4, 2, 2, 32, 1024), BF16),
    wr=((4, 2, 128, 512), BF16),
    wc=((16, 32, 128), BF16),
    wcs=((32, 128), BF16),
    gains=((8, 128), F32),
    wcv=((32, 40), BF16),
    cct=((2, 40, 80), BF16),
    ctf=((128, 128), F32),
    xh=((320, 1024), BF16),
    wh=((9, 4, 2, 2, 32, 256), BF16),
    wq=((9, 4, 2, 2, 32, 256), BF16),
    wg=((4, 2, 2, 32, 256), BF16),
    xall=((320, 2048), BF16),
    maskp=((1280, 128), F32),
    pre1=((320, 256), F32),
    pre2=((320, 256), F32),
    pre3=((320, 1024), F32),
    bnp1=((8, 256), F32),
    bnp2=((8, 256), F32),
    bnp3=((8, 1024), F32),
    a1=((320, 512), BF16),
    a2=((320, 512), BF16),
    a3=((480, 1536), BF16),
    blk=((320, 1024), BF16),
    rps=((160, 512), BF16),
    rpr=((160, 512), BF16),
    rbuf=((1280, 512), BF16),
    fown=((1280, 256), BF16),
    ffull=((1280, 512), BF16),
    msgb=((1280, 256), BF16),
    gateb=((1280, 256), BF16),
    mrecv=((4, 160, 512), BF16),
    dm=((4, 160, 512), BF16),
    eu=((2, 160, 512), BF16),
    dcotv=((160, 512), BF16),
    ccotv=((160, 128), BF16),
    olt=((2, 40, 80), BF16),
    ods=((160, 512), BF16),
    olg=((160, 128), BF16),
    mrg=((160, 512), BF16),
    fg=((2, 2, 160, 512), BF16),
    dmg=((1280, 256), BF16),
    exg=((2, 1280, 256), BF16),
    gm=((9, 4, 2, 2, 32, 256), BF16),
    gh=((9, 4, 2, 2, 32, 256), BF16),
    gg=((4, 2, 2, 32, 256), BF16),
    rg=((3, 2, 2, 32, 256), BF16),
    hop=((2, 9, 2, 2, 32, 256), BF16),
    gcls=((16, 32, 128), BF16),
    rcls=((15, 32, 128), BF16),
    clsr=((32, 128), F32),
    dfs=((1280, 256), BF16),
    dfr=((1280, 256), BF16),
    drs=((640, 512), BF16),
    drr=((640, 512), BF16),
    dro=((3, 160, 512), BF16),
    dred=((320, 512), BF16),
    dsr=((160, 1024), BF16),
    par2=((320, 256), BF16),
    par1=((320, 256), BF16),
    dp1r=((160, 256), BF16),
    rcr=((4, 2, 128, 512), BF16),
    rcl=((4, 2, 32, 1024), BF16),
    rcm=((9, 4, 2, 32, 256), BF16),
    rcf=((4, 2, 128, 256), BF16),
    ryr=((4, 128, 512), BF16),
    hpr=((128, 512), BF16),
    hpl=((32, 1024), BF16),
    hpf=((128, 256), BF16),
    hpm=((9, 32, 256), BF16),
    ryl=((4, 32, 1024), BF16),
    rym=((9, 4, 32, 256), BF16),
    ryf=((4, 128, 256), BF16),
    rzr=((3, 128, 512), BF16),
    rzl=((3, 32, 1024), BF16),
    rzm=((3, 9, 32, 256), BF16),
    rzf=((3, 128, 256), BF16),
)
for _i, _w in enumerate((256, 256, 512, 512, 256, 256)):
    SHAPES["am%d" % _i] = ((8, _w), F32)
    SHAPES["as%d" % _i] = ((8, _w), F32)
    SHAPES["at%d" % _i] = ((8, _w), F32)
    SHAPES["ar%d" % _i] = ((3, 8, _w), F32)
    SHAPES["az%d" % _i] = ((3, 8, _w), F32)

INS = (
    "crop_h", "crop_w", "images", "first", "middle", "last", "reduce", "gates",
    "classes", "heads", "messages", "gain1", "shift1", "gain2", "shift2", "gain3", "shift3", "dcot", "ccot",
)
OUTS = dict(
    o_depth=((160, 512), BF16),
    o_logits=((2, 40, 80), BF16),
    o_img=((160, 2048), BF16),
    o_first=((128, 512), BF16),
    o_gs1=((2, 8, 256), F32),
    o_mid=((9, 32, 512), BF16),
    o_gs2=((2, 8, 256), F32),
    o_last=((2, 32, 1024), BF16),
    o_gs3=((2, 8, 512), F32),
    o_red=((128, 512), BF16),
    o_heads=((2, 9, 32, 512), BF16),
    o_mess=((2, 9, 32, 512), BF16),
    o_gates=((2, 32, 512), BF16),
    o_cls=((32, 128), F32),
    rm=((3, 9, 2, 2, 32, 256), BF16),
    rh=((3, 9, 2, 2, 32, 256), BF16),
    wfo=((4, 2, 2, 128, 256), BF16),
    st_h=((9, 32, 512), BF16),
    st_m=((9, 32, 512), BF16),
)


def shift_columns(v):
    rows, width = v.shape
    col = lax.broadcasted_iota(jnp.int32, (rows, width), 0)
    left = jnp.where(col == 0, 0.0, pltpu.roll(v, 1, 0))
    right = jnp.where(col == rows - 1, 0.0, pltpu.roll(v, rows - 1, 0))
    return left, right


def spread(src, dst, n_img, width):
    zero = jnp.zeros((80, 3 * width), BF16)
    for pad in range(n_img + 1):
        dst[pl.ds(pad * 400, 80), :] = zero

    def body(i, carry):
        v = src[pl.ds(pl.multiple_of(i * 80, 16), 80), :]
        left, right = shift_columns(v.astype(F32))
        row = pl.multiple_of((i + lax.div(i, np.int32(4)) + 1) * 80, 16)
        dst[pl.ds(row, 80), 0:width] = left.astype(BF16)
        dst[pl.ds(row, 80), width : 2 * width] = v
        dst[pl.ds(row, 80), 2 * width : 3 * width] = right.astype(BF16)
        return carry

    lax.fori_loop(0, 4 * n_img, body, 0)


def conv_rows(a3, w, img):
    acc = None
    for a in range(3):
        base = pl.multiple_of((5 * img + a) * 80, 16)
        part = dot(a3[pl.ds(base, 320), :], w[3 * a : 3 * a + 3].reshape(1536, 256))
        acc = part if acc is None else acc + part
    return acc


def conv_back(d3, w, img):
    acc = None
    for a in range(3):
        for q in range(3):
            base = pl.multiple_of((5 * img + a) * 80, 16)
            tap = 3 * (2 - a) + (2 - q)
            part = dot_last(d3[pl.ds(base, 320), 256 * q : 256 * q + 256], w[tap].reshape(512, 256))
            acc = part if acc is None else acc + part
    return acc


def conv_weight(a3, d3, out, n_img, first, last):
    depth = (5 * n_img - 1) * 80

    def body(tap, carry):
        a = lax.div(tap, np.int32(3))
        q = tap - 3 * a
        left = a3[pl.ds(pl.multiple_of(a * 80, 16), depth), pl.ds(pl.multiple_of(q * 512, 128), 512)]
        out[tap] = dot_first(left, d3[pl.ds(80, depth), 256:512]).astype(BF16).reshape(out.shape[1:])
        return carry

    lax.fori_loop(first, last, body, 0)


def body(names, *refs):
    s = SimpleNamespace(**dict(zip(names, refs)))
    b, r = lax.axis_index("batch"), lax.axis_index("rows")
    z = lax.div(b, np.int32(4))
    y = lax.rem(lax.div(b, np.int32(2)), np.int32(2))
    c = lax.rem(b, np.int32(2))
    ln = Links(s.send_sems, s.recv_sems, s.near_sems)
    half, fhalf = 256 * r, 256 * c

    def dev(zz, yy, cc, rr):
        return (4 * zz + 2 * yy + cc, rr)

    def zk(k):
        return lax.rem(z + k, np.int32(4))

    core, ypeer, xpeer = dev(z, y, 1 - c, r), dev(z, 1 - y, c, r), dev(z, y, c, 1 - r)
    special = r == y
    plain = r != y
    task = 2 * r + y
    img = 2 * y + c
    own_px = pl.multiple_of(320 * img + 160 * r, 16)
    my_rows = pl.multiple_of(160 * r, 16)
    other_rows = pl.multiple_of(160 * (1 - r), 16)
    half = pl.multiple_of(half, 128)
    ohalf = pl.multiple_of(256 * (1 - r), 128)
    fhalf = pl.multiple_of(fhalf, 128)
    offsets = [(dr, dy, dc) for dr in range(2) for dy in range(2) for dc in range(2) if dr + dy + dc]

    def peer(dr, dy, dc):
        rr = 1 - r if dr else r
        yy = 1 - y if dy else y
        cc = 1 - c if dc else c
        return rr, yy, cc

    def px_of(rr, yy, cc):
        return pl.multiple_of(320 * (2 * yy + cc) + 160 * rr, 16)

    ends = (z == 0) | (z == 3)
    inner = jnp.logical_not(ends)
    not_first, not_last = z != 0, z != 3
    far_end = dev(jnp.where(z == 1, 0, 3), y, c, r)
    odd = c == r

    def both(p, q):
        return q if p is None else (p if q is None else p & q)

    def line_start(src, at, pair, when=None, relay=True):
        sides = ln.group(pair, when)
        for q in (1, 3):
            sides.push(src, at(z), dev(zk(q), y, c, r), when)
        across = ln.push(src, at(z), dev(zk(2), y, c, r), both(when, ends) if relay else when)
        return [sides, across, relay, None, None]

    def line_y(state, src, at, four, when=None):
        state[4] = ln.group(four, when)
        state[4].push(src, at(z), ypeer, when)

    def line_relay(state, at, when=None):
        sides, _, relay = state[:3]
        wait([sides], when)
        if relay:
            state[3] = ln.push(at(3 - z), at(3 - z), far_end, both(when, inner))

    def line_sides(state, at, when=None):
        ys = state[4]
        ys.push(at(zk(3)), at(zk(3)), ypeer, when)
        ys.push(at(zk(1)), at(zk(1)), ypeer, when)

    def line_last(state, at, col, when=None):
        _, across, relay, hand, ys = state
        if relay:
            wait([across], both(when, inner))
            wait([hand], both(when, ends))
        else:
            wait([across], when)
        ys.push(at(zk(2)), at(zk(2)), ypeer, when)
        return [ln.push(col(y), col(y), core, when)]

    def line_core(state, col, cores, when=None):
        wait([state[4]], when)
        cores.append(ln.push(col(1 - y), col(1 - y), core, when))

    def at_wf(zz):
        return s.wf.at[zz, y, c]

    def at_wm(zz):
        return s.wm.at[:, zz, y, c]

    def at_wl(zz):
        return s.wl.at[zz, y, c]

    def at_wr(zz):
        return s.wr.at[zz, y]

    def col_wf(yy):
        return s.wf.at[:, yy, c]

    def col_wm(yy):
        return s.wm.at[:, :, yy, c]

    def col_wl(yy):
        return s.wl.at[:, yy, c]

    def col_wr(yy):
        return s.wr.at[:, yy]

    near_last = [
        ln.near(s.last.at[:, pl.ds(pl.multiple_of((2 * i + r) * 128, 128), 128)], s.wl.at[z, y, c, :, 128 * i : 128 * i + 128])
        for i in range(8)
    ]
    near_own = ln.near(s.images, s.xall.at[pl.ds(my_rows, 160)])
    near_cls = ln.near(s.classes, s.wcv)
    near_wf = ln.near(s.first.at[:, pl.ds(half, 256)], s.wf.at[z, y, c])
    near_wm = ln.near(s.middle.at[:, :, pl.ds(half, 256)], s.wm.at[:, z, y, c])
    red_local = pltpu.make_async_copy(s.reduce, s.wr.at[z, y], s.near_sems.at[NEAR - 1])
    pl.when(odd)(red_local.start)
    near_late = [
        ln.near(s.dcot, s.dcotv),
        ln.near(s.ccot, s.cct),
        ln.near(s.heads.at[y, :, :, pl.ds(fhalf, 256)], s.wh.at[:, z, y, c]),
        ln.near(s.messages.at[y, :, :, pl.ds(fhalf, 256)], s.wq.at[:, z, y, c]),
        ln.near(s.gates.at[r, :, pl.ds(fhalf, 256)], s.wg.at[z, y, c]),
    ]
    barrier = pltpu.get_barrier_semaphore()
    friends = [
        dev(zk(q), 1 - y if j else y, 1 - c if i else c, r) for q in range(4) for j in range(2) for i in range(2) if q + j + i
    ] + [dev(z, 1 - y if j else y, 1 - c if i else c, 1 - r) for j in range(2) for i in range(2)]
    for friend in friends:
        pl.semaphore_signal(barrier, inc=1, device_id=friend, device_id_type=MESH)
    pl.semaphore_wait(barrier, len(friends))

    src_wf, src_wm = s.first.at[:, pl.ds(half, 256)], s.middle.at[:, :, pl.ds(half, 256)]
    go_wf = line_start(src_wf, at_wf, lambda: s.wf.at[0, 0], relay=False)
    line_y(go_wf, src_wf, at_wf, lambda: s.wf.at[:, 0, 0])
    img_x = ln.push(s.images, s.xall.at[pl.ds(my_rows, 160)], xpeer)
    go_wm = line_start(src_wm, at_wm, lambda: s.wm.at[:, 0, 0])
    line_y(go_wm, src_wm, at_wm, lambda: s.wm.at[:, :, 0, 0])
    for cp in near_last:
        cp.wait()

    for i in range(4):
        high, wide = s.crop_h[4 * z + i], s.crop_w[4 * z + i]
        for row in range(4):
            col = lax.broadcasted_iota(jnp.int32, (80, 128), 0)
            inside = (col < wide) & (row < high)
            s.maskp[pl.ds(320 * i + 80 * row, 80), :] = jnp.where(inside, 1.0, 0.0)
    total = s.crop_h[0] * s.crop_w[0]
    for i in range(1, 16):
        total = total + s.crop_h[i] * s.crop_w[i]
    count = total.astype(F32)
    mine = pl.multiple_of(320 * img, 16)

    def mask_at(base, rows, width):
        return lanes(s.maskp[pl.ds(mine + base, rows), :], width)

    s.gains[...] = jnp.zeros((8, 128), F32)
    for i, ref in enumerate((s.gain1, s.shift1, s.gain2, s.shift2)):
        s.gains[i : i + 1, 0:32] = ref[...].astype(F32)
    s.gains[4:5, :] = s.gain3[...].astype(F32)
    s.gains[5:6, :] = s.shift3[...].astype(F32)
    near_cls.wait()
    s.wcs[...] = jnp.zeros(s.wcs.shape, BF16)
    s.wcs[:, 0:40] = s.wcv[...]
    s.wc[b] = s.wcs[...]
    near_own.wait()
    near_wf.wait()
    line_relay(go_wf, at_wf)
    line_sides(go_wf, at_wf)
    cores_wf = line_last(go_wf, at_wf, col_wf)
    near_wm.wait()
    line_relay(go_wm, at_wm)
    go_wl = line_start(at_wl(z), at_wl, lambda: s.wl.at[0, 0])
    line_core(go_wf, col_wf, cores_wf)
    wait([img_x])

    def mask_x(base):
        rows = pl.ds(base, 80)
        v = (s.xall[rows, :].astype(F32) * mask_at(base, 80, 2048)).astype(BF16)
        s.xall[rows, :] = v
        for i in range(8):
            pick = jnp.where(r == 0, v[:, 256 * i : 256 * i + 128].astype(F32), v[:, 256 * i + 128 : 256 * i + 256].astype(F32))
            s.xh[rows, 128 * i : 128 * i + 128] = pick.astype(BF16)

    rows_loop(320, 80, mask_x)
    wait(cores_wf)
    wfo_x = ln.group(lambda: s.wf)
    for zz in (0, 1):
        wfo_x.push(s.wf.at[zz], s.wfo.at[zz], xpeer)

    def task_push(src, dst, lo, hi, staged):
        yy = 1 - y if staged else y
        taps = hi - lo
        sides = ln.group(lambda: s.rbuf.at[0 : 80 * taps])
        across = ln.group(lambda: dst.at[lo:hi, 0, 0], ends)
        for q in (1, 3, 2, 0):
            for i in range(2):
                if q + i == 0:
                    continue
                cc = 1 - c if i else c
                (across if q == 2 else sides).push(
                    src.at[lo:hi, :, pl.ds(pl.multiple_of(256 * cc, 128), 256)],
                    dst.at[lo:hi, z, yy, c],
                    dev(zk(q) if q else z, y, cc, r),
                    ends if q == 2 else None,
                )
        return sides, across, lo, hi, yy

    def task_relay(state, dst):
        sides, across, lo, hi, yy = state
        wait([sides])
        hand = ln.push(dst.at[lo:hi, 3 - z, yy], dst.at[lo:hi, 3 - z, yy], far_end, inner)
        return across, hand

    def task_ready(state):
        across, hand = state
        wait([across], inner)
        wait([hand], ends)

    def plane_start(n):
        m, ar = (getattr(s, p + str(n)) for p in ("am", "ar"))
        one = ln.group(lambda: ar)
        for i in (1, 2, 3):
            yy = 1 - y if i & 2 else y
            cc = 1 - c if i & 1 else c
            one.push(m, ar.at[i - 1], dev(z, yy, cc, r))
        return one

    def plane_end(n, one):
        m, sm, ar = (getattr(s, p + str(n)) for p in ("am", "as", "ar"))
        wait([one])
        sm[...] = (m[...] + ar[0]) + (ar[1] + ar[2])

    def reduce_plane(n):
        plane_end(n, plane_start(n))

    def reduce_line(n, bulk=None):
        sm, t, az = (getattr(s, p + str(n)) for p in ("as", "at", "az"))
        two = ln.group(lambda: az)
        for q in (1, 2, 3):
            two.push(sm, az.at[q - 1], dev(zk(q), y, c, r))
        if bulk is not None and n in BEHIND:
            bulk()
        wait([two])
        if bulk is not None and n not in BEHIND:
            bulk()
        t[...] = (sm[...] + az[0]) + (az[1] + az[2])
        return t[...]

    def stats_of(pre, width, msg):
        m = lanes(s.maskp[pl.ds(mine, 320), :], width)
        v = pre * m
        sums = jnp.sum(v, axis=0, keepdims=True)
        squares = jnp.sum(v * pre, axis=0, keepdims=True)
        return sums, squares

    def norm_terms(n, bnp, width, bulk=None):
        t = reduce_line(n, bulk)
        if width == 256:
            rows = [t[i : i + 1] for i in range(4)]
        else:
            rows = [jnp.concatenate([t[2 * i : 2 * i + 1], t[2 * i + 1 : 2 * i + 2]], axis=1) for i in range(4)]
        mean = rows[0] / count
        inv = lax.rsqrt(rows[1] / count - mean * mean + EPS)
        bnp[0:1], bnp[1:2], bnp[2:3], bnp[3:4] = mean, inv, rows[2], rows[3]

    quarter = lax.div(b, np.int32(4))
    spot = 32 * lax.rem(b, np.int32(4))

    def placed(n):
        lane = lax.broadcasted_iota(jnp.int32, (8, 128), 1)
        out = []
        for p in range(2):
            if n < 2:
                v = jnp.broadcast_to(s.gains[2 * n + p : 2 * n + p + 1, :], (8, 128))
                v = pltpu.roll(v, spot, 1)
                v = jnp.where((lane >= spot) & (lane < spot + 32), v, 0.0)
                out.append(jnp.concatenate([jnp.where(quarter == 2 * r + i, v[0:1], 0.0) for i in range(2)], axis=1))
            else:
                v = s.gains[4 + p : 5 + p, :]
                out.append(
                    [
                        jnp.concatenate(
                            [jnp.where(odd & (lax.div(b, np.int32(2)) == 4 * h + i), v, 0.0) for i in range(4)], axis=1
                        )
                        for h in range(2)
                    ]
                )
        return out

    def put_stats(n, first, second, width, layer):
        m = getattr(s, "am%d" % n)
        m[...] = jnp.zeros(m.shape, F32)
        if width == 256:
            m[0:1], m[1:2] = first, second
            if layer is not None:
                m[2:3], m[3:4] = placed(layer)
        else:
            m[0:1], m[1:2] = first[:, :512], first[:, 512:]
            m[2:3], m[3:4] = second[:, :512], second[:, 512:]
            if layer is not None:
                gain, shift = placed(layer)
                m[4:5], m[5:6] = gain
                m[6:7], m[7:8] = shift

    pre = dot(s.xall[...], s.wf[...].reshape(2048, 256))
    s.pre1[...] = pre
    first_sum, first_sq = stats_of(pre, 256, None)
    put_stats(0, first_sum, first_sq, 256, 0)
    plane_one = plane_start(0)
    line_sides(go_wm, at_wm)
    plane_end(0, plane_one)
    line_y(go_wl, at_wl(z), at_wl, lambda: s.wl.at[:, 0, 0])
    pl.when(odd)(red_local.wait)
    heads = []
    late_wr = []

    def bulk_one():
        line_relay(go_wl, at_wl)
        line_sides(go_wl, at_wl)
        late_wr.append(line_start(s.reduce, at_wr, lambda: s.wr.at[0], odd))
        heads.append(task_push(s.heads.at[y], s.wh, 0, 6, False))
        late_wr.append(line_last(go_wm, at_wm, col_wm))

    norm_terms(0, s.bnp1, 256, bulk_one)
    go_wr = late_wr[0]
    cores_wm = late_wr[1]

    def act_from(prebuf, bnp, dst):
        def step(base):
            x = (prebuf[pl.ds(base, 80), :] - bnp[0:1]) * bnp[1:2] * bnp[2:3] + bnp[3:4]
            dst[pl.ds(base, 80), pl.ds(half, 256)] = (gelu_of(x) * mask_at(base, 80, 256)).astype(BF16)

        rows_loop(320, 80, step)

    act_from(s.pre1, s.bnp1, s.a1)
    a1_x = ln.push(s.a1.at[:, pl.ds(half, 256)], s.a1.at[:, pl.ds(half, 256)], xpeer)
    line_core(go_wm, col_wm, cores_wm)
    cores_wl = line_last(go_wl, at_wl, col_wl)
    wait(cores_wm)
    wait([a1_x])
    wfo_x.push(s.wf.at[2], s.wfo.at[2], xpeer)
    spread(s.a1, s.a3, 1, 512)
    pre = conv_rows(s.a3, s.wm, 0)
    s.pre2[...] = pre
    first_sum, first_sq = stats_of(pre, 256, None)
    put_stats(1, first_sum, first_sq, 256, 1)
    plane_two = plane_start(1)
    over_h = ln.push(s.heads.at[1 - y], s.st_h, ypeer)
    plane_end(1, plane_two)
    relayed_h = []
    mess = []

    def mess_push(a, staged):
        return task_push(s.st_m if staged else s.messages.at[y], s.wq, 3 * a, 3 * a + 3, staged)

    def bulk_two():
        line_relay(go_wr, at_wr, odd)
        relayed_h.append(task_relay(heads[0], s.wh))
        heads.append(task_push(s.heads.at[y], s.wh, 6, 9, False))
        mess.append([mess_push(0, False)])

    norm_terms(1, s.bnp2, 256, bulk_two)
    line_y(go_wr, s.reduce, at_wr, lambda: s.wr.at[:, 0], odd)
    line_sides(go_wr, at_wr, odd)
    act_from(s.pre2, s.bnp2, s.a2)
    a2_x = ln.push(s.a2.at[:, pl.ds(half, 256)], s.a2.at[:, pl.ds(half, 256)], xpeer)
    line_core(go_wl, col_wl, cores_wl)
    cores_wr = line_last(go_wr, at_wr, col_wr, odd)
    wait(cores_wl)
    wait([a2_x])
    wfo_x.push(s.wf.at[3], s.wfo.at[3], xpeer)
    pre = dot(s.a2[...], s.wl[...].reshape(512, 1024))
    s.pre3[...] = pre
    first_sum, first_sq = stats_of(pre, 1024, None)
    put_stats(2, first_sum, first_sq, 1024, 2)
    plane_three = plane_start(2)
    over_m = ln.push(s.messages.at[1 - y], s.st_m, ypeer)
    plane_end(2, plane_three)
    def bulk_three():
        relayed_h.append(task_relay(heads[1], s.wh))
        heads.append(task_push(s.st_h, s.wh, 0, 5, True))
        heads.append(task_push(s.st_h, s.wh, 5, 9, True))

    wait([over_h])
    norm_terms(2, s.bnp3, 1024, bulk_three)
    staged_h = ln.near(s.st_h.at[:, :, pl.ds(fhalf, 256)], s.wh.at[:, z, 1 - y, c])
    gate_got = {}
    cls_got = ln.group(lambda: s.wc.at[0:15])
    for q in range(4):
        for j in range(2):
            if q + j:
                gate_got[q, j] = ln.group(lambda: s.wg.at[0, 0], (y == r) if j == 0 else (y != r))
            for i in range(2):
                if q + j + i == 0:
                    continue
                yy = 1 - y if j else y
                cc = 1 - c if i else c
                to = dev(zk(q) if q else z, yy, cc, r)
                cls_got.push(s.wcs, s.wc.at[b], to)
                src = s.gates.at[r, :, pl.ds(pl.multiple_of(256 * cc, 128), 256)]
                if q + j:
                    gate_got[q, j].push(src, s.wg.at[z, y, c], to, (y == r) if j == 0 else (y != r))
                else:
                    gate_got[0, 0] = ln.push(src, s.wg.at[z, y, c], to, y == r)

    def summed_at(base, rows):
        x = (s.pre3[pl.ds(base, rows), :] - s.bnp3[0:1]) * s.bnp3[1:2]
        return x, x * s.bnp3[2:3] + s.bnp3[3:4] + s.xh[pl.ds(base, rows), :].astype(F32)

    def block_step(base):
        _, v = summed_at(base, 32)
        s.blk[pl.ds(base, 32), :] = (gelu_of(v) * mask_at(base, 32, 1024)).astype(BF16)

    rows_loop(320, 32, block_step)
    line_core(go_wr, col_wr, cores_wr, odd)
    wait(cores_wr, jnp.logical_not(odd))
    wred = s.wr[...].reshape(1024, 512)
    s.rps[...] = dot(s.blk[pl.ds(other_rows, 160), :], wred).astype(BF16)
    red_x = ln.push(s.rps, s.rpr, xpeer)
    part = dot(s.blk[pl.ds(my_rows, 160), :], wred)
    wait([red_x])
    s.rbuf[pl.ds(own_px, 160), :] = (part + s.rpr[...].astype(F32)).astype(BF16)

    def block_of(rr, yy, cc, lo=0, n=160):
        return s.rbuf.at[pl.ds(pl.multiple_of(px_of(rr, yy, cc) + lo, 16), n)]

    for cp in near_late:
        cp.wait()
    own = block_of(r, y, c)
    g_x = ln.push(own, own, xpeer)
    g_y = ln.push(own, own, ypeer)
    g_c = ln.push(own, own, core)
    wait([g_x])
    relayed_h.append(task_relay(heads[2], s.wh))
    bx = block_of(1 - r, y, c, 0, 80)
    g_xy = ln.push(bx, bx, ypeer)
    wait([g_y])
    by = block_of(r, 1 - y, c, 80, 80)
    g_yx = ln.push(by, by, xpeer)
    bx = block_of(1 - r, y, c)
    g_c1 = ln.push(bx, bx, core)
    by = block_of(r, 1 - y, c)
    g_c2 = ln.push(by, by, core)
    relayed_h.append(task_relay(heads[3], s.wh))
    wait([g_xy, g_yx])
    bd = block_of(1 - r, 1 - y, c)
    g_c3 = ln.push(bd, bd, core)
    wait([over_m])
    staged_m = ln.near(s.st_m.at[:, :, pl.ds(fhalf, 256)], s.wq.at[:, z, 1 - y, c])
    mess[0].append(mess_push(0, True))
    mess.append([mess_push(1, False), mess_push(1, True)])
    mess.append([mess_push(2, False)])
    wait([g_c, g_c1, g_c2, g_c3])

    near_end = dev(jnp.where(z == 0, 1, 2), y, c, r)
    other_end = dev(jnp.where(z == 1, 3, 0), y, c, r)

    def grad_push(n, g, rm, lo, hi):
        def like(slot):
            return lambda side: rm.at[slot, lo:hi] if side else g.at[lo:hi, 0]

        got = {}
        for q in (1, 2, 3):
            direct = {1: not_last, 2: ends, 3: not_first}[q]
            got[q] = ln.push(g.at[lo:hi, zk(q)], rm.at[q - 1, lo:hi], dev(zk(q), y, c, r), direct, like(q - 1))
        hop = s.hop.at[n, lo:hi]
        got[0] = ln.push(
            g.at[lo:hi, 3 - z], hop, near_end, ends, lambda side: s.hop.at[n, lo:hi] if side else g.at[lo:hi, 0]
        )
        return got, n, g, rm, lo, hi

    def grad_hop(state):
        got, n, g, rm, lo, hi = state

        def add():
            got[0].wait_recv()
            far = jnp.where(z == 1, 3, 0)
            for t in range(lo, hi):
                s.hop[n, t] = (s.hop[n, t].astype(F32) + g[t, far].astype(F32)).astype(BF16)

        pl.when(inner)(add)
        got[4] = ln.push(
            s.hop.at[n, lo:hi], rm.at[1, lo:hi], other_end, inner,
            lambda side: rm.at[1, lo:hi] if side else s.hop.at[n, lo:hi],
        )

    def grad_wait(state):
        got = state[0]
        wait([got[1]], not_first)
        wait([got[3]], not_last)
        wait([got[2]], inner)
        wait([got[4]], ends)

    def tasks(r3, f3, d3, preh, dfull):
        spread(s.rbuf, r3, 4, 512)
        for part in relayed_h:
            task_ready(part)
        staged_h.wait()

        def head_step(i, carry):
            v = conv_rows(r3, s.wh, i)
            px = pl.multiple_of(i * 320, 16)
            preh[pl.ds(px, 320), :] = v
            return carry

        lax.fori_loop(0, 4, head_step, 0)

        def feat_step(base):
            m = lanes(s.maskp[pl.ds(base, 80), :], 256)
            s.fown[pl.ds(base, 80), :] = (gelu_of(preh[pl.ds(base, 80), :]) * m).astype(BF16)

        rows_loop(1280, 80, feat_step)
        f_c = ln.push(s.fown, s.ffull.at[:, pl.ds(fhalf, 256)], core)
        f_n = ln.near(s.fown, s.ffull.at[:, pl.ds(fhalf, 256)])

        def seven():
            return s.dmg.at[0:1120]

        def pieces(n):
            return lambda: s.dmg.at[0 : 160 * n]

        even = [o for o in offsets if (o[0] + o[1]) % 2 == 0]
        uneven = [o for o in offsets if (o[0] + o[1]) % 2]

        def to_owners(src, dst_of):
            got = [ln.group(pieces(len(o)), special) for o in (even, uneven)]
            for g, group in zip(got, (even, uneven)):
                for o in group:
                    rr, yy, cc = peer(*o)
                    g.push(src.at[pl.ds(px_of(rr, yy, cc), 160)], dst_of().at[:, pl.ds(fhalf, 256)], dev(z, yy, cc, rr), special)
            return got

        def from_tasks(got):
            wait([got[0]], special)
            wait([got[1]], plain)

        def to_tasks(src_of, dst):
            got = [ln.group(pieces(len(o)), w) for o, w in ((even, special), (uneven, plain))]
            for g, group, w in zip(got, (even, uneven), (special, plain)):
                for o in group:
                    rr, yy, cc = peer(*o)
                    ll = pl.ds(pl.multiple_of(256 * cc, 128), 256)
                    g.push(src_of(rr).at[:, ll], dst.at[pl.ds(own_px, 160)], dev(z, yy, cc, rr), w)
            return got

        def keep(dst, src):
            def run():
                dst[:, pl.ds(fhalf, 256)] = src[pl.ds(own_px, 160), :]

            return run

        pl.when(special)(keep(s.fg.at[r, 0], s.fown))
        f_n.wait()
        wait([f_c])

        def gate_ready():
            for cp in gate_got.values():
                cp.wait_recv()

        pl.when(special)(gate_ready)

        @pl.when(special)
        def _():
            def gate_step(base):
                v = dot(s.ffull[pl.ds(base, 320), :], s.wg[...].reshape(512, 256))
                s.gateb[pl.ds(base, 320), :] = (1.0 / (1.0 + jnp.exp(-v))).astype(BF16)

            rows_loop(1280, 320, gate_step)

        g_own = to_owners(s.gateb, lambda: s.fg.at[r, 1])
        pl.when(special)(keep(s.fg.at[r, 1], s.gateb))

        relayed = [[task_relay(p, s.wq) for p in mess[0]]]
        mess[2].append(mess_push(2, True))
        spread(s.ffull, f3, 4, 512)

        wait([cls_got])
        for i in range(2):
            s.ctf[...] = jnp.zeros((128, 128), F32)
            s.ctf[0:40, 0:80] = s.cct[i].astype(F32)
            turned = s.ctf[...].T
            s.ccotv[80 * i : 80 * i + 80, :] = turned[0:80, :].astype(BF16)
        from_tasks(g_own)

        def early_step(base):
            rows = pl.ds(base, 32)
            m = lanes(s.maskp[pl.ds(own_px + base, 32), :], 512)
            gd, gc = s.fg[0, 1, rows, :].astype(F32), s.fg[1, 1, rows, :].astype(F32)
            dj = (s.ccotv[rows, :].astype(F32) * m[:, :128]).astype(BF16)
            s.ccotv[rows, :] = dj
            dd = s.dcotv[rows, :].astype(F32) * m
            dmer = dot_last(dj, s.wc[...].reshape(512, 128))
            s.eu[0, rows, :] = dd.astype(BF16)
            s.eu[1, rows, :] = dmer.astype(BF16)
            down, up = dd * gd, dmer * gc
            both = (down + up).astype(BF16)
            s.dm[0, rows, :] = up.astype(BF16)
            s.dm[1, rows, :] = both
            s.dm[2, rows, :] = both
            s.dm[3, rows, :] = down.astype(BF16)

        rows_loop(160, 32, early_step)
        d_got = ln.group(seven)
        for o in offsets:
            rr, yy, cc = peer(*o)
            ll = pl.ds(pl.multiple_of(256 * cc, 128), 256)
            d_got.push(s.dm.at[2 * rr + yy, :, ll], s.dmg.at[pl.ds(own_px, 160)], dev(z, yy, cc, rr))
        s.dmg[pl.ds(own_px, 160), :] = s.dm[task, :, pl.ds(fhalf, 256)]

        @pl.when(special)
        def _():
            s.exg[0, pl.ds(own_px, 160), :] = s.eu[r, :, pl.ds(fhalf, 256)]

        @pl.when(jnp.logical_not(special))
        def _():
            s.exg[0] = jnp.zeros(s.exg.shape[1:], BF16)

        relayed.append([task_relay(p, s.wq) for p in mess[1]])

        def mess_conv(a):
            for p in relayed[a]:
                task_ready(p)

            def mess_step(i, carry):
                rows = pl.ds(pl.multiple_of(i * 320, 16), 320)
                base = pl.multiple_of((5 * i + a) * 80, 16)
                v = dot(f3[pl.ds(base, 320), :], s.wq[3 * a : 3 * a + 3].reshape(1536, 256))
                if a:
                    v = dfull[rows, 0:256] + v
                if a < 2:
                    dfull[rows, 0:256] = v
                else:
                    s.msgb[rows, :] = v.astype(BF16)
                return carry

            lax.fori_loop(0, 4, mess_step, 0)

        staged_m.wait()
        mess_conv(0)
        wait([d_got])
        f_own = to_owners(s.fown, lambda: s.fg.at[r, 0])
        u_got = to_tasks(lambda rr: s.eu.at[rr], s.exg.at[0])
        spread(s.dmg, d3, 4, 256)
        conv_weight(f3, d3, s.gm, 4, 0, 6)
        relayed.append([task_relay(p, s.wq) for p in mess[2]])
        gm_z = [grad_push(0, s.gm, s.rm, 0, 3), grad_push(0, s.gm, s.rm, 3, 6)]
        mess_conv(1)
        conv_weight(f3, d3, s.gm, 4, 6, 9)
        gm_z.append(grad_push(0, s.gm, s.rm, 6, 9))
        mess_conv(2)
        m_own = ln.group(seven)
        for o in offsets:
            rr, yy, cc = peer(*o)
            m_own.push(s.msgb.at[pl.ds(px_of(rr, yy, cc), 160)], s.mrecv.at[task, :, pl.ds(fhalf, 256)], dev(z, yy, cc, rr))
        keep(s.mrecv.at[task], s.msgb)()

        def back_step(i, carry):
            px = pl.multiple_of(i * 320, 16)
            dfull[pl.ds(px, 320), :] = conv_back(d3, s.wq, i)
            return carry

        lax.fori_loop(0, 4, back_step, 0)

        from_tasks(f_own)
        wait([m_own])

        def stream_step(base):
            rows = pl.ds(base, 32)
            m = lanes(s.maskp[pl.ds(own_px + base, 32), :], 512)
            m0, m1, m2, m3 = (s.mrecv[t, rows, :].astype(F32) for t in range(4))
            f0, f3_ = s.fg[0, 0, rows, :].astype(F32), s.fg[1, 0, rows, :].astype(F32)
            mid = m1 + m2
            sd, sc = mid + m3, m0 + mid
            gd, gc = s.fg[0, 1, rows, :].astype(F32), s.fg[1, 1, rows, :].astype(F32)
            s.ods[rows, :] = ((f0 + gd * sd) * m).astype(BF16)
            merged = (f3_ + gc * sc).astype(BF16)
            s.mrg[rows, :] = merged
            s.olg[rows, :] = (dot(merged, s.wc[...].reshape(512, 128)) * m[:, :128]).astype(BF16)
            dd, dmer = s.eu[0, rows, :].astype(F32), s.eu[1, rows, :].astype(F32)
            s.fg[0, 1, rows, :] = (dd * sd * gd * (1.0 - gd)).astype(BF16)
            s.fg[1, 1, rows, :] = (dmer * sc * gc * (1.0 - gc)).astype(BF16)

        rows_loop(160, 32, stream_step)
        e_got = to_tasks(lambda rr: s.fg.at[rr, 1], s.exg.at[1])

        @pl.when(special)
        def _():
            s.exg[1, pl.ds(own_px, 160), :] = s.fg[r, 1, :, pl.ds(fhalf, 256)]

        for i in range(2):
            s.ctf[...] = jnp.zeros((128, 128), F32)
            s.ctf[0:80, :] = s.olg[80 * i : 80 * i + 80, :].astype(F32)
            turned = s.ctf[...].T
            s.olt[i] = turned[0:40, 0:80].astype(BF16)
        out_near = [ln.near(s.ods, s.o_depth), ln.near(s.olt, s.o_logits)]
        s.gcls[...] = dot_first(s.mrg[...], s.ccotv[...]).astype(BF16).reshape(16, 32, 128)
        grad_hop(gm_z[0])
        wait(u_got + e_got, special)

        @pl.when(special)
        def _():
            def gate_back(base):
                rows = pl.ds(base, 320)
                dfull[rows, :] = dfull[rows, :] + dot_last(s.exg[1, rows, :], s.wg[...].reshape(512, 256))

            rows_loop(1280, 320, gate_back)

        chalf = pl.ds(pl.multiple_of(256 * (1 - c), 128), 256)

        def give(base):
            rows = pl.ds(base, 80)
            s.dfs[rows, :] = dfull[rows, chalf].astype(BF16)

        rows_loop(1280, 80, give)
        df_c = ln.push(s.dfs, s.dfr, core)

        @pl.when(special)
        def _():
            s.gg[...] = dot_first(s.ffull[...], s.exg[1]).astype(BF16).reshape(s.gg.shape)

        gg_z = [ln.push(s.gg.at[zk(k)], s.rg.at[k - 1], dev(zk(k), y, c, r), special, lambda side, k=k: s.rg.at[k - 1] if side else s.gg.at[0]) for k in (1, 2, 3)]
        cg = ln.group(lambda: s.rcls)
        n_cls = 0
        for q in range(4):
            for j in range(2):
                for i in range(2):
                    if q + j + i == 0:
                        continue
                    yy = 1 - y if j else y
                    cc = 1 - c if i else c
                    zz = zk(q) if q else z
                    cg.push(s.gcls.at[4 * zz + 2 * yy + cc], s.rcls.at[n_cls], dev(zz, yy, cc, r))
                    n_cls += 1
        wait([df_c])

        def dhead_step(base):
            rows = pl.ds(base, 80)
            m = lanes(s.maskp[rows, :], 256)
            d = dfull[rows, pl.ds(fhalf, 256)] + s.dfr[rows, :].astype(F32) + s.exg[0, rows, :].astype(F32)
            s.dmg[rows, :] = (slope_of(preh[rows, :]) * d * m).astype(BF16)

        rows_loop(1280, 80, dhead_step)
        spread(s.dmg, d3, 4, 256)

        def back_step2(i, carry):
            px = pl.multiple_of(i * 320, 16)
            dfull[pl.ds(px, 320), :] = conv_back(d3, s.wh, i)
            return carry

        lax.fori_loop(0, 4, back_step2, 0)
        for yy in range(2):
            src = pl.multiple_of(320 * (2 * yy) + 320 * (1 - c), 16)
            s.drs[pl.ds(320 * yy, 320), :] = dfull[pl.ds(src, 320), :].astype(BF16)
        dr_c = ln.push(s.drs, s.drr, core)
        grad_hop(gm_z[1])
        wait([dr_c])
        for yy in range(2):
            src = pl.multiple_of(320 * (2 * yy) + 320 * c, 16)
            rows = pl.ds(320 * yy, 320)
            s.drr[rows, :] = (dfull[pl.ds(src, 320), :] + s.drr[rows, :].astype(F32)).astype(BF16)
        ro = []
        for dr, dy in ((1, 0), (0, 1), (1, 1)):
            rr, yy, _ = peer(dr, dy, 0)
            src = s.drr.at[pl.ds(pl.multiple_of(320 * yy + 160 * rr, 16), 160)]
            ro.append(ln.push(src, s.dro.at[len(ro)], dev(z, yy, c, rr)))
        gh_z = []
        conv_weight(r3, d3, s.gh, 4, 0, 3)
        gh_z.append(grad_push(1, s.gh, s.rh, 0, 3))
        conv_weight(r3, d3, s.gh, 4, 3, 9)
        wait(ro)
        keep_rows = pl.ds(pl.multiple_of(320 * y + 160 * r, 16), 160)
        total_red = s.drr[keep_rows, :].astype(F32)
        for i in range(3):
            total_red = total_red + s.dro[i].astype(F32)
        s.dred[pl.ds(my_rows, 160), :] = total_red.astype(BF16)
        for cp in out_near:
            cp.wait()
        ln.drain(scoped=True)
        return cg, gm_z, gg_z, gh_z

    state = {}

    def scope_tasks(*scr):
        state["t"] = tasks(*scr)

    pl.run_scoped(
        scope_tasks,
        pltpu.VMEM((1680, 1536), BF16),
        pltpu.VMEM((1680, 1536), BF16),
        pltpu.VMEM((1680, 768), BF16),
        pltpu.VMEM((1280, 256), F32),
        pltpu.VMEM((1280, 512), F32),
    )
    cg, gm_z, gg_z, gh_z = state["t"]

    dr_x = ln.push(s.dred.at[pl.ds(my_rows, 160)], s.dred.at[pl.ds(my_rows, 160)], xpeer)

    def block_back(*late):
        for name, ref in zip(LATE, late):
            setattr(s, name, ref)
        gr, gl, gq, gf = s.gr, s.gl, s.gq, s.gf

        def to_core(g, rc, lead):
            at = g.at[:, :, :, 1 - c] if lead else g.at[:, :, 1 - c]
            return ln.push(at, rc, core)

        def add_core(g, rc, lead):
            if lead:
                for t in range(9):
                    rc[t] = (rc[t].astype(F32) + g[t, :, :, c].astype(F32)).astype(BF16)
            else:
                for t in range(rc.shape[0]):
                    rc[t] = (rc[t].astype(F32) + g[t, :, c].astype(F32)).astype(BF16)

        def to_y(rc, ry, lead):
            return ln.push(rc.at[:, :, 1 - y] if lead else rc.at[:, 1 - y], ry, ypeer)

        def add_y(rc, ry, lead):
            for t in range(ry.shape[0]):
                mine_y = rc[t, :, y] if lead else rc[t, y]
                ry[t] = (ry[t].astype(F32) + mine_y.astype(F32)).astype(BF16)

        def to_z(ry, rz, lead, when=None, hop=None):
            def part(zz):
                return ry.at[:, zz] if lead else ry.at[zz]

            got = {}
            for q in (1, 2, 3):
                direct = None if hop is None else {1: not_last, 2: ends, 3: not_first}[q]
                got[q] = ln.push(part(zk(q)), rz.at[q - 1], dev(zk(q), y, c, r), both(when, direct))
            if hop is not None:
                got[0] = ln.push(part(3 - z), hop, near_end, both(when, ends))
            return got, part, rz, hop, when

        def hop_z(state):
            got, part, rz, hop, when = state

            def add():
                got[0].wait_recv()
                hop[...] = (hop[...].astype(F32) + part(jnp.where(z == 1, 3, 0))[...].astype(F32)).astype(BF16)

            pl.when(both(when, inner))(add)
            got[4] = ln.push(hop, rz.at[1], other_end, both(when, inner))

        def wait_z(state):
            got, _, _, hop, when = state
            if hop is None:
                wait([got[1], got[2], got[3]], when)
            else:
                wait([got[1]], both(when, not_first))
                wait([got[3]], both(when, not_last))
                wait([got[2]], both(when, inner))
                wait([got[4]], both(when, ends))

        def add_z(ry, rz, fin, lead, hop=True):
            mine_z = (ry[:, z] if lead else ry[z]).astype(F32)
            v0, v2 = rz[0].astype(F32), rz[2].astype(F32)
            if hop:
                v0, v2 = jnp.where(z == 0, 0.0, v0), jnp.where(z == 3, 0.0, v2)
            fin[...] = ((mine_z + v0) + (rz[1].astype(F32) + v2)).astype(BF16)

        def task_out(states, rm, g, ps, out):
            for part in states:
                grad_wait(part)
            loads = [[ln.near(rm.at[q, 3 * part : 3 * part + 3], s.zst.at[part % 2, q]) for q in range(3)] for part in range(2)]
            for part in range(3):
                for cp in loads[part]:
                    cp.wait()
                v0 = s.zst.at[part % 2]
                for t in range(3):
                    first_in = jnp.where(z == 0, 0.0, v0[0, t].astype(F32))
                    third_in = jnp.where(z == 3, 0.0, v0[2, t].astype(F32))
                    v = g[3 * part + t, z].astype(F32) + first_in + (v0[1, t].astype(F32) + third_in)
                    ps[3 * part + t] = v.astype(BF16)
                if part == 0:
                    loads.append([ln.near(rm.at[q, 6:9], s.zst.at[0, q]) for q in range(3)])
            lanes_out = pl.ds(fhalf, 256)
            sent = []
            for i in (1, 2, 3):
                yy = 1 - y if i & 2 else y
                cc = 1 - c if i & 1 else c
                sent.append(ln.push(ps.at[:, yy, cc], out.at[y, :, :, lanes_out], dev(z, yy, cc, r)))
            return sent, ln.near(ps.at[:, y, c], out.at[y, :, :, lanes_out])

        wait([dr_x])

        def d3_step(i, carry):
            su, sux = carry
            rows = pl.ds(pl.multiple_of(i * 32, 16), 32)
            x, v = summed_at(i * 32, 32)
            u = slope_of(v) * s.u3[rows, :] * mask_at(i * 32, 32, 1024)
            s.u3[rows, :] = u
            s.dsum[rows, :] = u.astype(BF16)
            return su + jnp.sum(u, axis=0, keepdims=True), sux + jnp.sum(u * x, axis=0, keepdims=True)

        s.u3[...] = dot_last(s.dred[...], s.wr[...].reshape(1024, 512))
        nil = jnp.zeros((1, 1024), F32)
        su, sux = lax.fori_loop(0, 10, d3_step, (nil, nil))
        put_stats(3, su, sux, 1024, None)
        ar3 = plane_start(3)
        ds_x = ln.push(s.dsum.at[pl.ds(other_rows, 160)], s.dsr, xpeer)
        grad_hop(gm_z[2])
        gr[...] = dot_first(s.blk[...], s.dred[...]).astype(BF16).reshape(gr.shape)
        gr_c = ln.push(gr, s.rcr, core, jnp.logical_not(odd))
        plane_end(3, ar3)
        t = reduce_line(3, lambda: gh_z.append(grad_push(1, s.gh, s.rh, 3, 6)))
        gs3 = ln.push(s.at3, s.o_gs3.at[r], xpeer)
        gs3n = ln.near(s.at3, s.o_gs3.at[r])
        mu = jnp.concatenate([t[0:1], t[1:2]], axis=1) / count
        mux = jnp.concatenate([t[2:3], t[3:4]], axis=1) / count

        def dp3_step(base):
            rows = pl.ds(base, 32)
            x = (s.pre3[rows, :] - s.bnp3[0:1]) * s.bnp3[1:2]
            d = mask_at(base, 32, 1024) * (s.bnp3[2:3] * s.bnp3[1:2]) * (s.u3[rows, :] - mu - x * mux)
            s.dp3[rows, :] = d.astype(BF16)

        rows_loop(320, 32, dp3_step)

        def partial_out(pas, value_of):
            pas[...] = value_of(ohalf).astype(BF16)

        wlast = s.wl
        s.u3[:, 0:512] = dot_last(s.dp3[...], wlast[...].reshape(512, 1024))
        s.pas2[...] = s.u3[:, pl.ds(ohalf, 256)].astype(BF16)
        pa2 = ln.push(s.pas2, s.par2, xpeer)
        gl[...] = dot_first(s.a2[...], s.dp3[...]).astype(BF16).reshape(gl.shape)
        gl_c = to_core(gl, s.rcl, False)
        wait([gr_c], odd)

        @pl.when(odd)
        def _():
            for q in range(4):
                s.rcr[q] = (s.rcr[q].astype(F32) + gr[q].astype(F32)).astype(BF16)

        later = {"gr_y": ln.push(s.rcr.at[:, 1 - y], s.ryr, ypeer, odd)}

        def after_plane_two():
            wait([gl_c])
            add_core(gl, s.rcl, False)
            later["gl_y"] = to_y(s.rcl, s.ryl, False)

        def after_plane_one():
            wait([gq_c])
            add_core(gq, s.rcm, True)
            later["gq_y"] = [
                ln.push(s.rcm.at[3 * a : 3 * a + 3, :, 1 - y], s.rym.at[3 * a : 3 * a + 3], ypeer) for a in range(3)
            ]

        wait([pa2])

        def norm_back(n, par, prebuf, bnp, dst, out_gs, middle, after):
            def u_step(i, carry):
                su_, sux_ = carry
                base = pl.multiple_of(i * 80, 16)
                rows = pl.ds(base, 80)
                x = (prebuf[rows, :] - bnp[0:1]) * bnp[1:2]
                v = x * bnp[2:3] + bnp[3:4]
                d = s.u3[rows, pl.ds(half, 256)] + par[rows, :].astype(F32)
                u = slope_of(v) * d * mask_at(base, 80, 256)
                s.u3[rows, 512:768] = u
                return su_ + jnp.sum(u, axis=0, keepdims=True), sux_ + jnp.sum(u * x, axis=0, keepdims=True)

            nil_ = jnp.zeros((1, 256), F32)
            su_, sux_ = lax.fori_loop(0, 4, u_step, (nil_, nil_))
            put_stats(n, su_, sux_, 256, None)
            reduce_plane(n)

            def bulk():
                middle()
                after()

            t_ = reduce_line(n, bulk)
            gsx = ln.push(getattr(s, "at%d" % n), out_gs.at[r], xpeer)
            gsn = ln.near(getattr(s, "at%d" % n), out_gs.at[r])
            mu_, mux_ = t_[0:1] / count, t_[1:2] / count

            def d_step(base):
                rows = pl.ds(base, 80)
                x = (prebuf[rows, :] - bnp[0:1]) * bnp[1:2]
                d = mask_at(base, 80, 256) * (bnp[2:3] * bnp[1:2]) * (s.u3[rows, 512:768] - mu_ - x * mux_)
                dst[rows, :] = d.astype(BF16)

            rows_loop(320, 80, d_step)
            return gsx, gsn

        def window_two():
            grad_hop(gh_z[0])
            gh_z.append(grad_push(1, s.gh, s.rh, 6, 9))
            later["mess"] = task_out(gm_z, s.rm, s.gm, s.psm, s.o_mess)

        def window_one():
            grad_hop(gh_z[1])
            wait([later["gr_y"]], odd)

            @pl.when(odd)
            def _():
                for q in range(4):
                    s.ryr[q] = (s.ryr[q].astype(F32) + s.rcr[q, y].astype(F32)).astype(BF16)

            later["gr_z"] = to_z(s.ryr, s.rzr, False, odd, s.hpr)
            wait([later["gl_y"]])
            add_y(s.rcl, s.ryl, False)
            later["gl_z"] = to_z(s.ryl, s.rzl, False, None, s.hpl)

        gs2, gs2n = norm_back(4, s.par2, s.pre2, s.bnp2, s.dp2, s.o_gs2, after_plane_two, window_two)
        spread(s.dp2, s.d3m, 1, 256)
        s.u3[:, 0:512] = conv_back(s.d3m, s.wm, 0)
        s.pas1[...] = s.u3[:, pl.ds(ohalf, 256)].astype(BF16)
        pa1 = ln.push(s.pas1, s.par1, xpeer)
        conv_weight(s.a3, s.d3m, gq, 1, 0, 9)
        gq_c = to_core(gq, s.rcm, True)
        wait([pa1])
        gs1, gs1n = norm_back(5, s.par1, s.pre1, s.bnp1, s.dp1, s.o_gs1, after_plane_one, window_one)
        dp_x = ln.push(s.dp1.at[pl.ds(other_rows, 160)], s.dp1r, xpeer)
        gf[...] = dot_first(s.xall[...], s.dp1[...]).astype(BF16).reshape(gf.shape)
        gf_c = to_core(gf, s.rcf, False)
        wait([gf_c])
        add_core(gf, s.rcf, False)
        gf_y = to_y(s.rcf, s.ryf, False)
        ms, mn = later["mess"]
        gr_z, gl_z = later["gr_z"], later["gl_z"]
        grad_hop(gh_z[2])
        gq_z = []
        for a in range(3):
            wait([later["gq_y"][a]])
            for t in range(3 * a, 3 * a + 3):
                s.rym[t] = (s.rym[t].astype(F32) + s.rcm[t, :, y].astype(F32)).astype(BF16)
            lead = slice(3 * a, 3 * a + 3)
            rz = SimpleNamespace(at=[s.rzm.at[q, lead] for q in range(3)])
            gq_z.append(to_z(s.rym.at[lead], rz, True, None, s.hpm.at[lead]))
            if a == 0:
                hop_z(gr_z)
                hop_z(gl_z)
            else:
                hop_z(gq_z[a - 1])
        wait([gf_y])
        add_y(s.rcf, s.ryf, False)
        gf_z = to_z(s.ryf, s.rzf, False, None, s.hpf)

        hs, hn = task_out(gh_z, s.rh, s.gh, s.psh, s.o_heads)
        wait([wfo_x])
        wfo_n = ln.near(s.wfo, s.wfov)
        wait([dp_x, ds_x])
        wfo_n.wait()
        mine_d = s.dp1[pl.ds(my_rows, 160), :]
        other_d = s.dp1r[...]
        for q in range(2):
            cols = slice(1024 * q, 1024 * q + 1024)
            wa = s.wf[2 * q : 2 * q + 2].reshape(1024, 256)
            wb = s.wfov[2 * q : 2 * q + 2].reshape(1024, 256)
            s.u3[pl.ds(0, 160), :] = dot_last(mine_d, wa) + dot_last(other_d, wb)

            def img_step(base):
                rows = pl.ds(base, 32)
                m = mask_at(my_rows + base, 32, 1024)
                own_d = s.dsum[pl.ds(my_rows + base, 32), 512 * q : 512 * q + 512].astype(F32)
                far_d = s.dsr[rows, 512 * q : 512 * q + 512].astype(F32)
                d = jnp.concatenate(
                    [
                        jnp.where(r == j % 2, own_d[:, 64 * (j - j % 2) :][:, :128], far_d[:, 64 * (j - j % 2) :][:, :128])
                        for j in range(8)
                    ],
                    axis=1,
                )
                s.oimg[rows, cols] = ((s.u3[rows, :] + d) * m).astype(BF16)

            rows_loop(160, 32, img_step)
        img_n = ln.near(s.oimg, s.o_img)
        hop_z(gq_z[2])

        hop_z(gf_z)

        @pl.when(special)
        def _():
            for cp in gg_z:
                cp.wait_recv()
            v = (s.gg[z].astype(F32) + s.rg[0].astype(F32)) + (s.rg[1].astype(F32) + s.rg[2].astype(F32))
            s.pg[...] = v.astype(BF16)

        gx = [ln.group(lambda n=n: s.wg.at[0:3, 0, 0] if n == 3 else s.wg.at[0:4, 0, 0], special) for n in (3, 4)]
        for g, odd_one in zip(gx, (0, 1)):
            for o in offsets:
                if (o[0] + o[1]) % 2 == odd_one:
                    rr, yy, cc = peer(*o)
                    g.push(s.pg.at[yy, cc], s.o_gates.at[r, :, pl.ds(fhalf, 256)], dev(z, yy, cc, rr), special)
        gate_near = pltpu.make_async_copy(
            s.pg.at[y, c], s.o_gates.at[r, :, pl.ds(fhalf, 256)], s.near_sems.at[NEAR - 2]
        )
        pl.when(special)(gate_near.start)

        wait([cg])
        v = s.gcls[b].astype(F32)
        for i in range(15):
            v = v + s.rcls[i].astype(F32)
        s.clss[...] = v
        cls_x = ln.push(s.clss, s.clsr, xpeer)

        wait_z(gr_z)
        pl.when(odd)(lambda: add_z(s.ryr, s.rzr, s.fnr, False))
        gr_x = ln.push(s.fnr, s.o_red, xpeer, odd)
        red_near = pltpu.make_async_copy(s.fnr, s.o_red, s.near_sems.at[NEAR - 3])
        pl.when(odd)(red_near.start)
        wait_z(gl_z)
        add_z(s.ryl, s.rzl, s.fnl, False)
        gl_x = ln.push(s.fnl, s.o_last.at[r], xpeer)
        n1 = ln.near(s.fnl, s.o_last.at[r])
        for a in range(3):
            wait_z(gq_z[a])
            lead = slice(3 * a, 3 * a + 3)
            add_z(s.rym.at[lead], s.rzm.at[:, lead], s.fnm.at[lead], True)
        gq_x = ln.push(s.fnm, s.o_mid.at[:, :, pl.ds(half, 256)], xpeer)
        n2 = ln.near(s.fnm, s.o_mid.at[:, :, pl.ds(half, 256)])
        wait_z(gf_z)
        add_z(s.ryf, s.rzf, s.fnf, False)
        gf_x = ln.push(s.fnf, s.o_first.at[:, pl.ds(half, 256)], xpeer)
        n3 = ln.near(s.fnf, s.o_first.at[:, pl.ds(half, 256)])
        wait([cls_x])
        s.clso[...] = s.clss[...] + s.clsr[...]
        n4 = ln.near(s.clso, s.o_cls)
        wait([gr_x], jnp.logical_not(odd))
        wait([gl_x, gq_x, gf_x, gs1, gs2, gs3])
        wait(ms + hs)
        wait([gx[0]], special)
        wait([gx[1]], plain)
        pl.when(special)(gate_near.wait)
        pl.when(odd)(red_near.wait)
        for cp in (gs1n, gs2n, gs3n, img_n, mn, hn, n1, n2, n3, n4):
            cp.wait()
        ln.drain()

    pl.run_scoped(block_back, *[pltpu.VMEM(*v) for v in LATE.values()])


LATE = dict(
    zst=((2, 3, 3, 2, 2, 32, 256), BF16),
    psm=((9, 2, 2, 32, 256), BF16),
    psh=((9, 2, 2, 32, 256), BF16),
    fnr=((128, 512), BF16),
    fnl=((32, 1024), BF16),
    fnm=((9, 32, 256), BF16),
    fnf=((128, 256), BF16),
    pg=((2, 2, 32, 256), BF16),
    clss=((32, 128), F32),
    clso=((32, 128), F32),
    u3=((320, 1024), F32),
    dp3=((320, 1024), BF16),
    d3m=((480, 768), BF16),
    dsum=((320, 1024), BF16),
    oimg=((160, 2048), BF16),
    pas1=((320, 256), BF16),
    pas2=((320, 256), BF16),
    dp1=((320, 256), BF16),
    dp2=((320, 256), BF16),
    wfov=((4, 2, 2, 128, 256), BF16),
    gr=((4, 2, 128, 512), BF16),
    gl=((4, 2, 2, 32, 1024), BF16),
    gq=((9, 4, 2, 2, 32, 256), BF16),
    gf=((4, 2, 2, 128, 256), BF16),
)


FINAL = dict(
    depth=((160, 512), BF16),
    logits=((2, 40, 80), BF16),
    img=((160, 2048), F32),
    first=((128, 512), F32),
    gain1=((1, 32), F32),
    shift1=((1, 32), F32),
    mid=((9, 32, 512), F32),
    gain2=((1, 32), F32),
    shift2=((1, 32), F32),
    last=((32, 2048), F32),
    gain3=((1, 128), F32),
    shift3=((1, 128), F32),
    red=((128, 512), F32),
    heads=((2, 9, 32, 512), F32),
    mess=((2, 9, 32, 512), F32),
    gates=((2, 32, 512), F32),
    cls=((32, 40), F32),
)


def widen_out(names, *refs):
    s = SimpleNamespace(**dict(zip(names, refs)))
    b = lax.axis_index("batch")
    used = [0]

    def move(src, dst):
        cp = pltpu.make_async_copy(src, dst, s.sems.at[used[0]])
        used[0] += 1
        cp.start()
        return cp

    wide = [("img", slice(lo, lo + n)) for lo, n in ((0, 64), (64, 48), (112, 48))]
    wide += [(n, slice(i, i + 1)) for n in ("mess", "heads") for i in range(2)]
    wide += [("mid", slice(0, 9)), ("red", slice(0, 128)), ("first", slice(0, 128)), ("last", slice(0, 2)), ("gates", slice(0, 2))]
    loads = [move(getattr(s, "o_" + n).at[at], getattr(s, "i_" + n).at[at]) for n, at in wide]
    small = [move(getattr(s, "o_" + n), getattr(s, "i_" + n)) for n in ("gs1", "gs2", "gs3", "cls")]
    done = []
    narrow = [move(s.o_depth, s.i_depth), move(s.o_logits, s.i_logits)]
    for (n, at), cp in zip(wide, loads):
        cp.wait()
        src, dst = getattr(s, "i_" + n), getattr(s, "v_" + n)
        if n == "last":
            for i in range(8):
                for h in range(2):
                    lane = 128 * (2 * i + h)
                    dst[:, lane : lane + 128] = src[h, :, 128 * i : 128 * i + 128].astype(F32)
            done.append(move(dst, s.last))
            continue
        if n in ("mess", "heads"):
            for t in range(9):
                dst[at.start, t] = src[at.start, t].astype(F32)
        elif len(src.shape) > 2:
            for t in range(at.start, at.stop):
                dst[t] = src[t].astype(F32)
        else:
            dst[at] = src[at].astype(F32)
        done.append(move(dst.at[at], getattr(s, n).at[at]))
    for cp in narrow:
        cp.wait()
    done += [move(s.i_depth, s.depth), move(s.i_logits, s.logits)]
    for cp in small:
        cp.wait()
    quarter, spot = lax.div(b, np.int32(4)), lax.rem(b, np.int32(4))
    at = pl.ds(pl.multiple_of(128 * lax.rem(quarter, np.int32(2)), 128), 128)
    for n, layer in ((1, s.i_gs1), (2, s.i_gs2)):
        v = pltpu.roll(layer[lax.div(quarter, np.int32(2)), :, at], lax.rem(128 - 32 * spot, np.int32(128)), 1)
        for row, kind in ((1, "gain"), (0, "shift")):
            keep = getattr(s, "v_%s%d" % (kind, n))
            keep[...] = v[row : row + 1, 0:32]
            done.append(move(keep, getattr(s, "%s%d" % (kind, n))))
    block = lax.div(b, np.int32(2))
    at = pl.ds(pl.multiple_of(128 * lax.rem(block, np.int32(4)), 128), 128)
    v = s.i_gs3[lax.rem(b, np.int32(2)), :, at]
    low = lax.div(block, np.int32(4)) == 0
    s.v_shift3[...] = jnp.where(low, v[0:1], v[1:2])
    s.v_gain3[...] = jnp.where(low, v[2:3], v[3:4])
    done.append(move(s.v_shift3, s.shift3))
    done.append(move(s.v_gain3, s.gain3))
    s.v_cls[...] = s.i_cls[:, 0:40]
    done.append(move(s.v_cls, s.cls))
    for cp in done:
        cp.wait()


def fast(args):
    (
        images, crop_height, crop_width, w_first, gain_first, shift_first, w_middle, gain_middle, shift_middle,
        w_last, gain_last, shift_last, w_reduce, w_heads, w_message, w_gates, w_classes, depth_cot, class_cot,
    ) = args
    ins = (
        crop_height, crop_width, images.reshape(160, 2048), w_first, w_middle, w_last, w_reduce, w_gates, w_classes,
        w_heads, w_message, *(v.reshape(1, -1) for v in (gain_first, shift_first, gain_middle, shift_middle, gain_last, shift_last)), depth_cot.reshape(160, 512), class_cot.transpose(0, 1, 3, 2).reshape(2, 40, 80),
    )
    names = list(INS) + list(OUTS) + list(SHAPES) + ["send_sems", "recv_sems", "near_sems"]
    smem, hbm, vmem = (pl.BlockSpec(memory_space=m) for m in (pltpu.SMEM, pltpu.HBM, pltpu.VMEM))
    spec = {"crop_h": smem, "crop_w": smem}
    spec.update({n: vmem for n in INS if n[:4] in ("gain", "shif")})
    outs = pl.pallas_call(
        functools.partial(body, names),
        out_shape=[jax.ShapeDtypeStruct(*v) for v in OUTS.values()],
        in_specs=[spec.get(n, hbm) for n in INS],
        out_specs=[hbm] * len(OUTS),
        scratch_shapes=[pltpu.VMEM(*v) for v in SHAPES.values()]
        + [pltpu.SemaphoreType.DMA((n,)) for n in (SENDS, RECVS, NEAR)],
        compiler_params=pltpu.CompilerParams(has_side_effects=True, collective_id=0, vmem_limit_bytes=64 * 2**20),
        name="residual_distill",
    )(*ins)
    o = dict(zip(OUTS, outs))
    taken = [n for n in OUTS if n.startswith("o_")]
    staged = {"i_" + n[2:]: OUTS[n] for n in taken}
    staged.update({"v_" + n: v for n, v in FINAL.items() if n not in ("depth", "logits")})
    final = pl.pallas_call(
        functools.partial(widen_out, taken + list(FINAL) + list(staged) + ["sems"]),
        out_shape=[jax.ShapeDtypeStruct(*v) for v in FINAL.values()],
        in_specs=[hbm] * len(taken),
        out_specs=[hbm] * len(FINAL),
        scratch_shapes=[pltpu.VMEM(*v) for v in staged.values()] + [pltpu.SemaphoreType.DMA((41,))],
        compiler_params=pltpu.CompilerParams(vmem_limit_bytes=64 * 2**20),
        name="widen_out",
    )(*[o[n] for n in taken])
    f = dict(zip(FINAL, final))
    f["depth"] = f["depth"].reshape(1, 2, 80, 512)
    f["logits"] = f["logits"].reshape(1, 2, 40, 80).transpose(0, 1, 3, 2)
    f["img"] = f["img"].reshape(1, 2, 80, 2048)
    for n in ("gain1", "shift1", "gain2", "shift2", "gain3", "shift3"):
        f[n] = f[n].reshape(-1)
    return tuple(f.values())


def solution(mesh):
    def step(*args):
        if mesh.shape["batch"] == 16 and mesh.shape["rows"] == 2:
            return fast(args)
        return shards(*args)

    placed = (
        P("batch", "rows", None, None),
        P(),
        P(),
        P("batch", None),
        P("batch"),
        P("batch"),
        P(None, "batch", None),
        P("batch"),
        P("batch"),
        P("batch", None),
        P("batch"),
        P("batch"),
        P("batch", None),
        P("rows", None, "batch", None),
        P("rows", None, "batch", None),
        P(None, "batch", None),
        P("batch", None),
        P("batch", "rows", None, None),
        P("batch", "rows", None, None),
    )
    return jax.shard_map(
        step,
        mesh=mesh,
        in_specs=placed,
        out_specs=(
            P("batch", "rows", None, None),
            P("batch", "rows", None, None),
            P("batch", "rows", None, None),
            P("batch", None),
            P("batch"),
            P("batch"),
            P(None, "batch", None),
            P("batch"),
            P("batch"),
            P("batch", None),
            P("batch"),
            P("batch"),
            P("batch", None),
            P("rows", None, "batch", None),
            P("rows", None, "batch", None),
            P(None, "batch", None),
            P("batch", None),
        ),
        check_vma=False,
    )
```

```python
import functools
from types import SimpleNamespace

import numpy as np
import jax
import jax.numpy as jnp
from jax import lax
from jax.sharding import PartitionSpec as P
from jax.experimental import pallas as pl
from jax.experimental.pallas import tpu as pltpu

EPS = 1e-05
MESH = pl.DeviceIdType.MESH
F32 = jnp.float32
BF16 = jnp.bfloat16
ROOT = 0.7978845608028654
CUBE = 0.044715
SENDS = 122
RECVS = 201
NEAR = 21


def dot(left, right):
    return jnp.dot(left, right, preferred_element_type=F32)


def dot_last(left, right):
    return lax.dot_general(left, right, (((1,), (1,)), ((), ())), preferred_element_type=F32)


def dot_first(left, right):
    return lax.dot_general(left, right, (((0,), (0,)), ((), ())), preferred_element_type=F32)


def gelu_of(v):
    return 0.5 * v * (1.0 + jnp.tanh(ROOT * (v + CUBE * v * v * v)))


def slope_of(v):
    t = jnp.tanh(ROOT * (v + CUBE * v * v * v))
    return 0.5 * (1.0 + t) + 0.5 * v * (1.0 - t * t) * (ROOT * (1.0 + 3.0 * CUBE * v * v))


def rows_loop(total, chunk, step):
    def body(index, carry):
        step(pl.multiple_of(index * chunk, chunk))
        return carry

    lax.fori_loop(0, total // chunk, body, 0)


class Copy:
    def __init__(self, remote, links, send, recv, like):
        self.remote, self.links, self.send, self.recv, self.like = remote, links, send, recv, like
        self.scoped = like is None

    def wait_recv(self):
        if self.like is None:
            self.remote.wait_recv()
        else:
            ref = self.like(1)
            pltpu.make_async_copy(ref, ref, self.links.recv.at[self.recv]).wait()

    def wait_send(self):
        if self.like is None:
            self.remote.wait_send()
        else:
            ref = self.like(0)
            pltpu.make_async_copy(ref, ref, self.links.send.at[self.send]).wait()


class Group:
    scoped = True

    def __init__(self, links, send, recv, like):
        self.links, self.send, self.recv, self.like = links, send, recv, like

    def push(self, src, dst, device, when=None):
        self.links.start(src, dst, device, self.send, self.recv, when)

    def wait_recv(self):
        ref = self.like()
        pltpu.make_async_copy(ref, ref, self.links.recv.at[self.recv]).wait()

    def wait_send(self):
        ref = self.like()
        pltpu.make_async_copy(ref, ref, self.links.send.at[self.send]).wait()


class Near:
    def __init__(self, links, src, dst):
        self.links, self.index = links, links.local_free.pop(0)
        self.copy = pltpu.make_async_copy(src, dst, links.local.at[self.index])
        self.copy.start()

    def wait(self):
        self.copy.wait()
        self.links.local_free.insert(0, self.index)


class Links:
    def __init__(self, send, recv, local):
        self.send, self.recv, self.local = send, recv, local
        self.used = 0
        self.send_free = list(range(SENDS))
        self.local_free = list(range(NEAR - 4))
        self.open = []

    def start(self, src, dst, device, send, recv, when):
        remote = pltpu.make_async_remote_copy(
            src_ref=src,
            dst_ref=dst,
            send_sem=self.send.at[send],
            recv_sem=self.recv.at[recv],
            device_id=device,
            device_id_type=MESH,
        )
        if when is None:
            remote.start()
        else:
            pl.when(when)(remote.start)
        return remote

    def pair(self):
        self.used += 1
        return self.send_free.pop(0), self.used - 1

    def push(self, src, dst, device, when=None, like=None):
        send, recv = self.pair()
        cp = Copy(self.start(src, dst, device, send, recv, when), self, send, recv, like)
        self.open.append((cp, when))
        return cp

    def group(self, like, when=None):
        cp = Group(self, *self.pair(), like)
        self.open.append((cp, when))
        return cp

    def near(self, src, dst):
        return Near(self, src, dst)

    def drain(self, scoped=False):
        kept = []
        for cp, when in self.open:
            if scoped and not cp.scoped:
                kept.append((cp, when))
                continue
            if when is None:
                cp.wait_send()
            else:
                pl.when(when)(cp.wait_send)
            self.send_free.insert(0, cp.send)
        self.open = kept


def wait(copies, when=None):
    def run():
        for cp in copies:
            cp.wait_recv()

    if when is None:
        run()
    else:
        pl.when(when)(run)


def lanes(mask, width):
    return jnp.concatenate([mask] * (width // 128), axis=1) if width > 128 else mask


def padded_2(cells, sides, width):
    for axis, dim in sides:
        count = lax.axis_size(axis)
        ends = count - 1
        head = lax.slice_in_dim(cells, 0, width, axis=dim)
        tail = lax.slice_in_dim(cells, cells.shape[dim] - width, cells.shape[dim], axis=dim)
        cells = jnp.concatenate(
            [
                lax.ppermute(tail, axis, [(i, (i + 1) % count) for i in range(ends)]),
                cells,
                lax.ppermute(head, axis, [((i + 1) % count, i) for i in range(ends)]),
            ],
            axis=dim,
        )
    return cells


def gelu_tanh(values):
    return jax.nn.gelu(values, approximate=True)


def gelu_slope(values, upstream):
    return jax.vjp(gelu_tanh, values)[1](upstream)[0]


def project(values, weight):
    return jnp.einsum("nrcj,jk->nrck", values, weight, preferred_element_type=jnp.float32)


def project_back(upstream, weight):
    return jnp.einsum("nrck,jk->nrcj", upstream, weight, preferred_element_type=jnp.float32)


def outer_sum(values, upstream):
    return jnp.einsum("nrcj,nrck->jk", values, upstream, preferred_element_type=jnp.float32)


def widen(padded):
    return jnp.pad(padded, ((0, 0), (0, 0), (1, 1), (0, 0)))


def halo_value(values):
    return padded_2(values, (("rows", 1),), 1)


def halo_grad(values):
    return padded_2(values, (("rows", 1),), 1)


def conv_apply(padded, kernel):
    row_count = padded.shape[1] - 2
    col_count = padded.shape[2]
    widened = widen(padded)
    running = jnp.zeros((padded.shape[0], row_count, col_count, kernel.shape[2]), jnp.float32)
    for tap_index in range(9):
        shift_down = tap_index // 3
        shift_right = tap_index % 3
        running = running + project(
            widened[
                :, shift_down : shift_down + row_count, shift_right : shift_right + col_count, :
            ],
            kernel[tap_index],
        )
    return running


def conv_kernel_grad(padded, upstream):
    row_count = upstream.shape[1]
    col_count = upstream.shape[2]
    widened = widen(padded)
    return jnp.stack(
        [
            outer_sum(
                widened[
                    :,
                    tap_index // 3 : tap_index // 3 + row_count,
                    tap_index % 3 : tap_index % 3 + col_count,
                    :,
                ],
                upstream,
            )
            for tap_index in range(9)
        ]
    )


def conv_input_grad(padded_grad, kernel):
    row_count = padded_grad.shape[1] - 2
    col_count = padded_grad.shape[2]
    widened = widen(padded_grad)
    running = jnp.zeros((padded_grad.shape[0], row_count, col_count, kernel.shape[1]), jnp.float32)
    for tap_index in range(9):
        shift_down = tap_index // 3
        shift_right = tap_index % 3
        running = running + project_back(
            widened[
                :,
                2 - shift_down : 2 - shift_down + row_count,
                2 - shift_right : 2 - shift_right + col_count,
                :,
            ],
            kernel[tap_index],
        )
    return running


def crop_mask(height, width, first_row, row_count, col_count):
    row_ids = first_row + jnp.arange(row_count, dtype=jnp.int32)
    col_ids = jnp.arange(col_count, dtype=jnp.int32)
    inside = (row_ids[None, :, None] < height[:, None, None]) & (
        col_ids[None, None, :] < width[:, None, None]
    )
    return inside.astype(jnp.float32)[..., None]


def norm_forward(pre_act, pixel_mask, gain_vec, shift_vec, valid_count):
    sums = jnp.sum(pre_act * pixel_mask, axis=(0, 1, 2))
    squares = jnp.sum(pre_act * pre_act * pixel_mask, axis=(0, 1, 2))
    sums, squares = lax.psum((sums, squares), ("batch", "rows"))
    mean_vec = sums / valid_count
    inv_std = lax.rsqrt(squares / valid_count - mean_vec * mean_vec + EPS)
    normal = (pre_act - mean_vec) * inv_std
    return (normal, inv_std, normal * gain_vec + shift_vec)


def norm_backward(upstream, normal, inv_std, gain_vec, pixel_mask, valid_count):
    shift_part = jnp.sum(upstream, axis=(0, 1, 2))
    gain_part = jnp.sum(upstream * normal, axis=(0, 1, 2))
    shift_part, gain_part = lax.psum((shift_part, gain_part), ("batch", "rows"))
    d_pre = (
        pixel_mask
        * gain_vec
        * inv_std
        * (upstream - shift_part / valid_count - normal * gain_part / valid_count)
    )
    return (d_pre, gain_part, shift_part)


def task_forward(padded_in, heads, messages, pixel_mask, pad_rows):
    pre_list = []
    feat_list = []
    padded_feats = []
    message_list = []
    for task in range(heads.shape[0]):
        pre_act = conv_apply(padded_in, heads[task])
        feature = (gelu_tanh(pre_act) * pixel_mask).astype(jnp.bfloat16)
        padded_feat = pad_rows(feature)
        pre_list.append(pre_act)
        feat_list.append(feature)
        padded_feats.append(padded_feat)
        message_list.append(conv_apply(padded_feat, messages[task]).astype(jnp.bfloat16))
    return (pre_list, feat_list, padded_feats, message_list)


def task_backward(
    padded_in,
    heads,
    messages,
    pixel_mask,
    pre_list,
    padded_feats,
    feat_grads,
    message_grads,
    pad_grad,
):
    input_grad = jnp.zeros(
        padded_in.shape[:1] + (padded_in.shape[1] - 2,) + padded_in.shape[2:], jnp.float32
    )
    head_grads = []
    kernel_grads = []
    for task in range(heads.shape[0]):
        low_message = message_grads[task].astype(jnp.bfloat16)
        kernel_grads.append(conv_kernel_grad(padded_feats[task], low_message))
        feat_grad = feat_grads[task] + conv_input_grad(pad_grad(low_message), messages[task])
        low_pre = gelu_slope(pre_list[task], feat_grad * pixel_mask).astype(jnp.bfloat16)
        head_grads.append(conv_kernel_grad(padded_in, low_pre))
        input_grad = input_grad + conv_input_grad(pad_grad(low_pre), heads[task])
    return (input_grad, jnp.stack(head_grads), jnp.stack(kernel_grads))


def streams_forward(features, messages, gates_all, classes_all, pixel_mask):
    gate_depth = jax.nn.sigmoid(project(features[0], gates_all[0]))
    gate_class = jax.nn.sigmoid(project(features[3], gates_all[1]))
    depth_sum = (
        messages[1].astype(jnp.float32)
        + messages[2].astype(jnp.float32)
        + messages[3].astype(jnp.float32)
    )
    class_sum = (
        messages[0].astype(jnp.float32)
        + messages[1].astype(jnp.float32)
        + messages[2].astype(jnp.float32)
    )
    depth_stream = (features[0].astype(jnp.float32) + gate_depth * depth_sum) * pixel_mask
    merged = (features[3].astype(jnp.float32) + gate_class * class_sum).astype(jnp.bfloat16)
    class_logits = project(merged, classes_all) * pixel_mask
    return (depth_stream, class_logits, merged, gate_depth, gate_class, depth_sum, class_sum)


def streams_backward(
    features,
    merged,
    gate_depth,
    gate_class,
    depth_sum,
    class_sum,
    depth_cot,
    class_cot,
    gates_all,
    classes_all,
    pixel_mask,
):
    depth_grad = depth_cot.astype(jnp.float32) * pixel_mask
    logit_grad = (class_cot.astype(jnp.float32) * pixel_mask).astype(jnp.bfloat16)
    grad_classes = outer_sum(merged, logit_grad)
    merged_grad = project_back(logit_grad, classes_all)
    gate_depth_grad = (depth_grad * depth_sum * gate_depth * (1.0 - gate_depth)).astype(
        jnp.bfloat16
    )
    gate_class_grad = (merged_grad * class_sum * gate_class * (1.0 - gate_class)).astype(
        jnp.bfloat16
    )
    grad_gates = jnp.stack(
        [outer_sum(features[0], gate_depth_grad), outer_sum(features[3], gate_class_grad)]
    )
    depth_feat = depth_grad + project_back(gate_depth_grad, gates_all[0])
    class_feat = merged_grad + project_back(gate_class_grad, gates_all[1])
    depth_message = depth_grad * gate_depth
    class_message = merged_grad * gate_class
    nothing = jnp.zeros_like(depth_grad)
    feat_grads = [depth_feat, nothing, nothing, class_feat]
    message_grads = [
        class_message,
        depth_message + class_message,
        depth_message + class_message,
        depth_message,
    ]
    return (feat_grads, message_grads, grad_gates, grad_classes)


def shards(
    images,
    crop_height,
    crop_width,
    w_first,
    gain_first,
    shift_first,
    w_middle,
    gain_middle,
    shift_middle,
    w_last,
    gain_last,
    shift_last,
    w_reduce,
    w_heads,
    w_message,
    w_gates,
    w_classes,
    depth_cot,
    class_cot,
):
    image_index = lax.axis_index("batch")
    batch_count = lax.axis_size("batch")
    row_count = images.shape[1]
    col_count = images.shape[2]
    height = lax.dynamic_slice_in_dim(crop_height, image_index, 1, 0)
    width = lax.dynamic_slice_in_dim(crop_width, image_index, 1, 0)
    pixel_mask = crop_mask(height, width, lax.axis_index("rows") * row_count, row_count, col_count)
    valid_count = jnp.sum(crop_height * crop_width).astype(jnp.float32)
    gathered = (
        lax.all_gather(w_first, "batch", axis=0, tiled=True),
        lax.all_gather(w_middle, "batch", axis=1, tiled=True),
        lax.all_gather(w_last, "batch", axis=0, tiled=True),
        lax.all_gather(w_reduce, "batch", axis=0, tiled=True),
        lax.all_gather(w_gates, "batch", axis=1, tiled=True),
        lax.all_gather(w_classes, "batch", axis=0, tiled=True),
        lax.all_gather(gain_first, "batch", axis=0, tiled=True),
        lax.all_gather(shift_first, "batch", axis=0, tiled=True),
        lax.all_gather(gain_middle, "batch", axis=0, tiled=True),
        lax.all_gather(shift_middle, "batch", axis=0, tiled=True),
        lax.all_gather(gain_last, "batch", axis=0, tiled=True),
        lax.all_gather(shift_last, "batch", axis=0, tiled=True),
        lax.all_gather(w_heads, "batch", axis=2, tiled=True),
        lax.all_gather(w_message, "batch", axis=2, tiled=True),
    )
    first_all = gathered[0]
    middle_all = gathered[1]
    last_all = gathered[2]
    reduce_all = gathered[3]
    gates_all = gathered[4]
    classes_all = gathered[5]
    gain_one = gathered[6].astype(jnp.float32)
    shift_one = gathered[7].astype(jnp.float32)
    gain_two = gathered[8].astype(jnp.float32)
    shift_two = gathered[9].astype(jnp.float32)
    gain_three = gathered[10].astype(jnp.float32)
    shift_three = gathered[11].astype(jnp.float32)
    heads_own = gathered[12]
    message_own = gathered[13]
    masked_in = images.astype(jnp.float32) * pixel_mask
    low_in = masked_in.astype(jnp.bfloat16)
    pre_first = project(low_in, first_all)
    normal_first, std_first, out_first = norm_forward(
        pre_first, pixel_mask, gain_one, shift_one, valid_count
    )
    act_first = (gelu_tanh(out_first) * pixel_mask).astype(jnp.bfloat16)
    padded_first = halo_value(act_first)
    pre_middle = conv_apply(padded_first, middle_all)
    normal_middle, std_middle, out_middle = norm_forward(
        pre_middle, pixel_mask, gain_two, shift_two, valid_count
    )
    act_middle = (gelu_tanh(out_middle) * pixel_mask).astype(jnp.bfloat16)
    pre_last = project(act_middle, last_all)
    normal_last, std_last, out_last = norm_forward(
        pre_last, pixel_mask, gain_three, shift_three, valid_count
    )
    summed = out_last + masked_in
    block_out = (gelu_tanh(summed) * pixel_mask).astype(jnp.bfloat16)
    low_reduced = project(block_out, reduce_all).astype(jnp.bfloat16)
    heads_all, message_all = (
        lax.all_gather(heads_own, "rows", axis=0, tiled=True),
        lax.all_gather(message_own, "rows", axis=0, tiled=True),
    )
    padded_in = halo_value(low_reduced)
    pre_list, feat_list, padded_feats, message_list = task_forward(
        padded_in, heads_all, message_all, pixel_mask, halo_value
    )
    depth_stream, class_logits, merged, gate_depth, gate_class, depth_sum, class_sum = (
        streams_forward(feat_list, message_list, gates_all, classes_all, pixel_mask)
    )
    feat_grads, message_grads, grad_gates, grad_classes = streams_backward(
        feat_list,
        merged,
        gate_depth,
        gate_class,
        depth_sum,
        class_sum,
        depth_cot,
        class_cot,
        gates_all,
        classes_all,
        pixel_mask,
    )
    reduced_grad, grad_heads, grad_message = task_backward(
        padded_in,
        heads_all,
        message_all,
        pixel_mask,
        pre_list,
        padded_feats,
        feat_grads,
        message_grads,
        halo_grad,
    )
    low_reduced_grad = reduced_grad.astype(jnp.bfloat16)
    grad_reduce = outer_sum(block_out, low_reduced_grad)
    block_grad = project_back(low_reduced_grad, reduce_all)
    sum_grad = gelu_slope(summed, block_grad * pixel_mask)
    d_last, gain_grad_three, shift_grad_three = norm_backward(
        sum_grad, normal_last, std_last, gain_three, pixel_mask, valid_count
    )
    low_last = d_last.astype(jnp.bfloat16)
    grad_last = outer_sum(act_middle, low_last)
    middle_grad = project_back(low_last, last_all)
    d_middle, gain_grad_two, shift_grad_two = norm_backward(
        gelu_slope(out_middle, middle_grad * pixel_mask),
        normal_middle,
        std_middle,
        gain_two,
        pixel_mask,
        valid_count,
    )
    low_middle = d_middle.astype(jnp.bfloat16)
    grad_middle = conv_kernel_grad(padded_first, low_middle)
    first_grad = conv_input_grad(halo_grad(low_middle), middle_all)
    d_first, gain_grad_one, shift_grad_one = norm_backward(
        gelu_slope(out_first, first_grad * pixel_mask),
        normal_first,
        std_first,
        gain_one,
        pixel_mask,
        valid_count,
    )
    low_first = d_first.astype(jnp.bfloat16)
    grad_first = outer_sum(low_in, low_first)
    image_grad = (project_back(low_first, first_all) + sum_grad) * pixel_mask
    summed_grads = (
        lax.psum_scatter(grad_first, "batch", scatter_dimension=0, tiled=True),
        lax.psum_scatter(grad_middle, "batch", scatter_dimension=1, tiled=True),
        lax.psum_scatter(grad_last, "batch", scatter_dimension=0, tiled=True),
        lax.psum_scatter(grad_reduce, "batch", scatter_dimension=0, tiled=True),
        lax.psum_scatter(grad_gates, "batch", scatter_dimension=1, tiled=True),
        lax.psum_scatter(grad_classes, "batch", scatter_dimension=0, tiled=True),
        lax.psum_scatter(grad_heads, "batch", scatter_dimension=2, tiled=True),
        lax.psum_scatter(grad_message, "batch", scatter_dimension=2, tiled=True),
    )
    shared = (
        lax.psum(summed_grads[0].astype(jnp.bfloat16), "rows").astype(jnp.float32),
        lax.psum(summed_grads[1].astype(jnp.bfloat16), "rows").astype(jnp.float32),
        lax.psum(summed_grads[2].astype(jnp.bfloat16), "rows").astype(jnp.float32),
        lax.psum(summed_grads[3].astype(jnp.bfloat16), "rows").astype(jnp.float32),
        lax.psum(summed_grads[4].astype(jnp.bfloat16), "rows").astype(jnp.float32),
        lax.psum(summed_grads[5].astype(jnp.bfloat16), "rows").astype(jnp.float32),
    )
    heads_out, message_out = (
        lax.psum_scatter(
            summed_grads[6].astype(jnp.bfloat16), "rows", scatter_dimension=0, tiled=True
        ).astype(jnp.float32),
        lax.psum_scatter(
            summed_grads[7].astype(jnp.bfloat16), "rows", scatter_dimension=0, tiled=True
        ).astype(jnp.float32),
    )

    def own_share(member):
        share = member.shape[0] // batch_count
        return lax.dynamic_slice_in_dim(member, image_index * share, share, 0)

    return (
        depth_stream.astype(jnp.bfloat16),
        class_logits.astype(jnp.bfloat16),
        image_grad,
        shared[0],
        own_share(gain_grad_one),
        own_share(shift_grad_one),
        shared[1],
        own_share(gain_grad_two),
        own_share(shift_grad_two),
        shared[2],
        own_share(gain_grad_three),
        own_share(shift_grad_three),
        shared[3],
        heads_out,
        message_out,
        shared[4],
        shared[5],
    )


BEHIND = (0, 1, 2, 3, 4, 5, )

SHAPES = dict(
    wf=((4, 2, 2, 128, 256), BF16),
    wm=((9, 4, 2, 2, 32, 256), BF16),
    wl=((4, 2, 2, 32, 1024), BF16),
    wr=((4, 2, 128, 512), BF16),
    wc=((16, 32, 128), BF16),
    wcs=((32, 128), BF16),
    gains=((8, 128), F32),
    wcv=((32, 40), BF16),
    cct=((2, 40, 80), BF16),
    ctf=((128, 128), F32),
    xh=((320, 1024), BF16),
    wh=((9, 4, 2, 2, 32, 256), BF16),
    wq=((9, 4, 2, 2, 32, 256), BF16),
    wg=((4, 2, 2, 32, 256), BF16),
    xall=((320, 2048), BF16),
    maskp=((1280, 128), F32),
    pre1=((320, 256), F32),
    pre2=((320, 256), F32),
    pre3=((320, 1024), F32),
    bnp1=((8, 256), F32),
    bnp2=((8, 256), F32),
    bnp3=((8, 1024), F32),
    a1=((320, 512), BF16),
    a2=((320, 512), BF16),
    a3=((480, 1536), BF16),
    blk=((320, 1024), BF16),
    rps=((160, 512), BF16),
    rpr=((160, 512), BF16),
    rbuf=((1280, 512), BF16),
    fown=((1280, 256), BF16),
    ffull=((1280, 512), BF16),
    msgb=((1280, 256), BF16),
    gateb=((1280, 256), BF16),
    mrecv=((4, 160, 512), BF16),
    dm=((4, 160, 512), BF16),
    eu=((2, 160, 512), BF16),
    dcotv=((160, 512), BF16),
    ccotv=((160, 128), BF16),
    olt=((2, 40, 80), BF16),
    ods=((160, 512), BF16),
    olg=((160, 128), BF16),
    mrg=((160, 512), BF16),
    fg=((2, 2, 160, 512), BF16),
    dmg=((1280, 256), BF16),
    exg=((2, 1280, 256), BF16),
    gm=((9, 4, 2, 2, 32, 256), BF16),
    gh=((9, 4, 2, 2, 32, 256), BF16),
    gg=((4, 2, 2, 32, 256), BF16),
    rg=((3, 2, 2, 32, 256), BF16),
    hop=((2, 9, 2, 2, 32, 256), BF16),
    gcls=((16, 32, 128), BF16),
    rcls=((15, 32, 128), BF16),
    clsr=((32, 128), F32),
    dfs=((1280, 256), BF16),
    dfr=((1280, 256), BF16),
    drs=((640, 512), BF16),
    drr=((640, 512), BF16),
    dro=((3, 160, 512), BF16),
    dred=((320, 512), BF16),
    dsr=((160, 1024), BF16),
    par2=((320, 256), BF16),
    par1=((320, 256), BF16),
    dp1r=((160, 256), BF16),
    rcr=((4, 2, 128, 512), BF16),
    rcl=((4, 2, 32, 1024), BF16),
    rcm=((9, 4, 2, 32, 256), BF16),
    rcf=((4, 2, 128, 256), BF16),
    ryr=((4, 128, 512), BF16),
    hpr=((128, 512), BF16),
    hpl=((32, 1024), BF16),
    hpf=((128, 256), BF16),
    hpm=((9, 32, 256), BF16),
    ryl=((4, 32, 1024), BF16),
    rym=((9, 4, 32, 256), BF16),
    ryf=((4, 128, 256), BF16),
    rzr=((3, 128, 512), BF16),
    rzl=((3, 32, 1024), BF16),
    rzm=((3, 9, 32, 256), BF16),
    rzf=((3, 128, 256), BF16),
)
for _i, _w in enumerate((256, 256, 512, 512, 256, 256)):
    SHAPES["am%d" % _i] = ((8, _w), F32)
    SHAPES["as%d" % _i] = ((8, _w), F32)
    SHAPES["at%d" % _i] = ((8, _w), F32)
    SHAPES["ar%d" % _i] = ((3, 8, _w), F32)
    SHAPES["az%d" % _i] = ((3, 8, _w), F32)

INS = (
    "crop_h", "crop_w", "images", "first", "middle", "last", "reduce", "gates",
    "classes", "heads", "messages", "gain1", "shift1", "gain2", "shift2", "gain3", "shift3", "dcot", "ccot",
)
OUTS = dict(
    o_depth=((160, 512), BF16),
    o_logits=((2, 40, 80), BF16),
    o_img=((160, 2048), BF16),
    o_first=((128, 512), BF16),
    o_gs1=((2, 8, 256), F32),
    o_mid=((9, 32, 512), BF16),
    o_gs2=((2, 8, 256), F32),
    o_last=((2, 32, 1024), BF16),
    o_gs3=((2, 8, 512), F32),
    o_red=((128, 512), BF16),
    o_heads=((2, 9, 32, 512), BF16),
    o_mess=((2, 9, 32, 512), BF16),
    o_gates=((2, 32, 512), BF16),
    o_cls=((32, 128), F32),
    rm=((3, 9, 2, 2, 32, 256), BF16),
    rh=((3, 9, 2, 2, 32, 256), BF16),
    wfo=((4, 2, 2, 128, 256), BF16),
    st_h=((9, 32, 512), BF16),
    st_m=((9, 32, 512), BF16),
)


def shift_columns(v):
    rows, width = v.shape
    col = lax.broadcasted_iota(jnp.int32, (rows, width), 0)
    left = jnp.where(col == 0, 0.0, pltpu.roll(v, 1, 0))
    right = jnp.where(col == rows - 1, 0.0, pltpu.roll(v, rows - 1, 0))
    return left, right


def spread(src, dst, n_img, width):
    zero = jnp.zeros((80, 3 * width), BF16)
    for pad in range(n_img + 1):
        dst[pl.ds(pad * 400, 80), :] = zero

    def body(i, carry):
        v = src[pl.ds(pl.multiple_of(i * 80, 16), 80), :]
        left, right = shift_columns(v.astype(F32))
        row = pl.multiple_of((i + lax.div(i, np.int32(4)) + 1) * 80, 16)
        dst[pl.ds(row, 80), 0:width] = left.astype(BF16)
        dst[pl.ds(row, 80), width : 2 * width] = v
        dst[pl.ds(row, 80), 2 * width : 3 * width] = right.astype(BF16)
        return carry

    lax.fori_loop(0, 4 * n_img, body, 0)


def conv_rows(a3, w, img):
    acc = None
    for a in range(3):
        base = pl.multiple_of((5 * img + a) * 80, 16)
        part = dot(a3[pl.ds(base, 320), :], w[3 * a : 3 * a + 3].reshape(1536, 256))
        acc = part if acc is None else acc + part
    return acc


def conv_back(d3, w, img):
    acc = None
    for a in range(3):
        for q in range(3):
            base = pl.multiple_of((5 * img + a) * 80, 16)
            tap = 3 * (2 - a) + (2 - q)
            part = dot_last(d3[pl.ds(base, 320), 256 * q : 256 * q + 256], w[tap].reshape(512, 256))
            acc = part if acc is None else acc + part
    return acc


def conv_weight(a3, d3, out, n_img, first, last):
    depth = (5 * n_img - 1) * 80

    def body(tap, carry):
        a = lax.div(tap, np.int32(3))
        q = tap - 3 * a
        left = a3[pl.ds(pl.multiple_of(a * 80, 16), depth), pl.ds(pl.multiple_of(q * 512, 128), 512)]
        out[tap] = dot_first(left, d3[pl.ds(80, depth), 256:512]).astype(BF16).reshape(out.shape[1:])
        return carry

    lax.fori_loop(first, last, body, 0)


def body(names, *refs):
    s = SimpleNamespace(**dict(zip(names, refs)))
    b, r = lax.axis_index("batch"), lax.axis_index("rows")
    z = lax.div(b, np.int32(4))
    y = lax.rem(lax.div(b, np.int32(2)), np.int32(2))
    c = lax.rem(b, np.int32(2))
    ln = Links(s.send_sems, s.recv_sems, s.near_sems)
    half, fhalf = 256 * r, 256 * c

    def dev(zz, yy, cc, rr):
        return (4 * zz + 2 * yy + cc, rr)

    def zk(k):
        return lax.rem(z + k, np.int32(4))

    core, ypeer, xpeer = dev(z, y, 1 - c, r), dev(z, 1 - y, c, r), dev(z, y, c, 1 - r)
    special = r == y
    plain = r != y
    task = 2 * r + y
    img = 2 * y + c
    own_px = pl.multiple_of(320 * img + 160 * r, 16)
    my_rows = pl.multiple_of(160 * r, 16)
    other_rows = pl.multiple_of(160 * (1 - r), 16)
    half = pl.multiple_of(half, 128)
    ohalf = pl.multiple_of(256 * (1 - r), 128)
    fhalf = pl.multiple_of(fhalf, 128)
    offsets = [(dr, dy, dc) for dr in range(2) for dy in range(2) for dc in range(2) if dr + dy + dc]

    def peer(dr, dy, dc):
        rr = 1 - r if dr else r
        yy = 1 - y if dy else y
        cc = 1 - c if dc else c
        return rr, yy, cc

    def px_of(rr, yy, cc):
        return pl.multiple_of(320 * (2 * yy + cc) + 160 * rr, 16)

    ends = (z == 0) | (z == 3)
    inner = jnp.logical_not(ends)
    not_first, not_last = z != 0, z != 3
    far_end = dev(jnp.where(z == 1, 0, 3), y, c, r)
    odd = c == r

    def both(p, q):
        return q if p is None else (p if q is None else p & q)

    def line_start(src, at, pair, when=None, relay=True):
        sides = ln.group(pair, when)
        for q in (1, 3):
            sides.push(src, at(z), dev(zk(q), y, c, r), when)
        across = ln.push(src, at(z), dev(zk(2), y, c, r), both(when, ends) if relay else when)
        return [sides, across, relay, None, None]

    def line_y(state, src, at, four, when=None):
        state[4] = ln.group(four, when)
        state[4].push(src, at(z), ypeer, when)

    def line_relay(state, at, when=None):
        sides, _, relay = state[:3]
        wait([sides], when)
        if relay:
            state[3] = ln.push(at(3 - z), at(3 - z), far_end, both(when, inner))

    def line_sides(state, at, when=None):
        ys = state[4]
        ys.push(at(zk(3)), at(zk(3)), ypeer, when)
        ys.push(at(zk(1)), at(zk(1)), ypeer, when)

    def line_last(state, at, col, when=None):
        _, across, relay, hand, ys = state
        if relay:
            wait([across], both(when, inner))
            wait([hand], both(when, ends))
        else:
            wait([across], when)
        ys.push(at(zk(2)), at(zk(2)), ypeer, when)
        return [ln.push(col(y), col(y), core, when)]

    def line_core(state, col, cores, when=None):
        wait([state[4]], when)
        cores.append(ln.push(col(1 - y), col(1 - y), core, when))

    def at_wf(zz):
        return s.wf.at[zz, y, c]

    def at_wm(zz):
        return s.wm.at[:, zz, y, c]

    def at_wl(zz):
        return s.wl.at[zz, y, c]

    def at_wr(zz):
        return s.wr.at[zz, y]

    def col_wf(yy):
        return s.wf.at[:, yy, c]

    def col_wm(yy):
        return s.wm.at[:, :, yy, c]

    def col_wl(yy):
        return s.wl.at[:, yy, c]

    def col_wr(yy):
        return s.wr.at[:, yy]

    near_last = [
        ln.near(s.last.at[:, pl.ds(pl.multiple_of((2 * i + r) * 128, 128), 128)], s.wl.at[z, y, c, :, 128 * i : 128 * i + 128])
        for i in range(8)
    ]
    near_own = ln.near(s.images, s.xall.at[pl.ds(my_rows, 160)])
    near_cls = ln.near(s.classes, s.wcv)
    near_wf = ln.near(s.first.at[:, pl.ds(half, 256)], s.wf.at[z, y, c])
    near_wm = ln.near(s.middle.at[:, :, pl.ds(half, 256)], s.wm.at[:, z, y, c])
    red_local = pltpu.make_async_copy(s.reduce, s.wr.at[z, y], s.near_sems.at[NEAR - 1])
    pl.when(odd)(red_local.start)
    near_late = [
        ln.near(s.dcot, s.dcotv),
        ln.near(s.ccot, s.cct),
        ln.near(s.heads.at[y, :, :, pl.ds(fhalf, 256)], s.wh.at[:, z, y, c]),
        ln.near(s.messages.at[y, :, :, pl.ds(fhalf, 256)], s.wq.at[:, z, y, c]),
        ln.near(s.gates.at[r, :, pl.ds(fhalf, 256)], s.wg.at[z, y, c]),
    ]
    barrier = pltpu.get_barrier_semaphore()
    friends = [
        dev(zk(q), 1 - y if j else y, 1 - c if i else c, r) for q in range(4) for j in range(2) for i in range(2) if q + j + i
    ] + [dev(z, 1 - y if j else y, 1 - c if i else c, 1 - r) for j in range(2) for i in range(2)]
    for friend in friends:
        pl.semaphore_signal(barrier, inc=1, device_id=friend, device_id_type=MESH)
    pl.semaphore_wait(barrier, len(friends))

    src_wf, src_wm = s.first.at[:, pl.ds(half, 256)], s.middle.at[:, :, pl.ds(half, 256)]
    go_wf = line_start(src_wf, at_wf, lambda: s.wf.at[0, 0])
    line_y(go_wf, src_wf, at_wf, lambda: s.wf.at[:, 0, 0])
    img_x = ln.push(s.images, s.xall.at[pl.ds(my_rows, 160)], xpeer)
    go_wm = line_start(src_wm, at_wm, lambda: s.wm.at[:, 0, 0])
    line_y(go_wm, src_wm, at_wm, lambda: s.wm.at[:, :, 0, 0])
    for cp in near_last:
        cp.wait()

    for i in range(4):
        high, wide = s.crop_h[4 * z + i], s.crop_w[4 * z + i]
        for row in range(4):
            col = lax.broadcasted_iota(jnp.int32, (80, 128), 0)
            inside = (col < wide) & (row < high)
            s.maskp[pl.ds(320 * i + 80 * row, 80), :] = jnp.where(inside, 1.0, 0.0)
    total = s.crop_h[0] * s.crop_w[0]
    for i in range(1, 16):
        total = total + s.crop_h[i] * s.crop_w[i]
    count = total.astype(F32)
    mine = pl.multiple_of(320 * img, 16)

    def mask_at(base, rows, width):
        return lanes(s.maskp[pl.ds(mine + base, rows), :], width)

    s.gains[...] = jnp.zeros((8, 128), F32)
    for i, ref in enumerate((s.gain1, s.shift1, s.gain2, s.shift2)):
        s.gains[i : i + 1, 0:32] = ref[...].astype(F32)
    s.gains[4:5, :] = s.gain3[...].astype(F32)
    s.gains[5:6, :] = s.shift3[...].astype(F32)
    near_cls.wait()
    s.wcs[...] = jnp.zeros(s.wcs.shape, BF16)
    s.wcs[:, 0:40] = s.wcv[...]
    s.wc[b] = s.wcs[...]
    near_own.wait()
    near_wf.wait()
    line_relay(go_wf, at_wf)
    line_sides(go_wf, at_wf)
    cores_wf = line_last(go_wf, at_wf, col_wf)
    near_wm.wait()
    line_relay(go_wm, at_wm)
    go_wl = line_start(at_wl(z), at_wl, lambda: s.wl.at[0, 0])
    line_core(go_wf, col_wf, cores_wf)
    wait([img_x])

    def mask_x(base):
        rows = pl.ds(base, 80)
        v = (s.xall[rows, :].astype(F32) * mask_at(base, 80, 2048)).astype(BF16)
        s.xall[rows, :] = v
        for i in range(8):
            pick = jnp.where(r == 0, v[:, 256 * i : 256 * i + 128].astype(F32), v[:, 256 * i + 128 : 256 * i + 256].astype(F32))
            s.xh[rows, 128 * i : 128 * i + 128] = pick.astype(BF16)

    rows_loop(320, 80, mask_x)
    wait(cores_wf)
    wfo_x = ln.group(lambda: s.wf)
    for zz in (0, 1):
        wfo_x.push(s.wf.at[zz], s.wfo.at[zz], xpeer)

    def task_push(src, dst, lo, hi, staged):
        yy = 1 - y if staged else y
        taps = hi - lo
        sides = ln.group(lambda: s.rbuf.at[0 : 80 * taps])
        across = ln.group(lambda: dst.at[lo:hi, 0, 0], ends)
        for q in (1, 3, 2, 0):
            for i in range(2):
                if q + i == 0:
                    continue
                cc = 1 - c if i else c
                (across if q == 2 else sides).push(
                    src.at[lo:hi, :, pl.ds(pl.multiple_of(256 * cc, 128), 256)],
                    dst.at[lo:hi, z, yy, c],
                    dev(zk(q) if q else z, y, cc, r),
                    ends if q == 2 else None,
                )
        return sides, across, lo, hi, yy

    def task_relay(state, dst):
        sides, across, lo, hi, yy = state
        wait([sides])
        hand = ln.push(dst.at[lo:hi, 3 - z, yy], dst.at[lo:hi, 3 - z, yy], far_end, inner)
        return across, hand

    def task_ready(state):
        across, hand = state
        wait([across], inner)
        wait([hand], ends)

    def plane_start(n):
        m, ar = (getattr(s, p + str(n)) for p in ("am", "ar"))
        one = ln.group(lambda: ar)
        for i in (1, 2, 3):
            yy = 1 - y if i & 2 else y
            cc = 1 - c if i & 1 else c
            one.push(m, ar.at[i - 1], dev(z, yy, cc, r))
        return one

    def plane_end(n, one):
        m, sm, ar = (getattr(s, p + str(n)) for p in ("am", "as", "ar"))
        wait([one])
        sm[...] = (m[...] + ar[0]) + (ar[1] + ar[2])

    def reduce_plane(n):
        plane_end(n, plane_start(n))

    def reduce_line(n, bulk=None):
        sm, t, az = (getattr(s, p + str(n)) for p in ("as", "at", "az"))
        two = ln.group(lambda: az)
        for q in (1, 2, 3):
            two.push(sm, az.at[q - 1], dev(zk(q), y, c, r))
        if bulk is not None and n in BEHIND:
            bulk()
        wait([two])
        if bulk is not None and n not in BEHIND:
            bulk()
        t[...] = (sm[...] + az[0]) + (az[1] + az[2])
        return t[...]

    def stats_of(pre, width, msg):
        m = lanes(s.maskp[pl.ds(mine, 320), :], width)
        v = pre * m
        sums = jnp.sum(v, axis=0, keepdims=True)
        squares = jnp.sum(v * pre, axis=0, keepdims=True)
        return sums, squares

    def norm_terms(n, bnp, width, bulk=None):
        t = reduce_line(n, bulk)
        if width == 256:
            rows = [t[i : i + 1] for i in range(4)]
        else:
            rows = [jnp.concatenate([t[2 * i : 2 * i + 1], t[2 * i + 1 : 2 * i + 2]], axis=1) for i in range(4)]
        mean = rows[0] / count
        inv = lax.rsqrt(rows[1] / count - mean * mean + EPS)
        bnp[0:1], bnp[1:2], bnp[2:3], bnp[3:4] = mean, inv, rows[2], rows[3]

    quarter = lax.div(b, np.int32(4))
    spot = 32 * lax.rem(b, np.int32(4))

    def placed(n):
        lane = lax.broadcasted_iota(jnp.int32, (8, 128), 1)
        out = []
        for p in range(2):
            if n < 2:
                v = jnp.broadcast_to(s.gains[2 * n + p : 2 * n + p + 1, :], (8, 128))
                v = pltpu.roll(v, spot, 1)
                v = jnp.where((lane >= spot) & (lane < spot + 32), v, 0.0)
                out.append(jnp.concatenate([jnp.where(quarter == 2 * r + i, v[0:1], 0.0) for i in range(2)], axis=1))
            else:
                v = s.gains[4 + p : 5 + p, :]
                out.append(
                    [
                        jnp.concatenate(
                            [jnp.where(odd & (lax.div(b, np.int32(2)) == 4 * h + i), v, 0.0) for i in range(4)], axis=1
                        )
                        for h in range(2)
                    ]
                )
        return out

    def put_stats(n, first, second, width, layer):
        m = getattr(s, "am%d" % n)
        m[...] = jnp.zeros(m.shape, F32)
        if width == 256:
            m[0:1], m[1:2] = first, second
            if layer is not None:
                m[2:3], m[3:4] = placed(layer)
        else:
            m[0:1], m[1:2] = first[:, :512], first[:, 512:]
            m[2:3], m[3:4] = second[:, :512], second[:, 512:]
            if layer is not None:
                gain, shift = placed(layer)
                m[4:5], m[5:6] = gain
                m[6:7], m[7:8] = shift

    pre = dot(s.xall[...], s.wf[...].reshape(2048, 256))
    s.pre1[...] = pre
    first_sum, first_sq = stats_of(pre, 256, None)
    put_stats(0, first_sum, first_sq, 256, 0)
    plane_one = plane_start(0)
    line_sides(go_wm, at_wm)
    plane_end(0, plane_one)
    line_y(go_wl, at_wl(z), at_wl, lambda: s.wl.at[:, 0, 0])
    pl.when(odd)(red_local.wait)
    heads = []
    late_wr = []

    def bulk_one():
        line_relay(go_wl, at_wl)
        line_sides(go_wl, at_wl)
        late_wr.append(line_start(s.reduce, at_wr, lambda: s.wr.at[0], odd))
        heads.append(task_push(s.heads.at[y], s.wh, 0, 6, False))
        late_wr.append(line_last(go_wm, at_wm, col_wm))

    norm_terms(0, s.bnp1, 256, bulk_one)
    go_wr = late_wr[0]
    cores_wm = late_wr[1]

    def act_from(prebuf, bnp, dst):
        def step(base):
            x = (prebuf[pl.ds(base, 80), :] - bnp[0:1]) * bnp[1:2] * bnp[2:3] + bnp[3:4]
            dst[pl.ds(base, 80), pl.ds(half, 256)] = (gelu_of(x) * mask_at(base, 80, 256)).astype(BF16)

        rows_loop(320, 80, step)

    act_from(s.pre1, s.bnp1, s.a1)
    a1_x = ln.push(s.a1.at[:, pl.ds(half, 256)], s.a1.at[:, pl.ds(half, 256)], xpeer)
    line_core(go_wm, col_wm, cores_wm)
    cores_wl = line_last(go_wl, at_wl, col_wl)
    wait(cores_wm)
    wait([a1_x])
    wfo_x.push(s.wf.at[2], s.wfo.at[2], xpeer)
    spread(s.a1, s.a3, 1, 512)
    pre = conv_rows(s.a3, s.wm, 0)
    s.pre2[...] = pre
    first_sum, first_sq = stats_of(pre, 256, None)
    put_stats(1, first_sum, first_sq, 256, 1)
    plane_two = plane_start(1)
    over_h = ln.push(s.heads.at[1 - y], s.st_h, ypeer)
    plane_end(1, plane_two)
    relayed_h = []
    mess = []

    def mess_push(a, staged):
        return task_push(s.st_m if staged else s.messages.at[y], s.wq, 3 * a, 3 * a + 3, staged)

    def bulk_two():
        line_relay(go_wr, at_wr, odd)
        relayed_h.append(task_relay(heads[0], s.wh))
        heads.append(task_push(s.heads.at[y], s.wh, 6, 9, False))
        mess.append([mess_push(0, False)])

    norm_terms(1, s.bnp2, 256, bulk_two)
    line_y(go_wr, s.reduce, at_wr, lambda: s.wr.at[:, 0], odd)
    line_sides(go_wr, at_wr, odd)
    act_from(s.pre2, s.bnp2, s.a2)
    a2_x = ln.push(s.a2.at[:, pl.ds(half, 256)], s.a2.at[:, pl.ds(half, 256)], xpeer)
    line_core(go_wl, col_wl, cores_wl)
    cores_wr = line_last(go_wr, at_wr, col_wr, odd)
    wait(cores_wl)
    wait([a2_x])
    wfo_x.push(s.wf.at[3], s.wfo.at[3], xpeer)
    pre = dot(s.a2[...], s.wl[...].reshape(512, 1024))
    s.pre3[...] = pre
    first_sum, first_sq = stats_of(pre, 1024, None)
    put_stats(2, first_sum, first_sq, 1024, 2)
    plane_three = plane_start(2)
    over_m = ln.push(s.messages.at[1 - y], s.st_m, ypeer)
    plane_end(2, plane_three)
    def bulk_three():
        relayed_h.append(task_relay(heads[1], s.wh))
        heads.append(task_push(s.st_h, s.wh, 0, 5, True))
        heads.append(task_push(s.st_h, s.wh, 5, 9, True))

    wait([over_h])
    norm_terms(2, s.bnp3, 1024, bulk_three)
    staged_h = ln.near(s.st_h.at[:, :, pl.ds(fhalf, 256)], s.wh.at[:, z, 1 - y, c])
    gate_got = {}
    cls_got = ln.group(lambda: s.wc.at[0:15])
    for q in range(4):
        for j in range(2):
            if q + j:
                gate_got[q, j] = ln.group(lambda: s.wg.at[0, 0], (y == r) if j == 0 else (y != r))
            for i in range(2):
                if q + j + i == 0:
                    continue
                yy = 1 - y if j else y
                cc = 1 - c if i else c
                to = dev(zk(q) if q else z, yy, cc, r)
                cls_got.push(s.wcs, s.wc.at[b], to)
                src = s.gates.at[r, :, pl.ds(pl.multiple_of(256 * cc, 128), 256)]
                if q + j:
                    gate_got[q, j].push(src, s.wg.at[z, y, c], to, (y == r) if j == 0 else (y != r))
                else:
                    gate_got[0, 0] = ln.push(src, s.wg.at[z, y, c], to, y == r)

    def summed_at(base, rows):
        x = (s.pre3[pl.ds(base, rows), :] - s.bnp3[0:1]) * s.bnp3[1:2]
        return x, x * s.bnp3[2:3] + s.bnp3[3:4] + s.xh[pl.ds(base, rows), :].astype(F32)

    def block_step(base):
        _, v = summed_at(base, 32)
        s.blk[pl.ds(base, 32), :] = (gelu_of(v) * mask_at(base, 32, 1024)).astype(BF16)

    rows_loop(320, 32, block_step)
    line_core(go_wr, col_wr, cores_wr, odd)
    wait(cores_wr, jnp.logical_not(odd))
    wred = s.wr[...].reshape(1024, 512)
    s.rps[...] = dot(s.blk[pl.ds(other_rows, 160), :], wred).astype(BF16)
    red_x = ln.push(s.rps, s.rpr, xpeer)
    part = dot(s.blk[pl.ds(my_rows, 160), :], wred)
    wait([red_x])
    s.rbuf[pl.ds(own_px, 160), :] = (part + s.rpr[...].astype(F32)).astype(BF16)

    def block_of(rr, yy, cc, lo=0, n=160):
        return s.rbuf.at[pl.ds(pl.multiple_of(px_of(rr, yy, cc) + lo, 16), n)]

    for cp in near_late:
        cp.wait()
    own = block_of(r, y, c)
    g_x = ln.push(own, own, xpeer)
    g_y = ln.push(own, own, ypeer)
    g_c = ln.push(own, own, core)
    wait([g_x])
    relayed_h.append(task_relay(heads[2], s.wh))
    bx = block_of(1 - r, y, c, 0, 80)
    g_xy = ln.push(bx, bx, ypeer)
    wait([g_y])
    by = block_of(r, 1 - y, c, 80, 80)
    g_yx = ln.push(by, by, xpeer)
    bx = block_of(1 - r, y, c)
    g_c1 = ln.push(bx, bx, core)
    by = block_of(r, 1 - y, c)
    g_c2 = ln.push(by, by, core)
    relayed_h.append(task_relay(heads[3], s.wh))
    wait([g_xy, g_yx])
    bd = block_of(1 - r, 1 - y, c)
    g_c3 = ln.push(bd, bd, core)
    wait([over_m])
    staged_m = ln.near(s.st_m.at[:, :, pl.ds(fhalf, 256)], s.wq.at[:, z, 1 - y, c])
    mess[0].append(mess_push(0, True))
    mess.append([mess_push(1, False), mess_push(1, True)])
    mess.append([mess_push(2, False)])
    wait([g_c, g_c1, g_c2, g_c3])

    near_end = dev(jnp.where(z == 0, 1, 2), y, c, r)
    other_end = dev(jnp.where(z == 1, 3, 0), y, c, r)

    def grad_push(n, g, rm, lo, hi):
        def like(slot):
            return lambda side: rm.at[slot, lo:hi] if side else g.at[lo:hi, 0]

        got = {}
        for q in (1, 2, 3):
            direct = {1: not_last, 2: ends, 3: not_first}[q]
            got[q] = ln.push(g.at[lo:hi, zk(q)], rm.at[q - 1, lo:hi], dev(zk(q), y, c, r), direct, like(q - 1))
        hop = s.hop.at[n, lo:hi]
        got[0] = ln.push(
            g.at[lo:hi, 3 - z], hop, near_end, ends, lambda side: s.hop.at[n, lo:hi] if side else g.at[lo:hi, 0]
        )
        return got, n, g, rm, lo, hi

    def grad_hop(state):
        got, n, g, rm, lo, hi = state

        def add():
            got[0].wait_recv()
            far = jnp.where(z == 1, 3, 0)
            for t in range(lo, hi):
                s.hop[n, t] = (s.hop[n, t].astype(F32) + g[t, far].astype(F32)).astype(BF16)

        pl.when(inner)(add)
        got[4] = ln.push(
            s.hop.at[n, lo:hi], rm.at[1, lo:hi], other_end, inner,
            lambda side: rm.at[1, lo:hi] if side else s.hop.at[n, lo:hi],
        )

    def grad_wait(state):
        got = state[0]
        wait([got[1]], not_first)
        wait([got[3]], not_last)
        wait([got[2]], inner)
        wait([got[4]], ends)

    def tasks(r3, f3, d3, preh, dfull):
        spread(s.rbuf, r3, 4, 512)
        for part in relayed_h:
            task_ready(part)
        staged_h.wait()

        def head_step(i, carry):
            v = conv_rows(r3, s.wh, i)
            px = pl.multiple_of(i * 320, 16)
            preh[pl.ds(px, 320), :] = v
            return carry

        lax.fori_loop(0, 4, head_step, 0)

        def feat_step(base):
            m = lanes(s.maskp[pl.ds(base, 80), :], 256)
            s.fown[pl.ds(base, 80), :] = (gelu_of(preh[pl.ds(base, 80), :]) * m).astype(BF16)

        rows_loop(1280, 80, feat_step)
        f_c = ln.push(s.fown, s.ffull.at[:, pl.ds(fhalf, 256)], core)
        f_n = ln.near(s.fown, s.ffull.at[:, pl.ds(fhalf, 256)])

        def seven():
            return s.dmg.at[0:1120]

        def pieces(n):
            return lambda: s.dmg.at[0 : 160 * n]

        even = [o for o in offsets if (o[0] + o[1]) % 2 == 0]
        uneven = [o for o in offsets if (o[0] + o[1]) % 2]

        def to_owners(src, dst_of):
            got = [ln.group(pieces(len(o)), special) for o in (even, uneven)]
            for g, group in zip(got, (even, uneven)):
                for o in group:
                    rr, yy, cc = peer(*o)
                    g.push(src.at[pl.ds(px_of(rr, yy, cc), 160)], dst_of().at[:, pl.ds(fhalf, 256)], dev(z, yy, cc, rr), special)
            return got

        def from_tasks(got):
            wait([got[0]], special)
            wait([got[1]], plain)

        def to_tasks(src_of, dst):
            got = [ln.group(pieces(len(o)), w) for o, w in ((even, special), (uneven, plain))]
            for g, group, w in zip(got, (even, uneven), (special, plain)):
                for o in group:
                    rr, yy, cc = peer(*o)
                    ll = pl.ds(pl.multiple_of(256 * cc, 128), 256)
                    g.push(src_of(rr).at[:, ll], dst.at[pl.ds(own_px, 160)], dev(z, yy, cc, rr), w)
            return got

        def keep(dst, src):
            def run():
                dst[:, pl.ds(fhalf, 256)] = src[pl.ds(own_px, 160), :]

            return run

        pl.when(special)(keep(s.fg.at[r, 0], s.fown))
        f_n.wait()
        wait([f_c])

        def gate_ready():
            for cp in gate_got.values():
                cp.wait_recv()

        pl.when(special)(gate_ready)

        @pl.when(special)
        def _():
            def gate_step(base):
                v = dot(s.ffull[pl.ds(base, 320), :], s.wg[...].reshape(512, 256))
                s.gateb[pl.ds(base, 320), :] = (1.0 / (1.0 + jnp.exp(-v))).astype(BF16)

            rows_loop(1280, 320, gate_step)

        g_own = to_owners(s.gateb, lambda: s.fg.at[r, 1])
        pl.when(special)(keep(s.fg.at[r, 1], s.gateb))

        relayed = [[task_relay(p, s.wq) for p in mess[0]]]
        mess[2].append(mess_push(2, True))
        spread(s.ffull, f3, 4, 512)

        wait([cls_got])
        for i in range(2):
            s.ctf[...] = jnp.zeros((128, 128), F32)
            s.ctf[0:40, 0:80] = s.cct[i].astype(F32)
            turned = s.ctf[...].T
            s.ccotv[80 * i : 80 * i + 80, :] = turned[0:80, :].astype(BF16)
        from_tasks(g_own)

        def early_step(base):
            rows = pl.ds(base, 32)
            m = lanes(s.maskp[pl.ds(own_px + base, 32), :], 512)
            gd, gc = s.fg[0, 1, rows, :].astype(F32), s.fg[1, 1, rows, :].astype(F32)
            dj = (s.ccotv[rows, :].astype(F32) * m[:, :128]).astype(BF16)
            s.ccotv[rows, :] = dj
            dd = s.dcotv[rows, :].astype(F32) * m
            dmer = dot_last(dj, s.wc[...].reshape(512, 128))
            s.eu[0, rows, :] = dd.astype(BF16)
            s.eu[1, rows, :] = dmer.astype(BF16)
            down, up = dd * gd, dmer * gc
            both = (down + up).astype(BF16)
            s.dm[0, rows, :] = up.astype(BF16)
            s.dm[1, rows, :] = both
            s.dm[2, rows, :] = both
            s.dm[3, rows, :] = down.astype(BF16)

        rows_loop(160, 32, early_step)
        d_got = ln.group(seven)
        for o in offsets:
            rr, yy, cc = peer(*o)
            ll = pl.ds(pl.multiple_of(256 * cc, 128), 256)
            d_got.push(s.dm.at[2 * rr + yy, :, ll], s.dmg.at[pl.ds(own_px, 160)], dev(z, yy, cc, rr))
        s.dmg[pl.ds(own_px, 160), :] = s.dm[task, :, pl.ds(fhalf, 256)]

        @pl.when(special)
        def _():
            s.exg[0, pl.ds(own_px, 160), :] = s.eu[r, :, pl.ds(fhalf, 256)]

        @pl.when(jnp.logical_not(special))
        def _():
            s.exg[0] = jnp.zeros(s.exg.shape[1:], BF16)

        relayed.append([task_relay(p, s.wq) for p in mess[1]])

        def mess_conv(a):
            for p in relayed[a]:
                task_ready(p)

            def mess_step(i, carry):
                rows = pl.ds(pl.multiple_of(i * 320, 16), 320)
                base = pl.multiple_of((5 * i + a) * 80, 16)
                v = dot(f3[pl.ds(base, 320), :], s.wq[3 * a : 3 * a + 3].reshape(1536, 256))
                if a:
                    v = dfull[rows, 0:256] + v
                if a < 2:
                    dfull[rows, 0:256] = v
                else:
                    s.msgb[rows, :] = v.astype(BF16)
                return carry

            lax.fori_loop(0, 4, mess_step, 0)

        staged_m.wait()
        mess_conv(0)
        wait([d_got])
        f_own = to_owners(s.fown, lambda: s.fg.at[r, 0])
        u_got = to_tasks(lambda rr: s.eu.at[rr], s.exg.at[0])
        spread(s.dmg, d3, 4, 256)
        conv_weight(f3, d3, s.gm, 4, 0, 6)
        relayed.append([task_relay(p, s.wq) for p in mess[2]])
        gm_z = [grad_push(0, s.gm, s.rm, 0, 3), grad_push(0, s.gm, s.rm, 3, 6)]
        mess_conv(1)
        conv_weight(f3, d3, s.gm, 4, 6, 9)
        gm_z.append(grad_push(0, s.gm, s.rm, 6, 9))
        mess_conv(2)
        m_own = ln.group(seven)
        for o in offsets:
            rr, yy, cc = peer(*o)
            m_own.push(s.msgb.at[pl.ds(px_of(rr, yy, cc), 160)], s.mrecv.at[task, :, pl.ds(fhalf, 256)], dev(z, yy, cc, rr))
        keep(s.mrecv.at[task], s.msgb)()

        def back_step(i, carry):
            px = pl.multiple_of(i * 320, 16)
            dfull[pl.ds(px, 320), :] = conv_back(d3, s.wq, i)
            return carry

        lax.fori_loop(0, 4, back_step, 0)

        from_tasks(f_own)
        wait([m_own])

        def stream_step(base):
            rows = pl.ds(base, 32)
            m = lanes(s.maskp[pl.ds(own_px + base, 32), :], 512)
            m0, m1, m2, m3 = (s.mrecv[t, rows, :].astype(F32) for t in range(4))
            f0, f3_ = s.fg[0, 0, rows, :].astype(F32), s.fg[1, 0, rows, :].astype(F32)
            mid = m1 + m2
            sd, sc = mid + m3, m0 + mid
            gd, gc = s.fg[0, 1, rows, :].astype(F32), s.fg[1, 1, rows, :].astype(F32)
            s.ods[rows, :] = ((f0 + gd * sd) * m).astype(BF16)
            merged = (f3_ + gc * sc).astype(BF16)
            s.mrg[rows, :] = merged
            s.olg[rows, :] = (dot(merged, s.wc[...].reshape(512, 128)) * m[:, :128]).astype(BF16)
            dd, dmer = s.eu[0, rows, :].astype(F32), s.eu[1, rows, :].astype(F32)
            s.fg[0, 1, rows, :] = (dd * sd * gd * (1.0 - gd)).astype(BF16)
            s.fg[1, 1, rows, :] = (dmer * sc * gc * (1.0 - gc)).astype(BF16)

        rows_loop(160, 32, stream_step)
        e_got = to_tasks(lambda rr: s.fg.at[rr, 1], s.exg.at[1])

        @pl.when(special)
        def _():
            s.exg[1, pl.ds(own_px, 160), :] = s.fg[r, 1, :, pl.ds(fhalf, 256)]

        for i in range(2):
            s.ctf[...] = jnp.zeros((128, 128), F32)
            s.ctf[0:80, :] = s.olg[80 * i : 80 * i + 80, :].astype(F32)
            turned = s.ctf[...].T
            s.olt[i] = turned[0:40, 0:80].astype(BF16)
        out_near = [ln.near(s.ods, s.o_depth), ln.near(s.olt, s.o_logits)]
        s.gcls[...] = dot_first(s.mrg[...], s.ccotv[...]).astype(BF16).reshape(16, 32, 128)
        grad_hop(gm_z[0])
        wait(u_got + e_got, special)

        @pl.when(special)
        def _():
            def gate_back(base):
                rows = pl.ds(base, 320)
                dfull[rows, :] = dfull[rows, :] + dot_last(s.exg[1, rows, :], s.wg[...].reshape(512, 256))

            rows_loop(1280, 320, gate_back)

        chalf = pl.ds(pl.multiple_of(256 * (1 - c), 128), 256)

        def give(base):
            rows = pl.ds(base, 80)
            s.dfs[rows, :] = dfull[rows, chalf].astype(BF16)

        rows_loop(1280, 80, give)
        df_c = ln.push(s.dfs, s.dfr, core)

        @pl.when(special)
        def _():
            s.gg[...] = dot_first(s.ffull[...], s.exg[1]).astype(BF16).reshape(s.gg.shape)

        gg_z = [ln.push(s.gg.at[zk(k)], s.rg.at[k - 1], dev(zk(k), y, c, r), special, lambda side, k=k: s.rg.at[k - 1] if side else s.gg.at[0]) for k in (1, 2, 3)]
        cg = ln.group(lambda: s.rcls)
        n_cls = 0
        for q in range(4):
            for j in range(2):
                for i in range(2):
                    if q + j + i == 0:
                        continue
                    yy = 1 - y if j else y
                    cc = 1 - c if i else c
                    zz = zk(q) if q else z
                    cg.push(s.gcls.at[4 * zz + 2 * yy + cc], s.rcls.at[n_cls], dev(zz, yy, cc, r))
                    n_cls += 1
        wait([df_c])

        def dhead_step(base):
            rows = pl.ds(base, 80)
            m = lanes(s.maskp[rows, :], 256)
            d = dfull[rows, pl.ds(fhalf, 256)] + s.dfr[rows, :].astype(F32) + s.exg[0, rows, :].astype(F32)
            s.dmg[rows, :] = (slope_of(preh[rows, :]) * d * m).astype(BF16)

        rows_loop(1280, 80, dhead_step)
        spread(s.dmg, d3, 4, 256)

        def back_step2(i, carry):
            px = pl.multiple_of(i * 320, 16)
            dfull[pl.ds(px, 320), :] = conv_back(d3, s.wh, i)
            return carry

        lax.fori_loop(0, 4, back_step2, 0)
        for yy in range(2):
            src = pl.multiple_of(320 * (2 * yy) + 320 * (1 - c), 16)
            s.drs[pl.ds(320 * yy, 320), :] = dfull[pl.ds(src, 320), :].astype(BF16)
        dr_c = ln.push(s.drs, s.drr, core)
        grad_hop(gm_z[1])
        wait([dr_c])
        for yy in range(2):
            src = pl.multiple_of(320 * (2 * yy) + 320 * c, 16)
            rows = pl.ds(320 * yy, 320)
            s.drr[rows, :] = (dfull[pl.ds(src, 320), :] + s.drr[rows, :].astype(F32)).astype(BF16)
        ro = []
        for dr, dy in ((1, 0), (0, 1), (1, 1)):
            rr, yy, _ = peer(dr, dy, 0)
            src = s.drr.at[pl.ds(pl.multiple_of(320 * yy + 160 * rr, 16), 160)]
            ro.append(ln.push(src, s.dro.at[len(ro)], dev(z, yy, c, rr)))
        gh_z = []
        conv_weight(r3, d3, s.gh, 4, 0, 3)
        gh_z.append(grad_push(1, s.gh, s.rh, 0, 3))
        conv_weight(r3, d3, s.gh, 4, 3, 9)
        wait(ro)
        keep_rows = pl.ds(pl.multiple_of(320 * y + 160 * r, 16), 160)
        total_red = s.drr[keep_rows, :].astype(F32)
        for i in range(3):
            total_red = total_red + s.dro[i].astype(F32)
        s.dred[pl.ds(my_rows, 160), :] = total_red.astype(BF16)
        for cp in out_near:
            cp.wait()
        ln.drain(scoped=True)
        return cg, gm_z, gg_z, gh_z

    state = {}

    def scope_tasks(*scr):
        state["t"] = tasks(*scr)

    pl.run_scoped(
        scope_tasks,
        pltpu.VMEM((1680, 1536), BF16),
        pltpu.VMEM((1680, 1536), BF16),
        pltpu.VMEM((1680, 768), BF16),
        pltpu.VMEM((1280, 256), F32),
        pltpu.VMEM((1280, 512), F32),
    )
    cg, gm_z, gg_z, gh_z = state["t"]

    dr_x = ln.push(s.dred.at[pl.ds(my_rows, 160)], s.dred.at[pl.ds(my_rows, 160)], xpeer)

    def block_back(*late):
        for name, ref in zip(LATE, late):
            setattr(s, name, ref)
        gr, gl, gq, gf = s.gr, s.gl, s.gq, s.gf

        def to_core(g, rc, lead):
            at = g.at[:, :, :, 1 - c] if lead else g.at[:, :, 1 - c]
            return ln.push(at, rc, core)

        def add_core(g, rc, lead):
            if lead:
                for t in range(9):
                    rc[t] = (rc[t].astype(F32) + g[t, :, :, c].astype(F32)).astype(BF16)
            else:
                for t in range(rc.shape[0]):
                    rc[t] = (rc[t].astype(F32) + g[t, :, c].astype(F32)).astype(BF16)

        def to_y(rc, ry, lead):
            return ln.push(rc.at[:, :, 1 - y] if lead else rc.at[:, 1 - y], ry, ypeer)

        def add_y(rc, ry, lead):
            for t in range(ry.shape[0]):
                mine_y = rc[t, :, y] if lead else rc[t, y]
                ry[t] = (ry[t].astype(F32) + mine_y.astype(F32)).astype(BF16)

        def to_z(ry, rz, lead, when=None, hop=None):
            def part(zz):
                return ry.at[:, zz] if lead else ry.at[zz]

            got = {}
            for q in (1, 2, 3):
                direct = None if hop is None else {1: not_last, 2: ends, 3: not_first}[q]
                got[q] = ln.push(part(zk(q)), rz.at[q - 1], dev(zk(q), y, c, r), both(when, direct))
            if hop is not None:
                got[0] = ln.push(part(3 - z), hop, near_end, both(when, ends))
            return got, part, rz, hop, when

        def hop_z(state):
            got, part, rz, hop, when = state

            def add():
                got[0].wait_recv()
                hop[...] = (hop[...].astype(F32) + part(jnp.where(z == 1, 3, 0))[...].astype(F32)).astype(BF16)

            pl.when(both(when, inner))(add)
            got[4] = ln.push(hop, rz.at[1], other_end, both(when, inner))

        def wait_z(state):
            got, _, _, hop, when = state
            if hop is None:
                wait([got[1], got[2], got[3]], when)
            else:
                wait([got[1]], both(when, not_first))
                wait([got[3]], both(when, not_last))
                wait([got[2]], both(when, inner))
                wait([got[4]], both(when, ends))

        def add_z(ry, rz, fin, lead, hop=True):
            mine_z = (ry[:, z] if lead else ry[z]).astype(F32)
            v0, v2 = rz[0].astype(F32), rz[2].astype(F32)
            if hop:
                v0, v2 = jnp.where(z == 0, 0.0, v0), jnp.where(z == 3, 0.0, v2)
            fin[...] = ((mine_z + v0) + (rz[1].astype(F32) + v2)).astype(BF16)

        def task_out(states, rm, g, ps, out):
            for part in states:
                grad_wait(part)
            loads = [[ln.near(rm.at[q, 3 * part : 3 * part + 3], s.zst.at[part % 2, q]) for q in range(3)] for part in range(2)]
            for part in range(3):
                for cp in loads[part]:
                    cp.wait()
                v0 = s.zst.at[part % 2]
                for t in range(3):
                    first_in = jnp.where(z == 0, 0.0, v0[0, t].astype(F32))
                    third_in = jnp.where(z == 3, 0.0, v0[2, t].astype(F32))
                    v = g[3 * part + t, z].astype(F32) + first_in + (v0[1, t].astype(F32) + third_in)
                    ps[3 * part + t] = v.astype(BF16)
                if part == 0:
                    loads.append([ln.near(rm.at[q, 6:9], s.zst.at[0, q]) for q in range(3)])
            lanes_out = pl.ds(fhalf, 256)
            sent = []
            for i in (1, 2, 3):
                yy = 1 - y if i & 2 else y
                cc = 1 - c if i & 1 else c
                sent.append(ln.push(ps.at[:, yy, cc], out.at[y, :, :, lanes_out], dev(z, yy, cc, r)))
            return sent, ln.near(ps.at[:, y, c], out.at[y, :, :, lanes_out])

        wait([dr_x])

        def d3_step(i, carry):
            su, sux = carry
            rows = pl.ds(pl.multiple_of(i * 32, 16), 32)
            x, v = summed_at(i * 32, 32)
            u = slope_of(v) * s.u3[rows, :] * mask_at(i * 32, 32, 1024)
            s.u3[rows, :] = u
            s.dsum[rows, :] = u.astype(BF16)
            return su + jnp.sum(u, axis=0, keepdims=True), sux + jnp.sum(u * x, axis=0, keepdims=True)

        s.u3[...] = dot_last(s.dred[...], s.wr[...].reshape(1024, 512))
        nil = jnp.zeros((1, 1024), F32)
        su, sux = lax.fori_loop(0, 10, d3_step, (nil, nil))
        put_stats(3, su, sux, 1024, None)
        ar3 = plane_start(3)
        ds_x = ln.push(s.dsum.at[pl.ds(other_rows, 160)], s.dsr, xpeer)
        grad_hop(gm_z[2])
        gr[...] = dot_first(s.blk[...], s.dred[...]).astype(BF16).reshape(gr.shape)
        gr_c = ln.push(gr, s.rcr, core, jnp.logical_not(odd))
        plane_end(3, ar3)
        t = reduce_line(3, lambda: gh_z.append(grad_push(1, s.gh, s.rh, 3, 6)))
        gs3 = ln.push(s.at3, s.o_gs3.at[r], xpeer)
        gs3n = ln.near(s.at3, s.o_gs3.at[r])
        mu = jnp.concatenate([t[0:1], t[1:2]], axis=1) / count
        mux = jnp.concatenate([t[2:3], t[3:4]], axis=1) / count

        def dp3_step(base):
            rows = pl.ds(base, 32)
            x = (s.pre3[rows, :] - s.bnp3[0:1]) * s.bnp3[1:2]
            d = mask_at(base, 32, 1024) * (s.bnp3[2:3] * s.bnp3[1:2]) * (s.u3[rows, :] - mu - x * mux)
            s.dp3[rows, :] = d.astype(BF16)

        rows_loop(320, 32, dp3_step)

        def partial_out(pas, value_of):
            pas[...] = value_of(ohalf).astype(BF16)

        wlast = s.wl
        s.u3[:, 0:512] = dot_last(s.dp3[...], wlast[...].reshape(512, 1024))
        s.pas2[...] = s.u3[:, pl.ds(ohalf, 256)].astype(BF16)
        pa2 = ln.push(s.pas2, s.par2, xpeer)
        gl[...] = dot_first(s.a2[...], s.dp3[...]).astype(BF16).reshape(gl.shape)
        gl_c = to_core(gl, s.rcl, False)
        wait([gr_c], odd)

        @pl.when(odd)
        def _():
            for q in range(4):
                s.rcr[q] = (s.rcr[q].astype(F32) + gr[q].astype(F32)).astype(BF16)

        later = {"gr_y": ln.push(s.rcr.at[:, 1 - y], s.ryr, ypeer, odd)}

        def after_plane_two():
            wait([gl_c])
            add_core(gl, s.rcl, False)
            later["gl_y"] = to_y(s.rcl, s.ryl, False)

        def after_plane_one():
            wait([gq_c])
            add_core(gq, s.rcm, True)
            later["gq_y"] = [
                ln.push(s.rcm.at[3 * a : 3 * a + 3, :, 1 - y], s.rym.at[3 * a : 3 * a + 3], ypeer) for a in range(3)
            ]

        wait([pa2])

        def norm_back(n, par, prebuf, bnp, dst, out_gs, middle, after):
            def u_step(i, carry):
                su_, sux_ = carry
                base = pl.multiple_of(i * 80, 16)
                rows = pl.ds(base, 80)
                x = (prebuf[rows, :] - bnp[0:1]) * bnp[1:2]
                v = x * bnp[2:3] + bnp[3:4]
                d = s.u3[rows, pl.ds(half, 256)] + par[rows, :].astype(F32)
                u = slope_of(v) * d * mask_at(base, 80, 256)
                s.u3[rows, 512:768] = u
                return su_ + jnp.sum(u, axis=0, keepdims=True), sux_ + jnp.sum(u * x, axis=0, keepdims=True)

            nil_ = jnp.zeros((1, 256), F32)
            su_, sux_ = lax.fori_loop(0, 4, u_step, (nil_, nil_))
            put_stats(n, su_, sux_, 256, None)
            reduce_plane(n)

            def bulk():
                middle()
                after()

            t_ = reduce_line(n, bulk)
            gsx = ln.push(getattr(s, "at%d" % n), out_gs.at[r], xpeer)
            gsn = ln.near(getattr(s, "at%d" % n), out_gs.at[r])
            mu_, mux_ = t_[0:1] / count, t_[1:2] / count

            def d_step(base):
                rows = pl.ds(base, 80)
                x = (prebuf[rows, :] - bnp[0:1]) * bnp[1:2]
                d = mask_at(base, 80, 256) * (bnp[2:3] * bnp[1:2]) * (s.u3[rows, 512:768] - mu_ - x * mux_)
                dst[rows, :] = d.astype(BF16)

            rows_loop(320, 80, d_step)
            return gsx, gsn

        def window_two():
            grad_hop(gh_z[0])
            gh_z.append(grad_push(1, s.gh, s.rh, 6, 9))
            later["mess"] = task_out(gm_z, s.rm, s.gm, s.psm, s.o_mess)

        def window_one():
            grad_hop(gh_z[1])
            wait([later["gr_y"]], odd)

            @pl.when(odd)
            def _():
                for q in range(4):
                    s.ryr[q] = (s.ryr[q].astype(F32) + s.rcr[q, y].astype(F32)).astype(BF16)

            later["gr_z"] = to_z(s.ryr, s.rzr, False, odd, s.hpr)
            wait([later["gl_y"]])
            add_y(s.rcl, s.ryl, False)
            later["gl_z"] = to_z(s.ryl, s.rzl, False, None, s.hpl)

        gs2, gs2n = norm_back(4, s.par2, s.pre2, s.bnp2, s.dp2, s.o_gs2, after_plane_two, window_two)
        spread(s.dp2, s.d3m, 1, 256)
        s.u3[:, 0:512] = conv_back(s.d3m, s.wm, 0)
        s.pas1[...] = s.u3[:, pl.ds(ohalf, 256)].astype(BF16)
        pa1 = ln.push(s.pas1, s.par1, xpeer)
        conv_weight(s.a3, s.d3m, gq, 1, 0, 9)
        gq_c = to_core(gq, s.rcm, True)
        wait([pa1])
        gs1, gs1n = norm_back(5, s.par1, s.pre1, s.bnp1, s.dp1, s.o_gs1, after_plane_one, window_one)
        dp_x = ln.push(s.dp1.at[pl.ds(other_rows, 160)], s.dp1r, xpeer)
        gf[...] = dot_first(s.xall[...], s.dp1[...]).astype(BF16).reshape(gf.shape)
        gf_c = to_core(gf, s.rcf, False)
        wait([gf_c])
        add_core(gf, s.rcf, False)
        gf_y = to_y(s.rcf, s.ryf, False)
        ms, mn = later["mess"]
        gr_z, gl_z = later["gr_z"], later["gl_z"]
        grad_hop(gh_z[2])
        gq_z = []
        for a in range(3):
            wait([later["gq_y"][a]])
            for t in range(3 * a, 3 * a + 3):
                s.rym[t] = (s.rym[t].astype(F32) + s.rcm[t, :, y].astype(F32)).astype(BF16)
            lead = slice(3 * a, 3 * a + 3)
            rz = SimpleNamespace(at=[s.rzm.at[q, lead] for q in range(3)])
            gq_z.append(to_z(s.rym.at[lead], rz, True, None, s.hpm.at[lead]))
            if a == 0:
                hop_z(gr_z)
                hop_z(gl_z)
            else:
                hop_z(gq_z[a - 1])
        wait([gf_y])
        add_y(s.rcf, s.ryf, False)
        gf_z = to_z(s.ryf, s.rzf, False, None, s.hpf)

        hs, hn = task_out(gh_z, s.rh, s.gh, s.psh, s.o_heads)
        wait([wfo_x])
        wfo_n = ln.near(s.wfo, s.wfov)
        wait([dp_x, ds_x])
        wfo_n.wait()
        mine_d = s.dp1[pl.ds(my_rows, 160), :]
        other_d = s.dp1r[...]
        for q in range(2):
            cols = slice(1024 * q, 1024 * q + 1024)
            wa = s.wf[2 * q : 2 * q + 2].reshape(1024, 256)
            wb = s.wfov[2 * q : 2 * q + 2].reshape(1024, 256)
            s.u3[pl.ds(0, 160), :] = dot_last(mine_d, wa) + dot_last(other_d, wb)

            def img_step(base):
                rows = pl.ds(base, 32)
                m = mask_at(my_rows + base, 32, 1024)
                own_d = s.dsum[pl.ds(my_rows + base, 32), 512 * q : 512 * q + 512].astype(F32)
                far_d = s.dsr[rows, 512 * q : 512 * q + 512].astype(F32)
                d = jnp.concatenate(
                    [
                        jnp.where(r == j % 2, own_d[:, 64 * (j - j % 2) :][:, :128], far_d[:, 64 * (j - j % 2) :][:, :128])
                        for j in range(8)
                    ],
                    axis=1,
                )
                s.oimg[rows, cols] = ((s.u3[rows, :] + d) * m).astype(BF16)

            rows_loop(160, 32, img_step)
        img_n = ln.near(s.oimg, s.o_img)
        hop_z(gq_z[2])

        hop_z(gf_z)

        @pl.when(special)
        def _():
            for cp in gg_z:
                cp.wait_recv()
            v = (s.gg[z].astype(F32) + s.rg[0].astype(F32)) + (s.rg[1].astype(F32) + s.rg[2].astype(F32))
            s.pg[...] = v.astype(BF16)

        gx = [ln.group(lambda n=n: s.wg.at[0:3, 0, 0] if n == 3 else s.wg.at[0:4, 0, 0], special) for n in (3, 4)]
        for g, odd_one in zip(gx, (0, 1)):
            for o in offsets:
                if (o[0] + o[1]) % 2 == odd_one:
                    rr, yy, cc = peer(*o)
                    g.push(s.pg.at[yy, cc], s.o_gates.at[r, :, pl.ds(fhalf, 256)], dev(z, yy, cc, rr), special)
        gate_near = pltpu.make_async_copy(
            s.pg.at[y, c], s.o_gates.at[r, :, pl.ds(fhalf, 256)], s.near_sems.at[NEAR - 2]
        )
        pl.when(special)(gate_near.start)

        wait([cg])
        v = s.gcls[b].astype(F32)
        for i in range(15):
            v = v + s.rcls[i].astype(F32)
        s.clss[...] = v
        cls_x = ln.push(s.clss, s.clsr, xpeer)

        wait_z(gr_z)
        pl.when(odd)(lambda: add_z(s.ryr, s.rzr, s.fnr, False))
        gr_x = ln.push(s.fnr, s.o_red, xpeer, odd)
        red_near = pltpu.make_async_copy(s.fnr, s.o_red, s.near_sems.at[NEAR - 3])
        pl.when(odd)(red_near.start)
        wait_z(gl_z)
        add_z(s.ryl, s.rzl, s.fnl, False)
        gl_x = ln.push(s.fnl, s.o_last.at[r], xpeer)
        n1 = ln.near(s.fnl, s.o_last.at[r])
        for a in range(3):
            wait_z(gq_z[a])
            lead = slice(3 * a, 3 * a + 3)
            add_z(s.rym.at[lead], s.rzm.at[:, lead], s.fnm.at[lead], True)
        gq_x = ln.push(s.fnm, s.o_mid.at[:, :, pl.ds(half, 256)], xpeer)
        n2 = ln.near(s.fnm, s.o_mid.at[:, :, pl.ds(half, 256)])
        wait_z(gf_z)
        add_z(s.ryf, s.rzf, s.fnf, False)
        gf_x = ln.push(s.fnf, s.o_first.at[:, pl.ds(half, 256)], xpeer)
        n3 = ln.near(s.fnf, s.o_first.at[:, pl.ds(half, 256)])
        wait([cls_x])
        s.clso[...] = s.clss[...] + s.clsr[...]
        n4 = ln.near(s.clso, s.o_cls)
        wait([gr_x], jnp.logical_not(odd))
        wait([gl_x, gq_x, gf_x, gs1, gs2, gs3])
        wait(ms + hs)
        wait([gx[0]], special)
        wait([gx[1]], plain)
        pl.when(special)(gate_near.wait)
        pl.when(odd)(red_near.wait)
        for cp in (gs1n, gs2n, gs3n, img_n, mn, hn, n1, n2, n3, n4):
            cp.wait()
        ln.drain()

    pl.run_scoped(block_back, *[pltpu.VMEM(*v) for v in LATE.values()])


LATE = dict(
    zst=((2, 3, 3, 2, 2, 32, 256), BF16),
    psm=((9, 2, 2, 32, 256), BF16),
    psh=((9, 2, 2, 32, 256), BF16),
    fnr=((128, 512), BF16),
    fnl=((32, 1024), BF16),
    fnm=((9, 32, 256), BF16),
    fnf=((128, 256), BF16),
    pg=((2, 2, 32, 256), BF16),
    clss=((32, 128), F32),
    clso=((32, 128), F32),
    u3=((320, 1024), F32),
    dp3=((320, 1024), BF16),
    d3m=((480, 768), BF16),
    dsum=((320, 1024), BF16),
    oimg=((160, 2048), BF16),
    pas1=((320, 256), BF16),
    pas2=((320, 256), BF16),
    dp1=((320, 256), BF16),
    dp2=((320, 256), BF16),
    wfov=((4, 2, 2, 128, 256), BF16),
    gr=((4, 2, 128, 512), BF16),
    gl=((4, 2, 2, 32, 1024), BF16),
    gq=((9, 4, 2, 2, 32, 256), BF16),
    gf=((4, 2, 2, 128, 256), BF16),
)


FINAL = dict(
    depth=((160, 512), BF16),
    logits=((2, 40, 80), BF16),
    img=((160, 2048), F32),
    first=((128, 512), F32),
    gain1=((1, 32), F32),
    shift1=((1, 32), F32),
    mid=((9, 32, 512), F32),
    gain2=((1, 32), F32),
    shift2=((1, 32), F32),
    last=((32, 2048), F32),
    gain3=((1, 128), F32),
    shift3=((1, 128), F32),
    red=((128, 512), F32),
    heads=((2, 9, 32, 512), F32),
    mess=((2, 9, 32, 512), F32),
    gates=((2, 32, 512), F32),
    cls=((32, 40), F32),
)


def widen_out(names, *refs):
    s = SimpleNamespace(**dict(zip(names, refs)))
    b = lax.axis_index("batch")
    used = [0]

    def move(src, dst):
        cp = pltpu.make_async_copy(src, dst, s.sems.at[used[0]])
        used[0] += 1
        cp.start()
        return cp

    wide = [("img", slice(lo, lo + n)) for lo, n in ((0, 64), (64, 48), (112, 48))]
    wide += [(n, slice(i, i + 1)) for n in ("mess", "heads") for i in range(2)]
    wide += [("mid", slice(0, 9)), ("red", slice(0, 128)), ("first", slice(0, 128)), ("last", slice(0, 2)), ("gates", slice(0, 2))]
    loads = [move(getattr(s, "o_" + n).at[at], getattr(s, "i_" + n).at[at]) for n, at in wide]
    small = [move(getattr(s, "o_" + n), getattr(s, "i_" + n)) for n in ("gs1", "gs2", "gs3", "cls")]
    done = []
    narrow = [move(s.o_depth, s.i_depth), move(s.o_logits, s.i_logits)]
    for (n, at), cp in zip(wide, loads):
        cp.wait()
        src, dst = getattr(s, "i_" + n), getattr(s, "v_" + n)
        if n == "last":
            for i in range(8):
                for h in range(2):
                    lane = 128 * (2 * i + h)
                    dst[:, lane : lane + 128] = src[h, :, 128 * i : 128 * i + 128].astype(F32)
            done.append(move(dst, s.last))
            continue
        if n in ("mess", "heads"):
            for t in range(9):
                dst[at.start, t] = src[at.start, t].astype(F32)
        elif len(src.shape) > 2:
            for t in range(at.start, at.stop):
                dst[t] = src[t].astype(F32)
        else:
            dst[at] = src[at].astype(F32)
        done.append(move(dst.at[at], getattr(s, n).at[at]))
    for cp in narrow:
        cp.wait()
    done += [move(s.i_depth, s.depth), move(s.i_logits, s.logits)]
    for cp in small:
        cp.wait()
    quarter, spot = lax.div(b, np.int32(4)), lax.rem(b, np.int32(4))
    at = pl.ds(pl.multiple_of(128 * lax.rem(quarter, np.int32(2)), 128), 128)
    for n, layer in ((1, s.i_gs1), (2, s.i_gs2)):
        v = pltpu.roll(layer[lax.div(quarter, np.int32(2)), :, at], lax.rem(128 - 32 * spot, np.int32(128)), 1)
        for row, kind in ((1, "gain"), (0, "shift")):
            keep = getattr(s, "v_%s%d" % (kind, n))
            keep[...] = v[row : row + 1, 0:32]
            done.append(move(keep, getattr(s, "%s%d" % (kind, n))))
    block = lax.div(b, np.int32(2))
    at = pl.ds(pl.multiple_of(128 * lax.rem(block, np.int32(4)), 128), 128)
    v = s.i_gs3[lax.rem(b, np.int32(2)), :, at]
    low = lax.div(block, np.int32(4)) == 0
    s.v_shift3[...] = jnp.where(low, v[0:1], v[1:2])
    s.v_gain3[...] = jnp.where(low, v[2:3], v[3:4])
    done.append(move(s.v_shift3, s.shift3))
    done.append(move(s.v_gain3, s.gain3))
    s.v_cls[...] = s.i_cls[:, 0:40]
    done.append(move(s.v_cls, s.cls))
    for cp in done:
        cp.wait()


def fast(args):
    (
        images, crop_height, crop_width, w_first, gain_first, shift_first, w_middle, gain_middle, shift_middle,
        w_last, gain_last, shift_last, w_reduce, w_heads, w_message, w_gates, w_classes, depth_cot, class_cot,
    ) = args
    ins = (
        crop_height, crop_width, images.reshape(160, 2048), w_first, w_middle, w_last, w_reduce, w_gates, w_classes,
        w_heads, w_message, *(v.reshape(1, -1) for v in (gain_first, shift_first, gain_middle, shift_middle, gain_last, shift_last)), depth_cot.reshape(160, 512), class_cot.transpose(0, 1, 3, 2).reshape(2, 40, 80),
    )
    names = list(INS) + list(OUTS) + list(SHAPES) + ["send_sems", "recv_sems", "near_sems"]
    smem, hbm, vmem = (pl.BlockSpec(memory_space=m) for m in (pltpu.SMEM, pltpu.HBM, pltpu.VMEM))
    spec = {"crop_h": smem, "crop_w": smem}
    spec.update({n: vmem for n in INS if n[:4] in ("gain", "shif")})
    outs = pl.pallas_call(
        functools.partial(body, names),
        out_shape=[jax.ShapeDtypeStruct(*v) for v in OUTS.values()],
        in_specs=[spec.get(n, hbm) for n in INS],
        out_specs=[hbm] * len(OUTS),
        scratch_shapes=[pltpu.VMEM(*v) for v in SHAPES.values()]
        + [pltpu.SemaphoreType.DMA((n,)) for n in (SENDS, RECVS, NEAR)],
        compiler_params=pltpu.CompilerParams(has_side_effects=True, collective_id=0, vmem_limit_bytes=64 * 2**20),
        name="residual_distill",
    )(*ins)
    o = dict(zip(OUTS, outs))
    taken = [n for n in OUTS if n.startswith("o_")]
    staged = {"i_" + n[2:]: OUTS[n] for n in taken}
    staged.update({"v_" + n: v for n, v in FINAL.items() if n not in ("depth", "logits")})
    final = pl.pallas_call(
        functools.partial(widen_out, taken + list(FINAL) + list(staged) + ["sems"]),
        out_shape=[jax.ShapeDtypeStruct(*v) for v in FINAL.values()],
        in_specs=[hbm] * len(taken),
        out_specs=[hbm] * len(FINAL),
        scratch_shapes=[pltpu.VMEM(*v) for v in staged.values()] + [pltpu.SemaphoreType.DMA((41,))],
        compiler_params=pltpu.CompilerParams(vmem_limit_bytes=64 * 2**20),
        name="widen_out",
    )(*[o[n] for n in taken])
    f = dict(zip(FINAL, final))
    f["depth"] = f["depth"].reshape(1, 2, 80, 512)
    f["logits"] = f["logits"].reshape(1, 2, 40, 80).transpose(0, 1, 3, 2)
    f["img"] = f["img"].reshape(1, 2, 80, 2048)
    for n in ("gain1", "shift1", "gain2", "shift2", "gain3", "shift3"):
        f[n] = f[n].reshape(-1)
    return tuple(f.values())


def solution(mesh):
    def step(*args):
        if mesh.shape["batch"] == 16 and mesh.shape["rows"] == 2:
            return fast(args)
        return shards(*args)

    placed = (
        P("batch", "rows", None, None),
        P(),
        P(),
        P("batch", None),
        P("batch"),
        P("batch"),
        P(None, "batch", None),
        P("batch"),
        P("batch"),
        P("batch", None),
        P("batch"),
        P("batch"),
        P("batch", None),
        P("rows", None, "batch", None),
        P("rows", None, "batch", None),
        P(None, "batch", None),
        P("batch", None),
        P("batch", "rows", None, None),
        P("batch", "rows", None, None),
    )
    return jax.shard_map(
        step,
        mesh=mesh,
        in_specs=placed,
        out_specs=(
            P("batch", "rows", None, None),
            P("batch", "rows", None, None),
            P("batch", "rows", None, None),
            P("batch", None),
            P("batch"),
            P("batch"),
            P(None, "batch", None),
            P("batch"),
            P("batch"),
            P("batch", None),
            P("batch"),
            P("batch"),
            P("batch", None),
            P("rows", None, "batch", None),
            P("rows", None, "batch", None),
            P(None, "batch", None),
            P("batch", None),
        ),
        check_vma=False,
    )
```
